256 devices in a mesh: ctx: 32 (over y_hi, z, core), dp: 8 (over y_lo, x).
Axes of the slice: x: 4, y: 4 (y_hi: 2, y_lo: 2; y = y_hi * 2 + y_lo), z: 8, core: 2. Of those that a mesh axis runs over, the one named last changes fastest.
Arguments:
- inputs: bfloat16 [8, 4096, 2048], P('dp', 'ctx'), may hold values from -6 to 6
- gate_weight: bfloat16 [256, 2, 8, 256], P('ctx'), may hold values from -0.375 to 0.375
- gate_bias: float32 [2, 2048], replicated, may hold values from -4 to 4
- decay_param: float32 [2048], replicated, may hold values from 4 to 14
- conv_weight: float32 [4, 2048], replicated, may hold values from -3 to 3
- conv_bias: float32 [2048], replicated, may hold values from -3 to 3
- cotangent: bfloat16 [8, 4096, 2048], P('dp', 'ctx'), may hold values from -6 to 6
Outputs:
- grad_input: bfloat16 [8, 4096, 2048], P('dp', 'ctx')
- grad_gate_weight: float32 [256, 2, 8, 256], P('ctx')
- grad_decay: float32 [2048], replicated
- grad_gate_bias: float32 [2, 2048], replicated
- grad_conv_weight: float32 [4, 2048], replicated
- grad_conv_bias: float32 [2048], replicated
The draws below stay inside these ranges and needn't reach their ends.
All inputs are finite; a program needn't handle non-finite values.
Results may differ from the reference program's by a relative error of at most 0.015.
Values may be sent and summed in bfloat16 or wider, within the bound.
A program may use at most 64 MiB of HBM per device.

```python
import jax
import jax.numpy as jnp
from jax import lax

WIDTH = 2048
BLOCK_W = 256
TAPS = 4
BLOCKS = 8
SEQS = 8
TOKENS = 4096


def draw_decay_param(key, part):
    key = jax.random.fold_in(key, 7)
    return jax.random.uniform(key, (WIDTH,), jnp.float32, 4.0, 14.0)


def block_scale(key, shape, pieces, smallest, largest):
    def one(dim, shards_of):
        heights = jax.random.uniform(jax.random.fold_in(jax.random.fold_in(key, 6), dim), (shards_of,), jnp.float32, smallest / len(pieces), largest / len(pieces))
        return jnp.repeat(jnp.exp(heights), shape[dim] // shards_of).reshape((-1,) + (1,) * (len(shape) - dim - 1))

    loudness = one(*pieces[0])
    for cut in pieces[1:]:
        loudness = loudness * one(*cut)
    return loudness


def noise(own_key, extent, width, reach, shards=(), kind=jnp.bfloat16):
    values = width * jax.random.normal(own_key, extent, jnp.float32)
    if shards:
        values = values * block_scale(own_key, extent, shards, -0.22, 0.18)
    return jnp.clip(values, -reach, reach).astype(kind)


def setup_inputs(seed: int = 0) -> dict:
    key_list = jax.random.split(jax.random.key(seed), 8)
    return {
        "inputs": noise(key_list[0], (SEQS, TOKENS, WIDTH), 1.0, 6.0, ((0, 8), (1, 32))),
        "gate_weight": noise(key_list[1], (BLOCK_W, 2, BLOCKS, BLOCK_W), BLOCK_W ** -0.5, 0.375, ((0, 32),)),
        "gate_bias": noise(key_list[2], (2, WIDTH), 1.0, 4.0, (), jnp.float32),
        "decay_param": draw_decay_param(jax.random.fold_in(key_list[7], 71), 0),
        "conv_weight": noise(key_list[4], (TAPS, WIDTH), 0.5, 3.0, (), jnp.float32),
        "conv_bias": noise(key_list[5], (WIDTH,), 0.5, 3.0, (), jnp.float32),
        "cotangent": noise(key_list[6], (SEQS, TOKENS, WIDTH), 1.0, 6.0, ((0, 8), (1, 32))),
    }


def affine(first, second):
    return (first[0] * second[0], second[0] * first[1] + second[1])

def reference(inputs, gate_weight, gate_bias, decay_param, conv_weight, conv_bias, cotangent):

    def job(index):
        seq = (index // BLOCKS).astype(jnp.int32)
        blk = (index % BLOCKS).astype(jnp.int32)
        low = (blk * BLOCK_W).astype(jnp.int32)
        zero = jnp.zeros((), jnp.int32)
        source = lax.dynamic_slice(inputs, (seq, zero, low), (1, TOKENS, BLOCK_W))[0]
        upper = lax.dynamic_slice(cotangent, (seq, zero, low), (1, TOKENS, BLOCK_W))[0].astype(jnp.float32)
        weights = lax.dynamic_index_in_dim(gate_weight, blk, 2, keepdims=False).astype(jnp.float32)
        biases = lax.dynamic_slice_in_dim(gate_bias, low, BLOCK_W, 1)
        lam = lax.dynamic_slice_in_dim(decay_param, low, BLOCK_W, 0)
        taps = lax.dynamic_slice_in_dim(conv_weight, low, BLOCK_W, 1)
        shift = lax.dynamic_slice_in_dim(conv_bias, low, BLOCK_W, 0)
        extended = jnp.concatenate([jnp.zeros((TAPS - 1, BLOCK_W), jnp.float32), source.astype(jnp.float32)], 0)
        mixed = shift + taps[0] * extended[0:TOKENS]
        for k in range(1, TAPS):
            mixed = mixed + taps[k] * extended[k:k + TOKENS]
        mixed_half = mixed.astype(jnp.bfloat16)
        mixed_full = mixed_half.astype(jnp.float32)
        pre = jnp.einsum('ti,icj->tcj', mixed_full, weights)
        gate_a = jax.nn.sigmoid(pre[:, 0] + biases[0])
        gate_x = jax.nn.sigmoid(pre[:, 1] + biases[1])
        rate = jax.nn.softplus(-lam)
        decay = jnp.exp(-8.0 * gate_a * rate)
        square = 1.0 - decay * decay
        mult = jnp.sqrt(square)
        drive = mult * gate_x * mixed_full
        cum_a, hidden = lax.associative_scan(affine, (decay, drive), axis=0)
        hidden_prev = jnp.concatenate([jnp.zeros((1, BLOCK_W), jnp.float32), hidden[:-1]], 0)
        shifted = jnp.concatenate([decay[1:], jnp.ones((1, BLOCK_W), jnp.float32)], 0)
        suffix, grad_h = lax.associative_scan(affine, (shifted, upper), axis=0, reverse=True)
        grad_log = decay * grad_h * (hidden_prev - gate_x * mixed_full * decay / jnp.sqrt(jnp.maximum(square, 0.05)))
        grad_pre_a = grad_log * (-8.0 * rate) * gate_a * (1.0 - gate_a)
        grad_pre_x = grad_h * mult * mixed_full * gate_x * (1.0 - gate_x)
        grad_pre = jnp.stack([grad_pre_a, grad_pre_x], 1).astype(jnp.bfloat16).astype(jnp.float32)
        lam_grad = lax.optimization_barrier(jnp.sum(grad_log * 8.0 * gate_a, 0)) * jax.nn.sigmoid(-lam)
        bias_grad = jnp.stack([lax.optimization_barrier(jnp.sum(grad_pre_a, 0)), lax.optimization_barrier(jnp.sum(grad_pre_x, 0))], 0)
        weight_grad = jnp.einsum('ti,tcj->icj', mixed_full, grad_pre)
        grad_mixed = grad_h * mult * gate_x + jnp.einsum('tcj,icj->ti', grad_pre, weights)
        taps_grad = jnp.stack([lax.optimization_barrier(jnp.sum(grad_mixed * extended[k:k + TOKENS], 0)) for k in range(TAPS)], 0)
        shift_grad = lax.optimization_barrier(jnp.sum(grad_mixed, 0))
        padded = jnp.concatenate([grad_mixed, jnp.zeros((TAPS - 1, BLOCK_W), jnp.float32)], 0)
        back = taps[0] * padded[TAPS - 1:TAPS - 1 + TOKENS]
        for k in range(1, TAPS):
            back = back + taps[k] * padded[TAPS - 1 - k:TAPS - 1 - k + TOKENS]
        return (back.astype(jnp.bfloat16), weight_grad, lam_grad, bias_grad, taps_grad, shift_grad)
    results = lax.map(job, jnp.arange(SEQS * BLOCKS, dtype=jnp.int32))
    back, weight_grad, lam_grad, bias_grad, taps_grad, shift_grad = results
    grad_input = back.reshape(SEQS, BLOCKS, TOKENS, BLOCK_W).transpose(0, 2, 1, 3).reshape(SEQS, TOKENS, WIDTH)
    grad_gate_weight = lax.optimization_barrier(jnp.sum(weight_grad.reshape(SEQS, BLOCKS, BLOCK_W, 2, BLOCK_W), 0)).transpose(1, 2, 0, 3)
    grad_decay = lax.optimization_barrier(jnp.sum(lam_grad.reshape(SEQS, BLOCKS, BLOCK_W), 0)).reshape(WIDTH)
    grad_gate_bias = lax.optimization_barrier(jnp.sum(bias_grad.reshape(SEQS, BLOCKS, 2, BLOCK_W), 0)).transpose(1, 0, 2).reshape(2, WIDTH)
    grad_conv_weight = lax.optimization_barrier(jnp.sum(taps_grad.reshape(SEQS, BLOCKS, TAPS, BLOCK_W), 0)).transpose(1, 0, 2).reshape(TAPS, WIDTH)
    grad_conv_bias = lax.optimization_barrier(jnp.sum(shift_grad.reshape(SEQS, BLOCKS, BLOCK_W), 0)).reshape(WIDTH)
    return (grad_input, grad_gate_weight, grad_decay, grad_gate_bias, grad_conv_weight, grad_conv_bias)
```

```python
import jax
import jax.numpy as jnp
from jax import lax
from jax.experimental import pallas as pl
from jax.experimental.pallas import tpu as pltpu
from jax.sharding import PartitionSpec as P

MESH = pl.DeviceIdType.MESH
F32 = jnp.float32
BF16 = jnp.bfloat16
CHIPS = 16
REPL = 8
ROWS = 128
SPAN = 256
WIDTH = 2048
HALF = 1024
BW = 256
NB = HALF // BW
R = SPAN // 8
TILES = HALF // 128


def wait_for(ref, sem):
    pltpu.make_async_copy(ref, ref, sem).wait()


def sublane(shape):
    return lax.broadcasted_iota(jnp.int32, shape, 0)


def sigmoid(x):
    return 0.5 * jnp.tanh(0.5 * x) + 0.5


def softplus(x):
    e = jnp.exp(-jnp.abs(x))
    z = e / (2.0 + e)
    z2 = z * z
    s = jnp.full_like(z, 1.0 / 17.0)
    for n in (15, 13, 11, 9, 7, 5, 3, 1):
        s = s * z2 + 1.0 / n
    return jnp.maximum(x, 0.0) + 2.0 * z * s


def lane_tile(i):
    return slice(i * 128, (i + 1) * 128)


def block(b):
    return slice(b * BW, (b + 1) * BW)


def main_kernel(
    x_hbm, w_hbm, gb_ref, lam_ref, cw_ref, cb_ref, cot_hbm,
    gi_hbm, all_hbm,
    xb, cotb, wsh, wf, wu, wpair, W, xhalo, nat, natc, xs, cs, mb, mt, pre,
    dec, drv, qq, m1, m2, m3, oma, hp, gp, gm, tot, dsend, drecv, sin, ghs, ghr,
    wsend, frecv, own, fsum, zrecv, ssend, srecv, ssum, szrecv, G, gib,
    lsem, sib_s, sib_r, c1_s, c1_r, hal_s, hal_r, c2_s, c2_r, d_s, d_r, e_s, e_r,
    f_s, f_r, fs_s, fs_r, z_s, z_r, zs_s, zs_r, g_s, g_r,
):
    ctx = lax.axis_index("ctx")
    d = lax.axis_index("dp")
    p = ctx // 2
    c = ctx % 2
    sibling = {"ctx": 2 * p + 1 - c, "dp": d}

    def chip(j):
        return {"ctx": 2 * j + c, "dp": d}

    def peer(u):
        return {"ctx": ctx, "dp": u}

    def send(src, dst, ss, rs, dev):
        cp = pltpu.make_async_remote_copy(
            src_ref=src, dst_ref=dst, send_sem=ss, recv_sem=rs, device_id=dev, device_id_type=MESH
        )
        cp.start()
        return cp

    bar = pltpu.get_barrier_semaphore()
    pl.semaphore_signal(bar, inc=1, device_id=sibling, device_id_type=MESH)

    @pl.loop(1, CHIPS)
    def _(j):
        pl.semaphore_signal(bar, inc=1, device_id=chip((p + j) % CHIPS), device_id_type=MESH)

    @pl.loop(1, REPL)
    def _(j):
        pl.semaphore_signal(bar, inc=1, device_id=peer((d + j) % REPL), device_id_type=MESH)

    mine = pl.ds(pl.multiple_of(HALF * c, HALF), HALF)
    theirs = pl.ds(pl.multiple_of(HALF * (1 - c), HALF), HALF)
    my_rows = pl.ds(pl.multiple_of(ROWS * c, ROWS), ROWS)
    sib_rows = pl.ds(pl.multiple_of(ROWS * (1 - c), ROWS), ROWS)

    ld_w = pltpu.make_async_copy(w_hbm, wsh, lsem.at[0])
    ld_w.start()
    ld_x = pltpu.make_async_copy(x_hbm.at[0, :, mine], xb.at[my_rows], lsem.at[1])
    ld_x.start()
    ld_c = pltpu.make_async_copy(cot_hbm.at[0, :, mine], cotb.at[my_rows], lsem.at[2])
    ld_c.start()

    ld_w.wait()
    for i in range(8):
        for g in range(2):
            v = wsh[i, g].astype(F32)
            for lh in range(2):
                wf[lh, i * 16 + g * 8 : i * 16 + g * 8 + 8, :] = v[:, lane_tile(lh)]
    for h in range(2):
        for u in range(8):
            for lh in range(2):
                first = (u % 2) * 8 + 4 * h + u // 2
                wu[h, u, :, lane_tile(lh)] = wf[lh, pl.ds(first, 8, stride=16), :]

    pl.semaphore_wait(bar, 1 + (CHIPS - 1) + (REPL - 1))

    part = pl.ds(pl.multiple_of(8 * c, 8), 8)
    s_w = send(wu.at[1 - c, d], wpair.at[part], sib_s.at[0], sib_r.at[0], sibling)
    s_x = send(x_hbm.at[0, :, theirs], xb.at[my_rows], sib_s.at[1], sib_r.at[1], sibling)
    s_c = send(cot_hbm.at[0, :, theirs], cotb.at[my_rows], sib_s.at[2], sib_r.at[2], sibling)
    wpair[part, :] = wu[c, d]
    s_w.wait_recv()
    my16 = pl.ds(pl.multiple_of(16 * p, 16), 16)
    W[d, my16, :] = wpair[...].astype(BF16)

    @pl.loop(1, CHIPS)
    def _(j):
        send(W.at[d, my16], W.at[d, my16], c1_s, c1_r, chip((p + j) % CHIPS))

    ld_x.wait()
    s_x.wait_recv()
    send(xb.at[pl.ds(SPAN - 16, 16)], xhalo, hal_s, hal_r, chip((p + 1) % CHIPS))
    for k in range(TILES):
        nat[k] = xb[:, lane_tile(k)].astype(F32)

    @pl.loop(0, R)
    def _(r):
        for k in range(TILES):
            xs[3 + r, :, lane_tile(k)] = nat[k, pl.ds(r, 8, stride=R), :]

    ld_c.wait()
    s_c.wait_recv()
    for k in range(TILES):
        natc[k] = cotb[:, lane_tile(k)].astype(F32)

    @pl.loop(0, R)
    def _(r):
        for k in range(TILES):
            cs[r, :, lane_tile(k)] = natc[k, pl.ds(r, 8, stride=R), :]

    wait_for(xhalo, hal_r)
    hal = xhalo[...].astype(F32)
    hal = jnp.where(p == 0, jnp.zeros_like(hal), hal)
    sub = sublane((8, HALF))
    for k in range(3):
        rolled = pltpu.roll(xs[3 + R - 3 + k], 1, 0)
        xs[k] = jnp.where(sub == 0, jnp.broadcast_to(hal[13 + k : 14 + k], (8, HALF)), rolled)

    conv_w = cw_ref[:, mine]
    conv_b = cb_ref[:, mine]
    for b in range(NB):
        taps = [jnp.broadcast_to(conv_w[k : k + 1, block(b)], (8, BW)) for k in range(4)]
        shift = jnp.broadcast_to(conv_b[:, block(b)], (8, BW))

        @pl.loop(0, R // 2)
        def _(i):
            v = [xs[2 * i + k, :, block(b)] for k in range(5)]
            out = []
            for o in range(2):
                m = shift + taps[0] * v[o]
                for k in range(1, 4):
                    m = m + taps[k] * v[o + k]
                out.append(m)
            mb[pl.ds(pl.multiple_of(16 * i, 16), 16), block(b)] = jnp.concatenate(out, 0).astype(BF16)

        mt[b] = mb[:, block(b)].astype(F32).T.astype(BF16)

    wait_for(W.at[0, pl.ds(0, 16 * (CHIPS - 1))], c1_r)

    @pl.loop(1, REPL)
    def _(j):
        send(W.at[d], W.at[d], c2_s, c2_r.at[d], peer((d + j) % REPL))

    lam = lam_ref[:, mine]
    neg8rate = -8.0 * softplus(-lam)
    gate_b = gb_ref[:, mine]
    ends = []
    for b in range(NB):
        for u in (2 * b, 2 * b + 1):
            @pl.when(d != u)
            def _():
                wait_for(W.at[u], c2_r.at[u])

            pre[u] = jnp.dot(mb[:, block(b)], W[u], preferred_element_type=F32)
        nr = jnp.broadcast_to(neg8rate[:, block(b)], (8, BW))
        ba = jnp.broadcast_to(gate_b[0:1, block(b)], (8, BW))
        bx = jnp.broadcast_to(gate_b[1:2, block(b)], (8, BW))

        def step(i, carry):
            prod, hid, kk, logs = carry
            two = mb[pl.ds(pl.multiple_of(16 * i, 16), 16), block(b)].astype(F32)
            for o in range(2):
                r = 2 * i + o
                at = pl.ds(pl.multiple_of(8 * r, 8), 8)
                ga = sigmoid(pre[2 * b, at, :] + ba)
                gx = sigmoid(pre[2 * b + 1, at, :] + bx)
                m = two[8 * o : 8 * o + 8]
                ld = ga * nr
                a = jnp.exp(ld)
                sq = 1.0 - a * a
                mult = jnp.sqrt(sq)
                gm_ = gx * m
                drive = mult * gm_
                dec[r, :, block(b)] = a
                drv[r, :, block(b)] = drive
                qq[r, :, block(b)] = gm_ * a * lax.rsqrt(jnp.maximum(sq, 0.05))
                m1[r, :, block(b)] = a * ga
                oma[r, :, block(b)] = (1.0 - ga) * nr
                m2[r, :, block(b)] = drive * (1.0 - gx)
                m3[r, :, block(b)] = mult * gx
                hid = a * hid + drive
                prod = prod * a
                kk = kk + prod * cs[r, :, block(b)]
                logs = logs + ld
            return prod, hid, kk, logs

        zero = jnp.zeros((8, BW), F32)
        prod, hid, kk, logs = lax.fori_loop(
            0, R // 2, step, (jnp.ones((8, BW), F32), zero, zero, zero)
        )
        sb = sublane((8, BW))
        fp, fh = prod, hid
        bp, bk = prod, kk
        for s in (1, 2, 4):
            mp, mh = pltpu.roll(fp, s, 0), pltpu.roll(fh, s, 0)
            fh = jnp.where(sb >= s, fp * mh + fh, fh)
            fp = jnp.where(sb >= s, fp * mp, fp)
            mp, mk = pltpu.roll(bp, 8 - s, 0), pltpu.roll(bk, 8 - s, 0)
            bk = jnp.where(sb < 8 - s, bp * mk + bk, bk)
            bp = jnp.where(sb < 8 - s, bp * mp, bp)
            logs = logs + pltpu.roll(logs, s, 0)
        one = jnp.ones((8, BW), F32)
        ends.append((
            jnp.where(sb == 0, one, pltpu.roll(fp, 1, 0)),
            jnp.where(sb == 0, zero, pltpu.roll(fh, 1, 0)),
            jnp.where(sb == 7, one, pltpu.roll(bp, 7, 0)),
            jnp.where(sb == 7, zero, pltpu.roll(bk, 7, 0)),
        ))
        for lh in range(2):
            k = 2 * b + lh
            tot[0, k : k + 1, :] = logs[0:1, lane_tile(lh)]
            tot[1, k : k + 1, :] = fh[7:8, lane_tile(lh)]
            tot[2, k : k + 1, :] = bk[0:1, lane_tile(lh)]

    dsend[0] = jnp.concatenate([tot[0], tot[1]], 0).astype(BF16)
    dsend[1] = jnp.concatenate([tot[0], tot[2]], 0).astype(BF16)

    @pl.loop(1, CHIPS)
    def _(j):
        to = (p + j) % CHIPS
        send(dsend.at[jnp.where(to > p, 0, 1)], drecv.at[p], d_s, d_r, chip(to))

    drecv[p] = jnp.zeros((16, 128), BF16)
    wait_for(drecv.at[pl.ds(0, CHIPS - 1)], d_r)
    state = jnp.zeros((8, 128), F32)
    carry_in = jnp.zeros((8, 128), F32)
    for j in range(CHIPS):
        v = drecv[j].astype(F32)
        state = jnp.where(j < p, jnp.exp(v[:8]) * state + v[8:], state)
        v = drecv[CHIPS - 1 - j].astype(F32)
        carry_in = jnp.where(CHIPS - 1 - j > p, jnp.exp(v[:8]) * carry_in + v[8:], carry_in)
    sin[0] = state
    sin[1] = carry_in

    sums = []
    for b in range(NB):
        def wide(n):
            return jnp.concatenate(
                [jnp.broadcast_to(sin[n, 2 * b + lh : 2 * b + lh + 1, :], (8, 128)) for lh in range(2)], 1
            )

        hin = ends[b][1] + ends[b][0] * wide(0)
        kin = ends[b][3] + ends[b][2] * wide(1)

        def up(r, h):
            hp[r, :, block(b)] = h
            return dec[r, :, block(b)] * h + drv[r, :, block(b)]

        lax.fori_loop(0, R, up, hin, unroll=4)

        def down(n, carry):
            kk, st, sa, sx = carry
            i = R // 2 - 1 - n
            outs = [[None, None], [None, None]]
            for o in (1, 0):
                r = 2 * i + o
                gr = cs[r, :, block(b)] + kk
                kk = dec[r, :, block(b)] * gr
                t = (hp[r, :, block(b)] - qq[r, :, block(b)]) * m1[r, :, block(b)] * gr
                ga = t * oma[r, :, block(b)]
                gx = gr * m2[r, :, block(b)]
                gm[r, :, block(b)] = gr * m3[r, :, block(b)]
                st, sa, sx = st + t, sa + ga, sx + gx
                outs[0][o], outs[1][o] = ga, gx
            at = pl.ds(pl.multiple_of(16 * i, 16), 16)
            gp[2 * b, at, :] = jnp.concatenate(outs[0], 0).astype(BF16)
            gp[2 * b + 1, at, :] = jnp.concatenate(outs[1], 0).astype(BF16)
            return kk, st, sa, sx

        zero = jnp.zeros((8, BW), F32)
        _, st, sa, sx = lax.fori_loop(0, R // 2, down, (kin, zero, zero, zero))
        sums.append([st, sa, sx])
        for u in (2 * b, 2 * b + 1):
            grad = jnp.dot(mt[b], gp[u], preferred_element_type=F32)
            wsend[u] = grad.astype(BF16)

            @pl.when(d != u)
            def _():
                send(wsend.at[u], frecv.at[d], f_s, f_r, peer(u))

        nt = (((1,), (1,)), ((), ()))
        back = lax.dot_general(gp[2 * b], W[2 * b], nt, preferred_element_type=F32)
        back = back + lax.dot_general(gp[2 * b + 1], W[2 * b + 1], nt, preferred_element_type=F32)
        gm[0:R, :, block(b)] = gm[0:R, :, block(b)] + back.reshape(R, 8, BW)

    for k in range(3):
        ghs[k : k + 1, :] = gm[k, 0:1, :]
    send(ghs, ghr, e_s, e_r, chip((p + CHIPS - 1) % CHIPS))

    sig = 1.0 / (1.0 + jnp.exp(lam))
    for b in range(NB):
        def add(r, carry):
            g = gm[r, :, block(b)]
            return tuple(carry[k] + g * xs[r + k, :, block(b)] for k in range(4)) + (carry[4] + g,)

        zero = jnp.zeros((8, BW), F32)
        acc = lax.fori_loop(0, R, add, (zero,) * 5, unroll=4)
        st, sa, sx = sums[b]
        st = st * (8.0 * jnp.broadcast_to(sig[:, block(b)], (8, BW)))
        sb = sublane((8, BW))
        rows = zero
        for n, v in enumerate((st, sa, sx) + tuple(acc)):
            for s in (1, 2, 4):
                v = v + pltpu.roll(v, s, 0)
            rows = jnp.where(sb == n, v, rows)
        for lh in range(2):
            u = 2 * b + lh
            ssend[u] = rows[:, lane_tile(lh)]

            @pl.when(d != u)
            def _():
                send(ssend.at[u], srecv.at[d], fs_s, fs_r, peer(u))

    srecv[d] = ssend[d]
    frecv[d] = wsend[d]

    wait_for(ghr, e_r)
    halo = ghr[...]
    halo = jnp.where(p == CHIPS - 1, jnp.zeros_like(halo), halo)
    for k in range(3):
        rolled = pltpu.roll(gm[k], 7, 0)
        gm[R + k] = jnp.where(sub == 7, jnp.broadcast_to(halo[k : k + 1], (8, HALF)), rolled)

    for b in range(NB):
        taps = [jnp.broadcast_to(conv_w[k : k + 1, block(b)], (8, BW)) for k in range(4)]

        @pl.loop(0, R)
        def _(r):
            v = taps[0] * gm[r + 3, :, block(b)]
            for k in range(1, 4):
                v = v + taps[k] * gm[r + 3 - k, :, block(b)]
            for lh in range(2):
                nat[2 * b + lh, pl.ds(r, 8, stride=R), :] = v[:, lane_tile(lh)]

    for k in range(TILES):
        gib[:, lane_tile(k)] = nat[k].astype(BF16)
    s_g = send(gib.at[sib_rows], gi_hbm.at[:, mine], sib_s.at[3], sib_r.at[3], sibling)
    st_g = pltpu.make_async_copy(gib.at[my_rows], gi_hbm.at[:, mine], lsem.at[3])
    st_g.start()

    wait_for(srecv.at[pl.ds(0, REPL - 1)], fs_r)
    ssum[...] = jnp.sum(srecv[...], 0)

    @pl.loop(1, CHIPS)
    def _(j):
        send(ssum, szrecv.at[p], zs_s, zs_r, chip((p + j) % CHIPS))

    szrecv[p] = ssum[...]

    wait_for(frecv.at[pl.ds(0, REPL - 1)], f_r)

    @pl.loop(0, 16)
    def _(i):
        at = pl.ds(pl.multiple_of(16 * i, 16), 16)
        v = frecv[0, at, :].astype(F32)
        for u in range(1, REPL):
            v = v + frecv[u, at, :].astype(F32)
        fsum[i] = v.astype(BF16)

    @pl.loop(1, CHIPS)
    def _(j):
        to = (p + j) % CHIPS
        send(fsum.at[to], zrecv.at[p], z_s, z_r, chip(to))

    zrecv[p] = fsum[p]
    wait_for(szrecv.at[pl.ds(0, CHIPS - 1)], zs_r)
    small = jnp.sum(szrecv[...], 0)
    wait_for(zrecv.at[pl.ds(0, CHIPS - 1)], z_r)
    whole = zrecv[0].astype(F32)
    for j in range(1, CHIPS):
        whole = whole + zrecv[j].astype(F32)
    own[...] = whole
    G[d, c, :, 0:BW] = own[part, :]
    G[d, c, :, BW:] = small
    other = pl.ds(pl.multiple_of(8 * (1 - c), 8), 8)
    fin = tot
    for lh in range(2):
        fin[lh] = own[other, lane_tile(lh)]
    fin[2] = small
    cps = []
    for n in range(3):
        cps.append(send(fin.at[n], G.at[d, c, :, pl.ds(128 * n, 128)], sib_s.at[4 + n], sib_r.at[4 + n], sibling))
    for cp in cps:
        cp.wait_recv()

    @pl.loop(1, REPL)
    def _(j):
        send(G.at[d], G.at[d], g_s, g_r, peer((d + j) % REPL))

    wait_for(G.at[pl.ds(0, REPL - 1)], g_r)
    st_a = pltpu.make_async_copy(G, all_hbm, lsem.at[4])
    st_a.start()

    for cp in [s_w, s_x, s_c, s_g] + cps:
        cp.wait_send()
    s_g.wait_recv()
    wait_for(W.at[0, pl.ds(0, 16 * (CHIPS - 1))], c1_s)
    wait_for(xhalo, hal_s)
    wait_for(W.at[pl.ds(0, REPL - 1)], c2_s)
    wait_for(drecv.at[pl.ds(0, CHIPS - 1)], d_s)
    wait_for(ghr, e_s)
    wait_for(frecv.at[pl.ds(0, REPL - 1)], f_s)
    wait_for(srecv.at[pl.ds(0, REPL - 1)], fs_s)
    wait_for(szrecv.at[pl.ds(0, CHIPS - 1)], zs_s)
    wait_for(zrecv.at[pl.ds(0, CHIPS - 1)], z_s)
    wait_for(G.at[pl.ds(0, REPL - 1)], g_s)
    st_g.wait()
    st_a.wait()


def last_kernel(gi_in, all_ref, gi_out, gw_out, dec_out, bias_out, taps_out, shift_out, gws):
    gi_out[0] = gi_in[...]
    for h in range(2):
        for u in range(8):
            at = slice(h * HALF + 128 * u, h * HALF + 128 * (u + 1))
            v = all_ref[u, h, :, BW:]
            dec_out[:, at] = v[0:1]
            bias_out[:, at] = v[1:3]
            taps_out[:, at] = v[3:7]
            shift_out[:, at] = v[7:8]
            first = (u % 2) * 8 + 4 * h + u // 2
            for lh in range(2):
                gws[lh, pl.ds(first, 8, stride=16), :] = all_ref[u, h, :, lane_tile(lh)]
    for i in range(8):
        for g in range(2):
            for lh in range(2):
                gw_out[i, g, :, lane_tile(lh)] = gws[lh, i * 16 + g * 8 : i * 16 + g * 8 + 8, :]


def per_device(inputs, gate_weight, gate_bias, decay_param, conv_weight, conv_bias, cotangent):
    vmem = pl.BlockSpec(memory_space=pltpu.VMEM)
    anyw = pl.BlockSpec(memory_space=pl.ANY)
    dma = pltpu.SemaphoreType.DMA
    big = pltpu.VMEM((R, 8, HALF), F32)
    gi, packed = pl.pallas_call(
        main_kernel,
        name="main",
        out_shape=(
            jax.ShapeDtypeStruct((ROWS, WIDTH), BF16),
            jax.ShapeDtypeStruct((REPL, 2, 8, BW + 128), F32),
        ),
        in_specs=[anyw, anyw, vmem, vmem, vmem, vmem, anyw],
        out_specs=(anyw, anyw),
        scratch_shapes=[
            pltpu.VMEM((SPAN, HALF), BF16),
            pltpu.VMEM((SPAN, HALF), BF16),
            pltpu.VMEM((8, 2, 8, BW), BF16),
            pltpu.VMEM((2, 128, 128), F32),
            pltpu.VMEM((2, 8, 8, BW), F32),
            pltpu.VMEM((16, BW), F32),
            pltpu.VMEM((8, BW, BW), BF16),
            pltpu.VMEM((16, HALF), BF16),
            pltpu.VMEM((TILES, SPAN, 128), F32),
            pltpu.VMEM((TILES, SPAN, 128), F32),
            pltpu.VMEM((R + 3, 8, HALF), F32),
            big,
            pltpu.VMEM((SPAN, HALF), BF16),
            pltpu.VMEM((NB, BW, SPAN), BF16),
            pltpu.VMEM((8, SPAN, BW), F32),
            big, big, big, big, big, big, big, big,
            pltpu.VMEM((8, SPAN, BW), BF16),
            pltpu.VMEM((R + 3, 8, HALF), F32),
            pltpu.VMEM((3, 8, 128), F32),
            pltpu.VMEM((2, 16, 128), BF16),
            pltpu.VMEM((CHIPS, 16, 128), BF16),
            pltpu.VMEM((2, 8, 128), F32),
            pltpu.VMEM((8, HALF), F32),
            pltpu.VMEM((8, HALF), F32),
            pltpu.VMEM((8, BW, BW), BF16),
            pltpu.VMEM((8, BW, BW), BF16),
            pltpu.VMEM((16, BW), F32),
            pltpu.VMEM((CHIPS, 16, BW), BF16),
            pltpu.VMEM((CHIPS, 16, BW), BF16),
            pltpu.VMEM((8, 8, 128), F32),
            pltpu.VMEM((8, 8, 128), F32),
            pltpu.VMEM((8, 128), F32),
            pltpu.VMEM((CHIPS, 8, 128), F32),
            pltpu.VMEM((REPL, 2, 8, BW + 128), F32),
            pltpu.VMEM((SPAN, HALF), BF16),
            dma((5,)), dma((7,)), dma((7,)),
            dma, dma, dma, dma, dma, dma((REPL,)),
            dma, dma, dma, dma, dma, dma, dma, dma,
            dma, dma, dma, dma, dma, dma,
        ],
        compiler_params=pltpu.CompilerParams(
            collective_id=0, has_side_effects=True, vmem_limit_bytes=48 * 2**20
        ),
    )(
        inputs, gate_weight, gate_bias, decay_param.reshape(1, WIDTH), conv_weight,
        conv_bias.reshape(1, WIDTH), cotangent,
    )
    gi, gw, dec, bias, taps, shift = pl.pallas_call(
        last_kernel,
        name="last",
        out_shape=(
            jax.ShapeDtypeStruct((1, ROWS, WIDTH), BF16),
            jax.ShapeDtypeStruct((8, 2, 8, BW), F32),
            jax.ShapeDtypeStruct((1, WIDTH), F32),
            jax.ShapeDtypeStruct((2, WIDTH), F32),
            jax.ShapeDtypeStruct((4, WIDTH), F32),
            jax.ShapeDtypeStruct((1, WIDTH), F32),
        ),
        in_specs=[vmem, vmem],
        out_specs=(vmem,) * 6,
        scratch_shapes=[pltpu.VMEM((2, 128, 128), F32)],
    )(gi, packed)
    return gi, gw, dec.reshape(WIDTH), bias, taps, shift.reshape(WIDTH)


def solution(mesh):
    placed = (
        P("dp", "ctx", None),
        P("ctx", None, None, None),
        P(),
        P(),
        P(),
        P(),
        P("dp", "ctx", None),
    )
    return jax.shard_map(
        per_device,
        mesh=mesh,
        in_specs=placed,
        out_specs=(P("dp", "ctx", None), P("ctx", None, None, None), P(), P(), P(), P()),
        check_vma=False,
    )
```

```python
import jax
import jax.numpy as jnp
from jax import lax
from jax.experimental import pallas as pl
from jax.experimental.pallas import tpu as pltpu
from jax.sharding import PartitionSpec as P

MESH = pl.DeviceIdType.MESH
F32 = jnp.float32
BF16 = jnp.bfloat16
CHIPS = 16
PLANE = 16
DEPTH = 8
REPL = 8
ROWS = 128
SPAN = 256
WIDTH = 2048
HALF = 1024
BW = 256
NB = HALF // BW
R = SPAN // 8
TILES = HALF // 128
STAGES = 2


def wait_for(ref, sem):
    pltpu.make_async_copy(ref, ref, sem).wait()


def sublane(shape):
    return lax.broadcasted_iota(jnp.int32, shape, 0)


def sigmoid(x):
    return 0.5 * jnp.tanh(0.5 * x) + 0.5


def softplus(x):
    e = jnp.exp(-jnp.abs(x))
    z = e / (2.0 + e)
    z2 = z * z
    s = jnp.full_like(z, 1.0 / 17.0)
    for n in (15, 13, 11, 9, 7, 5, 3, 1):
        s = s * z2 + 1.0 / n
    return jnp.maximum(x, 0.0) + 2.0 * z * s


def lane_tile(i):
    return slice(i * 128, (i + 1) * 128)


def block(b):
    return slice(b * BW, (b + 1) * BW)


def main_kernel(
    x_hbm, w_hbm, gb_hbm, lam_hbm, cw_hbm, cb_hbm, cot_hbm,
    gi_hbm, all_hbm,
    gb_ref, lam_ref, cw_ref, cb_ref, xb, cotb, wsh, wf, wu, wpair, W, xhalo, nat, natc, xs, cs, mb, mt, pre,
    dec, drv, qq, m1, m2, m3, oma, hp, gp, gm, dsend, drecv, sin, ghs, ghr,
    wsend, frecv, own, fsum, zrecv, ssend, srecv, ssum, szrecv, fin, G, gib,
    lsem, sib_s, sib_r, c1_s, c1_r, hal_s, hal_r, c2_s, c2_r, d_s, d_r, e_s, e_r,
    f_s, f_r, fs_s, fs_r, z_s, z_r, zs_s, zs_r, g_s, g_r,
):
    ctx = lax.axis_index("ctx")
    d = lax.axis_index("dp")
    p = ctx // 2
    c = ctx % 2
    z = p % DEPTH
    y = 2 * (p // DEPTH) + d // 4
    x = d % 4
    spot = 4 * y + x
    sibling = {"ctx": 2 * p + 1 - c, "dp": d}

    def chip(j):
        return {"ctx": 2 * j + c, "dp": d}

    def deep(j):
        return {"ctx": 2 * (p - z + j) + c, "dp": d}

    def peer(u):
        return {"ctx": ctx, "dp": u}

    def plane(j):
        to_x, to_y = (x + j % 4) % 4, (y + j // 4) % 4
        to_d = 4 * (to_y % 2) + to_x
        return {"ctx": 2 * (DEPTH * (to_y // 2) + z) + c, "dp": to_d}, to_y // 2, to_d

    def rows_of(h):
        return pl.ds(pl.multiple_of(128 * h, 128), 128)

    def lanes_of(u):
        return pl.ds(pl.multiple_of(128 * (u % 2), 128), 128)

    def send(src, dst, ss, rs, dev):
        cp = pltpu.make_async_remote_copy(
            src_ref=src, dst_ref=dst, send_sem=ss, recv_sem=rs, device_id=dev, device_id_type=MESH
        )
        cp.start()
        return cp

    bar = pltpu.get_barrier_semaphore()
    pl.semaphore_signal(bar, inc=1, device_id=sibling, device_id_type=MESH)

    @pl.loop(1, CHIPS)
    def _(j):
        pl.semaphore_signal(bar, inc=1, device_id=chip((p + j) % CHIPS), device_id_type=MESH)

    @pl.loop(1, PLANE)
    def _(j):
        @pl.when(j != PLANE // 2)
        def _():
            pl.semaphore_signal(bar, inc=1, device_id=plane(j)[0], device_id_type=MESH)

    mine = pl.ds(pl.multiple_of(HALF * c, HALF), HALF)
    theirs = pl.ds(pl.multiple_of(HALF * (1 - c), HALF), HALF)
    my_rows = pl.ds(pl.multiple_of(ROWS * c, ROWS), ROWS)
    sib_rows = pl.ds(pl.multiple_of(ROWS * (1 - c), ROWS), ROWS)

    ld_w = pltpu.make_async_copy(w_hbm, wsh, lsem.at[0])
    ld_w.start()
    ld_x = pltpu.make_async_copy(x_hbm.at[0, :, mine], xb.at[my_rows], lsem.at[1])
    ld_x.start()
    ld_c = pltpu.make_async_copy(cot_hbm.at[0, :, mine], cotb.at[my_rows], lsem.at[2])
    ld_c.start()
    lds = []
    for n, (src, dst) in enumerate(
        ((gb_hbm, gb_ref), (lam_hbm, lam_ref), (cw_hbm, cw_ref), (cb_hbm, cb_ref))
    ):
        lds.append(pltpu.make_async_copy(src.at[:, mine], dst, lsem.at[5 + n]))
        lds[-1].start()
    pending = []

    ld_w.wait()
    for i in range(8):
        for g in range(2):
            v = wsh[i, g].astype(F32)
            for lh in range(2):
                wf[lh, i * 16 + g * 8 : i * 16 + g * 8 + 8, :] = v[:, lane_tile(lh)]
    for h in range(2):
        for u in range(REPL):
            for st in range(STAGES):
                first = ((u // 2) % 2) * 8 + 4 * h + 2 * st + u // 4
                wu[h, u, st] = wf[u % 2, pl.ds(first, 8, stride=16), :]

    pl.semaphore_wait(bar, 1 + (CHIPS - 1) + (PLANE - 2))

    part = pl.ds(pl.multiple_of(8 * c, 8), 8)
    s_w = send(wu.at[1 - c, d], wpair.at[:, part], sib_s.at[0], sib_r.at[0], sibling)
    s_x = send(x_hbm.at[0, :, theirs], xb.at[my_rows], sib_s.at[1], sib_r.at[1], sibling)
    s_c = send(cot_hbm.at[0, :, theirs], cotb.at[my_rows], sib_s.at[2], sib_r.at[2], sibling)
    wpair[:, part, :] = wu[c, d]
    s_w.wait_recv()
    my16 = pl.ds(pl.multiple_of(16 * p, 16), 16)
    mine_w = W.at[d // 2, :, my16, lanes_of(d)]
    mine_w[...] = wpair[...].astype(BF16)

    @pl.loop(1, DEPTH)
    def _(j):
        send(mine_w, mine_w, c1_s, c1_r, deep((z + j) % DEPTH))

    seven = wsend.at[0, :, pl.ds(0, 16 * (DEPTH - 1)), pl.ds(0, 128)]
    pending.append((seven, c1_s))

    ld_x.wait()
    s_x.wait_recv()
    send(xb.at[pl.ds(SPAN - 16, 16)], xhalo, hal_s, hal_r, chip((p + 1) % CHIPS))
    pending.append((xhalo, hal_s))
    for k in range(TILES):
        nat[k] = xb[:, lane_tile(k)].astype(F32)

    @pl.loop(0, R)
    def _(r):
        for k in range(TILES):
            xs[3 + r, :, lane_tile(k)] = nat[k, pl.ds(r, 8, stride=R), :]

    wait_for(seven, c1_r)
    fifteen = frecv.at[0, pl.ds(0, PLANE - 1)]
    for st in range(STAGES):
        @pl.loop(1, PLANE)
        def _(j):
            mine_s = W.at[d // 2, st, rows_of(y // 2), lanes_of(d)]
            send(mine_s, mine_s, c2_s.at[st], c2_r.at[st], plane(j)[0])

        pending.append((fifteen, c2_s.at[st]))

    ld_c.wait()
    s_c.wait_recv()
    for k in range(TILES):
        natc[k] = cotb[:, lane_tile(k)].astype(F32)

    @pl.loop(0, R)
    def _(r):
        for k in range(TILES):
            cs[r, :, lane_tile(k)] = natc[k, pl.ds(r, 8, stride=R), :]

    wait_for(xhalo, hal_r)
    hal = xhalo[...].astype(F32)
    hal = jnp.where(p == 0, jnp.zeros_like(hal), hal)
    sub = sublane((8, HALF))
    for k in range(3):
        rolled = pltpu.roll(xs[3 + R - 3 + k], 1, 0)
        xs[k] = jnp.where(sub == 0, jnp.broadcast_to(hal[13 + k : 14 + k], (8, HALF)), rolled)

    for ld in lds:
        ld.wait()
    conv_w = cw_ref[...]
    conv_b = cb_ref[...]
    for b in range(NB):
        taps = [jnp.broadcast_to(conv_w[k : k + 1, block(b)], (8, BW)) for k in range(4)]
        shift = jnp.broadcast_to(conv_b[:, block(b)], (8, BW))

        @pl.loop(0, R // 2)
        def _(i):
            v = [xs[2 * i + k, :, block(b)] for k in range(5)]
            out = []
            for o in range(2):
                m = shift + taps[0] * v[o]
                for k in range(1, 4):
                    m = m + taps[k] * v[o + k]
                out.append(m)
            mb[pl.ds(pl.multiple_of(16 * i, 16), 16), block(b)] = jnp.concatenate(out, 0).astype(BF16)

        mt[b] = mb[:, block(b)].astype(F32).T.astype(BF16)

    lam = lam_ref[...]
    neg8rate = -8.0 * softplus(-lam)
    gate_b = gb_ref[...]
    ends = []

    def gates(b):
        st, k = b // 2, 2 * (b % 2)
        for g in range(2):
            pre[2 * b + g] = jnp.dot(mb[:, block(b)], W[k + g, st], preferred_element_type=F32)
        nr = jnp.broadcast_to(neg8rate[:, block(b)], (8, BW))
        ba = jnp.broadcast_to(gate_b[0:1, block(b)], (8, BW))
        bx = jnp.broadcast_to(gate_b[1:2, block(b)], (8, BW))

        def step(i, carry):
            prod, hid, kk, logs = carry
            two = mb[pl.ds(pl.multiple_of(16 * i, 16), 16), block(b)].astype(F32)
            for o in range(2):
                r = 2 * i + o
                at = pl.ds(pl.multiple_of(8 * r, 8), 8)
                ga = sigmoid(pre[2 * b, at, :] + ba)
                gx = sigmoid(pre[2 * b + 1, at, :] + bx)
                m = two[8 * o : 8 * o + 8]
                ld = ga * nr
                a = jnp.exp(ld)
                sq = 1.0 - a * a
                mult = jnp.sqrt(sq)
                gm_ = gx * m
                drive = mult * gm_
                dec[r, :, block(b)] = a
                drv[r, :, block(b)] = drive
                qq[r, :, block(b)] = gm_ * a * lax.rsqrt(jnp.maximum(sq, 0.05))
                m1[r, :, block(b)] = a * ga
                oma[r, :, block(b)] = (1.0 - ga) * nr
                m2[r, :, block(b)] = drive * (1.0 - gx)
                m3[r, :, block(b)] = mult * gx
                hid = a * hid + drive
                prod = prod * a
                kk = kk + prod * cs[r, :, block(b)]
                logs = logs + ld
            return prod, hid, kk, logs

        zero = jnp.zeros((8, BW), F32)
        prod, hid, kk, logs = lax.fori_loop(
            0, R // 2, step, (jnp.ones((8, BW), F32), zero, zero, zero)
        )
        sb = sublane((8, BW))
        fp, fh = prod, hid
        bp, bk = prod, kk
        for s in (1, 2, 4):
            mp, mh = pltpu.roll(fp, s, 0), pltpu.roll(fh, s, 0)
            fh = jnp.where(sb >= s, fp * mh + fh, fh)
            fp = jnp.where(sb >= s, fp * mp, fp)
            mp, mk = pltpu.roll(bp, 8 - s, 0), pltpu.roll(bk, 8 - s, 0)
            bk = jnp.where(sb < 8 - s, bp * mk + bk, bk)
            bp = jnp.where(sb < 8 - s, bp * mp, bp)
            logs = logs + pltpu.roll(logs, s, 0)
        one = jnp.ones((8, BW), F32)
        ends.append((
            jnp.where(sb == 0, one, pltpu.roll(fp, 1, 0)),
            jnp.where(sb == 0, zero, pltpu.roll(fh, 1, 0)),
            jnp.where(sb == 7, one, pltpu.roll(bp, 7, 0)),
            jnp.where(sb == 7, zero, pltpu.roll(bk, 7, 0)),
        ))
        for lh in range(2):
            k = 2 * (b % 2) + lh
            dsend[st, 0, k : k + 1, :] = logs[0:1, lane_tile(lh)]
            dsend[st, 1, k : k + 1, :] = logs[0:1, lane_tile(lh)]
            dsend[st, 0, 4 + k : 5 + k, :] = fh[7:8, lane_tile(lh)]
            dsend[st, 1, 4 + k : 5 + k, :] = bk[0:1, lane_tile(lh)]

    for st in range(STAGES):
        wait_for(fifteen, c2_r.at[st])
        for b in (2 * st, 2 * st + 1):
            gates(b)

        @pl.loop(1, CHIPS)
        def _(j):
            to = (p + j) % CHIPS
            send(dsend.at[st, jnp.where(to > p, 0, 1)], drecv.at[st, p], d_s.at[st], d_r.at[st], chip(to))

        pending.append((drecv.at[st, pl.ds(0, CHIPS - 1)], d_s.at[st]))
        drecv[st, p] = jnp.zeros((8, 128), F32)

    sums = []

    def grads(b):
        st, k = b // 2, 2 * (b % 2)

        def wide(n):
            return jnp.concatenate(
                [jnp.broadcast_to(sin[st, n, k + lh : k + lh + 1, :], (8, 128)) for lh in range(2)], 1
            )

        hin = ends[b][1] + ends[b][0] * wide(0)
        kin = ends[b][3] + ends[b][2] * wide(1)

        def up(r, h):
            hp[r, :, block(b)] = h
            return dec[r, :, block(b)] * h + drv[r, :, block(b)]

        lax.fori_loop(0, R, up, hin, unroll=4)

        def down(n, carry):
            kk, t_sum, a_sum, x_sum = carry
            i = R // 2 - 1 - n
            outs = [[None, None], [None, None]]
            for o in (1, 0):
                r = 2 * i + o
                gr = cs[r, :, block(b)] + kk
                kk = dec[r, :, block(b)] * gr
                t = (hp[r, :, block(b)] - qq[r, :, block(b)]) * m1[r, :, block(b)] * gr
                ga = t * oma[r, :, block(b)]
                gx = gr * m2[r, :, block(b)]
                gm[r, :, block(b)] = gr * m3[r, :, block(b)]
                t_sum, a_sum, x_sum = t_sum + t, a_sum + ga, x_sum + gx
                outs[0][o], outs[1][o] = ga, gx
            at = pl.ds(pl.multiple_of(16 * i, 16), 16)
            gp[2 * b, at, :] = jnp.concatenate(outs[0], 0).astype(BF16)
            gp[2 * b + 1, at, :] = jnp.concatenate(outs[1], 0).astype(BF16)
            return kk, t_sum, a_sum, x_sum

        zero = jnp.zeros((8, BW), F32)
        _, t_sum, a_sum, x_sum = lax.fori_loop(0, R // 2, down, (kin, zero, zero, zero))
        sums.append([t_sum, a_sum, x_sum])
        for g in range(2):
            wsend[k + g, st] = jnp.dot(mt[b], gp[2 * b + g], preferred_element_type=F32).astype(BF16)

    def through(b):
        st, k = b // 2, 2 * (b % 2)
        nt = (((1,), (1,)), ((), ()))
        back = lax.dot_general(gp[2 * b], W[k, st], nt, preferred_element_type=F32)
        back = back + lax.dot_general(gp[2 * b + 1], W[k + 1, st], nt, preferred_element_type=F32)
        gm[0:R, :, block(b)] = gm[0:R, :, block(b)] + back.reshape(R, 8, BW)

    for st in range(STAGES):
        wait_for(drecv.at[st, pl.ds(0, CHIPS - 1)], d_r.at[st])
        state = jnp.zeros((4, 128), F32)
        carry_in = jnp.zeros((4, 128), F32)
        for j in range(CHIPS):
            v = drecv[st, j]
            state = jnp.where(j < p, jnp.exp(v[:4]) * state + v[4:], state)
            v = drecv[st, CHIPS - 1 - j]
            carry_in = jnp.where(CHIPS - 1 - j > p, jnp.exp(v[:4]) * carry_in + v[4:], carry_in)
        sin[st, 0] = state
        sin[st, 1] = carry_in
        for b in (2 * st, 2 * st + 1):
            grads(b)

        @pl.loop(1, PLANE)
        def _(j):
            dev, to_h, to_d = plane(j)
            send(
                wsend.at[to_d // 2, st, rows_of(to_h), lanes_of(to_d)],
                frecv.at[st, spot], f_s.at[st], f_r.at[st], dev,
            )

        pending.append((fifteen, f_s.at[st]))
        frecv[st, spot] = wsend[d // 2, st, rows_of(y // 2), lanes_of(d)]
        for b in (2 * st, 2 * st + 1):
            through(b)

    for k in range(3):
        ghs[k : k + 1, :] = gm[k, 0:1, :]
    send(ghs, ghr, e_s, e_r, chip((p + CHIPS - 1) % CHIPS))
    pending.append((ghr, e_s))

    sig = 1.0 / (1.0 + jnp.exp(lam))
    for b in range(NB):
        def add(r, carry):
            g = gm[r, :, block(b)]
            return tuple(carry[k] + g * xs[r + k, :, block(b)] for k in range(4)) + (carry[4] + g,)

        zero = jnp.zeros((8, BW), F32)
        acc = lax.fori_loop(0, R, add, (zero,) * 5, unroll=4)
        t_sum, a_sum, x_sum = sums[b]
        t_sum = t_sum * (8.0 * jnp.broadcast_to(sig[:, block(b)], (8, BW)))
        sb = sublane((8, BW))
        rows = zero
        for n, v in enumerate((t_sum, a_sum, x_sum) + tuple(acc)):
            for s in (1, 2, 4):
                v = v + pltpu.roll(v, s, 0)
            rows = jnp.where(sb == n, v, rows)
        for lh in range(2):
            ssend[2 * b + lh] = rows[:, lane_tile(lh)]

    @pl.loop(1, PLANE)
    def _(j):
        dev, _, to_d = plane(j)
        send(ssend.at[to_d], srecv.at[spot], fs_s, fs_r, dev)

    pending.append((srecv.at[pl.ds(0, PLANE - 1)], fs_s))
    srecv[spot] = ssend[d]

    def fold(st):
        wait_for(fifteen, f_r.at[st])

        @pl.loop(0, DEPTH)
        def _(i):
            at = pl.ds(pl.multiple_of(16 * i, 16), 16)
            v = frecv[st, 0, at, :].astype(F32)
            for u in range(1, PLANE):
                v = v + frecv[st, u, at, :].astype(F32)
            fsum[st, i] = v.astype(BF16)

        @pl.loop(1, DEPTH)
        def _(j):
            to = (z + j) % DEPTH
            send(fsum.at[st, to], zrecv.at[st, z], z_s.at[st], z_r.at[st], deep(to))

        pending.append((zrecv.at[st, pl.ds(0, DEPTH - 1)], z_s.at[st]))
        zrecv[st, z] = fsum[st, z]

    fold(0)
    wait_for(ghr, e_r)
    halo = ghr[...]
    halo = jnp.where(p == CHIPS - 1, jnp.zeros_like(halo), halo)
    for k in range(3):
        rolled = pltpu.roll(gm[k], 7, 0)
        gm[R + k] = jnp.where(sub == 7, jnp.broadcast_to(halo[k : k + 1], (8, HALF)), rolled)

    for b in range(NB):
        taps = [jnp.broadcast_to(conv_w[k : k + 1, block(b)], (8, BW)) for k in range(4)]

        @pl.loop(0, R)
        def _(r):
            v = taps[0] * gm[r + 3, :, block(b)]
            for k in range(1, 4):
                v = v + taps[k] * gm[r + 3 - k, :, block(b)]
            for lh in range(2):
                nat[2 * b + lh, pl.ds(r, 8, stride=R), :] = v[:, lane_tile(lh)]

    for k in range(TILES):
        gib[:, lane_tile(k)] = nat[k].astype(BF16)
    s_g = send(gib.at[sib_rows], gi_hbm.at[:, mine], sib_s.at[3], sib_r.at[3], sibling)
    st_g = pltpu.make_async_copy(gib.at[my_rows], gi_hbm.at[:, mine], lsem.at[3])
    st_g.start()
    pending.append((gib.at[my_rows], lsem.at[3]))

    wait_for(srecv.at[pl.ds(0, PLANE - 1)], fs_r)
    ssum[...] = jnp.sum(srecv[...], 0)

    @pl.loop(1, DEPTH)
    def _(j):
        send(ssum, szrecv.at[z], zs_s, zs_r, deep((z + j) % DEPTH))

    pending.append((szrecv.at[pl.ds(0, DEPTH - 1)], zs_s))
    szrecv[z] = ssum[...]
    fold(1)
    wait_for(szrecv.at[pl.ds(0, DEPTH - 1)], zs_r)
    small = jnp.sum(szrecv[...], 0)
    for st in range(STAGES):
        wait_for(zrecv.at[st, pl.ds(0, DEPTH - 1)], z_r.at[st])
    other = pl.ds(pl.multiple_of(8 * (1 - c), 8), 8)
    for st in range(STAGES):
        whole = zrecv[st, 0].astype(F32)
        for j in range(1, DEPTH):
            whole = whole + zrecv[st, j].astype(F32)
        own[...] = whole
        G[d, c, :, lane_tile(st)] = own[part, :]
        fin[:, lane_tile(st)] = own[other, :]
    G[d, c, :, lane_tile(STAGES)] = small
    fin[:, lane_tile(STAGES)] = small
    s_f = send(fin, G.at[d, c], sib_s.at[4], sib_r.at[4], sibling)
    s_f.wait_recv()

    @pl.loop(1, REPL)
    def _(j):
        send(G.at[d], G.at[d], g_s, g_r, peer((d + j) % REPL))

    pending.append((G.at[pl.ds(0, REPL - 1)], g_s))
    wait_for(G.at[pl.ds(0, REPL - 1)], g_r)
    st_a = pltpu.make_async_copy(G, all_hbm, lsem.at[4])
    st_a.start()

    for cp in [s_w, s_x, s_c, s_g, s_f]:
        cp.wait_send()
    s_g.wait_recv()
    for ref, sem in pending:
        wait_for(ref, sem)
    st_a.wait()


def last_kernel(gi_in, all_ref, gi_out, gw_out, dec_out, bias_out, taps_out, shift_out, gws, sem):
    copy = pltpu.make_async_copy(gi_in, gi_out.at[0], sem)
    copy.start()
    for h in range(2):
        for u in range(8):
            at = slice(h * HALF + 128 * u, h * HALF + 128 * (u + 1))
            v = all_ref[u, h, :, BW:]
            dec_out[:, at] = v[0:1]
            bias_out[:, at] = v[1:3]
            taps_out[:, at] = v[3:7]
            shift_out[:, at] = v[7:8]
            for st in range(STAGES):
                first = ((u // 2) % 2) * 8 + 4 * h + 2 * st + u // 4
                gws[u % 2, pl.ds(first, 8, stride=16), :] = all_ref[u, h, :, lane_tile(st)]
    for i in range(8):
        for g in range(2):
            for lh in range(2):
                gw_out[i, g, :, lane_tile(lh)] = gws[lh, i * 16 + g * 8 : i * 16 + g * 8 + 8, :]
    copy.wait()


def per_device(inputs, gate_weight, gate_bias, decay_param, conv_weight, conv_bias, cotangent):
    vmem = pl.BlockSpec(memory_space=pltpu.VMEM)
    hbm = pl.BlockSpec(memory_space=pltpu.HBM)
    dma = pltpu.SemaphoreType.DMA
    big = pltpu.VMEM((R, 8, HALF), F32)
    gi, packed = pl.pallas_call(
        main_kernel,
        name="main",
        out_shape=(
            jax.ShapeDtypeStruct((ROWS, WIDTH), BF16),
            jax.ShapeDtypeStruct((REPL, 2, 8, BW + 128), F32),
        ),
        in_specs=[hbm] * 7,
        out_specs=(hbm, hbm),
        scratch_shapes=[
            pltpu.VMEM((2, HALF), F32),
            pltpu.VMEM((1, HALF), F32),
            pltpu.VMEM((4, HALF), F32),
            pltpu.VMEM((1, HALF), F32),
            pltpu.VMEM((SPAN, HALF), BF16),
            pltpu.VMEM((SPAN, HALF), BF16),
            pltpu.VMEM((8, 2, 8, BW), BF16),
            pltpu.VMEM((2, 128, 128), F32),
            pltpu.VMEM((2, REPL, STAGES, 8, 128), F32),
            pltpu.VMEM((STAGES, 16, 128), F32),
            pltpu.VMEM((4, STAGES, BW, BW), BF16),
            pltpu.VMEM((16, HALF), BF16),
            pltpu.VMEM((TILES, SPAN, 128), F32),
            pltpu.VMEM((TILES, SPAN, 128), F32),
            pltpu.VMEM((R + 3, 8, HALF), F32),
            big,
            pltpu.VMEM((SPAN, HALF), BF16),
            pltpu.VMEM((NB, BW, SPAN), BF16),
            pltpu.VMEM((8, SPAN, BW), F32),
            big, big, big, big, big, big, big, big,
            pltpu.VMEM((8, SPAN, BW), BF16),
            pltpu.VMEM((R + 3, 8, HALF), F32),
            pltpu.VMEM((STAGES, 2, 8, 128), F32),
            pltpu.VMEM((STAGES, CHIPS, 8, 128), F32),
            pltpu.VMEM((STAGES, 2, 4, 128), F32),
            pltpu.VMEM((8, HALF), F32),
            pltpu.VMEM((8, HALF), F32),
            pltpu.VMEM((4, STAGES, BW, BW), BF16),
            pltpu.VMEM((STAGES, PLANE, 128, 128), BF16),
            pltpu.VMEM((16, 128), F32),
            pltpu.VMEM((STAGES, DEPTH, 16, 128), BF16),
            pltpu.VMEM((STAGES, DEPTH, 16, 128), BF16),
            pltpu.VMEM((8, 8, 128), F32),
            pltpu.VMEM((PLANE, 8, 128), F32),
            pltpu.VMEM((8, 128), F32),
            pltpu.VMEM((DEPTH, 8, 128), F32),
            pltpu.VMEM((8, BW + 128), F32),
            pltpu.VMEM((REPL, 2, 8, BW + 128), F32),
            pltpu.VMEM((SPAN, HALF), BF16),
            dma((9,)), dma((7,)), dma((7,)),
            dma, dma, dma, dma, dma((STAGES,)), dma((STAGES,)),
            dma((STAGES,)), dma((STAGES,)), dma, dma, dma((STAGES,)), dma((STAGES,)), dma, dma,
            dma((STAGES,)), dma((STAGES,)), dma, dma, dma, dma,
        ],
        compiler_params=pltpu.CompilerParams(
            collective_id=0, has_side_effects=True, vmem_limit_bytes=60 * 2**20
        ),
    )(
        inputs, gate_weight, gate_bias, decay_param.reshape(1, WIDTH), conv_weight,
        conv_bias.reshape(1, WIDTH), cotangent,
    )
    gi, gw, dec, bias, taps, shift = pl.pallas_call(
        last_kernel,
        name="last",
        out_shape=(
            jax.ShapeDtypeStruct((1, ROWS, WIDTH), BF16),
            jax.ShapeDtypeStruct((8, 2, 8, BW), F32),
            jax.ShapeDtypeStruct((1, WIDTH), F32),
            jax.ShapeDtypeStruct((2, WIDTH), F32),
            jax.ShapeDtypeStruct((4, WIDTH), F32),
            jax.ShapeDtypeStruct((1, WIDTH), F32),
        ),
        in_specs=[hbm, vmem],
        out_specs=(hbm,) + (vmem,) * 5,
        scratch_shapes=[pltpu.VMEM((2, 128, 128), F32), dma],
        compiler_params=pltpu.CompilerParams(vmem_limit_bytes=60 * 2**20),
    )(gi, packed)
    return gi, gw, dec.reshape(WIDTH), bias, taps, shift.reshape(WIDTH)


def solution(mesh):
    placed = (
        P("dp", "ctx", None),
        P("ctx", None, None, None),
        P(),
        P(),
        P(),
        P(),
        P("dp", "ctx", None),
    )
    return jax.shard_map(
        per_device,
        mesh=mesh,
        in_specs=placed,
        out_specs=(P("dp", "ctx", None), P("ctx", None, None, None), P(), P(), P(), P()),
        check_vma=False,
    )
```

```python
import jax
import jax.numpy as jnp
from jax import lax
from jax.experimental import pallas as pl
from jax.experimental.pallas import tpu as pltpu
from jax.sharding import PartitionSpec as P

MESH = pl.DeviceIdType.MESH
F32 = jnp.float32
BF16 = jnp.bfloat16
CHIPS = 16
PLANE = 16
DEPTH = 8
REPL = 8
ROWS = 128
SPAN = 256
WIDTH = 2048
HALF = 1024
BW = 256
NB = HALF // BW
R = SPAN // 8
TILES = HALF // 128
STAGES = 2


def wait_for(ref, sem):
    pltpu.make_async_copy(ref, ref, sem).wait()


def sublane(shape):
    return lax.broadcasted_iota(jnp.int32, shape, 0)


def sigmoid(x):
    return 0.5 * jnp.tanh(0.5 * x) + 0.5


def softplus(x):
    e = jnp.exp(-jnp.abs(x))
    z = e / (2.0 + e)
    z2 = z * z
    s = jnp.full_like(z, 1.0 / 17.0)
    for n in (15, 13, 11, 9, 7, 5, 3, 1):
        s = s * z2 + 1.0 / n
    return jnp.maximum(x, 0.0) + 2.0 * z * s


def lane_tile(i):
    return slice(i * 128, (i + 1) * 128)


def block(b):
    return slice(b * BW, (b + 1) * BW)


def main_kernel(
    x_hbm, w_hbm, gb_hbm, lam_hbm, cw_hbm, cb_hbm, cot_hbm,
    gi_hbm, all_hbm,
    gb_ref, lam_ref, cw_ref, cb_ref, xb, cotb, wsh, wf, wu, wpair, W, xhalo, nat, natc, xs, cs, mb, mt, pre,
    dec, drv, qq, m1, m2, m3, oma, hp, gp, gm, dsend, drecv, sin, ghs, ghr,
    wsend, frecv, own, fsum, zrecv, ssend, srecv, ssum, szrecv, fin, G, gib,
    lsem, sib_s, sib_r, c1_s, c1_r, hal_s, hal_r, c2_s, c2_r, d_s, d_r, e_s, e_r,
    f_s, f_r, fs_s, fs_r, z_s, z_r, zs_s, zs_r, g_s, g_r,
):
    ctx = lax.axis_index("ctx")
    d = lax.axis_index("dp")
    p = ctx // 2
    c = ctx % 2
    z = p % DEPTH
    y = 2 * (p // DEPTH) + d // 4
    x = d % 4
    spot = 4 * y + x
    sibling = {"ctx": 2 * p + 1 - c, "dp": d}

    def chip(j):
        return {"ctx": 2 * j + c, "dp": d}

    def deep(j):
        return {"ctx": 2 * (p - z + j) + c, "dp": d}

    def peer(u):
        return {"ctx": ctx, "dp": u}

    def plane(j):
        to_x, to_y = (x + j % 4) % 4, (y + j // 4) % 4
        to_d = 4 * (to_y % 2) + to_x
        return {"ctx": 2 * (DEPTH * (to_y // 2) + z) + c, "dp": to_d}, to_y // 2, to_d

    def rows_of(h):
        return pl.ds(pl.multiple_of(128 * h, 128), 128)

    def lanes_of(u):
        return pl.ds(pl.multiple_of(128 * (u % 2), 128), 128)

    def send(src, dst, ss, rs, dev):
        cp = pltpu.make_async_remote_copy(
            src_ref=src, dst_ref=dst, send_sem=ss, recv_sem=rs, device_id=dev, device_id_type=MESH
        )
        cp.start()
        return cp

    bar = pltpu.get_barrier_semaphore()
    pl.semaphore_signal(bar, inc=1, device_id=sibling, device_id_type=MESH)

    @pl.loop(1, CHIPS)
    def _(j):
        pl.semaphore_signal(bar, inc=1, device_id=chip((p + j) % CHIPS), device_id_type=MESH)

    @pl.loop(1, PLANE)
    def _(j):
        @pl.when(j != PLANE // 2)
        def _():
            pl.semaphore_signal(bar, inc=1, device_id=plane(j)[0], device_id_type=MESH)

    mine = pl.ds(pl.multiple_of(HALF * c, HALF), HALF)
    theirs = pl.ds(pl.multiple_of(HALF * (1 - c), HALF), HALF)
    my_rows = pl.ds(pl.multiple_of(ROWS * c, ROWS), ROWS)
    sib_rows = pl.ds(pl.multiple_of(ROWS * (1 - c), ROWS), ROWS)

    ld_w = pltpu.make_async_copy(w_hbm, wsh, lsem.at[0])
    ld_w.start()
    ld_x = pltpu.make_async_copy(x_hbm.at[0, :, mine], xb.at[my_rows], lsem.at[1])
    ld_x.start()
    ld_c = pltpu.make_async_copy(cot_hbm.at[0, :, mine], cotb.at[my_rows], lsem.at[2])
    ld_c.start()
    lds = []
    for n, (src, dst) in enumerate(
        ((gb_hbm, gb_ref), (lam_hbm, lam_ref), (cw_hbm, cw_ref), (cb_hbm, cb_ref))
    ):
        lds.append(pltpu.make_async_copy(src.at[:, mine], dst, lsem.at[5 + n]))
        lds[-1].start()
    pending = []

    ld_w.wait()
    for i in range(8):
        for g in range(2):
            v = wsh[i, g].astype(F32)
            for lh in range(2):
                wf[lh, i * 16 + g * 8 : i * 16 + g * 8 + 8, :] = v[:, lane_tile(lh)]
    for h in range(2):
        for u in range(REPL):
            for st in range(STAGES):
                first = ((u // 2) % 2) * 8 + 4 * h + 2 * st + u // 4
                wu[h, u, st] = wf[u % 2, pl.ds(first, 8, stride=16), :]

    pl.semaphore_wait(bar, 1 + (CHIPS - 1) + (PLANE - 2))

    part = pl.ds(pl.multiple_of(8 * c, 8), 8)
    s_w = send(wu.at[1 - c, d], wpair.at[:, part], sib_s.at[0], sib_r.at[0], sibling)
    s_x = send(x_hbm.at[0, :, theirs], xb.at[my_rows], sib_s.at[1], sib_r.at[1], sibling)
    s_c = send(cot_hbm.at[0, :, theirs], cotb.at[my_rows], sib_s.at[2], sib_r.at[2], sibling)
    wpair[:, part, :] = wu[c, d]
    s_w.wait_recv()
    my16 = pl.ds(pl.multiple_of(16 * p, 16), 16)
    mine_w = W.at[d // 2, :, my16, lanes_of(d)]
    mine_w[...] = wpair[...].astype(BF16)

    @pl.loop(1, DEPTH)
    def _(j):
        send(mine_w, mine_w, c1_s, c1_r, deep((z + j) % DEPTH))

    seven = wsend.at[0, :, pl.ds(0, 16 * (DEPTH - 1)), pl.ds(0, 128)]
    pending.append((seven, c1_s))

    ld_x.wait()
    s_x.wait_recv()
    send(xb.at[pl.ds(SPAN - 16, 16)], xhalo, hal_s, hal_r, chip((p + 1) % CHIPS))
    pending.append((xhalo, hal_s))
    for k in range(TILES):
        nat[k] = xb[:, lane_tile(k)].astype(F32)

    @pl.loop(0, R)
    def _(r):
        for k in range(TILES):
            xs[3 + r, :, lane_tile(k)] = nat[k, pl.ds(r, 8, stride=R), :]

    wait_for(seven, c1_r)
    fifteen = frecv.at[0, pl.ds(0, PLANE - 1)]
    for st in range(STAGES):
        @pl.loop(1, PLANE)
        def _(j):
            mine_s = W.at[d // 2, st, rows_of(y // 2), lanes_of(d)]
            send(mine_s, mine_s, c2_s.at[st], c2_r.at[st], plane(j)[0])

        pending.append((fifteen, c2_s.at[st]))

    ld_c.wait()
    s_c.wait_recv()
    for k in range(TILES):
        natc[k] = cotb[:, lane_tile(k)].astype(F32)

    @pl.loop(0, R)
    def _(r):
        for k in range(TILES):
            cs[r, :, lane_tile(k)] = natc[k, pl.ds(r, 8, stride=R), :]

    wait_for(xhalo, hal_r)
    hal = xhalo[...].astype(F32)
    hal = jnp.where(p == 0, jnp.zeros_like(hal), hal)
    sub = sublane((8, HALF))
    for k in range(3):
        rolled = pltpu.roll(xs[3 + R - 3 + k], 1, 0)
        xs[k] = jnp.where(sub == 0, jnp.broadcast_to(hal[13 + k : 14 + k], (8, HALF)), rolled)

    for ld in lds:
        ld.wait()
    conv_w = cw_ref[...]
    conv_b = cb_ref[...]
    for b in range(NB):
        taps = [jnp.broadcast_to(conv_w[k : k + 1, block(b)], (8, BW)) for k in range(4)]
        shift = jnp.broadcast_to(conv_b[:, block(b)], (8, BW))

        @pl.loop(0, R // 2)
        def _(i):
            v = [xs[2 * i + k, :, block(b)] for k in range(5)]
            out = []
            for o in range(2):
                m = shift + taps[0] * v[o]
                for k in range(1, 4):
                    m = m + taps[k] * v[o + k]
                out.append(m)
            mb[pl.ds(pl.multiple_of(16 * i, 16), 16), block(b)] = jnp.concatenate(out, 0).astype(BF16)

        mt[b] = mb[:, block(b)].astype(F32).T.astype(BF16)

    lam = lam_ref[...]
    neg8rate = -8.0 * softplus(-lam)
    gate_b = gb_ref[...]
    ends = []

    def gates(b):
        st, k = b // 2, 2 * (b % 2)
        for g in range(2):
            pre[2 * b + g] = jnp.dot(mb[:, block(b)], W[k + g, st], preferred_element_type=F32)
        nr = jnp.broadcast_to(neg8rate[:, block(b)], (8, BW))
        ba = jnp.broadcast_to(gate_b[0:1, block(b)], (8, BW))
        bx = jnp.broadcast_to(gate_b[1:2, block(b)], (8, BW))

        def step(i, carry):
            prod, hid, kk, logs = carry
            two = mb[pl.ds(pl.multiple_of(16 * i, 16), 16), block(b)].astype(F32)
            for o in range(2):
                r = 2 * i + o
                at = pl.ds(pl.multiple_of(8 * r, 8), 8)
                ga = sigmoid(pre[2 * b, at, :] + ba)
                gx = sigmoid(pre[2 * b + 1, at, :] + bx)
                m = two[8 * o : 8 * o + 8]
                ld = ga * nr
                a = jnp.exp(ld)
                sq = 1.0 - a * a
                mult = jnp.sqrt(sq)
                gm_ = gx * m
                drive = mult * gm_
                dec[r, :, block(b)] = a
                drv[r, :, block(b)] = drive
                qq[r, :, block(b)] = gm_ * a * lax.rsqrt(jnp.maximum(sq, 0.05))
                m1[r, :, block(b)] = a * ga
                oma[r, :, block(b)] = (1.0 - ga) * nr
                m2[r, :, block(b)] = drive * (1.0 - gx)
                m3[r, :, block(b)] = mult * gx
                hid = a * hid + drive
                prod = prod * a
                kk = kk + prod * cs[r, :, block(b)]
                logs = logs + ld
            return prod, hid, kk, logs

        zero = jnp.zeros((8, BW), F32)
        prod, hid, kk, logs = lax.fori_loop(
            0, R // 2, step, (jnp.ones((8, BW), F32), zero, zero, zero)
        )
        sb = sublane((8, BW))
        fp, fh = prod, hid
        bp, bk = prod, kk
        for s in (1, 2, 4):
            mp, mh = pltpu.roll(fp, s, 0), pltpu.roll(fh, s, 0)
            fh = jnp.where(sb >= s, fp * mh + fh, fh)
            fp = jnp.where(sb >= s, fp * mp, fp)
            mp, mk = pltpu.roll(bp, 8 - s, 0), pltpu.roll(bk, 8 - s, 0)
            bk = jnp.where(sb < 8 - s, bp * mk + bk, bk)
            bp = jnp.where(sb < 8 - s, bp * mp, bp)
            logs = logs + pltpu.roll(logs, s, 0)
        one = jnp.ones((8, BW), F32)
        ends.append((
            jnp.where(sb == 0, one, pltpu.roll(fp, 1, 0)),
            jnp.where(sb == 0, zero, pltpu.roll(fh, 1, 0)),
            jnp.where(sb == 7, one, pltpu.roll(bp, 7, 0)),
            jnp.where(sb == 7, zero, pltpu.roll(bk, 7, 0)),
        ))
        for lh in range(2):
            k = 2 * (b % 2) + lh
            dsend[st, 0, k : k + 1, :] = logs[0:1, lane_tile(lh)]
            dsend[st, 1, k : k + 1, :] = logs[0:1, lane_tile(lh)]
            dsend[st, 0, 4 + k : 5 + k, :] = fh[7:8, lane_tile(lh)]
            dsend[st, 1, 4 + k : 5 + k, :] = bk[0:1, lane_tile(lh)]

    for st in range(STAGES):
        wait_for(fifteen, c2_r.at[st])
        for b in (2 * st, 2 * st + 1):
            gates(b)

        @pl.loop(1, CHIPS)
        def _(j):
            to = (p + j) % CHIPS
            send(dsend.at[st, jnp.where(to > p, 0, 1)], drecv.at[st, p], d_s.at[st], d_r.at[st], chip(to))

        pending.append((drecv.at[st, pl.ds(0, CHIPS - 1)], d_s.at[st]))
        drecv[st, p] = jnp.zeros((8, 128), F32)

    sums = []

    def grads(b):
        st, k = b // 2, 2 * (b % 2)

        def wide(n):
            return jnp.concatenate(
                [jnp.broadcast_to(sin[st, n, k + lh : k + lh + 1, :], (8, 128)) for lh in range(2)], 1
            )

        hin = ends[b][1] + ends[b][0] * wide(0)
        kin = ends[b][3] + ends[b][2] * wide(1)

        def up(r, h):
            hp[r, :, block(b)] = h
            return dec[r, :, block(b)] * h + drv[r, :, block(b)]

        lax.fori_loop(0, R, up, hin, unroll=4)

        def down(n, carry):
            kk, t_sum, a_sum, x_sum = carry
            i = R // 2 - 1 - n
            outs = [[None, None], [None, None]]
            for o in (1, 0):
                r = 2 * i + o
                gr = cs[r, :, block(b)] + kk
                kk = dec[r, :, block(b)] * gr
                t = (hp[r, :, block(b)] - qq[r, :, block(b)]) * m1[r, :, block(b)] * gr
                ga = t * oma[r, :, block(b)]
                gx = gr * m2[r, :, block(b)]
                gm[r, :, block(b)] = gr * m3[r, :, block(b)]
                t_sum, a_sum, x_sum = t_sum + t, a_sum + ga, x_sum + gx
                outs[0][o], outs[1][o] = ga, gx
            at = pl.ds(pl.multiple_of(16 * i, 16), 16)
            gp[2 * b, at, :] = jnp.concatenate(outs[0], 0).astype(BF16)
            gp[2 * b + 1, at, :] = jnp.concatenate(outs[1], 0).astype(BF16)
            return kk, t_sum, a_sum, x_sum

        zero = jnp.zeros((8, BW), F32)
        _, t_sum, a_sum, x_sum = lax.fori_loop(0, R // 2, down, (kin, zero, zero, zero))
        sums.append([t_sum, a_sum, x_sum])
        for g in range(2):
            wsend[k + g, st] = jnp.dot(mt[b], gp[2 * b + g], preferred_element_type=F32).astype(BF16)

    def through(b):
        st, k = b // 2, 2 * (b % 2)
        nt = (((1,), (1,)), ((), ()))
        back = lax.dot_general(gp[2 * b], W[k, st], nt, preferred_element_type=F32)
        back = back + lax.dot_general(gp[2 * b + 1], W[k + 1, st], nt, preferred_element_type=F32)
        gm[0:R, :, block(b)] = gm[0:R, :, block(b)] + back.reshape(R, 8, BW)

    for st in range(STAGES):
        wait_for(drecv.at[st, pl.ds(0, CHIPS - 1)], d_r.at[st])
        state = jnp.zeros((4, 128), F32)
        carry_in = jnp.zeros((4, 128), F32)
        for j in range(CHIPS):
            v = drecv[st, j]
            state = jnp.where(j < p, jnp.exp(v[:4]) * state + v[4:], state)
            v = drecv[st, CHIPS - 1 - j]
            carry_in = jnp.where(CHIPS - 1 - j > p, jnp.exp(v[:4]) * carry_in + v[4:], carry_in)
        sin[st, 0] = state
        sin[st, 1] = carry_in
        for b in (2 * st, 2 * st + 1):
            grads(b)

        @pl.loop(1, PLANE)
        def _(j):
            dev, to_h, to_d = plane(j)
            send(
                wsend.at[to_d // 2, st, rows_of(to_h), lanes_of(to_d)],
                frecv.at[st, spot], f_s.at[st], f_r.at[st], dev,
            )

        pending.append((fifteen, f_s.at[st]))
        frecv[st, spot] = wsend[d // 2, st, rows_of(y // 2), lanes_of(d)]
        for b in (2 * st, 2 * st + 1):
            through(b)

    for k in range(3):
        ghs[k : k + 1, :] = gm[k, 0:1, :]
    send(ghs, ghr, e_s, e_r, chip((p + CHIPS - 1) % CHIPS))
    pending.append((ghr, e_s))

    sig = 1.0 / (1.0 + jnp.exp(lam))
    for b in range(NB):
        def add(r, carry):
            g = gm[r, :, block(b)]
            return tuple(carry[k] + g * xs[r + k, :, block(b)] for k in range(4)) + (carry[4] + g,)

        zero = jnp.zeros((8, BW), F32)
        acc = lax.fori_loop(0, R, add, (zero,) * 5, unroll=4)
        t_sum, a_sum, x_sum = sums[b]
        t_sum = t_sum * (8.0 * jnp.broadcast_to(sig[:, block(b)], (8, BW)))
        sb = sublane((8, BW))
        rows = zero
        for n, v in enumerate((t_sum, a_sum, x_sum) + tuple(acc)):
            for s in (1, 2, 4):
                v = v + pltpu.roll(v, s, 0)
            rows = jnp.where(sb == n, v, rows)
        for lh in range(2):
            ssend[2 * b + lh] = rows[:, lane_tile(lh)]

    @pl.loop(1, PLANE)
    def _(j):
        dev, _, to_d = plane(j)
        send(ssend.at[to_d], srecv.at[spot], fs_s, fs_r, dev)

    pending.append((srecv.at[pl.ds(0, PLANE - 1)], fs_s))
    srecv[spot] = ssend[d]

    def fold(st):
        wait_for(fifteen, f_r.at[st])

        @pl.loop(0, DEPTH)
        def _(i):
            at = pl.ds(pl.multiple_of(16 * i, 16), 16)
            v = frecv[st, 0, at, :].astype(F32)
            for u in range(1, PLANE):
                v = v + frecv[st, u, at, :].astype(F32)
            fsum[st, i] = v.astype(BF16)

        @pl.loop(1, DEPTH)
        def _(j):
            to = (z + j) % DEPTH
            send(fsum.at[st, to], zrecv.at[st, z], z_s.at[st], z_r.at[st], deep(to))

        pending.append((zrecv.at[st, pl.ds(0, DEPTH - 1)], z_s.at[st]))
        zrecv[st, z] = fsum[st, z]

    fold(0)
    wait_for(ghr, e_r)
    halo = ghr[...]
    halo = jnp.where(p == CHIPS - 1, jnp.zeros_like(halo), halo)
    for k in range(3):
        rolled = pltpu.roll(gm[k], 7, 0)
        gm[R + k] = jnp.where(sub == 7, jnp.broadcast_to(halo[k : k + 1], (8, HALF)), rolled)

    for b in range(NB):
        taps = [jnp.broadcast_to(conv_w[k : k + 1, block(b)], (8, BW)) for k in range(4)]

        @pl.loop(0, R)
        def _(r):
            v = taps[0] * gm[r + 3, :, block(b)]
            for k in range(1, 4):
                v = v + taps[k] * gm[r + 3 - k, :, block(b)]
            for lh in range(2):
                nat[2 * b + lh, pl.ds(r, 8, stride=R), :] = v[:, lane_tile(lh)]

    for k in range(TILES):
        gib[:, lane_tile(k)] = nat[k].astype(BF16)
    s_g = send(gib.at[sib_rows], gi_hbm.at[:, mine], sib_s.at[3], sib_r.at[3], sibling)
    st_g = pltpu.make_async_copy(gib.at[my_rows], gi_hbm.at[:, mine], lsem.at[3])
    st_g.start()
    pending.append((gib.at[my_rows], lsem.at[3]))

    wait_for(srecv.at[pl.ds(0, PLANE - 1)], fs_r)
    ssum[...] = jnp.sum(srecv[...], 0)

    @pl.loop(1, DEPTH)
    def _(j):
        send(ssum, szrecv.at[z], zs_s, zs_r, deep((z + j) % DEPTH))

    pending.append((szrecv.at[pl.ds(0, DEPTH - 1)], zs_s))
    szrecv[z] = ssum[...]
    fold(1)
    wait_for(szrecv.at[pl.ds(0, DEPTH - 1)], zs_r)
    small = jnp.sum(szrecv[...], 0)
    for st in range(STAGES):
        wait_for(zrecv.at[st, pl.ds(0, DEPTH - 1)], z_r.at[st])
    other = pl.ds(pl.multiple_of(8 * (1 - c), 8), 8)
    for st in range(STAGES):
        whole = zrecv[st, 0].astype(F32)
        for j in range(1, DEPTH):
            whole = whole + zrecv[st, j].astype(F32)
        own[...] = whole
        G[d, c, :, lane_tile(st)] = own[part, :]
        fin[:, lane_tile(st)] = own[other, :]
    G[d, c, :, lane_tile(STAGES)] = small
    fin[:, lane_tile(STAGES)] = small
    s_f = send(fin, G.at[d, c], sib_s.at[4], sib_r.at[4], sibling)
    s_f.wait_recv()

    @pl.loop(1, REPL)
    def _(j):
        send(G.at[d], G.at[d], g_s, g_r, peer((d + j) % REPL))

    pending.append((G.at[pl.ds(0, REPL - 1)], g_s))
    wait_for(G.at[pl.ds(0, REPL - 1)], g_r)
    st_a = pltpu.make_async_copy(G, all_hbm, lsem.at[4])
    st_a.start()

    for cp in [s_w, s_x, s_c, s_g, s_f]:
        cp.wait_send()
    s_g.wait_recv()
    for ref, sem in pending:
        wait_for(ref, sem)
    st_a.wait()


def last_kernel(gi_in, all_ref, gi_out, gw_out, dec_out, bias_out, taps_out, shift_out, gws, via, l_sem, s_sem):
    parts = [pl.ds(k * (ROWS // 4), ROWS // 4) for k in range(4)]
    loads = [pltpu.make_async_copy(gi_in.at[at], via.at[at], l_sem.at[k]) for k, at in enumerate(parts)]
    stores = [pltpu.make_async_copy(via.at[at], gi_out.at[0, at], s_sem.at[k]) for k, at in enumerate(parts)]
    for cp in loads:
        cp.start()
    for k in range(4):
        loads[k].wait()
        stores[k].start()
    for h in range(2):
        for u in range(8):
            at = slice(h * HALF + 128 * u, h * HALF + 128 * (u + 1))
            v = all_ref[u, h, :, BW:]
            dec_out[:, at] = v[0:1]
            bias_out[:, at] = v[1:3]
            taps_out[:, at] = v[3:7]
            shift_out[:, at] = v[7:8]
            for st in range(STAGES):
                first = ((u // 2) % 2) * 8 + 4 * h + 2 * st + u // 4
                gws[u % 2, pl.ds(first, 8, stride=16), :] = all_ref[u, h, :, lane_tile(st)]
    for i in range(8):
        for g in range(2):
            for lh in range(2):
                gw_out[i, g, :, lane_tile(lh)] = gws[lh, i * 16 + g * 8 : i * 16 + g * 8 + 8, :]
    for cp in stores:
        cp.wait()


def per_device(inputs, gate_weight, gate_bias, decay_param, conv_weight, conv_bias, cotangent):
    vmem = pl.BlockSpec(memory_space=pltpu.VMEM)
    hbm = pl.BlockSpec(memory_space=pltpu.HBM)
    dma = pltpu.SemaphoreType.DMA
    big = pltpu.VMEM((R, 8, HALF), F32)
    gi, packed = pl.pallas_call(
        main_kernel,
        name="main",
        out_shape=(
            jax.ShapeDtypeStruct((ROWS, WIDTH), BF16),
            jax.ShapeDtypeStruct((REPL, 2, 8, BW + 128), F32),
        ),
        in_specs=[hbm] * 7,
        out_specs=(hbm, hbm),
        scratch_shapes=[
            pltpu.VMEM((2, HALF), F32),
            pltpu.VMEM((1, HALF), F32),
            pltpu.VMEM((4, HALF), F32),
            pltpu.VMEM((1, HALF), F32),
            pltpu.VMEM((SPAN, HALF), BF16),
            pltpu.VMEM((SPAN, HALF), BF16),
            pltpu.VMEM((8, 2, 8, BW), BF16),
            pltpu.VMEM((2, 128, 128), F32),
            pltpu.VMEM((2, REPL, STAGES, 8, 128), F32),
            pltpu.VMEM((STAGES, 16, 128), F32),
            pltpu.VMEM((4, STAGES, BW, BW), BF16),
            pltpu.VMEM((16, HALF), BF16),
            pltpu.VMEM((TILES, SPAN, 128), F32),
            pltpu.VMEM((TILES, SPAN, 128), F32),
            pltpu.VMEM((R + 3, 8, HALF), F32),
            big,
            pltpu.VMEM((SPAN, HALF), BF16),
            pltpu.VMEM((NB, BW, SPAN), BF16),
            pltpu.VMEM((8, SPAN, BW), F32),
            big, big, big, big, big, big, big, big,
            pltpu.VMEM((8, SPAN, BW), BF16),
            pltpu.VMEM((R + 3, 8, HALF), F32),
            pltpu.VMEM((STAGES, 2, 8, 128), F32),
            pltpu.VMEM((STAGES, CHIPS, 8, 128), F32),
            pltpu.VMEM((STAGES, 2, 4, 128), F32),
            pltpu.VMEM((8, HALF), F32),
            pltpu.VMEM((8, HALF), F32),
            pltpu.VMEM((4, STAGES, BW, BW), BF16),
            pltpu.VMEM((STAGES, PLANE, 128, 128), BF16),
            pltpu.VMEM((16, 128), F32),
            pltpu.VMEM((STAGES, DEPTH, 16, 128), BF16),
            pltpu.VMEM((STAGES, DEPTH, 16, 128), BF16),
            pltpu.VMEM((8, 8, 128), F32),
            pltpu.VMEM((PLANE, 8, 128), F32),
            pltpu.VMEM((8, 128), F32),
            pltpu.VMEM((DEPTH, 8, 128), F32),
            pltpu.VMEM((8, BW + 128), F32),
            pltpu.VMEM((REPL, 2, 8, BW + 128), F32),
            pltpu.VMEM((SPAN, HALF), BF16),
            dma((9,)), dma((7,)), dma((7,)),
            dma, dma, dma, dma, dma((STAGES,)), dma((STAGES,)),
            dma((STAGES,)), dma((STAGES,)), dma, dma, dma((STAGES,)), dma((STAGES,)), dma, dma,
            dma((STAGES,)), dma((STAGES,)), dma, dma, dma, dma,
        ],
        compiler_params=pltpu.CompilerParams(
            collective_id=0, has_side_effects=True, vmem_limit_bytes=60 * 2**20
        ),
    )(
        inputs, gate_weight, gate_bias, decay_param.reshape(1, WIDTH), conv_weight,
        conv_bias.reshape(1, WIDTH), cotangent,
    )
    gi, gw, dec, bias, taps, shift = pl.pallas_call(
        last_kernel,
        name="last",
        out_shape=(
            jax.ShapeDtypeStruct((1, ROWS, WIDTH), BF16),
            jax.ShapeDtypeStruct((8, 2, 8, BW), F32),
            jax.ShapeDtypeStruct((1, WIDTH), F32),
            jax.ShapeDtypeStruct((2, WIDTH), F32),
            jax.ShapeDtypeStruct((4, WIDTH), F32),
            jax.ShapeDtypeStruct((1, WIDTH), F32),
        ),
        in_specs=[hbm, vmem],
        out_specs=(hbm,) + (vmem,) * 5,
        scratch_shapes=[pltpu.VMEM((2, 128, 128), F32), pltpu.VMEM((ROWS, WIDTH), BF16), dma((4,)), dma((4,))],
        compiler_params=pltpu.CompilerParams(vmem_limit_bytes=60 * 2**20),
    )(gi, packed)
    return gi, gw, dec.reshape(WIDTH), bias, taps, shift.reshape(WIDTH)


def solution(mesh):
    placed = (
        P("dp", "ctx", None),
        P("ctx", None, None, None),
        P(),
        P(),
        P(),
        P(),
        P("dp", "ctx", None),
    )
    return jax.shard_map(
        per_device,
        mesh=mesh,
        in_specs=placed,
        out_specs=(P("dp", "ctx", None), P("ctx", None, None, None), P(), P(), P(), P()),
        check_vma=False,
    )
```

```python
import jax
import jax.numpy as jnp
from jax import lax
from jax.experimental import pallas as pl
from jax.experimental.pallas import tpu as pltpu
from jax.sharding import PartitionSpec as P

MESH = pl.DeviceIdType.MESH
F32 = jnp.float32
BF16 = jnp.bfloat16
CHIPS = 16
PLANE = 16
DEPTH = 8
REPL = 8
ROWS = 128
SPAN = 256
WIDTH = 2048
HALF = 1024
BW = 256
NB = HALF // BW
R = SPAN // 8
TILES = HALF // 128
STAGES = 2


def wait_for(ref, sem):
    pltpu.make_async_copy(ref, ref, sem).wait()


def sublane(shape):
    return lax.broadcasted_iota(jnp.int32, shape, 0)


def sigmoid(x):
    return 0.5 * jnp.tanh(0.5 * x) + 0.5


def softplus(x):
    e = jnp.exp(-jnp.abs(x))
    z = e / (2.0 + e)
    z2 = z * z
    s = jnp.full_like(z, 1.0 / 17.0)
    for n in (15, 13, 11, 9, 7, 5, 3, 1):
        s = s * z2 + 1.0 / n
    return jnp.maximum(x, 0.0) + 2.0 * z * s


def lane_tile(i):
    return slice(i * 128, (i + 1) * 128)


def block(b):
    return slice(b * BW, (b + 1) * BW)


def main_kernel(
    x_hbm, w_hbm, gb_hbm, lam_hbm, cw_hbm, cb_hbm, cot_hbm,
    gi_hbm, all_hbm,
    gb_ref, lam_ref, cw_ref, cb_ref, xb, cotb, wsh, wf, wu, wpair, W, xhalo, nat, natc, xs, cs, mb, mt, pre,
    dec, drv, qq, m1, m2, m3, oma, hp, gp, gm, dsend, drecv, sin, ghs, ghr,
    wsend, frecv, own, fsum, zrecv, ssend, srecv, ssum, szrecv, fin, G, gib,
    lsem, sib_s, sib_r, c1_s, c1_r, hal_s, hal_r, za_s, za_r, c2_s, c2_r, d_s, d_r, e_s, e_r,
    f_s, f_r, fs_s, fs_r, z_s, z_r, zs_s, zs_r, g_s, g_r,
):
    ctx = lax.axis_index("ctx")
    d = lax.axis_index("dp")
    p = ctx // 2
    c = ctx % 2
    z = p % DEPTH
    y = 2 * (p // DEPTH) + d // 4
    x = d % 4
    spot = 4 * y + x
    sibling = {"ctx": 2 * p + 1 - c, "dp": d}

    def chip(j):
        return {"ctx": 2 * j + c, "dp": d}

    def deep(j):
        return {"ctx": 2 * (p - z + j) + c, "dp": d}

    def peer(u):
        return {"ctx": ctx, "dp": u}

    def plane(j):
        to_x, to_y = (x + j % 4) % 4, (y + j // 4) % 4
        to_d = 4 * (to_y % 2) + to_x
        return {"ctx": 2 * (DEPTH * (to_y // 2) + z) + c, "dp": to_d}, to_y // 2, to_d

    def rows_of(h):
        return pl.ds(pl.multiple_of(128 * h, 128), 128)

    def lanes_of(u):
        return pl.ds(pl.multiple_of(128 * (u % 2), 128), 128)

    def send(src, dst, ss, rs, dev):
        cp = pltpu.make_async_remote_copy(
            src_ref=src, dst_ref=dst, send_sem=ss, recv_sem=rs, device_id=dev, device_id_type=MESH
        )
        cp.start()
        return cp

    bar = pltpu.get_barrier_semaphore()
    pl.semaphore_signal(bar, inc=1, device_id=sibling, device_id_type=MESH)

    @pl.loop(1, CHIPS)
    def _(j):
        pl.semaphore_signal(bar, inc=1, device_id=chip((p + j) % CHIPS), device_id_type=MESH)

    @pl.loop(1, PLANE)
    def _(j):
        @pl.when(j != PLANE // 2)
        def _():
            pl.semaphore_signal(bar, inc=1, device_id=plane(j)[0], device_id_type=MESH)

    @pl.loop(1, REPL)
    def _(j):
        dev = {"ctx": 2 * p + 1 - c, "dp": (d + j) % REPL}
        pl.semaphore_signal(bar, inc=1, device_id=dev, device_id_type=MESH)

    mine = pl.ds(pl.multiple_of(HALF * c, HALF), HALF)
    theirs = pl.ds(pl.multiple_of(HALF * (1 - c), HALF), HALF)
    my_rows = pl.ds(pl.multiple_of(ROWS * c, ROWS), ROWS)
    sib_rows = pl.ds(pl.multiple_of(ROWS * (1 - c), ROWS), ROWS)

    ld_w = pltpu.make_async_copy(w_hbm, wsh, lsem.at[0])
    ld_w.start()
    ld_x = pltpu.make_async_copy(x_hbm.at[0, :, mine], xb.at[my_rows], lsem.at[1])
    ld_x.start()
    ld_c = pltpu.make_async_copy(cot_hbm.at[0, :, mine], cotb.at[my_rows], lsem.at[2])
    ld_c.start()
    lds = []
    for n, (src, dst) in enumerate(
        ((gb_hbm, gb_ref), (lam_hbm, lam_ref), (cw_hbm, cw_ref), (cb_hbm, cb_ref))
    ):
        lds.append(pltpu.make_async_copy(src.at[:, mine], dst, lsem.at[5 + n]))
        lds[-1].start()
    pending = []

    ld_w.wait()
    for i in range(8):
        for g in range(2):
            v = wsh[i, g].astype(F32)
            for lh in range(2):
                wf[lh, i * 16 + g * 8 : i * 16 + g * 8 + 8, :] = v[:, lane_tile(lh)]
    for h in range(2):
        for u in range(REPL):
            for st in range(STAGES):
                first = ((u // 2) % 2) * 8 + 4 * h + 2 * st + u // 4
                wu[h, st, u] = wf[u % 2, pl.ds(first, 8, stride=16), :]

    pl.semaphore_wait(bar, 1 + (CHIPS - 1) + (PLANE - 2) + (REPL - 1))

    part = pl.ds(pl.multiple_of(8 * c, 8), 8)
    s_w = send(wu.at[1 - c, 0, d], wpair.at[0, part], sib_s.at[0], sib_r.at[0], sibling)
    s_v = send(wu.at[1 - c, 1], wpair.at[pl.ds(1, REPL), part], sib_s.at[5], sib_r.at[5], sibling)
    s_x = send(x_hbm.at[0, :, theirs], xb.at[my_rows], sib_s.at[1], sib_r.at[1], sibling)
    s_c = send(cot_hbm.at[0, :, theirs], cotb.at[my_rows], sib_s.at[2], sib_r.at[2], sibling)
    my16 = pl.ds(pl.multiple_of(16 * p, 16), 16)
    wpair[0, part, :] = wu[c, 0, d]
    s_w.wait_recv()
    mine_w = W.at[0, d // 2, my16, lanes_of(d)]
    mine_w[...] = wpair[0].astype(BF16)

    @pl.loop(1, DEPTH)
    def _(j):
        send(mine_w, mine_w, c1_s, c1_r, deep((z + j) % DEPTH))

    seven = wsend.at[0, 0, pl.ds(0, 16 * (DEPTH - 1)), pl.ds(0, 128)]
    pending.append((seven, c1_s))
    wpair[1:, part, :] = wu[c, 1]
    s_v.wait_recv()
    for u in range(REPL):
        W[1, u // 2, my16, lane_tile(u % 2)] = wpair[1 + u].astype(BF16)
    across = (p + DEPTH) % CHIPS
    rows_a = W.at[1, :, my16]
    rows_b = W.at[1, :, pl.ds(pl.multiple_of(16 * across, 16), 16)]
    send(rows_a, rows_a, za_s.at[0], za_r.at[0], chip(across))
    pending.append((rows_a, za_s.at[0]))

    @pl.loop(1, DEPTH)
    def _(j):
        send(rows_a, rows_a, za_s.at[1], za_r.at[1], deep((z + j) % DEPTH))

    ld_x.wait()
    s_x.wait_recv()
    send(xb.at[pl.ds(SPAN - 16, 16)], xhalo, hal_s, hal_r, chip((p + 1) % CHIPS))
    pending.append((xhalo, hal_s))
    for k in range(TILES):
        nat[k] = xb[:, lane_tile(k)].astype(F32)

    @pl.loop(0, R)
    def _(r):
        for k in range(TILES):
            xs[3 + r, :, lane_tile(k)] = nat[k, pl.ds(r, 8, stride=R), :]

    wait_for(rows_b, za_r.at[0])

    @pl.loop(1, DEPTH)
    def _(j):
        send(rows_b, rows_b, za_s.at[1], za_r.at[1], deep((z + j) % DEPTH))

    fourteen = wsend.at[1, :, pl.ds(0, 16 * 2 * (DEPTH - 1))]
    pending.append((fourteen, za_s.at[1]))
    wait_for(seven, c1_r)
    fifteen = frecv.at[0, pl.ds(0, PLANE - 1)]
    mine_s = W.at[0, d // 2, rows_of(y // 2), lanes_of(d)]

    @pl.loop(1, PLANE)
    def _(j):
        send(mine_s, mine_s, c2_s, c2_r, plane(j)[0])

    pending.append((fifteen, c2_s))

    ld_c.wait()
    s_c.wait_recv()
    for k in range(TILES):
        natc[k] = cotb[:, lane_tile(k)].astype(F32)

    @pl.loop(0, R)
    def _(r):
        for k in range(TILES):
            cs[r, :, lane_tile(k)] = natc[k, pl.ds(r, 8, stride=R), :]

    wait_for(xhalo, hal_r)
    hal = xhalo[...].astype(F32)
    hal = jnp.where(p == 0, jnp.zeros_like(hal), hal)
    sub = sublane((8, HALF))
    for k in range(3):
        rolled = pltpu.roll(xs[3 + R - 3 + k], 1, 0)
        xs[k] = jnp.where(sub == 0, jnp.broadcast_to(hal[13 + k : 14 + k], (8, HALF)), rolled)

    for ld in lds:
        ld.wait()
    conv_w = cw_ref[...]
    conv_b = cb_ref[...]
    for b in range(NB):
        taps = [jnp.broadcast_to(conv_w[k : k + 1, block(b)], (8, BW)) for k in range(4)]
        shift = jnp.broadcast_to(conv_b[:, block(b)], (8, BW))

        @pl.loop(0, R // 2)
        def _(i):
            v = [xs[2 * i + k, :, block(b)] for k in range(5)]
            out = []
            for o in range(2):
                m = shift + taps[0] * v[o]
                for k in range(1, 4):
                    m = m + taps[k] * v[o + k]
                out.append(m)
            mb[pl.ds(pl.multiple_of(16 * i, 16), 16), block(b)] = jnp.concatenate(out, 0).astype(BF16)

        mt[b] = mb[:, block(b)].astype(F32).T.astype(BF16)

    lam = lam_ref[...]
    neg8rate = -8.0 * softplus(-lam)
    gate_b = gb_ref[...]
    ends = []

    def gates(b):
        st, k = b // 2, 2 * (b % 2)
        for g in range(2):
            pre[2 * b + g] = jnp.dot(mb[:, block(b)], W[st, k + g], preferred_element_type=F32)
        nr = jnp.broadcast_to(neg8rate[:, block(b)], (8, BW))
        ba = jnp.broadcast_to(gate_b[0:1, block(b)], (8, BW))
        bx = jnp.broadcast_to(gate_b[1:2, block(b)], (8, BW))

        def step(i, carry):
            prod, hid, kk, logs = carry
            two = mb[pl.ds(pl.multiple_of(16 * i, 16), 16), block(b)].astype(F32)
            for o in range(2):
                r = 2 * i + o
                at = pl.ds(pl.multiple_of(8 * r, 8), 8)
                ga = sigmoid(pre[2 * b, at, :] + ba)
                gx = sigmoid(pre[2 * b + 1, at, :] + bx)
                m = two[8 * o : 8 * o + 8]
                ld = ga * nr
                a = jnp.exp(ld)
                sq = 1.0 - a * a
                mult = jnp.sqrt(sq)
                gm_ = gx * m
                drive = mult * gm_
                dec[r, :, block(b)] = a
                drv[r, :, block(b)] = drive
                qq[r, :, block(b)] = gm_ * a * lax.rsqrt(jnp.maximum(sq, 0.05))
                m1[r, :, block(b)] = a * ga
                oma[r, :, block(b)] = (1.0 - ga) * nr
                m2[r, :, block(b)] = drive * (1.0 - gx)
                m3[r, :, block(b)] = mult * gx
                hid = a * hid + drive
                prod = prod * a
                kk = kk + prod * cs[r, :, block(b)]
                logs = logs + ld
            return prod, hid, kk, logs

        zero = jnp.zeros((8, BW), F32)
        prod, hid, kk, logs = lax.fori_loop(
            0, R // 2, step, (jnp.ones((8, BW), F32), zero, zero, zero)
        )
        sb = sublane((8, BW))
        fp, fh = prod, hid
        bp, bk = prod, kk
        for s in (1, 2, 4):
            mp, mh = pltpu.roll(fp, s, 0), pltpu.roll(fh, s, 0)
            fh = jnp.where(sb >= s, fp * mh + fh, fh)
            fp = jnp.where(sb >= s, fp * mp, fp)
            mp, mk = pltpu.roll(bp, 8 - s, 0), pltpu.roll(bk, 8 - s, 0)
            bk = jnp.where(sb < 8 - s, bp * mk + bk, bk)
            bp = jnp.where(sb < 8 - s, bp * mp, bp)
            logs = logs + pltpu.roll(logs, s, 0)
        one = jnp.ones((8, BW), F32)
        ends.append((
            jnp.where(sb == 0, one, pltpu.roll(fp, 1, 0)),
            jnp.where(sb == 0, zero, pltpu.roll(fh, 1, 0)),
            jnp.where(sb == 7, one, pltpu.roll(bp, 7, 0)),
            jnp.where(sb == 7, zero, pltpu.roll(bk, 7, 0)),
        ))
        for lh in range(2):
            k = 2 * (b % 2) + lh
            dsend[st, 0, k : k + 1, :] = logs[0:1, lane_tile(lh)]
            dsend[st, 1, k : k + 1, :] = logs[0:1, lane_tile(lh)]
            dsend[st, 0, 4 + k : 5 + k, :] = fh[7:8, lane_tile(lh)]
            dsend[st, 1, 4 + k : 5 + k, :] = bk[0:1, lane_tile(lh)]

    for st in range(STAGES):
        wait_for(*((fifteen, c2_r) if st == 0 else (fourteen, za_r.at[1])))
        for b in (2 * st, 2 * st + 1):
            gates(b)

        @pl.loop(1, CHIPS)
        def _(j):
            to = (p + j) % CHIPS
            send(dsend.at[st, jnp.where(to > p, 0, 1)], drecv.at[st, p], d_s.at[st], d_r.at[st], chip(to))

        pending.append((drecv.at[st, pl.ds(0, CHIPS - 1)], d_s.at[st]))
        drecv[st, p] = jnp.zeros((8, 128), F32)

    sums = []

    def grads(b):
        st, k = b // 2, 2 * (b % 2)

        def wide(n):
            return jnp.concatenate(
                [jnp.broadcast_to(sin[st, n, k + lh : k + lh + 1, :], (8, 128)) for lh in range(2)], 1
            )

        hin = ends[b][1] + ends[b][0] * wide(0)
        kin = ends[b][3] + ends[b][2] * wide(1)

        def up(r, h):
            hp[r, :, block(b)] = h
            return dec[r, :, block(b)] * h + drv[r, :, block(b)]

        lax.fori_loop(0, R, up, hin, unroll=4)

        def down(n, carry):
            kk, t_sum, a_sum, x_sum = carry
            i = R // 2 - 1 - n
            outs = [[None, None], [None, None]]
            for o in (1, 0):
                r = 2 * i + o
                gr = cs[r, :, block(b)] + kk
                kk = dec[r, :, block(b)] * gr
                t = (hp[r, :, block(b)] - qq[r, :, block(b)]) * m1[r, :, block(b)] * gr
                ga = t * oma[r, :, block(b)]
                gx = gr * m2[r, :, block(b)]
                gm[r, :, block(b)] = gr * m3[r, :, block(b)]
                t_sum, a_sum, x_sum = t_sum + t, a_sum + ga, x_sum + gx
                outs[0][o], outs[1][o] = ga, gx
            at = pl.ds(pl.multiple_of(16 * i, 16), 16)
            gp[2 * b, at, :] = jnp.concatenate(outs[0], 0).astype(BF16)
            gp[2 * b + 1, at, :] = jnp.concatenate(outs[1], 0).astype(BF16)
            return kk, t_sum, a_sum, x_sum

        zero = jnp.zeros((8, BW), F32)
        _, t_sum, a_sum, x_sum = lax.fori_loop(0, R // 2, down, (kin, zero, zero, zero))
        sums.append([t_sum, a_sum, x_sum])
        for g in range(2):
            wsend[st, k + g] = jnp.dot(mt[b], gp[2 * b + g], preferred_element_type=F32).astype(BF16)

    def through(b):
        st, k = b // 2, 2 * (b % 2)
        nt = (((1,), (1,)), ((), ()))
        back = lax.dot_general(gp[2 * b], W[st, k], nt, preferred_element_type=F32)
        back = back + lax.dot_general(gp[2 * b + 1], W[st, k + 1], nt, preferred_element_type=F32)
        gm[0:R, :, block(b)] = gm[0:R, :, block(b)] + back.reshape(R, 8, BW)

    for st in range(STAGES):
        wait_for(drecv.at[st, pl.ds(0, CHIPS - 1)], d_r.at[st])
        state = jnp.zeros((4, 128), F32)
        carry_in = jnp.zeros((4, 128), F32)
        for j in range(CHIPS):
            v = drecv[st, j]
            state = jnp.where(j < p, jnp.exp(v[:4]) * state + v[4:], state)
            v = drecv[st, CHIPS - 1 - j]
            carry_in = jnp.where(CHIPS - 1 - j > p, jnp.exp(v[:4]) * carry_in + v[4:], carry_in)
        sin[st, 0] = state
        sin[st, 1] = carry_in
        for b in (2 * st, 2 * st + 1):
            grads(b)

        @pl.loop(1, PLANE)
        def _(j):
            dev, to_h, to_d = plane(j)
            send(
                wsend.at[st, to_d // 2, rows_of(to_h), lanes_of(to_d)],
                frecv.at[st, spot], f_s.at[st], f_r.at[st], dev,
            )

        pending.append((fifteen, f_s.at[st]))
        frecv[st, spot] = wsend[st, d // 2, rows_of(y // 2), lanes_of(d)]
        for b in (2 * st, 2 * st + 1):
            through(b)

    for k in range(3):
        ghs[k : k + 1, :] = gm[k, 0:1, :]
    send(ghs, ghr, e_s, e_r, chip((p + CHIPS - 1) % CHIPS))
    pending.append((ghr, e_s))

    sig = 1.0 / (1.0 + jnp.exp(lam))
    for b in range(NB):
        def add(r, carry):
            g = gm[r, :, block(b)]
            return tuple(carry[k] + g * xs[r + k, :, block(b)] for k in range(4)) + (carry[4] + g,)

        zero = jnp.zeros((8, BW), F32)
        acc = lax.fori_loop(0, R, add, (zero,) * 5, unroll=4)
        t_sum, a_sum, x_sum = sums[b]
        t_sum = t_sum * (8.0 * jnp.broadcast_to(sig[:, block(b)], (8, BW)))
        sb = sublane((8, BW))
        rows = zero
        for n, v in enumerate((t_sum, a_sum, x_sum) + tuple(acc)):
            for s in (1, 2, 4):
                v = v + pltpu.roll(v, s, 0)
            rows = jnp.where(sb == n, v, rows)
        for lh in range(2):
            ssend[2 * b + lh] = rows[:, lane_tile(lh)]

    @pl.loop(1, PLANE)
    def _(j):
        dev, _, to_d = plane(j)
        send(ssend.at[to_d], srecv.at[spot], fs_s, fs_r, dev)

    pending.append((srecv.at[pl.ds(0, PLANE - 1)], fs_s))
    srecv[spot] = ssend[d]

    def fold(st):
        wait_for(fifteen, f_r.at[st])

        @pl.loop(0, DEPTH)
        def _(i):
            at = pl.ds(pl.multiple_of(16 * i, 16), 16)
            v = frecv[st, 0, at, :].astype(F32)
            for u in range(1, PLANE):
                v = v + frecv[st, u, at, :].astype(F32)
            fsum[st, i] = v.astype(BF16)

        @pl.loop(1, DEPTH)
        def _(j):
            to = (z + j) % DEPTH
            send(fsum.at[st, to], zrecv.at[st, z], z_s.at[st], z_r.at[st], deep(to))

        pending.append((zrecv.at[st, pl.ds(0, DEPTH - 1)], z_s.at[st]))
        zrecv[st, z] = fsum[st, z]

    fold(0)
    wait_for(ghr, e_r)
    halo = ghr[...]
    halo = jnp.where(p == CHIPS - 1, jnp.zeros_like(halo), halo)
    for k in range(3):
        rolled = pltpu.roll(gm[k], 7, 0)
        gm[R + k] = jnp.where(sub == 7, jnp.broadcast_to(halo[k : k + 1], (8, HALF)), rolled)

    for b in range(NB):
        taps = [jnp.broadcast_to(conv_w[k : k + 1, block(b)], (8, BW)) for k in range(4)]

        @pl.loop(0, R)
        def _(r):
            v = taps[0] * gm[r + 3, :, block(b)]
            for k in range(1, 4):
                v = v + taps[k] * gm[r + 3 - k, :, block(b)]
            for lh in range(2):
                nat[2 * b + lh, pl.ds(r, 8, stride=R), :] = v[:, lane_tile(lh)]

    for k in range(TILES):
        gib[:, lane_tile(k)] = nat[k].astype(BF16)
    s_g = send(gib.at[sib_rows], gi_hbm.at[:, mine], sib_s.at[3], sib_r.at[3], sibling)
    st_g = pltpu.make_async_copy(gib.at[my_rows], gi_hbm.at[:, mine], lsem.at[3])
    st_g.start()
    pending.append((gib.at[my_rows], lsem.at[3]))

    wait_for(srecv.at[pl.ds(0, PLANE - 1)], fs_r)
    ssum[...] = jnp.sum(srecv[...], 0)

    @pl.loop(1, DEPTH)
    def _(j):
        send(ssum, szrecv.at[z], zs_s, zs_r, deep((z + j) % DEPTH))

    pending.append((szrecv.at[pl.ds(0, DEPTH - 1)], zs_s))
    szrecv[z] = ssum[...]
    fold(1)

    def spread(n, tile):
        G[d, c, :, lane_tile(n)] = tile(c)[...]

        @pl.loop(1, 2 * REPL)
        def _(j):
            to_c = (c + j // REPL) % 2
            dev = {"ctx": 2 * p + to_c, "dp": (d + j) % REPL}
            send(tile(to_c), G.at[d, c, :, lane_tile(n)], g_s.at[n], g_r.at[n], dev)

        pending.append((srecv.at[pl.ds(0, 2 * REPL - 1)], g_s.at[n]))

    def finish(st):
        wait_for(zrecv.at[st, pl.ds(0, DEPTH - 1)], z_r.at[st])
        whole = zrecv[st, 0].astype(F32)
        for j in range(1, DEPTH):
            whole = whole + zrecv[st, j].astype(F32)
        own[st] = whole
        spread(st, lambda core: own.at[st, pl.ds(pl.multiple_of(8 * core, 8), 8)])

    finish(0)
    wait_for(szrecv.at[pl.ds(0, DEPTH - 1)], zs_r)
    fin[...] = jnp.sum(szrecv[...], 0)
    spread(STAGES, lambda core: fin)
    finish(1)
    for n in range(STAGES + 1):
        wait_for(srecv.at[pl.ds(0, 2 * REPL - 1)], g_r.at[n])
    st_a = pltpu.make_async_copy(G, all_hbm, lsem.at[4])
    st_a.start()

    for cp in [s_w, s_v, s_x, s_c, s_g]:
        cp.wait_send()
    s_g.wait_recv()
    for ref, sem in pending:
        wait_for(ref, sem)
    st_a.wait()


def last_kernel(
    gi_in, all_in, gi_out, gw_out, dec_out, bias_out, taps_out, shift_out,
    all_ref, gws, gw, dec, bias, taps, shift, via, l_sem, s_sem,
):
    get = pltpu.make_async_copy(all_in, all_ref, l_sem.at[4])
    get.start()
    parts = [pl.ds(k * (ROWS // 4), ROWS // 4) for k in range(4)]
    loads = [pltpu.make_async_copy(gi_in.at[at], via.at[at], l_sem.at[k]) for k, at in enumerate(parts)]
    stores = [pltpu.make_async_copy(via.at[at], gi_out.at[0, at], s_sem.at[k]) for k, at in enumerate(parts)]
    for cp in loads:
        cp.start()
    get.wait()
    for h in range(2):
        for u in range(8):
            at = slice(h * HALF + 128 * u, h * HALF + 128 * (u + 1))
            v = all_ref[u, h, :, BW:]
            dec[:, at] = v[0:1]
            bias[:, at] = v[1:3]
            taps[:, at] = v[3:7]
            shift[:, at] = v[7:8]
            for st in range(STAGES):
                first = ((u // 2) % 2) * 8 + 4 * h + 2 * st + u // 4
                gws[u % 2, pl.ds(first, 8, stride=16), :] = all_ref[u, h, :, lane_tile(st)]
    for n, (src, dst) in enumerate(((dec, dec_out), (bias, bias_out), (taps, taps_out), (shift, shift_out))):
        stores.append(pltpu.make_async_copy(src, dst, s_sem.at[4 + n]))
        stores[-1].start()
    for k in range(4):
        loads[k].wait()
        stores[k].start()
    for i in range(8):
        for g in range(2):
            for lh in range(2):
                gw[i, g, :, lane_tile(lh)] = gws[lh, i * 16 + g * 8 : i * 16 + g * 8 + 8, :]
    stores.append(pltpu.make_async_copy(gw, gw_out, s_sem.at[8]))
    stores[-1].start()
    for cp in stores:
        cp.wait()


def per_device(inputs, gate_weight, gate_bias, decay_param, conv_weight, conv_bias, cotangent):
    hbm = pl.BlockSpec(memory_space=pltpu.HBM)
    dma = pltpu.SemaphoreType.DMA
    big = pltpu.VMEM((R, 8, HALF), F32)
    gi, packed = pl.pallas_call(
        main_kernel,
        name="main",
        out_shape=(
            jax.ShapeDtypeStruct((ROWS, WIDTH), BF16),
            jax.ShapeDtypeStruct((REPL, 2, 8, BW + 128), F32),
        ),
        in_specs=[hbm] * 7,
        out_specs=(hbm, hbm),
        scratch_shapes=[
            pltpu.VMEM((2, HALF), F32),
            pltpu.VMEM((1, HALF), F32),
            pltpu.VMEM((4, HALF), F32),
            pltpu.VMEM((1, HALF), F32),
            pltpu.VMEM((SPAN, HALF), BF16),
            pltpu.VMEM((SPAN, HALF), BF16),
            pltpu.VMEM((8, 2, 8, BW), BF16),
            pltpu.VMEM((2, 128, 128), F32),
            pltpu.VMEM((2, STAGES, REPL, 8, 128), F32),
            pltpu.VMEM((1 + REPL, 16, 128), F32),
            pltpu.VMEM((STAGES, 4, BW, BW), BF16),
            pltpu.VMEM((16, HALF), BF16),
            pltpu.VMEM((TILES, SPAN, 128), F32),
            pltpu.VMEM((TILES, SPAN, 128), F32),
            pltpu.VMEM((R + 3, 8, HALF), F32),
            big,
            pltpu.VMEM((SPAN, HALF), BF16),
            pltpu.VMEM((NB, BW, SPAN), BF16),
            pltpu.VMEM((8, SPAN, BW), F32),
            big, big, big, big, big, big, big, big,
            pltpu.VMEM((8, SPAN, BW), BF16),
            pltpu.VMEM((R + 3, 8, HALF), F32),
            pltpu.VMEM((STAGES, 2, 8, 128), F32),
            pltpu.VMEM((STAGES, CHIPS, 8, 128), F32),
            pltpu.VMEM((STAGES, 2, 4, 128), F32),
            pltpu.VMEM((8, HALF), F32),
            pltpu.VMEM((8, HALF), F32),
            pltpu.VMEM((STAGES, 4, BW, BW), BF16),
            pltpu.VMEM((STAGES, PLANE, 128, 128), BF16),
            pltpu.VMEM((STAGES, 16, 128), F32),
            pltpu.VMEM((STAGES, DEPTH, 16, 128), BF16),
            pltpu.VMEM((STAGES, DEPTH, 16, 128), BF16),
            pltpu.VMEM((8, 8, 128), F32),
            pltpu.VMEM((PLANE, 8, 128), F32),
            pltpu.VMEM((8, 128), F32),
            pltpu.VMEM((DEPTH, 8, 128), F32),
            pltpu.VMEM((8, 128), F32),
            pltpu.VMEM((REPL, 2, 8, BW + 128), F32),
            pltpu.VMEM((SPAN, HALF), BF16),
            dma((9,)), dma((7,)), dma((7,)),
            dma, dma, dma, dma, dma((2,)), dma((2,)), dma, dma,
            dma((STAGES,)), dma((STAGES,)), dma, dma, dma((STAGES,)), dma((STAGES,)), dma, dma,
            dma((STAGES,)), dma((STAGES,)), dma, dma, dma((STAGES + 1,)), dma((STAGES + 1,)),
        ],
        compiler_params=pltpu.CompilerParams(
            collective_id=0, has_side_effects=True, vmem_limit_bytes=60 * 2**20
        ),
    )(
        inputs, gate_weight, gate_bias, decay_param.reshape(1, WIDTH), conv_weight,
        conv_bias.reshape(1, WIDTH), cotangent,
    )
    gi, gw, dec, bias, taps, shift = pl.pallas_call(
        last_kernel,
        name="last",
        out_shape=(
            jax.ShapeDtypeStruct((1, ROWS, WIDTH), BF16),
            jax.ShapeDtypeStruct((8, 2, 8, BW), F32),
            jax.ShapeDtypeStruct((1, WIDTH), F32),
            jax.ShapeDtypeStruct((2, WIDTH), F32),
            jax.ShapeDtypeStruct((4, WIDTH), F32),
            jax.ShapeDtypeStruct((1, WIDTH), F32),
        ),
        in_specs=[hbm] * 2,
        out_specs=(hbm,) * 6,
        scratch_shapes=[
            pltpu.VMEM((REPL, 2, 8, BW + 128), F32),
            pltpu.VMEM((2, 128, 128), F32),
            pltpu.VMEM((8, 2, 8, BW), F32),
            pltpu.VMEM((1, WIDTH), F32),
            pltpu.VMEM((2, WIDTH), F32),
            pltpu.VMEM((4, WIDTH), F32),
            pltpu.VMEM((1, WIDTH), F32),
            pltpu.VMEM((ROWS, WIDTH), BF16),
            dma((5,)),
            dma((9,)),
        ],
        compiler_params=pltpu.CompilerParams(vmem_limit_bytes=60 * 2**20),
    )(gi, packed)
    return gi, gw, dec.reshape(WIDTH), bias, taps, shift.reshape(WIDTH)


def solution(mesh):
    placed = (
        P("dp", "ctx", None),
        P("ctx", None, None, None),
        P(),
        P(),
        P(),
        P(),
        P("dp", "ctx", None),
    )
    return jax.shard_map(
        per_device,
        mesh=mesh,
        in_specs=placed,
        out_specs=(P("dp", "ctx", None), P("ctx", None, None, None), P(), P(), P(), P()),
        check_vma=False,
    )
```

```python
import jax
import jax.numpy as jnp
from jax import lax
from jax.experimental import pallas as pl
from jax.experimental.pallas import tpu as pltpu
from jax.sharding import PartitionSpec as P

MESH = pl.DeviceIdType.MESH
F32 = jnp.float32
BF16 = jnp.bfloat16
CHIPS = 16
PLANE = 16
DEPTH = 8
REPL = 8
ROWS = 128
SPAN = 256
WIDTH = 2048
HALF = 1024
BW = 256
NB = HALF // BW
R = SPAN // 8
TILES = HALF // 128
STAGES = 2


def wait_for(ref, sem):
    pltpu.make_async_copy(ref, ref, sem).wait()


def sublane(shape):
    return lax.broadcasted_iota(jnp.int32, shape, 0)


def sigmoid(x):
    return 0.5 * jnp.tanh(0.5 * x) + 0.5


def softplus(x):
    e = jnp.exp(-jnp.abs(x))
    z = e / (2.0 + e)
    z2 = z * z
    s = jnp.full_like(z, 1.0 / 17.0)
    for n in (15, 13, 11, 9, 7, 5, 3, 1):
        s = s * z2 + 1.0 / n
    return jnp.maximum(x, 0.0) + 2.0 * z * s


def lane_tile(i):
    return slice(i * 128, (i + 1) * 128)


def block(b):
    return slice(b * BW, (b + 1) * BW)


def main_kernel(
    x_hbm, w_hbm, gb_hbm, lam_hbm, cw_hbm, cb_hbm, cot_hbm,
    gi_hbm, all_hbm, small_hbm,
    gb_ref, lam_ref, cw_ref, cb_ref, xb, cotb, wsh, wf, wu, wpair, W, xhalo, nat, natc, xs, cs, mb, mt, pre,
    dec, drv, qq, m1, m2, m3, oma, hp, gp, gm, dsend, drecv, sin, ghs, ghr,
    wsend, frecv, brecv, bsum, bz, own, fsum, zrecv, ssend, srecv, ssum, szrecv, fin, tiles, G, gib,
    lsem, sib_s, sib_r, c1_s, c1_r, hal_s, hal_r, za_s, za_r, c2_s, c2_r, d_s, d_r, e_s, e_r,
    f_s, f_r, b_s, b_r, fs_s, fs_r, z_s, z_r, g_s, g_r,
):
    ctx = lax.axis_index("ctx")
    d = lax.axis_index("dp")
    p = ctx // 2
    c = ctx % 2
    z = p % DEPTH
    y = 2 * (p // DEPTH) + d // 4
    x = d % 4
    spot = 4 * y + x
    sibling = {"ctx": 2 * p + 1 - c, "dp": d}

    def chip(j):
        return {"ctx": 2 * j + c, "dp": d}

    def deep(j):
        return {"ctx": 2 * (p - z + j) + c, "dp": d}

    def peer(u):
        return {"ctx": ctx, "dp": u}

    def plane(j):
        to_x, to_y = (x + j % 4) % 4, (y + j // 4) % 4
        to_d = 4 * (to_y % 2) + to_x
        return {"ctx": 2 * (DEPTH * (to_y // 2) + z) + c, "dp": to_d}, to_y // 2, to_d

    def rows_of(h):
        return pl.ds(pl.multiple_of(128 * h, 128), 128)

    def rows16(j):
        return pl.ds(pl.multiple_of(16 * j, 16), 16)

    def lanes_of(u):
        return pl.ds(pl.multiple_of(128 * (u % 2), 128), 128)

    def send(src, dst, ss, rs, dev):
        cp = pltpu.make_async_remote_copy(
            src_ref=src, dst_ref=dst, send_sem=ss, recv_sem=rs, device_id=dev, device_id_type=MESH
        )
        cp.start()
        return cp

    bar = pltpu.get_barrier_semaphore()
    pl.semaphore_signal(bar, inc=1, device_id=sibling, device_id_type=MESH)

    @pl.loop(1, CHIPS)
    def _(j):
        pl.semaphore_signal(bar, inc=1, device_id=chip((p + j) % CHIPS), device_id_type=MESH)

    @pl.loop(1, PLANE)
    def _(j):
        @pl.when(j != PLANE // 2)
        def _():
            pl.semaphore_signal(bar, inc=1, device_id=plane(j)[0], device_id_type=MESH)

    @pl.loop(1, REPL)
    def _(j):
        dev = {"ctx": 2 * p + 1 - c, "dp": (d + j) % REPL}
        pl.semaphore_signal(bar, inc=1, device_id=dev, device_id_type=MESH)

    mine = pl.ds(pl.multiple_of(HALF * c, HALF), HALF)
    theirs = pl.ds(pl.multiple_of(HALF * (1 - c), HALF), HALF)
    my_rows = pl.ds(pl.multiple_of(ROWS * c, ROWS), ROWS)
    sib_rows = pl.ds(pl.multiple_of(ROWS * (1 - c), ROWS), ROWS)

    ld_w = pltpu.make_async_copy(w_hbm, wsh, lsem.at[0])
    ld_w.start()
    ld_x = pltpu.make_async_copy(x_hbm.at[0, :, mine], xb.at[my_rows], lsem.at[1])
    ld_x.start()
    ld_c = pltpu.make_async_copy(cot_hbm.at[0, :, mine], cotb.at[my_rows], lsem.at[2])
    ld_c.start()
    lds = []
    for n, (src, dst) in enumerate(
        ((gb_hbm, gb_ref), (lam_hbm, lam_ref), (cw_hbm, cw_ref), (cb_hbm, cb_ref))
    ):
        lds.append(pltpu.make_async_copy(src.at[:, mine], dst, lsem.at[5 + n]))
        lds[-1].start()
    pending = []

    def later(ref, sem):
        pending.append(lambda: wait_for(ref, sem))


    ld_w.wait()
    for i in range(8):
        for g in range(2):
            v = wsh[i, g].astype(F32)
            for lh in range(2):
                wf[lh, i * 16 + g * 8 : i * 16 + g * 8 + 8, :] = v[:, lane_tile(lh)]
    for h in range(2):
        for u in range(REPL):
            for st in range(STAGES):
                first = ((u // 2) % 2) * 8 + 4 * h + 2 * st + u // 4
                wu[h, st, u] = wf[u % 2, pl.ds(first, 8, stride=16), :]

    pl.semaphore_wait(bar, 1 + (CHIPS - 1) + (PLANE - 2) + (REPL - 1))

    part = pl.ds(pl.multiple_of(8 * c, 8), 8)
    s_w = send(wu.at[1 - c, 0, d], wpair.at[0, part], sib_s.at[0], sib_r.at[0], sibling)
    s_v = send(wu.at[1 - c, 1], wpair.at[pl.ds(1, REPL), part], sib_s.at[5], sib_r.at[5], sibling)
    s_x = send(x_hbm.at[0, :, theirs], xb.at[my_rows], sib_s.at[1], sib_r.at[1], sibling)
    s_c = send(cot_hbm.at[0, :, theirs], cotb.at[my_rows], sib_s.at[2], sib_r.at[2], sibling)
    my16 = pl.ds(pl.multiple_of(16 * p, 16), 16)
    wpair[0, part, :] = wu[c, 0, d]
    s_w.wait_recv()
    mine_w = W.at[0, d // 2, my16, lanes_of(d)]
    mine_w[...] = wpair[0].astype(BF16)

    @pl.loop(1, DEPTH)
    def _(j):
        send(mine_w, mine_w, c1_s, c1_r, deep((z + j) % DEPTH))

    seven = W.at[0, 0, pl.ds(0, 16 * (DEPTH - 1)), pl.ds(0, 128)]
    later(seven, c1_s)
    wpair[1:, part, :] = wu[c, 1]
    s_v.wait_recv()
    for u in range(REPL):
        W[1, u // 2, my16, lane_tile(u % 2)] = wpair[1 + u].astype(BF16)
    across = (p + DEPTH) % CHIPS
    rows_a = W.at[1, :, my16]
    rows_b = W.at[1, :, pl.ds(pl.multiple_of(16 * across, 16), 16)]
    send(rows_a, rows_a, za_s.at[0], za_r.at[0], chip(across))
    later(rows_a, za_s.at[0])

    def at_depth(side, by):
        q = (p - z if side == 0 else across - z) + (z + by + DEPTH) % DEPTH
        return pl.ds(pl.multiple_of(16 * q, 16), 16)

    def near(side):
        rows = W.at[1, :, at_depth(side, 0)]
        for by in (1, -1):
            send(rows, rows, za_s.at[1], za_r.at[1], deep((z + by + DEPTH) % DEPTH))
        for by in (2, -2):
            arrive = za_r.at[2 + 2 * side + (0 if by > 0 else 1)]
            send(rows, rows, za_s.at[1], arrive, deep((z + by + DEPTH) % DEPTH))

    def onward(side):
        for way, by in ((0, 1), (1, -1)):
            rows = W.at[1, :, at_depth(side, -2 * by)]
            wait_for(rows, za_r.at[2 + 2 * side + way])
            send(rows, rows, za_s.at[1], za_r.at[1], deep((z + by + DEPTH) % DEPTH))
            half = W.at[1, pl.ds(2 * way, 2), at_depth(side, -2 * by)]
            send(half, half, za_s.at[1], za_r.at[1], deep((z + 2 * by + DEPTH) % DEPTH))

    near(0)

    ld_x.wait()
    s_x.wait_recv()
    send(xb.at[pl.ds(SPAN - 16, 16)], xhalo, hal_s, hal_r, chip((p + 1) % CHIPS))
    later(xhalo, hal_s)
    for k in range(TILES):
        nat[k] = xb[:, lane_tile(k)].astype(F32)

    @pl.loop(0, R)
    def _(r):
        for k in range(TILES):
            xs[3 + r, :, lane_tile(k)] = nat[k, pl.ds(r, 8, stride=R), :]

    wait_for(rows_b, za_r.at[0])

    near(1)
    later(W.at[1, :, pl.ds(0, 16 * 14)], za_s.at[1])
    ten = W.at[1, :, pl.ds(0, 16 * 10)]
    wait_for(seven, c1_r)
    fifteen = frecv.at[0, pl.ds(0, PLANE - 1)]
    mine_s = W.at[0, d // 2, rows_of(y // 2), lanes_of(d)]

    @pl.loop(1, PLANE)
    def _(j):
        send(mine_s, mine_s, c2_s, c2_r, plane(j)[0])

    later(fifteen, c2_s)
    onward(0)
    onward(1)
    ld_c.wait()
    s_c.wait_recv()
    for k in range(TILES):
        natc[k] = cotb[:, lane_tile(k)].astype(F32)

    @pl.loop(0, R)
    def _(r):
        for k in range(TILES):
            cs[r, :, lane_tile(k)] = natc[k, pl.ds(r, 8, stride=R), :]

    wait_for(xhalo, hal_r)
    hal = xhalo[...].astype(F32)
    hal = jnp.where(p == 0, jnp.zeros_like(hal), hal)
    sub = sublane((8, HALF))
    for k in range(3):
        rolled = pltpu.roll(xs[3 + R - 3 + k], 1, 0)
        xs[k] = jnp.where(sub == 0, jnp.broadcast_to(hal[13 + k : 14 + k], (8, HALF)), rolled)

    for ld in lds:
        ld.wait()
    conv_w = cw_ref[...]
    conv_b = cb_ref[...]
    for b in range(NB):
        taps = [jnp.broadcast_to(conv_w[k : k + 1, block(b)], (8, BW)) for k in range(4)]
        shift = jnp.broadcast_to(conv_b[:, block(b)], (8, BW))

        @pl.loop(0, R // 2)
        def _(i):
            v = [xs[2 * i + k, :, block(b)] for k in range(5)]
            out = []
            for o in range(2):
                m = shift + taps[0] * v[o]
                for k in range(1, 4):
                    m = m + taps[k] * v[o + k]
                out.append(m)
            mb[pl.ds(pl.multiple_of(16 * i, 16), 16), block(b)] = jnp.concatenate(out, 0).astype(BF16)

        mt[b] = mb[:, block(b)].astype(F32).T.astype(BF16)

    lam = lam_ref[...]
    neg8rate = -8.0 * softplus(-lam)
    gate_b = gb_ref[...]
    ends = []

    def gates(b):
        st, k = b // 2, 2 * (b % 2)
        for g in range(2):
            pre[2 * b + g] = jnp.dot(mb[:, block(b)], W[st, k + g], preferred_element_type=F32)
        nr = jnp.broadcast_to(neg8rate[:, block(b)], (8, BW))
        ba = jnp.broadcast_to(gate_b[0:1, block(b)], (8, BW))
        bx = jnp.broadcast_to(gate_b[1:2, block(b)], (8, BW))

        def step(i, carry):
            prod, hid, kk, logs = carry
            two = mb[pl.ds(pl.multiple_of(16 * i, 16), 16), block(b)].astype(F32)
            for o in range(2):
                r = 2 * i + o
                at = pl.ds(pl.multiple_of(8 * r, 8), 8)
                ga = sigmoid(pre[2 * b, at, :] + ba)
                gx = sigmoid(pre[2 * b + 1, at, :] + bx)
                m = two[8 * o : 8 * o + 8]
                ld = ga * nr
                a = jnp.exp(ld)
                sq = 1.0 - a * a
                mult = jnp.sqrt(sq)
                gm_ = gx * m
                drive = mult * gm_
                dec[r, :, block(b)] = a
                drv[r, :, block(b)] = drive
                qq[r, :, block(b)] = gm_ * a * lax.rsqrt(jnp.maximum(sq, 0.05))
                m1[r, :, block(b)] = a * ga
                oma[r, :, block(b)] = (1.0 - ga) * nr
                m2[r, :, block(b)] = drive * (1.0 - gx)
                m3[r, :, block(b)] = mult * gx
                hid = a * hid + drive
                prod = prod * a
                kk = kk + prod * cs[r, :, block(b)]
                logs = logs + ld
            return prod, hid, kk, logs

        zero = jnp.zeros((8, BW), F32)
        prod, hid, kk, logs = lax.fori_loop(
            0, R // 2, step, (jnp.ones((8, BW), F32), zero, zero, zero)
        )
        sb = sublane((8, BW))
        fp, fh = prod, hid
        bp, bk = prod, kk
        for s in (1, 2, 4):
            mp, mh = pltpu.roll(fp, s, 0), pltpu.roll(fh, s, 0)
            fh = jnp.where(sb >= s, fp * mh + fh, fh)
            fp = jnp.where(sb >= s, fp * mp, fp)
            mp, mk = pltpu.roll(bp, 8 - s, 0), pltpu.roll(bk, 8 - s, 0)
            bk = jnp.where(sb < 8 - s, bp * mk + bk, bk)
            bp = jnp.where(sb < 8 - s, bp * mp, bp)
            logs = logs + pltpu.roll(logs, s, 0)
        one = jnp.ones((8, BW), F32)
        ends.append((
            jnp.where(sb == 0, one, pltpu.roll(fp, 1, 0)),
            jnp.where(sb == 0, zero, pltpu.roll(fh, 1, 0)),
            jnp.where(sb == 7, one, pltpu.roll(bp, 7, 0)),
            jnp.where(sb == 7, zero, pltpu.roll(bk, 7, 0)),
        ))
        for lh in range(2):
            k = 2 * (b % 2) + lh
            dsend[st, 0, k : k + 1, :] = logs[0:1, lane_tile(lh)]
            dsend[st, 1, k : k + 1, :] = logs[0:1, lane_tile(lh)]
            dsend[st, 0, 4 + k : 5 + k, :] = fh[7:8, lane_tile(lh)]
            dsend[st, 1, 4 + k : 5 + k, :] = bk[0:1, lane_tile(lh)]

    for st in range(STAGES):
        wait_for(*((fifteen, c2_r) if st == 0 else (ten, za_r.at[1])))
        for b in (2 * st, 2 * st + 1):
            gates(b)

        @pl.loop(1, CHIPS)
        def _(j):
            to = (p + j) % CHIPS
            send(dsend.at[st, jnp.where(to > p, 0, 1)], drecv.at[st, p], d_s.at[st], d_r.at[st], chip(to))

        later(drecv.at[st, pl.ds(0, CHIPS - 1)], d_s.at[st])
        drecv[st, p] = jnp.zeros((8, 128), F32)

    sums = []

    def grads(b):
        st, k = b // 2, 2 * (b % 2)

        def wide(n):
            return jnp.concatenate(
                [jnp.broadcast_to(sin[st, n, k + lh : k + lh + 1, :], (8, 128)) for lh in range(2)], 1
            )

        hin = ends[b][1] + ends[b][0] * wide(0)
        kin = ends[b][3] + ends[b][2] * wide(1)

        def up(r, h):
            hp[r, :, block(b)] = h
            return dec[r, :, block(b)] * h + drv[r, :, block(b)]

        lax.fori_loop(0, R, up, hin, unroll=4)

        def down(n, carry):
            kk, t_sum, a_sum, x_sum = carry
            i = R // 2 - 1 - n
            outs = [[None, None], [None, None]]
            for o in (1, 0):
                r = 2 * i + o
                gr = cs[r, :, block(b)] + kk
                kk = dec[r, :, block(b)] * gr
                t = (hp[r, :, block(b)] - qq[r, :, block(b)]) * m1[r, :, block(b)] * gr
                ga = t * oma[r, :, block(b)]
                gx = gr * m2[r, :, block(b)]
                gm[r, :, block(b)] = gr * m3[r, :, block(b)]
                t_sum, a_sum, x_sum = t_sum + t, a_sum + ga, x_sum + gx
                outs[0][o], outs[1][o] = ga, gx
            at = pl.ds(pl.multiple_of(16 * i, 16), 16)
            gp[2 * b, at, :] = jnp.concatenate(outs[0], 0).astype(BF16)
            gp[2 * b + 1, at, :] = jnp.concatenate(outs[1], 0).astype(BF16)
            return kk, t_sum, a_sum, x_sum

        zero = jnp.zeros((8, BW), F32)
        _, t_sum, a_sum, x_sum = lax.fori_loop(0, R // 2, down, (kin, zero, zero, zero))
        sums.append([t_sum, a_sum, x_sum])
        for g in range(2):
            grad = jnp.dot(mt[b], gp[2 * b + g], preferred_element_type=F32).astype(BF16)
            for h in range(2):
                wsend[st, k + g, h] = grad[128 * h : 128 * (h + 1)]

    def through(b):
        st, k = b // 2, 2 * (b % 2)
        nt = (((1,), (1,)), ((), ()))
        back = lax.dot_general(gp[2 * b], W[st, k], nt, preferred_element_type=F32)
        back = back + lax.dot_general(gp[2 * b + 1], W[st, k + 1], nt, preferred_element_type=F32)
        gm[0:R, :, block(b)] = gm[0:R, :, block(b)] + back.reshape(R, 8, BW)

    for st in range(STAGES):
        wait_for(drecv.at[st, pl.ds(0, CHIPS - 1)], d_r.at[st])
        state = jnp.zeros((4, 128), F32)
        carry_in = jnp.zeros((4, 128), F32)
        for j in range(CHIPS):
            v = drecv[st, j]
            state = jnp.where(j < p, jnp.exp(v[:4]) * state + v[4:], state)
            v = drecv[st, CHIPS - 1 - j]
            carry_in = jnp.where(CHIPS - 1 - j > p, jnp.exp(v[:4]) * carry_in + v[4:], carry_in)
        sin[st, 0] = state
        sin[st, 1] = carry_in
        for b in (2 * st, 2 * st + 1):
            grads(b)

        @pl.loop(1, PLANE)
        def _(j):
            dev, to_h, to_d = plane(j)

            def go():
                send(
                    wsend.at[st, to_d // 2, to_h, :, lanes_of(to_d)],
                    frecv.at[st, spot], f_s.at[st], f_r.at[st], dev,
                )

            if st == 0:
                pl.when(to_d < 4)(go)
            else:
                go()

        if st == 0:
            @pl.when(y % 2 == 0)
            def _():
                frecv[st, spot] = wsend[st, d // 2, y // 2, :, lanes_of(d)]

            @pl.loop(1, DEPTH)
            def _(j):
                to = (z + j) % DEPTH
                send(wsend.at[0, pl.ds(2, 2), :, rows16(to)], brecv.at[z], b_s.at[0], b_r.at[0], deep(to))

            later(brecv.at[pl.ds(0, DEPTH - 1)], b_s.at[0])
            brecv[z] = wsend[0, 2:4, :, rows16(z)]
        else:
            later(fifteen, f_s.at[st])
            frecv[st, spot] = wsend[st, d // 2, y // 2, :, lanes_of(d)]
        for b in (2 * st, 2 * st + 1):
            through(b)

    for k in range(3):
        ghs[k : k + 1, :] = gm[k, 0:1, :]
    send(ghs, ghr, e_s, e_r, chip((p + CHIPS - 1) % CHIPS))
    later(ghr, e_s)

    sig = 1.0 / (1.0 + jnp.exp(lam))
    for b in range(NB):
        def add(r, carry):
            g = gm[r, :, block(b)]
            return tuple(carry[k] + g * xs[r + k, :, block(b)] for k in range(4)) + (carry[4] + g,)

        zero = jnp.zeros((8, BW), F32)
        acc = lax.fori_loop(0, R, add, (zero,) * 5, unroll=4)
        t_sum, a_sum, x_sum = sums[b]
        t_sum = t_sum * (8.0 * jnp.broadcast_to(sig[:, block(b)], (8, BW)))
        sb = sublane((8, BW))
        rows = zero
        for n, v in enumerate((t_sum, a_sum, x_sum) + tuple(acc)):
            for s in (1, 2, 4):
                v = v + pltpu.roll(v, s, 0)
            rows = jnp.where(sb == n, v, rows)
        for lh in range(2):
            ssend[2 * b + lh] = rows[:, lane_tile(lh)]

    @pl.loop(1, DEPTH)
    def _(j):
        to = (z + j) % DEPTH
        send(ssend.at[to], srecv.at[z], fs_s.at[0], fs_r.at[0], deep(to))

    later(srecv.at[pl.ds(0, DEPTH - 1)], fs_s.at[0])
    srecv[z] = ssend[z]

    def fold(st):
        wait_for(fifteen, f_r.at[st])

        @pl.loop(0, DEPTH)
        def _(i):
            at = rows16(i)
            v = frecv[st, 0, at, :].astype(F32)
            for u in range(1, PLANE):
                v = v + frecv[st, u, at, :].astype(F32)
            fsum[st, i] = v.astype(BF16)

        @pl.loop(1, DEPTH)
        def _(j):
            to = (z + j) % DEPTH
            send(fsum.at[st, to], zrecv.at[st, z], z_s.at[st], z_r.at[st], deep(to))

        zrecv[st, z] = fsum[st, z]

    wait_for(ghr, e_r)
    halo = ghr[...]
    halo = jnp.where(p == CHIPS - 1, jnp.zeros_like(halo), halo)
    for k in range(3):
        rolled = pltpu.roll(gm[k], 7, 0)
        gm[R + k] = jnp.where(sub == 7, jnp.broadcast_to(halo[k : k + 1], (8, HALF)), rolled)

    for b in range(NB):
        taps = [jnp.broadcast_to(conv_w[k : k + 1, block(b)], (8, BW)) for k in range(4)]

        @pl.loop(0, R)
        def _(r):
            v = taps[0] * gm[r + 3, :, block(b)]
            for k in range(1, 4):
                v = v + taps[k] * gm[r + 3 - k, :, block(b)]
            for lh in range(2):
                nat[2 * b + lh, pl.ds(r, 8, stride=R), :] = v[:, lane_tile(lh)]

    for k in range(TILES):
        gib[:, lane_tile(k)] = nat[k].astype(BF16)
    s_g = send(gib.at[sib_rows], gi_hbm.at[:, mine], sib_s.at[3], sib_r.at[3], sibling)
    st_g = pltpu.make_async_copy(gib.at[my_rows], gi_hbm.at[:, mine], lsem.at[3])
    st_g.start()
    later(gib.at[my_rows], lsem.at[3])

    wait_for(srecv.at[pl.ds(0, DEPTH - 1)], fs_r.at[0])
    ssum[...] = jnp.sum(srecv[...], 0)

    @pl.loop(1, PLANE)
    def _(j):
        send(ssum, szrecv.at[spot], fs_s.at[1], fs_r.at[1], plane(j)[0])

    later(szrecv.at[pl.ds(0, PLANE - 1)], fs_s.at[1])
    szrecv[spot] = ssum[...]

    pl.when(y % 2 == 0)(lambda: fold(0))
    wait_for(brecv.at[pl.ds(0, DEPTH - 1)], b_r.at[0])
    for k in range(2):
        for h in range(2):
            v = brecv[0, k, h].astype(F32)
            for j in range(1, DEPTH):
                v = v + brecv[j, k, h].astype(F32)
            for lh in range(2):
                bsum[h, 2 * k + lh] = v[:, lane_tile(lh)].astype(BF16)

    @pl.loop(1, PLANE)
    def _(j):
        dev, to_h, to_d = plane(j)

        @pl.when(to_d >= 4)
        def _():
            send(bsum.at[to_h, to_d % 4], bz.at[spot], b_s.at[1], b_r.at[1], dev)

    @pl.when(y % 2 == 1)
    def _():
        bz[spot] = bsum[y // 2, x]

    wait_for(szrecv.at[pl.ds(0, PLANE - 1)], fs_r.at[1])
    fin[...] = jnp.sum(szrecv[...], 0)

    @pl.loop(1, DEPTH)
    def _(j):
        send(fin, tiles.at[c, z], fs_s.at[2], fs_r.at[2], deep((z + j) % DEPTH))

    later(tiles.at[0, pl.ds(0, DEPTH - 1)], fs_s.at[2])
    tiles[c, z] = fin[...]
    fold(1)
    later(zrecv.at[1, pl.ds(0, DEPTH - 1)], z_s.at[1])

    @pl.when(y % 2 == 0)
    def _():
        wait_for(zrecv.at[0, pl.ds(0, DEPTH - 1)], z_s.at[0])
        wait_for(zrecv.at[0, pl.ds(0, DEPTH - 1)], z_r.at[0])
        wait_for(frecv.at[0, pl.ds(0, 7)], f_s.at[0])
        wait_for(bz.at[pl.ds(0, 8)], b_s.at[1])

    @pl.when(y % 2 == 1)
    def _():
        wait_for(bz.at[pl.ds(0, PLANE - 1)], b_r.at[1])
        wait_for(frecv.at[0, pl.ds(0, 8)], f_s.at[0])
        wait_for(bz.at[pl.ds(0, 7)], b_s.at[1])


    srecv15 = szrecv.at[pl.ds(0, 2 * REPL - 1)]

    def spread(n, tile):
        G[d, c, :, lane_tile(n)] = tile(c)[...]

        @pl.loop(1, 2 * REPL)
        def _(j):
            to_c = (c + j // REPL) % 2
            dev = {"ctx": 2 * p + to_c, "dp": (d + j) % REPL}
            send(tile(to_c), G.at[d, c, :, lane_tile(n)], g_s.at[n], g_r.at[n], dev)

        later(srecv15, g_s.at[n])

    def total(st, parts, count):
        whole = parts(0).astype(F32)
        for j in range(1, count):
            whole = whole + parts(j).astype(F32)
        own[st] = whole

    def finish(st):
        spread(st, lambda core: own.at[st, pl.ds(pl.multiple_of(8 * core, 8), 8)])

    pl.when(y % 2 == 0)(lambda: total(0, lambda j: zrecv[0, j], DEPTH))
    pl.when(y % 2 == 1)(lambda: total(0, lambda j: bz[j], PLANE))
    finish(0)
    wait_for(tiles.at[0, pl.ds(0, DEPTH - 1)], fs_r.at[2])
    s_t = send(tiles.at[c], tiles.at[c], sib_s.at[4], sib_r.at[4], sibling)
    wait_for(zrecv.at[1, pl.ds(0, DEPTH - 1)], z_r.at[1])
    total(1, lambda j: zrecv[1, j], DEPTH)
    finish(1)
    s_t.wait_recv()
    st_t = pltpu.make_async_copy(tiles, small_hbm, lsem.at[9])
    st_t.start()
    for n in range(STAGES):
        wait_for(srecv15, g_r.at[n])
    st_a = pltpu.make_async_copy(G, all_hbm, lsem.at[4])
    st_a.start()

    for cp in [s_w, s_v, s_x, s_c, s_g, s_t]:
        cp.wait_send()
    s_g.wait_recv()
    for finish_one in pending:
        finish_one()
    st_a.wait()
    st_t.wait()


def last_kernel(
    gi_in, all_in, small_in, gi_out, gw_out, dec_out, bias_out, taps_out, shift_out,
    all_ref, small_ref, gws, gw, dec, bias, taps, shift, via, l_sem, s_sem,
):
    get = pltpu.make_async_copy(all_in, all_ref, l_sem.at[4])
    get.start()
    get_small = pltpu.make_async_copy(small_in, small_ref, l_sem.at[5])
    get_small.start()
    parts = [pl.ds(k * (ROWS // 4), ROWS // 4) for k in range(4)]
    loads = [pltpu.make_async_copy(gi_in.at[at], via.at[at], l_sem.at[k]) for k, at in enumerate(parts)]
    stores = [pltpu.make_async_copy(via.at[at], gi_out.at[0, at], s_sem.at[k]) for k, at in enumerate(parts)]
    for cp in loads:
        cp.start()
    get.wait()
    get_small.wait()
    for h in range(2):
        for u in range(8):
            at = slice(h * HALF + 128 * u, h * HALF + 128 * (u + 1))
            v = small_ref[h, u]
            dec[:, at] = v[0:1]
            bias[:, at] = v[1:3]
            taps[:, at] = v[3:7]
            shift[:, at] = v[7:8]
            for st in range(STAGES):
                first = ((u // 2) % 2) * 8 + 4 * h + 2 * st + u // 4
                gws[u % 2, pl.ds(first, 8, stride=16), :] = all_ref[u, h, :, lane_tile(st)]
    for n, (src, dst) in enumerate(((dec, dec_out), (bias, bias_out), (taps, taps_out), (shift, shift_out))):
        stores.append(pltpu.make_async_copy(src, dst, s_sem.at[4 + n]))
        stores[-1].start()
    for k in range(4):
        loads[k].wait()
        stores[k].start()
    for i in range(8):
        for g in range(2):
            for lh in range(2):
                gw[i, g, :, lane_tile(lh)] = gws[lh, i * 16 + g * 8 : i * 16 + g * 8 + 8, :]
    stores.append(pltpu.make_async_copy(gw, gw_out, s_sem.at[8]))
    stores[-1].start()
    for cp in stores:
        cp.wait()


def per_device(inputs, gate_weight, gate_bias, decay_param, conv_weight, conv_bias, cotangent):
    hbm = pl.BlockSpec(memory_space=pltpu.HBM)
    dma = pltpu.SemaphoreType.DMA
    big = pltpu.VMEM((R, 8, HALF), F32)
    gi, packed, small = pl.pallas_call(
        main_kernel,
        name="main",
        out_shape=(
            jax.ShapeDtypeStruct((ROWS, WIDTH), BF16),
            jax.ShapeDtypeStruct((REPL, 2, 8, BW), F32),
            jax.ShapeDtypeStruct((2, DEPTH, 8, 128), F32),
        ),
        in_specs=[hbm] * 7,
        out_specs=(hbm,) * 3,
        scratch_shapes=[
            pltpu.VMEM((2, HALF), F32),
            pltpu.VMEM((1, HALF), F32),
            pltpu.VMEM((4, HALF), F32),
            pltpu.VMEM((1, HALF), F32),
            pltpu.VMEM((SPAN, HALF), BF16),
            pltpu.VMEM((SPAN, HALF), BF16),
            pltpu.VMEM((8, 2, 8, BW), BF16),
            pltpu.VMEM((2, 128, 128), F32),
            pltpu.VMEM((2, STAGES, REPL, 8, 128), F32),
            pltpu.VMEM((1 + REPL, 16, 128), F32),
            pltpu.VMEM((STAGES, 4, BW, BW), BF16),
            pltpu.VMEM((16, HALF), BF16),
            pltpu.VMEM((TILES, SPAN, 128), F32),
            pltpu.VMEM((TILES, SPAN, 128), F32),
            pltpu.VMEM((R + 3, 8, HALF), F32),
            big,
            pltpu.VMEM((SPAN, HALF), BF16),
            pltpu.VMEM((NB, BW, SPAN), BF16),
            pltpu.VMEM((8, SPAN, BW), F32),
            big, big, big, big, big, big, big, big,
            pltpu.VMEM((8, SPAN, BW), BF16),
            pltpu.VMEM((R + 3, 8, HALF), F32),
            pltpu.VMEM((STAGES, 2, 8, 128), F32),
            pltpu.VMEM((STAGES, CHIPS, 8, 128), F32),
            pltpu.VMEM((STAGES, 2, 4, 128), F32),
            pltpu.VMEM((8, HALF), F32),
            pltpu.VMEM((8, HALF), F32),
            pltpu.VMEM((STAGES, 4, 2, 128, BW), BF16),
            pltpu.VMEM((STAGES, PLANE, 128, 128), BF16),
            pltpu.VMEM((DEPTH, 2, 2, 16, BW), BF16),
            pltpu.VMEM((2, 4, 16, 128), BF16),
            pltpu.VMEM((PLANE, 16, 128), BF16),
            pltpu.VMEM((STAGES, 16, 128), F32),
            pltpu.VMEM((STAGES, DEPTH, 16, 128), BF16),
            pltpu.VMEM((STAGES, DEPTH, 16, 128), BF16),
            pltpu.VMEM((8, 8, 128), F32),
            pltpu.VMEM((DEPTH, 8, 128), F32),
            pltpu.VMEM((8, 128), F32),
            pltpu.VMEM((PLANE, 8, 128), F32),
            pltpu.VMEM((8, 128), F32),
            pltpu.VMEM((2, DEPTH, 8, 128), F32),
            pltpu.VMEM((REPL, 2, 8, BW), F32),
            pltpu.VMEM((SPAN, HALF), BF16),
            dma((10,)), dma((7,)), dma((7,)),
            dma, dma, dma, dma, dma((2,)), dma((6,)), dma, dma,
            dma((STAGES,)), dma((STAGES,)), dma, dma, dma((STAGES,)), dma((STAGES,)),
            dma((2,)), dma((2,)), dma((3,)), dma((3,)),
            dma((STAGES,)), dma((STAGES,)), dma((STAGES,)), dma((STAGES,)),
        ],
        compiler_params=pltpu.CompilerParams(
            collective_id=0, has_side_effects=True, vmem_limit_bytes=60 * 2**20
        ),
    )(
        inputs, gate_weight, gate_bias, decay_param.reshape(1, WIDTH), conv_weight,
        conv_bias.reshape(1, WIDTH), cotangent,
    )
    gi, gw, dec, bias, taps, shift = pl.pallas_call(
        last_kernel,
        name="last",
        out_shape=(
            jax.ShapeDtypeStruct((1, ROWS, WIDTH), BF16),
            jax.ShapeDtypeStruct((8, 2, 8, BW), F32),
            jax.ShapeDtypeStruct((1, WIDTH), F32),
            jax.ShapeDtypeStruct((2, WIDTH), F32),
            jax.ShapeDtypeStruct((4, WIDTH), F32),
            jax.ShapeDtypeStruct((1, WIDTH), F32),
        ),
        in_specs=[hbm] * 3,
        out_specs=(hbm,) * 6,
        scratch_shapes=[
            pltpu.VMEM((REPL, 2, 8, BW), F32),
            pltpu.VMEM((2, DEPTH, 8, 128), F32),
            pltpu.VMEM((2, 128, 128), F32),
            pltpu.VMEM((8, 2, 8, BW), F32),
            pltpu.VMEM((1, WIDTH), F32),
            pltpu.VMEM((2, WIDTH), F32),
            pltpu.VMEM((4, WIDTH), F32),
            pltpu.VMEM((1, WIDTH), F32),
            pltpu.VMEM((ROWS, WIDTH), BF16),
            dma((6,)),
            dma((9,)),
        ],
        compiler_params=pltpu.CompilerParams(vmem_limit_bytes=60 * 2**20),
    )(gi, packed, small)
    return gi, gw, dec.reshape(WIDTH), bias, taps, shift.reshape(WIDTH)


def solution(mesh):
    placed = (
        P("dp", "ctx", None),
        P("ctx", None, None, None),
        P(),
        P(),
        P(),
        P(),
        P("dp", "ctx", None),
    )
    return jax.shard_map(
        per_device,
        mesh=mesh,
        in_specs=placed,
        out_specs=(P("dp", "ctx", None), P("ctx", None, None, None), P(), P(), P(), P()),
        check_vma=False,
    )
```

```python
import jax
import jax.numpy as jnp
from jax import lax
from jax.experimental import pallas as pl
from jax.experimental.pallas import tpu as pltpu
from jax.sharding import PartitionSpec as P

MESH = pl.DeviceIdType.MESH
F32 = jnp.float32
BF16 = jnp.bfloat16
CHIPS = 16
PLANE = 16
DEPTH = 8
REPL = 8
ROWS = 128
SPAN = 256
WIDTH = 2048
HALF = 1024
BW = 256
NB = HALF // BW
R = SPAN // 8
TILES = HALF // 128
STAGES = 2


def wait_for(ref, sem):
    pltpu.make_async_copy(ref, ref, sem).wait()


def sublane(shape):
    return lax.broadcasted_iota(jnp.int32, shape, 0)


def sigmoid(x):
    return 0.5 * jnp.tanh(0.5 * x) + 0.5


def softplus(x):
    e = jnp.exp(-jnp.abs(x))
    z = e / (2.0 + e)
    z2 = z * z
    s = jnp.full_like(z, 1.0 / 17.0)
    for n in (15, 13, 11, 9, 7, 5, 3, 1):
        s = s * z2 + 1.0 / n
    return jnp.maximum(x, 0.0) + 2.0 * z * s


def lane_tile(i):
    return slice(i * 128, (i + 1) * 128)


def block(b):
    return slice(b * BW, (b + 1) * BW)


def main_kernel(
    x_hbm, w_hbm, gb_hbm, lam_hbm, cw_hbm, cb_hbm, cot_hbm,
    gi_hbm, all_hbm, small_hbm,
    gb_ref, lam_ref, cw_ref, cb_ref, xb, cotb, wsh, wf, wu, wpair, W0, W1, xhalo, nat, natc, xs, cs, mb, mt, pre,
    dec, drv, qq, m1, m2, m3, oma, hp, gp, gm, dsend, drecv, sin, ghs, ghr,
    wsend, wz, frecv, brecv, bsum, bz, own, fsum, zrecv, ssend, srecv, ssum, szrecv, fin, tiles, G, gib,
    lsem, sib_s, sib_r, c1_s, c1_r, hal_s, hal_r, za_s, za_r, c2_s, c2_r, d_s, d_r, e_s, e_r,
    f_s, f_r, b_s, b_r, fs_s, fs_r, z_s, z_r, g_s, g_r,
):
    ctx = lax.axis_index("ctx")
    d = lax.axis_index("dp")
    p = ctx // 2
    c = ctx % 2
    z = p % DEPTH
    y = 2 * (p // DEPTH) + d // 4
    x = d % 4
    spot = 4 * y + x
    sibling = {"ctx": 2 * p + 1 - c, "dp": d}

    def chip(j):
        return {"ctx": 2 * j + c, "dp": d}

    def deep(j):
        return {"ctx": 2 * (p - z + j) + c, "dp": d}

    def peer(u):
        return {"ctx": ctx, "dp": u}

    def plane(j):
        to_x, to_y = (x + j % 4) % 4, (y + j // 4) % 4
        to_d = 4 * (to_y % 2) + to_x
        return {"ctx": 2 * (DEPTH * (to_y // 2) + z) + c, "dp": to_d}, to_y // 2, to_d

    def rows16(j):
        return pl.ds(pl.multiple_of(16 * j, 16), 16)

    def send(src, dst, ss, rs, dev):
        cp = pltpu.make_async_remote_copy(
            src_ref=src, dst_ref=dst, send_sem=ss, recv_sem=rs, device_id=dev, device_id_type=MESH
        )
        cp.start()
        return cp

    bar = pltpu.get_barrier_semaphore()
    pl.semaphore_signal(bar, inc=1, device_id=sibling, device_id_type=MESH)

    @pl.loop(1, CHIPS)
    def _(j):
        pl.semaphore_signal(bar, inc=1, device_id=chip((p + j) % CHIPS), device_id_type=MESH)

    @pl.loop(1, PLANE)
    def _(j):
        @pl.when(j != PLANE // 2)
        def _():
            pl.semaphore_signal(bar, inc=1, device_id=plane(j)[0], device_id_type=MESH)

    @pl.loop(1, REPL)
    def _(j):
        dev = {"ctx": 2 * p + 1 - c, "dp": (d + j) % REPL}
        pl.semaphore_signal(bar, inc=1, device_id=dev, device_id_type=MESH)

    mine = pl.ds(pl.multiple_of(HALF * c, HALF), HALF)
    theirs = pl.ds(pl.multiple_of(HALF * (1 - c), HALF), HALF)
    my_rows = pl.ds(pl.multiple_of(ROWS * c, ROWS), ROWS)
    sib_rows = pl.ds(pl.multiple_of(ROWS * (1 - c), ROWS), ROWS)

    ld_w = pltpu.make_async_copy(w_hbm, wsh, lsem.at[0])
    ld_w.start()
    ld_x = pltpu.make_async_copy(x_hbm.at[0, :, mine], xb.at[my_rows], lsem.at[1])
    ld_x.start()
    ld_c = pltpu.make_async_copy(cot_hbm.at[0, :, mine], cotb.at[my_rows], lsem.at[2])
    ld_c.start()
    lds = []
    for n, (src, dst) in enumerate(
        ((gb_hbm, gb_ref), (lam_hbm, lam_ref), (cw_hbm, cw_ref), (cb_hbm, cb_ref))
    ):
        lds.append(pltpu.make_async_copy(src.at[:, mine], dst, lsem.at[5 + n]))
        lds[-1].start()
    pending = []

    def later(ref, sem):
        pending.append(lambda: wait_for(ref, sem))


    ld_w.wait()
    for i in range(8):
        for g in range(2):
            v = wsh[i, g].astype(F32)
            for lh in range(2):
                wf[lh, i * 16 + g * 8 : i * 16 + g * 8 + 8, :] = v[:, lane_tile(lh)]
    for h in range(2):
        for u in range(REPL):
            for st in range(STAGES):
                first = ((u // 2) % 2) * 8 + 4 * h + 2 * st + u // 4
                wu[h, st, u] = wf[u % 2, pl.ds(first, 8, stride=16), :]

    pl.semaphore_wait(bar, 1 + (CHIPS - 1) + (PLANE - 2) + (REPL - 1))

    part = pl.ds(pl.multiple_of(8 * c, 8), 8)
    s_w = send(wu.at[1 - c, 0, d], wpair.at[0, part], sib_s.at[0], sib_r.at[0], sibling)
    s_v = send(wu.at[1 - c, 1], wpair.at[pl.ds(1, REPL), part], sib_s.at[5], sib_r.at[5], sibling)
    s_x = send(x_hbm.at[0, :, theirs], xb.at[my_rows], sib_s.at[1], sib_r.at[1], sibling)
    s_c = send(cot_hbm.at[0, :, theirs], cotb.at[my_rows], sib_s.at[2], sib_r.at[2], sibling)
    wpair[0, part, :] = wu[c, 0, d]
    s_w.wait_recv()
    mine_w = W0.at[d, y // 2, rows16(z)]
    mine_w[...] = wpair[0].astype(BF16)

    @pl.loop(1, DEPTH)
    def _(j):
        send(mine_w, mine_w, c1_s, c1_r, deep((z + j) % DEPTH))

    seven = W1.at[0, pl.ds(0, DEPTH - 1)]
    later(seven, c1_s)
    wpair[1:, part, :] = wu[c, 1]
    s_v.wait_recv()
    for u in range(REPL):
        W1[p, u] = wpair[1 + u].astype(BF16)
    across = (p + DEPTH) % CHIPS
    rows_a, rows_b = W1.at[p], W1.at[across]
    send(rows_a, rows_a, za_s.at[0], za_r.at[0], chip(across))
    later(rows_a, za_s.at[0])

    def at_depth(side, by):
        return (p - z if side == 0 else across - z) + (z + by + DEPTH) % DEPTH

    def near(side):
        rows = W1.at[at_depth(side, 0)]
        for by in (1, -1):
            send(rows, rows, za_s.at[1], za_r.at[1], deep((z + by + DEPTH) % DEPTH))
        for by in (2, -2):
            arrive = za_r.at[2 + 2 * side + (0 if by > 0 else 1)]
            send(rows, rows, za_s.at[1], arrive, deep((z + by + DEPTH) % DEPTH))

    def onward(side):
        for way, by in ((0, 1), (1, -1)):
            rows = W1.at[at_depth(side, -2 * by)]
            wait_for(rows, za_r.at[2 + 2 * side + way])
            send(rows, rows, za_s.at[1], za_r.at[1], deep((z + by + DEPTH) % DEPTH))
            half = W1.at[at_depth(side, -2 * by), pl.ds(4 * way, 4)]
            send(half, half, za_s.at[1], za_r.at[1], deep((z + 2 * by + DEPTH) % DEPTH))

    near(0)

    ld_x.wait()
    s_x.wait_recv()
    send(xb.at[pl.ds(SPAN - 16, 16)], xhalo, hal_s, hal_r, chip((p + 1) % CHIPS))
    later(xhalo, hal_s)
    for k in range(TILES):
        nat[k] = xb[:, lane_tile(k)].astype(F32)

    @pl.loop(0, R)
    def _(r):
        for k in range(TILES):
            xs[3 + r, :, lane_tile(k)] = nat[k, pl.ds(r, 8, stride=R), :]

    wait_for(rows_b, za_r.at[0])

    near(1)
    later(W1.at[pl.ds(0, 14)], za_s.at[1])
    ten = W1.at[pl.ds(0, 10)]
    wait_for(seven, c1_r)
    fifteen = frecv.at[0, pl.ds(0, PLANE - 1)]
    mine_s = W0.at[d, y // 2]

    @pl.loop(1, PLANE)
    def _(j):
        send(mine_s, mine_s, c2_s, c2_r, plane(j)[0])

    later(fifteen, c2_s)
    onward(0)
    onward(1)
    ld_c.wait()
    s_c.wait_recv()
    for k in range(TILES):
        natc[k] = cotb[:, lane_tile(k)].astype(F32)

    @pl.loop(0, R)
    def _(r):
        for k in range(TILES):
            cs[r, :, lane_tile(k)] = natc[k, pl.ds(r, 8, stride=R), :]

    wait_for(xhalo, hal_r)
    hal = xhalo[...].astype(F32)
    hal = jnp.where(p == 0, jnp.zeros_like(hal), hal)
    sub = sublane((8, HALF))
    for k in range(3):
        rolled = pltpu.roll(xs[3 + R - 3 + k], 1, 0)
        xs[k] = jnp.where(sub == 0, jnp.broadcast_to(hal[13 + k : 14 + k], (8, HALF)), rolled)

    for ld in lds:
        ld.wait()
    conv_w = cw_ref[...]
    conv_b = cb_ref[...]
    for b in range(NB):
        taps = [jnp.broadcast_to(conv_w[k : k + 1, block(b)], (8, BW)) for k in range(4)]
        shift = jnp.broadcast_to(conv_b[:, block(b)], (8, BW))

        @pl.loop(0, R // 2)
        def _(i):
            v = [xs[2 * i + k, :, block(b)] for k in range(5)]
            out = []
            for o in range(2):
                m = shift + taps[0] * v[o]
                for k in range(1, 4):
                    m = m + taps[k] * v[o + k]
                out.append(m)
            mb[pl.ds(pl.multiple_of(16 * i, 16), 16), block(b)] = jnp.concatenate(out, 0).astype(BF16)

        mt[b] = mb[:, block(b)].astype(F32).T.astype(BF16)

    lam = lam_ref[...]
    neg8rate = -8.0 * softplus(-lam)
    gate_b = gb_ref[...]
    ends = []

    def weights(b, g):
        u = 4 * (b % 2) + 2 * g
        two = (W0[u + lh] if b < 2 else W1[:, u + lh] for lh in range(2))
        return jnp.concatenate([v.reshape(BW, 128) for v in two], 1)

    def gates(b):
        st = b // 2
        for g in range(2):
            pre[2 * b + g] = jnp.dot(mb[:, block(b)], weights(b, g), preferred_element_type=F32)
        nr = jnp.broadcast_to(neg8rate[:, block(b)], (8, BW))
        ba = jnp.broadcast_to(gate_b[0:1, block(b)], (8, BW))
        bx = jnp.broadcast_to(gate_b[1:2, block(b)], (8, BW))

        def step(i, carry):
            prod, hid, kk, logs = carry
            two = mb[pl.ds(pl.multiple_of(16 * i, 16), 16), block(b)].astype(F32)
            for o in range(2):
                r = 2 * i + o
                at = pl.ds(pl.multiple_of(8 * r, 8), 8)
                ga = sigmoid(pre[2 * b, at, :] + ba)
                gx = sigmoid(pre[2 * b + 1, at, :] + bx)
                m = two[8 * o : 8 * o + 8]
                ld = ga * nr
                a = jnp.exp(ld)
                sq = 1.0 - a * a
                mult = jnp.sqrt(sq)
                gm_ = gx * m
                drive = mult * gm_
                dec[r, :, block(b)] = a
                drv[r, :, block(b)] = drive
                qq[r, :, block(b)] = gm_ * a * lax.rsqrt(jnp.maximum(sq, 0.05))
                m1[r, :, block(b)] = a * ga
                oma[r, :, block(b)] = (1.0 - ga) * nr
                m2[r, :, block(b)] = drive * (1.0 - gx)
                m3[r, :, block(b)] = mult * gx
                hid = a * hid + drive
                prod = prod * a
                kk = kk + prod * cs[r, :, block(b)]
                logs = logs + ld
            return prod, hid, kk, logs

        zero = jnp.zeros((8, BW), F32)
        prod, hid, kk, logs = lax.fori_loop(
            0, R // 2, step, (jnp.ones((8, BW), F32), zero, zero, zero)
        )
        sb = sublane((8, BW))
        fp, fh = prod, hid
        bp, bk = prod, kk
        for s in (1, 2, 4):
            mp, mh = pltpu.roll(fp, s, 0), pltpu.roll(fh, s, 0)
            fh = jnp.where(sb >= s, fp * mh + fh, fh)
            fp = jnp.where(sb >= s, fp * mp, fp)
            mp, mk = pltpu.roll(bp, 8 - s, 0), pltpu.roll(bk, 8 - s, 0)
            bk = jnp.where(sb < 8 - s, bp * mk + bk, bk)
            bp = jnp.where(sb < 8 - s, bp * mp, bp)
            logs = logs + pltpu.roll(logs, s, 0)
        one = jnp.ones((8, BW), F32)
        ends.append((
            jnp.where(sb == 0, one, pltpu.roll(fp, 1, 0)),
            jnp.where(sb == 0, zero, pltpu.roll(fh, 1, 0)),
            jnp.where(sb == 7, one, pltpu.roll(bp, 7, 0)),
            jnp.where(sb == 7, zero, pltpu.roll(bk, 7, 0)),
        ))
        for lh in range(2):
            k = 2 * (b % 2) + lh
            dsend[st, 0, k : k + 1, :] = logs[0:1, lane_tile(lh)]
            dsend[st, 1, k : k + 1, :] = logs[0:1, lane_tile(lh)]
            dsend[st, 0, 4 + k : 5 + k, :] = fh[7:8, lane_tile(lh)]
            dsend[st, 1, 4 + k : 5 + k, :] = bk[0:1, lane_tile(lh)]

    for st in range(STAGES):
        wait_for(*((fifteen, c2_r) if st == 0 else (ten, za_r.at[1])))
        for b in (2 * st, 2 * st + 1):
            gates(b)

        @pl.loop(1, CHIPS)
        def _(j):
            to = (p + j) % CHIPS
            send(dsend.at[st, jnp.where(to > p, 0, 1)], drecv.at[st, p], d_s.at[st], d_r.at[st], chip(to))

        later(drecv.at[st, pl.ds(0, CHIPS - 1)], d_s.at[st])
        drecv[st, p] = jnp.zeros((8, 128), F32)

    sums = []

    def grads(b):
        st, k = b // 2, 2 * (b % 2)

        def wide(n):
            return jnp.concatenate(
                [jnp.broadcast_to(sin[st, n, k + lh : k + lh + 1, :], (8, 128)) for lh in range(2)], 1
            )

        hin = ends[b][1] + ends[b][0] * wide(0)
        kin = ends[b][3] + ends[b][2] * wide(1)

        def up(r, h):
            hp[r, :, block(b)] = h
            return dec[r, :, block(b)] * h + drv[r, :, block(b)]

        lax.fori_loop(0, R, up, hin, unroll=4)

        def down(n, carry):
            kk, t_sum, a_sum, x_sum = carry
            i = R // 2 - 1 - n
            outs = [[None, None], [None, None]]
            for o in (1, 0):
                r = 2 * i + o
                gr = cs[r, :, block(b)] + kk
                kk = dec[r, :, block(b)] * gr
                t = (hp[r, :, block(b)] - qq[r, :, block(b)]) * m1[r, :, block(b)] * gr
                ga = t * oma[r, :, block(b)]
                gx = gr * m2[r, :, block(b)]
                gm[r, :, block(b)] = gr * m3[r, :, block(b)]
                t_sum, a_sum, x_sum = t_sum + t, a_sum + ga, x_sum + gx
                outs[0][o], outs[1][o] = ga, gx
            at = pl.ds(pl.multiple_of(16 * i, 16), 16)
            gp[2 * b, at, :] = jnp.concatenate(outs[0], 0).astype(BF16)
            gp[2 * b + 1, at, :] = jnp.concatenate(outs[1], 0).astype(BF16)
            return kk, t_sum, a_sum, x_sum

        zero = jnp.zeros((8, BW), F32)
        _, t_sum, a_sum, x_sum = lax.fori_loop(0, R // 2, down, (kin, zero, zero, zero))
        sums.append([t_sum, a_sum, x_sum])
        for g in range(2):
            grad = jnp.dot(mt[b], gp[2 * b + g], preferred_element_type=F32).astype(BF16)
            for lh in range(2):
                for h in range(2):
                    if b == 1:
                        for j in range(DEPTH):
                            wz[j, h, 2 * g + lh] = grad[128 * h + 16 * j : 128 * h + 16 * j + 16, lane_tile(lh)]
                    else:
                        wsend[st, 2 * (k + g) + lh, h] = grad[128 * h : 128 * (h + 1), lane_tile(lh)]

    def through(b):
        nt = (((1,), (1,)), ((), ()))
        back = lax.dot_general(gp[2 * b], weights(b, 0), nt, preferred_element_type=F32)
        back = back + lax.dot_general(gp[2 * b + 1], weights(b, 1), nt, preferred_element_type=F32)
        gm[0:R, :, block(b)] = gm[0:R, :, block(b)] + back.reshape(R, 8, BW)

    for st in range(STAGES):
        wait_for(drecv.at[st, pl.ds(0, CHIPS - 1)], d_r.at[st])
        state = jnp.zeros((4, 128), F32)
        carry_in = jnp.zeros((4, 128), F32)
        for j in range(CHIPS):
            v = drecv[st, j]
            state = jnp.where(j < p, jnp.exp(v[:4]) * state + v[4:], state)
            v = drecv[st, CHIPS - 1 - j]
            carry_in = jnp.where(CHIPS - 1 - j > p, jnp.exp(v[:4]) * carry_in + v[4:], carry_in)
        sin[st, 0] = state
        sin[st, 1] = carry_in
        for b in (2 * st, 2 * st + 1):
            grads(b)

        @pl.loop(1, PLANE)
        def _(j):
            dev, to_h, to_d = plane(j)

            def go():
                send(
                    wsend.at[st, to_d, to_h],
                    frecv.at[st, spot], f_s.at[st], f_r.at[st], dev,
                )

            if st == 0:
                pl.when(to_d < 4)(go)
            else:
                go()

        if st == 0:
            @pl.when(y % 2 == 0)
            def _():
                frecv[st, spot] = wsend[st, d, y // 2]

            @pl.loop(1, DEPTH)
            def _(j):
                to = (z + j) % DEPTH
                send(wz.at[to], brecv.at[z], b_s.at[0], b_r.at[0], deep(to))

            later(brecv.at[pl.ds(0, DEPTH - 1)], b_s.at[0])
            brecv[z] = wz[z]
        else:
            later(fifteen, f_s.at[st])
            frecv[st, spot] = wsend[st, d, y // 2]
        for b in (2 * st, 2 * st + 1):
            through(b)

    for k in range(3):
        ghs[k : k + 1, :] = gm[k, 0:1, :]
    send(ghs, ghr, e_s, e_r, chip((p + CHIPS - 1) % CHIPS))
    later(ghr, e_s)

    sig = 1.0 / (1.0 + jnp.exp(lam))
    for b in range(NB):
        def add(r, carry):
            g = gm[r, :, block(b)]
            return tuple(carry[k] + g * xs[r + k, :, block(b)] for k in range(4)) + (carry[4] + g,)

        zero = jnp.zeros((8, BW), F32)
        acc = lax.fori_loop(0, R, add, (zero,) * 5, unroll=4)
        t_sum, a_sum, x_sum = sums[b]
        t_sum = t_sum * (8.0 * jnp.broadcast_to(sig[:, block(b)], (8, BW)))
        sb = sublane((8, BW))
        rows = zero
        for n, v in enumerate((t_sum, a_sum, x_sum) + tuple(acc)):
            for s in (1, 2, 4):
                v = v + pltpu.roll(v, s, 0)
            rows = jnp.where(sb == n, v, rows)
        for lh in range(2):
            ssend[2 * b + lh] = rows[:, lane_tile(lh)]

    @pl.loop(1, DEPTH)
    def _(j):
        to = (z + j) % DEPTH
        send(ssend.at[to], srecv.at[z], fs_s.at[0], fs_r.at[0], deep(to))

    later(srecv.at[pl.ds(0, DEPTH - 1)], fs_s.at[0])
    srecv[z] = ssend[z]

    def fold(st):
        wait_for(fifteen, f_r.at[st])

        @pl.loop(0, DEPTH)
        def _(i):
            at = rows16(i)
            v = frecv[st, 0, at, :].astype(F32)
            for u in range(1, PLANE):
                v = v + frecv[st, u, at, :].astype(F32)
            fsum[st, i] = v.astype(BF16)

        @pl.loop(1, DEPTH)
        def _(j):
            to = (z + j) % DEPTH
            send(fsum.at[st, to], zrecv.at[st, z], z_s.at[st], z_r.at[st], deep(to))

        zrecv[st, z] = fsum[st, z]

    pl.when(y % 2 == 0)(lambda: fold(0))
    wait_for(brecv.at[pl.ds(0, DEPTH - 1)], b_r.at[0])
    for h in range(2):
        for t in range(4):
            v = brecv[0, h, t].astype(F32)
            for j in range(1, DEPTH):
                v = v + brecv[j, h, t].astype(F32)
            bsum[h, t] = v.astype(BF16)

    @pl.loop(1, PLANE)
    def _(j):
        dev, to_h, to_d = plane(j)

        @pl.when(to_d >= 4)
        def _():
            send(bsum.at[to_h, to_d % 4], bz.at[spot], b_s.at[1], b_r.at[1], dev)

    @pl.when(y % 2 == 1)
    def _():
        bz[spot] = bsum[y // 2, x]

    wait_for(srecv.at[pl.ds(0, DEPTH - 1)], fs_r.at[0])
    ssum[...] = jnp.sum(srecv[...], 0)

    @pl.loop(1, PLANE)
    def _(j):
        send(ssum, szrecv.at[spot], fs_s.at[1], fs_r.at[1], plane(j)[0])

    later(szrecv.at[pl.ds(0, PLANE - 1)], fs_s.at[1])
    szrecv[spot] = ssum[...]

    wait_for(ghr, e_r)
    halo = ghr[...]
    halo = jnp.where(p == CHIPS - 1, jnp.zeros_like(halo), halo)
    for k in range(3):
        rolled = pltpu.roll(gm[k], 7, 0)
        gm[R + k] = jnp.where(sub == 7, jnp.broadcast_to(halo[k : k + 1], (8, HALF)), rolled)

    for b in range(NB):
        taps = [jnp.broadcast_to(conv_w[k : k + 1, block(b)], (8, BW)) for k in range(4)]

        @pl.loop(0, R)
        def _(r):
            v = taps[0] * gm[r + 3, :, block(b)]
            for k in range(1, 4):
                v = v + taps[k] * gm[r + 3 - k, :, block(b)]
            for lh in range(2):
                nat[2 * b + lh, pl.ds(r, 8, stride=R), :] = v[:, lane_tile(lh)]

    for k in range(TILES):
        gib[:, lane_tile(k)] = nat[k].astype(BF16)
    s_g = send(gib.at[sib_rows], gi_hbm.at[:, mine], sib_s.at[3], sib_r.at[3], sibling)
    st_g = pltpu.make_async_copy(gib.at[my_rows], gi_hbm.at[:, mine], lsem.at[3])
    st_g.start()
    later(gib.at[my_rows], lsem.at[3])
    fold(1)
    later(zrecv.at[1, pl.ds(0, DEPTH - 1)], z_s.at[1])

    @pl.when(y % 2 == 0)
    def _():
        wait_for(zrecv.at[0, pl.ds(0, DEPTH - 1)], z_s.at[0])
        wait_for(zrecv.at[0, pl.ds(0, DEPTH - 1)], z_r.at[0])
        wait_for(frecv.at[0, pl.ds(0, 7)], f_s.at[0])
        wait_for(bz.at[pl.ds(0, 8)], b_s.at[1])

    @pl.when(y % 2 == 1)
    def _():
        wait_for(bz.at[pl.ds(0, PLANE - 1)], b_r.at[1])
        wait_for(frecv.at[0, pl.ds(0, 8)], f_s.at[0])
        wait_for(bz.at[pl.ds(0, 7)], b_s.at[1])


    srecv15 = szrecv.at[pl.ds(0, 2 * REPL - 1)]

    def spread(n, tile):
        G[d, c, :, lane_tile(n)] = tile(c)[...]

        @pl.loop(1, 2 * REPL)
        def _(j):
            to_c = (c + j // REPL) % 2
            dev = {"ctx": 2 * p + to_c, "dp": (d + j) % REPL}
            send(tile(to_c), G.at[d, c, :, lane_tile(n)], g_s.at[n], g_r.at[n], dev)

        later(srecv15, g_s.at[n])

    def total(st, parts, count):
        whole = parts(0).astype(F32)
        for j in range(1, count):
            whole = whole + parts(j).astype(F32)
        own[st] = whole

    def finish(st):
        spread(st, lambda core: own.at[st, pl.ds(pl.multiple_of(8 * core, 8), 8)])

    pl.when(y % 2 == 0)(lambda: total(0, lambda j: zrecv[0, j], DEPTH))
    pl.when(y % 2 == 1)(lambda: total(0, lambda j: bz[j], PLANE))
    finish(0)
    wait_for(szrecv.at[pl.ds(0, PLANE - 1)], fs_r.at[1])
    fin[...] = jnp.sum(szrecv[...], 0)

    @pl.loop(1, DEPTH)
    def _(j):
        send(fin, tiles.at[c, z], fs_s.at[2], fs_r.at[2], deep((z + j) % DEPTH))

    later(tiles.at[0, pl.ds(0, DEPTH - 1)], fs_s.at[2])
    tiles[c, z] = fin[...]
    wait_for(zrecv.at[1, pl.ds(0, DEPTH - 1)], z_r.at[1])
    total(1, lambda j: zrecv[1, j], DEPTH)
    finish(1)
    wait_for(tiles.at[0, pl.ds(0, DEPTH - 1)], fs_r.at[2])
    s_t = send(tiles.at[c], tiles.at[c], sib_s.at[4], sib_r.at[4], sibling)
    s_t.wait_recv()
    st_t = pltpu.make_async_copy(tiles, small_hbm, lsem.at[9])
    st_t.start()
    for n in range(STAGES):
        wait_for(srecv15, g_r.at[n])
    st_a = pltpu.make_async_copy(G, all_hbm, lsem.at[4])
    st_a.start()

    for cp in [s_w, s_v, s_x, s_c, s_g, s_t]:
        cp.wait_send()
    s_g.wait_recv()
    for finish_one in pending:
        finish_one()
    st_a.wait()
    st_t.wait()


def last_kernel(
    gi_in, all_in, small_in, gi_out, gw_out, dec_out, bias_out, taps_out, shift_out,
    all_ref, small_ref, gws, gw, dec, bias, taps, shift, via, l_sem, s_sem,
):
    get = pltpu.make_async_copy(all_in, all_ref, l_sem.at[4])
    get.start()
    get_small = pltpu.make_async_copy(small_in, small_ref, l_sem.at[5])
    get_small.start()
    parts = [pl.ds(k * (ROWS // 4), ROWS // 4) for k in range(4)]
    loads = [pltpu.make_async_copy(gi_in.at[at], via.at[at], l_sem.at[k]) for k, at in enumerate(parts)]
    stores = [pltpu.make_async_copy(via.at[at], gi_out.at[0, at], s_sem.at[k]) for k, at in enumerate(parts)]
    for cp in loads:
        cp.start()
    get.wait()
    get_small.wait()
    for h in range(2):
        for u in range(8):
            at = slice(h * HALF + 128 * u, h * HALF + 128 * (u + 1))
            v = small_ref[h, u]
            dec[:, at] = v[0:1]
            bias[:, at] = v[1:3]
            taps[:, at] = v[3:7]
            shift[:, at] = v[7:8]
            for st in range(STAGES):
                first = ((u // 2) % 2) * 8 + 4 * h + 2 * st + u // 4
                gws[u % 2, pl.ds(first, 8, stride=16), :] = all_ref[u, h, :, lane_tile(st)]
    for n, (src, dst) in enumerate(((dec, dec_out), (bias, bias_out), (taps, taps_out), (shift, shift_out))):
        stores.append(pltpu.make_async_copy(src, dst, s_sem.at[4 + n]))
        stores[-1].start()
    for k in range(4):
        loads[k].wait()
        stores[k].start()
    for i in range(8):
        for g in range(2):
            for lh in range(2):
                gw[i, g, :, lane_tile(lh)] = gws[lh, i * 16 + g * 8 : i * 16 + g * 8 + 8, :]
    stores.append(pltpu.make_async_copy(gw, gw_out, s_sem.at[8]))
    stores[-1].start()
    for cp in stores:
        cp.wait()


def per_device(inputs, gate_weight, gate_bias, decay_param, conv_weight, conv_bias, cotangent):
    hbm = pl.BlockSpec(memory_space=pltpu.HBM)
    dma = pltpu.SemaphoreType.DMA
    big = pltpu.VMEM((R, 8, HALF), F32)
    gi, packed, small = pl.pallas_call(
        main_kernel,
        name="main",
        out_shape=(
            jax.ShapeDtypeStruct((ROWS, WIDTH), BF16),
            jax.ShapeDtypeStruct((REPL, 2, 8, BW), F32),
            jax.ShapeDtypeStruct((2, DEPTH, 8, 128), F32),
        ),
        in_specs=[hbm] * 7,
        out_specs=(hbm,) * 3,
        scratch_shapes=[
            pltpu.VMEM((2, HALF), F32),
            pltpu.VMEM((1, HALF), F32),
            pltpu.VMEM((4, HALF), F32),
            pltpu.VMEM((1, HALF), F32),
            pltpu.VMEM((SPAN, HALF), BF16),
            pltpu.VMEM((SPAN, HALF), BF16),
            pltpu.VMEM((8, 2, 8, BW), BF16),
            pltpu.VMEM((2, 128, 128), F32),
            pltpu.VMEM((2, STAGES, REPL, 8, 128), F32),
            pltpu.VMEM((1 + REPL, 16, 128), F32),
            pltpu.VMEM((REPL, 2, 128, 128), BF16),
            pltpu.VMEM((CHIPS, REPL, 16, 128), BF16),
            pltpu.VMEM((16, HALF), BF16),
            pltpu.VMEM((TILES, SPAN, 128), F32),
            pltpu.VMEM((TILES, SPAN, 128), F32),
            pltpu.VMEM((R + 3, 8, HALF), F32),
            big,
            pltpu.VMEM((SPAN, HALF), BF16),
            pltpu.VMEM((NB, BW, SPAN), BF16),
            pltpu.VMEM((8, SPAN, BW), F32),
            big, big, big, big, big, big, big, big,
            pltpu.VMEM((8, SPAN, BW), BF16),
            pltpu.VMEM((R + 3, 8, HALF), F32),
            pltpu.VMEM((STAGES, 2, 8, 128), F32),
            pltpu.VMEM((STAGES, CHIPS, 8, 128), F32),
            pltpu.VMEM((STAGES, 2, 4, 128), F32),
            pltpu.VMEM((8, HALF), F32),
            pltpu.VMEM((8, HALF), F32),
            pltpu.VMEM((STAGES, REPL, 2, 128, 128), BF16),
            pltpu.VMEM((DEPTH, 2, 4, 16, 128), BF16),
            pltpu.VMEM((STAGES, PLANE, 128, 128), BF16),
            pltpu.VMEM((DEPTH, 2, 4, 16, 128), BF16),
            pltpu.VMEM((2, 4, 16, 128), BF16),
            pltpu.VMEM((PLANE, 16, 128), BF16),
            pltpu.VMEM((STAGES, 16, 128), F32),
            pltpu.VMEM((STAGES, DEPTH, 16, 128), BF16),
            pltpu.VMEM((STAGES, DEPTH, 16, 128), BF16),
            pltpu.VMEM((8, 8, 128), F32),
            pltpu.VMEM((DEPTH, 8, 128), F32),
            pltpu.VMEM((8, 128), F32),
            pltpu.VMEM((PLANE, 8, 128), F32),
            pltpu.VMEM((8, 128), F32),
            pltpu.VMEM((2, DEPTH, 8, 128), F32),
            pltpu.VMEM((REPL, 2, 8, BW), F32),
            pltpu.VMEM((SPAN, HALF), BF16),
            dma((10,)), dma((7,)), dma((7,)),
            dma, dma, dma, dma, dma((2,)), dma((6,)), dma, dma,
            dma((STAGES,)), dma((STAGES,)), dma, dma, dma((STAGES,)), dma((STAGES,)),
            dma((2,)), dma((2,)), dma((3,)), dma((3,)),
            dma((STAGES,)), dma((STAGES,)), dma((STAGES,)), dma((STAGES,)),
        ],
        compiler_params=pltpu.CompilerParams(
            collective_id=0, has_side_effects=True, vmem_limit_bytes=60 * 2**20
        ),
    )(
        inputs, gate_weight, gate_bias, decay_param.reshape(1, WIDTH), conv_weight,
        conv_bias.reshape(1, WIDTH), cotangent,
    )
    gi, gw, dec, bias, taps, shift = pl.pallas_call(
        last_kernel,
        name="last",
        out_shape=(
            jax.ShapeDtypeStruct((1, ROWS, WIDTH), BF16),
            jax.ShapeDtypeStruct((8, 2, 8, BW), F32),
            jax.ShapeDtypeStruct((1, WIDTH), F32),
            jax.ShapeDtypeStruct((2, WIDTH), F32),
            jax.ShapeDtypeStruct((4, WIDTH), F32),
            jax.ShapeDtypeStruct((1, WIDTH), F32),
        ),
        in_specs=[hbm] * 3,
        out_specs=(hbm,) * 6,
        scratch_shapes=[
            pltpu.VMEM((REPL, 2, 8, BW), F32),
            pltpu.VMEM((2, DEPTH, 8, 128), F32),
            pltpu.VMEM((2, 128, 128), F32),
            pltpu.VMEM((8, 2, 8, BW), F32),
            pltpu.VMEM((1, WIDTH), F32),
            pltpu.VMEM((2, WIDTH), F32),
            pltpu.VMEM((4, WIDTH), F32),
            pltpu.VMEM((1, WIDTH), F32),
            pltpu.VMEM((ROWS, WIDTH), BF16),
            dma((6,)),
            dma((9,)),
        ],
        compiler_params=pltpu.CompilerParams(vmem_limit_bytes=60 * 2**20),
    )(gi, packed, small)
    return gi, gw, dec.reshape(WIDTH), bias, taps, shift.reshape(WIDTH)


def solution(mesh):
    placed = (
        P("dp", "ctx", None),
        P("ctx", None, None, None),
        P(),
        P(),
        P(),
        P(),
        P("dp", "ctx", None),
    )
    return jax.shard_map(
        per_device,
        mesh=mesh,
        in_specs=placed,
        out_specs=(P("dp", "ctx", None), P("ctx", None, None, None), P(), P(), P(), P()),
        check_vma=False,
    )
```

```python
import jax
import jax.numpy as jnp
from jax import lax
from jax.experimental import pallas as pl
from jax.experimental.pallas import tpu as pltpu
from jax.sharding import PartitionSpec as P

MESH = pl.DeviceIdType.MESH
F32 = jnp.float32
BF16 = jnp.bfloat16
CHIPS = 16
PLANE = 16
DEPTH = 8
REPL = 8
ROWS = 128
SPAN = 256
WIDTH = 2048
HALF = 1024
BW = 256
NB = HALF // BW
R = SPAN // 8
TILES = HALF // 128
STAGES = 2


def wait_for(ref, sem):
    pltpu.make_async_copy(ref, ref, sem).wait()


def sublane(shape):
    return lax.broadcasted_iota(jnp.int32, shape, 0)


def sigmoid(x):
    return 0.5 * jnp.tanh(0.5 * x) + 0.5


def softplus(x):
    e = jnp.exp(-jnp.abs(x))
    z = e / (2.0 + e)
    z2 = z * z
    s = jnp.full_like(z, 1.0 / 17.0)
    for n in (15, 13, 11, 9, 7, 5, 3, 1):
        s = s * z2 + 1.0 / n
    return jnp.maximum(x, 0.0) + 2.0 * z * s


def lane_tile(i):
    return slice(i * 128, (i + 1) * 128)


def block(b):
    return slice(b * BW, (b + 1) * BW)


def main_kernel(
    x_hbm, w_hbm, gb_hbm, lam_hbm, cw_hbm, cb_hbm, cot_hbm,
    gi_hbm, all_hbm, small_hbm,
    gb_ref, lam_ref, cw_ref, cb_ref, xb, cotb, wsh, wf, wu, wpair, W0, W1, xhalo, nat, natc, xs, cs, mb, mt, pre,
    dec, drv, qq, m1, m2, m3, oma, hp, gp, gm, dsend, drecv, sin, ghs, ghr,
    wsend, wz, frecv, brecv, bsum, bz, own, fsum, zrecv, ssend, srecv, ssum, szrecv, fin, tiles, gib,
    lsem, sib_s, sib_r, c1_s, c1_r, hal_s, hal_r, za_s, za_r, c2_s, c2_r, d_s, d_r, e_s, e_r,
    f_s, f_r, b_s, b_r, fs_s, fs_r, z_s, z_r, g_s, g_r,
):
    ctx = lax.axis_index("ctx")
    d = lax.axis_index("dp")
    div, rem = lax.div, lax.rem
    p, c = div(ctx, 2), rem(ctx, 2)
    z = rem(p, DEPTH)
    y = 2 * div(p, DEPTH) + div(d, 4)
    x = rem(d, 4)
    y_hi, y_odd = div(y, 2), rem(y, 2)
    spot = 4 * y + x
    sibling = {"ctx": 2 * p + 1 - c, "dp": d}

    def chip(j):
        return {"ctx": 2 * j + c, "dp": d}

    def deep(j):
        return {"ctx": 2 * (p - z + j) + c, "dp": d}

    def peer(u):
        return {"ctx": ctx, "dp": u}

    def plane(j):
        to_x, to_y = rem(x + rem(j, 4), 4), rem(y + div(j, 4), 4)
        to_h, to_d = div(to_y, 2), 4 * rem(to_y, 2) + to_x
        return {"ctx": 2 * (DEPTH * to_h + z) + c, "dp": to_d}, to_h, to_d

    def rows16(j):
        return pl.ds(pl.multiple_of(16 * j, 16), 16)

    def send(src, dst, ss, rs, dev):
        cp = pltpu.make_async_remote_copy(
            src_ref=src, dst_ref=dst, send_sem=ss, recv_sem=rs, device_id=dev, device_id_type=MESH
        )
        cp.start()
        return cp

    bar = pltpu.get_barrier_semaphore()
    pl.semaphore_signal(bar, inc=1, device_id=sibling, device_id_type=MESH)

    @pl.loop(1, CHIPS)
    def _(j):
        pl.semaphore_signal(bar, inc=1, device_id=chip(rem(p + j, CHIPS)), device_id_type=MESH)

    @pl.loop(1, PLANE)
    def _(j):
        @pl.when(j != PLANE // 2)
        def _():
            pl.semaphore_signal(bar, inc=1, device_id=plane(j)[0], device_id_type=MESH)

    @pl.loop(1, REPL)
    def _(j):
        dev = {"ctx": 2 * p + 1 - c, "dp": rem(d + j, REPL)}
        pl.semaphore_signal(bar, inc=1, device_id=dev, device_id_type=MESH)

    mine = pl.ds(pl.multiple_of(HALF * c, HALF), HALF)
    theirs = pl.ds(pl.multiple_of(HALF * (1 - c), HALF), HALF)
    my_rows = pl.ds(pl.multiple_of(ROWS * c, ROWS), ROWS)
    sib_rows = pl.ds(pl.multiple_of(ROWS * (1 - c), ROWS), ROWS)

    ld_w = pltpu.make_async_copy(w_hbm, wsh, lsem.at[0])
    ld_w.start()
    ld_x = pltpu.make_async_copy(x_hbm.at[0, :, mine], xb.at[my_rows], lsem.at[1])
    ld_x.start()
    ld_c = pltpu.make_async_copy(cot_hbm.at[0, :, mine], cotb.at[my_rows], lsem.at[2])
    ld_c.start()
    lds = []
    for n, (src, dst) in enumerate(
        ((gb_hbm, gb_ref), (lam_hbm, lam_ref), (cw_hbm, cw_ref), (cb_hbm, cb_ref))
    ):
        lds.append(pltpu.make_async_copy(src.at[:, mine], dst, lsem.at[5 + n]))
        lds[-1].start()
    pending = []

    def later(ref, sem):
        pending.append(lambda: wait_for(ref, sem))


    ld_w.wait()
    for i in range(8):
        for g in range(2):
            v = wsh[i, g].astype(F32)
            for lh in range(2):
                wf[lh, i * 16 + g * 8 : i * 16 + g * 8 + 8, :] = v[:, lane_tile(lh)]
    for h in range(2):
        for u in range(REPL):
            for st in range(STAGES):
                first = ((u // 2) % 2) * 8 + 4 * h + 2 * st + u // 4
                wu[h, st, u] = wf[u % 2, pl.ds(first, 8, stride=16), :]

    pl.semaphore_wait(bar, 1 + (CHIPS - 1) + (PLANE - 2) + (REPL - 1))

    part = pl.ds(pl.multiple_of(8 * c, 8), 8)
    s_w = send(wu.at[1 - c, 0, d], wpair.at[0, part], sib_s.at[0], sib_r.at[0], sibling)
    s_v = send(wu.at[1 - c, 1], wpair.at[pl.ds(1, REPL), part], sib_s.at[5], sib_r.at[5], sibling)
    wpair[0, part, :] = wu[c, 0, d]
    s_w.wait_recv()
    mine_w = W0.at[d, y_hi, rows16(z)]
    mine_w[...] = wpair[0].astype(BF16)

    @pl.loop(1, DEPTH)
    def _(j):
        send(mine_w, mine_w, c1_s, c1_r, deep(rem(z + j, DEPTH)))

    s_x = send(x_hbm.at[0, :, theirs], xb.at[my_rows], sib_s.at[1], sib_r.at[1], sibling)
    s_c = send(cot_hbm.at[0, :, theirs], cotb.at[my_rows], sib_s.at[2], sib_r.at[2], sibling)
    seven = W1.at[0, pl.ds(0, DEPTH - 1)]
    later(seven, c1_s)
    wpair[1:, part, :] = wu[c, 1]
    s_v.wait_recv()
    for u in range(REPL):
        W1[p, u] = wpair[1 + u].astype(BF16)
    across = rem(p + DEPTH, CHIPS)
    rows_a, rows_b = W1.at[p], W1.at[across]
    send(rows_a, rows_a, za_s.at[0], za_r.at[0], chip(across))
    later(rows_a, za_s.at[0])

    def at_depth(side, by):
        return (p - z if side == 0 else across - z) + rem(z + by + DEPTH, DEPTH)

    def near(side):
        rows = W1.at[at_depth(side, 0)]
        for by in (1, -1):
            send(rows, rows, za_s.at[1], za_r.at[1], deep(rem(z + by + DEPTH, DEPTH)))
        for by in (2, -2):
            arrive = za_r.at[2 + 2 * side + (0 if by > 0 else 1)]
            send(rows, rows, za_s.at[1], arrive, deep(rem(z + by + DEPTH, DEPTH)))

    def onward(side):
        for way, by in ((0, 1), (1, -1)):
            rows = W1.at[at_depth(side, -2 * by)]
            wait_for(rows, za_r.at[2 + 2 * side + way])
            send(rows, rows, za_s.at[1], za_r.at[1], deep(rem(z + by + DEPTH, DEPTH)))
            half = W1.at[at_depth(side, -2 * by), pl.ds(4 * way, 4)]
            send(half, half, za_s.at[1], za_r.at[1], deep(rem(z + 2 * by + DEPTH, DEPTH)))

    near(0)

    ld_x.wait()
    s_x.wait_recv()
    send(xb.at[pl.ds(SPAN - 16, 16)], xhalo, hal_s, hal_r, chip(rem(p + 1, CHIPS)))
    later(xhalo, hal_s)
    for k in range(TILES):
        nat[k] = xb[:, lane_tile(k)].astype(F32)

    @pl.loop(0, R)
    def _(r):
        for k in range(TILES):
            xs[3 + r, :, lane_tile(k)] = nat[k, pl.ds(r, 8, stride=R), :]

    wait_for(rows_b, za_r.at[0])

    near(1)
    later(W1.at[pl.ds(0, 14)], za_s.at[1])
    ten = W1.at[pl.ds(0, 10)]
    wait_for(seven, c1_r)
    fifteen = frecv.at[0, pl.ds(0, PLANE - 1)]
    mine_s = W0.at[d, y_hi]

    @pl.loop(1, PLANE)
    def _(j):
        send(mine_s, mine_s, c2_s, c2_r, plane(j)[0])

    later(fifteen, c2_s)
    onward(0)
    onward(1)
    ld_c.wait()
    s_c.wait_recv()
    for k in range(TILES):
        natc[k] = cotb[:, lane_tile(k)].astype(F32)

    @pl.loop(0, R)
    def _(r):
        for k in range(TILES):
            cs[r, :, lane_tile(k)] = natc[k, pl.ds(r, 8, stride=R), :]

    wait_for(xhalo, hal_r)
    hal = xhalo[...].astype(F32)
    hal = jnp.where(p == 0, jnp.zeros_like(hal), hal)
    sub = sublane((8, HALF))
    for k in range(3):
        rolled = pltpu.roll(xs[3 + R - 3 + k], 1, 0)
        xs[k] = jnp.where(sub == 0, jnp.broadcast_to(hal[13 + k : 14 + k], (8, HALF)), rolled)

    for ld in lds:
        ld.wait()
    conv_w = cw_ref[...]
    conv_b = cb_ref[...]
    for b in range(NB):
        taps = [jnp.broadcast_to(conv_w[k : k + 1, block(b)], (8, BW)) for k in range(4)]
        shift = jnp.broadcast_to(conv_b[:, block(b)], (8, BW))

        @pl.loop(0, R // 2)
        def _(i):
            v = [xs[2 * i + k, :, block(b)] for k in range(5)]
            out = []
            for o in range(2):
                m = shift + taps[0] * v[o]
                for k in range(1, 4):
                    m = m + taps[k] * v[o + k]
                out.append(m)
            mb[pl.ds(pl.multiple_of(16 * i, 16), 16), block(b)] = jnp.concatenate(out, 0).astype(BF16)

        mt[b] = mb[:, block(b)].astype(F32).T.astype(BF16)

    lam = lam_ref[...]
    neg8rate = -8.0 * softplus(-lam)
    gate_b = gb_ref[...]
    ends = []

    def weights(b, g):
        u = 4 * (b % 2) + 2 * g
        two = (W0[u + lh] if b < 2 else W1[:, u + lh] for lh in range(2))
        return jnp.concatenate([v.reshape(BW, 128) for v in two], 1)

    def gates(b):
        st = b // 2
        for g in range(2):
            pre[2 * b + g] = jnp.dot(mb[:, block(b)], weights(b, g), preferred_element_type=F32)
        nr = jnp.broadcast_to(neg8rate[:, block(b)], (8, BW))
        ba = jnp.broadcast_to(gate_b[0:1, block(b)], (8, BW))
        bx = jnp.broadcast_to(gate_b[1:2, block(b)], (8, BW))

        def step(i, carry):
            prod, hid, kk, logs = carry
            two = mb[pl.ds(pl.multiple_of(16 * i, 16), 16), block(b)].astype(F32)
            for o in range(2):
                r = 2 * i + o
                at = pl.ds(pl.multiple_of(8 * r, 8), 8)
                ga = sigmoid(pre[2 * b, at, :] + ba)
                gx = sigmoid(pre[2 * b + 1, at, :] + bx)
                m = two[8 * o : 8 * o + 8]
                ld = ga * nr
                a = jnp.exp(ld)
                sq = 1.0 - a * a
                mult = jnp.sqrt(sq)
                gm_ = gx * m
                drive = mult * gm_
                dec[r, :, block(b)] = a
                drv[r, :, block(b)] = drive
                qq[r, :, block(b)] = gm_ * a * lax.rsqrt(jnp.maximum(sq, 0.05))
                m1[r, :, block(b)] = a * ga
                oma[r, :, block(b)] = (1.0 - ga) * nr
                m2[r, :, block(b)] = drive * (1.0 - gx)
                m3[r, :, block(b)] = mult * gx
                hid = a * hid + drive
                prod = prod * a
                kk = kk + prod * cs[r, :, block(b)]
                logs = logs + ld
            return prod, hid, kk, logs

        zero = jnp.zeros((8, BW), F32)
        prod, hid, kk, logs = lax.fori_loop(
            0, R // 2, step, (jnp.ones((8, BW), F32), zero, zero, zero), unroll=2
        )
        sb = sublane((8, BW))
        fp, fh = prod, hid
        bp, bk = prod, kk
        for s in (1, 2, 4):
            mp, mh = pltpu.roll(fp, s, 0), pltpu.roll(fh, s, 0)
            fh = jnp.where(sb >= s, fp * mh + fh, fh)
            fp = jnp.where(sb >= s, fp * mp, fp)
            mp, mk = pltpu.roll(bp, 8 - s, 0), pltpu.roll(bk, 8 - s, 0)
            bk = jnp.where(sb < 8 - s, bp * mk + bk, bk)
            bp = jnp.where(sb < 8 - s, bp * mp, bp)
            logs = logs + pltpu.roll(logs, s, 0)
        one = jnp.ones((8, BW), F32)
        ends.append((
            jnp.where(sb == 0, one, pltpu.roll(fp, 1, 0)),
            jnp.where(sb == 0, zero, pltpu.roll(fh, 1, 0)),
            jnp.where(sb == 7, one, pltpu.roll(bp, 7, 0)),
            jnp.where(sb == 7, zero, pltpu.roll(bk, 7, 0)),
        ))
        for lh in range(2):
            k = 2 * (b % 2) + lh
            dsend[st, 0, k : k + 1, :] = logs[0:1, lane_tile(lh)]
            dsend[st, 1, k : k + 1, :] = logs[0:1, lane_tile(lh)]
            dsend[st, 0, 4 + k : 5 + k, :] = fh[7:8, lane_tile(lh)]
            dsend[st, 1, 4 + k : 5 + k, :] = bk[0:1, lane_tile(lh)]

    for st in range(STAGES):
        wait_for(*((fifteen, c2_r) if st == 0 else (ten, za_r.at[1])))
        for b in (2 * st, 2 * st + 1):
            gates(b)

        @pl.loop(1, CHIPS)
        def _(j):
            to = rem(p + j, CHIPS)
            send(dsend.at[st, jnp.where(to > p, 0, 1)], drecv.at[st, p], d_s.at[st], d_r.at[st], chip(to))

        later(drecv.at[st, pl.ds(0, CHIPS - 1)], d_s.at[st])
        drecv[st, p] = jnp.zeros((8, 128), F32)

    sums = []

    def grads(b):
        st, k = b // 2, 2 * (b % 2)

        def wide(n):
            return jnp.concatenate(
                [jnp.broadcast_to(sin[st, n, k + lh : k + lh + 1, :], (8, 128)) for lh in range(2)], 1
            )

        hin = ends[b][1] + ends[b][0] * wide(0)
        kin = ends[b][3] + ends[b][2] * wide(1)

        def up(r, h):
            hp[r, :, block(b)] = h
            return dec[r, :, block(b)] * h + drv[r, :, block(b)]

        lax.fori_loop(0, R, up, hin, unroll=4)

        def down(n, carry):
            kk, t_sum, a_sum, x_sum = carry
            i = R // 2 - 1 - n
            outs = [[None, None], [None, None]]
            for o in (1, 0):
                r = 2 * i + o
                gr = cs[r, :, block(b)] + kk
                kk = dec[r, :, block(b)] * gr
                t = (hp[r, :, block(b)] - qq[r, :, block(b)]) * m1[r, :, block(b)] * gr
                ga = t * oma[r, :, block(b)]
                gx = gr * m2[r, :, block(b)]
                gm[r, :, block(b)] = gr * m3[r, :, block(b)]
                t_sum, a_sum, x_sum = t_sum + t, a_sum + ga, x_sum + gx
                outs[0][o], outs[1][o] = ga, gx
            at = pl.ds(pl.multiple_of(16 * i, 16), 16)
            gp[2 * b, at, :] = jnp.concatenate(outs[0], 0).astype(BF16)
            gp[2 * b + 1, at, :] = jnp.concatenate(outs[1], 0).astype(BF16)
            return kk, t_sum, a_sum, x_sum

        zero = jnp.zeros((8, BW), F32)
        _, t_sum, a_sum, x_sum = lax.fori_loop(0, R // 2, down, (kin, zero, zero, zero), unroll=4)
        sums.append([t_sum, a_sum, x_sum])
        for g in range(2):
            grad = jnp.dot(mt[b], gp[2 * b + g], preferred_element_type=F32).astype(BF16)
            for lh in range(2):
                for h in range(2):
                    if b == 1:
                        for j in range(DEPTH):
                            wz[j, h, 2 * g + lh] = grad[128 * h + 16 * j : 128 * h + 16 * j + 16, lane_tile(lh)]
                    else:
                        wsend[st, 2 * (k + g) + lh, h] = grad[128 * h : 128 * (h + 1), lane_tile(lh)]

    def through(b):
        nt = (((1,), (1,)), ((), ()))
        back = lax.dot_general(gp[2 * b], weights(b, 0), nt, preferred_element_type=F32)
        back = back + lax.dot_general(gp[2 * b + 1], weights(b, 1), nt, preferred_element_type=F32)
        gm[0:R, :, block(b)] = gm[0:R, :, block(b)] + back.reshape(R, 8, BW)

    for st in range(STAGES):
        wait_for(drecv.at[st, pl.ds(0, CHIPS - 1)], d_r.at[st])
        state = jnp.zeros((4, 128), F32)
        carry_in = jnp.zeros((4, 128), F32)
        for j in range(CHIPS):
            v = drecv[st, j]
            state = jnp.where(j < p, jnp.exp(v[:4]) * state + v[4:], state)
            v = drecv[st, CHIPS - 1 - j]
            carry_in = jnp.where(CHIPS - 1 - j > p, jnp.exp(v[:4]) * carry_in + v[4:], carry_in)
        sin[st, 0] = state
        sin[st, 1] = carry_in
        for b in (2 * st, 2 * st + 1):
            grads(b)

        @pl.loop(1, PLANE)
        def _(j):
            dev, to_h, to_d = plane(j)

            def go():
                send(
                    wsend.at[st, to_d, to_h],
                    frecv.at[st, spot], f_s.at[st], f_r.at[st], dev,
                )

            if st == 0:
                pl.when(to_d < 4)(go)
            else:
                go()

        if st == 0:
            @pl.when(y_odd == 0)
            def _():
                frecv[st, spot] = wsend[st, d, y_hi]

            @pl.loop(1, DEPTH)
            def _(j):
                to = rem(z + j, DEPTH)
                send(wz.at[to], brecv.at[z], b_s.at[0], b_r.at[0], deep(to))

            later(brecv.at[pl.ds(0, DEPTH - 1)], b_s.at[0])
            brecv[z] = wz[z]
        else:
            later(fifteen, f_s.at[st])
            frecv[st, spot] = wsend[st, d, y_hi]
        for b in (2 * st, 2 * st + 1):
            through(b)

    for k in range(3):
        ghs[k : k + 1, :] = gm[k, 0:1, :]
    send(ghs, ghr, e_s, e_r, chip(rem(p + CHIPS - 1, CHIPS)))
    later(ghr, e_s)

    sig = 1.0 / (1.0 + jnp.exp(lam))
    for b in range(NB):
        def add(r, carry):
            g = gm[r, :, block(b)]
            return tuple(carry[k] + g * xs[r + k, :, block(b)] for k in range(4)) + (carry[4] + g,)

        zero = jnp.zeros((8, BW), F32)
        acc = lax.fori_loop(0, R, add, (zero,) * 5, unroll=4)
        t_sum, a_sum, x_sum = sums[b]
        t_sum = t_sum * (8.0 * jnp.broadcast_to(sig[:, block(b)], (8, BW)))
        sb = sublane((8, BW))
        rows = zero
        for n, v in enumerate((t_sum, a_sum, x_sum) + tuple(acc)):
            for s in (1, 2, 4):
                v = v + pltpu.roll(v, s, 0)
            rows = jnp.where(sb == n, v, rows)
        for lh in range(2):
            ssend[2 * b + lh] = rows[:, lane_tile(lh)]

    @pl.loop(1, DEPTH)
    def _(j):
        to = rem(z + j, DEPTH)
        send(ssend.at[to], srecv.at[z], fs_s.at[0], fs_r.at[0], deep(to))

    later(srecv.at[pl.ds(0, DEPTH - 1)], fs_s.at[0])
    srecv[z] = ssend[z]

    def fold(st):
        wait_for(fifteen, f_r.at[st])

        @pl.loop(0, DEPTH)
        def _(i):
            at = rows16(i)
            v = frecv[st, 0, at, :].astype(F32)
            for u in range(1, PLANE):
                v = v + frecv[st, u, at, :].astype(F32)
            fsum[st, i] = v.astype(BF16)

        @pl.loop(1, DEPTH)
        def _(j):
            to = rem(z + j, DEPTH)
            send(fsum.at[st, to], zrecv.at[st, z], z_s.at[st], z_r.at[st], deep(to))

        zrecv[st, z] = fsum[st, z]

    pl.when(y_odd == 0)(lambda: fold(0))
    wait_for(ghr, e_r)
    halo = ghr[...]
    halo = jnp.where(p == CHIPS - 1, jnp.zeros_like(halo), halo)
    for k in range(3):
        rolled = pltpu.roll(gm[k], 7, 0)
        gm[R + k] = jnp.where(sub == 7, jnp.broadcast_to(halo[k : k + 1], (8, HALF)), rolled)

    for b in range(NB):
        taps = [jnp.broadcast_to(conv_w[k : k + 1, block(b)], (8, BW)) for k in range(4)]

        @pl.loop(0, R)
        def _(r):
            v = taps[0] * gm[r + 3, :, block(b)]
            for k in range(1, 4):
                v = v + taps[k] * gm[r + 3 - k, :, block(b)]
            for lh in range(2):
                nat[2 * b + lh, pl.ds(r, 8, stride=R), :] = v[:, lane_tile(lh)]

    for k in range(TILES):
        gib[:, lane_tile(k)] = nat[k].astype(BF16)
    s_g = send(gib.at[sib_rows], gi_hbm.at[:, mine], sib_s.at[3], sib_r.at[3], sibling)
    st_g = pltpu.make_async_copy(gib.at[my_rows], gi_hbm.at[:, mine], lsem.at[3])
    st_g.start()
    later(gib.at[my_rows], lsem.at[3])
    wait_for(brecv.at[pl.ds(0, DEPTH - 1)], b_r.at[0])
    for h in range(2):
        for t in range(4):
            v = brecv[0, h, t].astype(F32)
            for j in range(1, DEPTH):
                v = v + brecv[j, h, t].astype(F32)
            bsum[h, t] = v.astype(BF16)

    @pl.loop(1, PLANE)
    def _(j):
        dev, to_h, to_d = plane(j)

        @pl.when(to_d >= 4)
        def _():
            send(bsum.at[to_h, rem(to_d, 4)], bz.at[spot], b_s.at[1], b_r.at[1], dev)

    @pl.when(y_odd == 1)
    def _():
        bz[spot] = bsum[y_hi, x]

    wait_for(srecv.at[pl.ds(0, DEPTH - 1)], fs_r.at[0])
    ssum[...] = jnp.sum(srecv[...], 0)

    @pl.loop(1, PLANE)
    def _(j):
        send(ssum, szrecv.at[spot], fs_s.at[1], fs_r.at[1], plane(j)[0])

    later(szrecv.at[pl.ds(0, PLANE - 1)], fs_s.at[1])
    szrecv[spot] = ssum[...]

    fold(1)
    later(zrecv.at[1, pl.ds(0, DEPTH - 1)], z_s.at[1])

    @pl.when(y_odd == 0)
    def _():
        wait_for(zrecv.at[0, pl.ds(0, DEPTH - 1)], z_s.at[0])
        wait_for(zrecv.at[0, pl.ds(0, DEPTH - 1)], z_r.at[0])
        wait_for(frecv.at[0, pl.ds(0, 7)], f_s.at[0])
        wait_for(bz.at[pl.ds(0, 8)], b_s.at[1])

    @pl.when(y_odd == 1)
    def _():
        wait_for(bz.at[pl.ds(0, PLANE - 1)], b_r.at[1])
        wait_for(frecv.at[0, pl.ds(0, 8)], f_s.at[0])
        wait_for(bz.at[pl.ds(0, 7)], b_s.at[1])


    srecv15 = szrecv.at[pl.ds(0, 2 * REPL - 1)]

    kept = []

    def spread(n, tile):
        keep = pltpu.make_async_copy(tile(c), all_hbm.at[d, c, :, lane_tile(n)], lsem.at[9 + n])
        keep.start()
        kept.append(keep)

        @pl.loop(1, 2 * REPL)
        def _(j):
            to_c = rem(c + div(j, REPL), 2)
            dev = {"ctx": 2 * p + to_c, "dp": rem(d + j, REPL)}
            send(tile(to_c), all_hbm.at[d, c, :, lane_tile(n)], g_s.at[n], g_r.at[n], dev)

        later(srecv15, g_s.at[n])

    def total(st, parts, count):
        whole = parts(0).astype(F32)
        for j in range(1, count):
            whole = whole + parts(j).astype(F32)
        own[st] = whole

    def finish(st):
        spread(st, lambda core: own.at[st, pl.ds(pl.multiple_of(8 * core, 8), 8)])

    pl.when(y_odd == 0)(lambda: total(0, lambda j: zrecv[0, j], DEPTH))
    pl.when(y_odd == 1)(lambda: total(0, lambda j: bz[j], PLANE))
    finish(0)
    wait_for(szrecv.at[pl.ds(0, PLANE - 1)], fs_r.at[1])
    fin[...] = jnp.sum(szrecv[...], 0)

    @pl.loop(1, DEPTH)
    def _(j):
        send(fin, tiles.at[c, z], fs_s.at[2], fs_r.at[2], deep(rem(z + j, DEPTH)))

    later(tiles.at[0, pl.ds(0, DEPTH - 1)], fs_s.at[2])
    tiles[c, z] = fin[...]
    wait_for(zrecv.at[1, pl.ds(0, DEPTH - 1)], z_r.at[1])
    total(1, lambda j: zrecv[1, j], DEPTH)
    finish(1)
    wait_for(tiles.at[0, pl.ds(0, DEPTH - 1)], fs_r.at[2])
    s_t = send(tiles.at[c], small_hbm.at[c], sib_s.at[4], sib_r.at[4], sibling)
    kept.append(pltpu.make_async_copy(tiles.at[c], small_hbm.at[c], lsem.at[4]))
    kept[-1].start()
    for n in range(STAGES):
        wait_for(srecv15, g_r.at[n])
    s_t.wait_recv()

    for cp in [s_w, s_v, s_x, s_c, s_g, s_t]:
        cp.wait_send()
    s_g.wait_recv()
    for finish_one in pending:
        finish_one()
    for cp in kept:
        cp.wait()


def last_kernel(
    gi_in, all_in, small_in, gi_out, gw_out, dec_out, bias_out, taps_out, shift_out,
    all_ref, small_ref, gws, gw, dec, bias, taps, shift, via, l_sem, s_sem,
):
    get = pltpu.make_async_copy(all_in, all_ref, l_sem.at[4])
    get.start()
    get_small = pltpu.make_async_copy(small_in, small_ref, l_sem.at[5])
    get_small.start()
    parts = [pl.ds(k * (ROWS // 4), ROWS // 4) for k in range(4)]
    loads = [pltpu.make_async_copy(gi_in.at[at], via.at[at], l_sem.at[k]) for k, at in enumerate(parts)]
    stores = [pltpu.make_async_copy(via.at[at], gi_out.at[0, at], s_sem.at[k]) for k, at in enumerate(parts)]
    for cp in loads:
        cp.start()
    get.wait()
    get_small.wait()
    for h in range(2):
        for u in range(8):
            at = slice(h * HALF + 128 * u, h * HALF + 128 * (u + 1))
            v = small_ref[h, u]
            dec[:, at] = v[0:1]
            bias[:, at] = v[1:3]
            taps[:, at] = v[3:7]
            shift[:, at] = v[7:8]
            for st in range(STAGES):
                first = ((u // 2) % 2) * 8 + 4 * h + 2 * st + u // 4
                gws[u % 2, pl.ds(first, 8, stride=16), :] = all_ref[u, h, :, lane_tile(st)]
    for n, (src, dst) in enumerate(((dec, dec_out), (bias, bias_out), (taps, taps_out), (shift, shift_out))):
        stores.append(pltpu.make_async_copy(src, dst, s_sem.at[4 + n]))
        stores[-1].start()
    for k in range(4):
        loads[k].wait()
        stores[k].start()
    for i in range(8):
        for g in range(2):
            for lh in range(2):
                gw[i, g, :, lane_tile(lh)] = gws[lh, i * 16 + g * 8 : i * 16 + g * 8 + 8, :]
    stores.append(pltpu.make_async_copy(gw, gw_out, s_sem.at[8]))
    stores[-1].start()
    for cp in stores:
        cp.wait()


def per_device(inputs, gate_weight, gate_bias, decay_param, conv_weight, conv_bias, cotangent):
    hbm = pl.BlockSpec(memory_space=pltpu.HBM)
    dma = pltpu.SemaphoreType.DMA
    big = pltpu.VMEM((R, 8, HALF), F32)
    gi, packed, small = pl.pallas_call(
        main_kernel,
        name="main",
        out_shape=(
            jax.ShapeDtypeStruct((ROWS, WIDTH), BF16),
            jax.ShapeDtypeStruct((REPL, 2, 8, BW), F32),
            jax.ShapeDtypeStruct((2, DEPTH, 8, 128), F32),
        ),
        in_specs=[hbm] * 7,
        out_specs=(hbm,) * 3,
        scratch_shapes=[
            pltpu.VMEM((2, HALF), F32),
            pltpu.VMEM((1, HALF), F32),
            pltpu.VMEM((4, HALF), F32),
            pltpu.VMEM((1, HALF), F32),
            pltpu.VMEM((SPAN, HALF), BF16),
            pltpu.VMEM((SPAN, HALF), BF16),
            pltpu.VMEM((8, 2, 8, BW), BF16),
            pltpu.VMEM((2, 128, 128), F32),
            pltpu.VMEM((2, STAGES, REPL, 8, 128), F32),
            pltpu.VMEM((1 + REPL, 16, 128), F32),
            pltpu.VMEM((REPL, 2, 128, 128), BF16),
            pltpu.VMEM((CHIPS, REPL, 16, 128), BF16),
            pltpu.VMEM((16, HALF), BF16),
            pltpu.VMEM((TILES, SPAN, 128), F32),
            pltpu.VMEM((TILES, SPAN, 128), F32),
            pltpu.VMEM((R + 3, 8, HALF), F32),
            big,
            pltpu.VMEM((SPAN, HALF), BF16),
            pltpu.VMEM((NB, BW, SPAN), BF16),
            pltpu.VMEM((8, SPAN, BW), F32),
            big, big, big, big, big, big, big, big,
            pltpu.VMEM((8, SPAN, BW), BF16),
            pltpu.VMEM((R + 3, 8, HALF), F32),
            pltpu.VMEM((STAGES, 2, 8, 128), F32),
            pltpu.VMEM((STAGES, CHIPS, 8, 128), F32),
            pltpu.VMEM((STAGES, 2, 4, 128), F32),
            pltpu.VMEM((8, HALF), F32),
            pltpu.VMEM((8, HALF), F32),
            pltpu.VMEM((STAGES, REPL, 2, 128, 128), BF16),
            pltpu.VMEM((DEPTH, 2, 4, 16, 128), BF16),
            pltpu.VMEM((STAGES, PLANE, 128, 128), BF16),
            pltpu.VMEM((DEPTH, 2, 4, 16, 128), BF16),
            pltpu.VMEM((2, 4, 16, 128), BF16),
            pltpu.VMEM((PLANE, 16, 128), BF16),
            pltpu.VMEM((STAGES, 16, 128), F32),
            pltpu.VMEM((STAGES, DEPTH, 16, 128), BF16),
            pltpu.VMEM((STAGES, DEPTH, 16, 128), BF16),
            pltpu.VMEM((8, 8, 128), F32),
            pltpu.VMEM((DEPTH, 8, 128), F32),
            pltpu.VMEM((8, 128), F32),
            pltpu.VMEM((PLANE, 8, 128), F32),
            pltpu.VMEM((8, 128), F32),
            pltpu.VMEM((2, DEPTH, 8, 128), F32),
            pltpu.VMEM((SPAN, HALF), BF16),
            dma((11,)), dma((7,)), dma((7,)),
            dma, dma, dma, dma, dma((2,)), dma((6,)), dma, dma,
            dma((STAGES,)), dma((STAGES,)), dma, dma, dma((STAGES,)), dma((STAGES,)),
            dma((2,)), dma((2,)), dma((3,)), dma((3,)),
            dma((STAGES,)), dma((STAGES,)), dma((STAGES,)), dma((STAGES,)),
        ],
        compiler_params=pltpu.CompilerParams(
            collective_id=0, has_side_effects=True, vmem_limit_bytes=60 * 2**20
        ),
    )(
        inputs, gate_weight, gate_bias, decay_param.reshape(1, WIDTH), conv_weight,
        conv_bias.reshape(1, WIDTH), cotangent,
    )
    gi, gw, dec, bias, taps, shift = pl.pallas_call(
        last_kernel,
        name="last",
        out_shape=(
            jax.ShapeDtypeStruct((1, ROWS, WIDTH), BF16),
            jax.ShapeDtypeStruct((8, 2, 8, BW), F32),
            jax.ShapeDtypeStruct((1, WIDTH), F32),
            jax.ShapeDtypeStruct((2, WIDTH), F32),
            jax.ShapeDtypeStruct((4, WIDTH), F32),
            jax.ShapeDtypeStruct((1, WIDTH), F32),
        ),
        in_specs=[hbm] * 3,
        out_specs=(hbm,) * 6,
        scratch_shapes=[
            pltpu.VMEM((REPL, 2, 8, BW), F32),
            pltpu.VMEM((2, DEPTH, 8, 128), F32),
            pltpu.VMEM((2, 128, 128), F32),
            pltpu.VMEM((8, 2, 8, BW), F32),
            pltpu.VMEM((1, WIDTH), F32),
            pltpu.VMEM((2, WIDTH), F32),
            pltpu.VMEM((4, WIDTH), F32),
            pltpu.VMEM((1, WIDTH), F32),
            pltpu.VMEM((ROWS, WIDTH), BF16),
            dma((6,)),
            dma((9,)),
        ],
        compiler_params=pltpu.CompilerParams(vmem_limit_bytes=60 * 2**20),
    )(gi, packed, small)
    return gi, gw, dec.reshape(WIDTH), bias, taps, shift.reshape(WIDTH)


def solution(mesh):
    placed = (
        P("dp", "ctx", None),
        P("ctx", None, None, None),
        P(),
        P(),
        P(),
        P(),
        P("dp", "ctx", None),
    )
    return jax.shard_map(
        per_device,
        mesh=mesh,
        in_specs=placed,
        out_specs=(P("dp", "ctx", None), P("ctx", None, None, None), P(), P(), P(), P()),
        check_vma=False,
    )
```

```python
import jax
import jax.numpy as jnp
from jax import lax
from jax.experimental import pallas as pl
from jax.experimental.pallas import tpu as pltpu
from jax.sharding import PartitionSpec as P

MESH = pl.DeviceIdType.MESH
F32 = jnp.float32
BF16 = jnp.bfloat16
CHIPS = 16
PLANE = 16
DEPTH = 8
REPL = 8
ROWS = 128
SPAN = 256
WIDTH = 2048
HALF = 1024
BW = 256
NB = HALF // BW
R = SPAN // 8
TILES = HALF // 128
STAGES = 2


def wait_for(ref, sem):
    pltpu.make_async_copy(ref, ref, sem).wait()


def sublane(shape):
    return lax.broadcasted_iota(jnp.int32, shape, 0)


def sigmoid(x):
    return 0.5 * jnp.tanh(0.5 * x) + 0.5


def softplus(x):
    e = jnp.exp(-jnp.abs(x))
    z = e / (2.0 + e)
    z2 = z * z
    s = jnp.full_like(z, 1.0 / 17.0)
    for n in (15, 13, 11, 9, 7, 5, 3, 1):
        s = s * z2 + 1.0 / n
    return jnp.maximum(x, 0.0) + 2.0 * z * s


def lane_tile(i):
    return slice(i * 128, (i + 1) * 128)


def block(b):
    return slice(b * BW, (b + 1) * BW)


def main_kernel(
    x_hbm, w_hbm, gb_hbm, lam_hbm, cw_hbm, cb_hbm, cot_hbm,
    gi_hbm, all_hbm, small_hbm,
    gb_ref, lam_ref, cw_ref, cb_ref, xb, cotb, wsh, wf, wu, wpair, W0, W1, xhalo, nat, natc, xs, cs, mb, mt, pre,
    dec, drv, qq, m1, m2, m3, oma, hp, gp, gm, dsend, drecv, sin, ghs, ghr,
    wsend, wz, frecv, brecv, bsum, bz, own, fsum, zrecv, ssend, srecv, ssum, szrecv, fin, gib,
    lsem, sib_s, sib_r, c1_s, c1_r, hal_s, hal_r, za_s, za_r, c2_s, c2_r, d_s, d_r, e_s, e_r,
    f_s, f_r, b_s, b_r, fs_s, fs_r, z_s, z_r, g_s, g_r,
):
    ctx = lax.axis_index("ctx")
    d = lax.axis_index("dp")
    div, rem = lax.div, lax.rem
    p, c = div(ctx, 2), rem(ctx, 2)
    z = rem(p, DEPTH)
    y = 2 * div(p, DEPTH) + div(d, 4)
    x = rem(d, 4)
    y_hi, y_odd = div(y, 2), rem(y, 2)
    spot = 4 * y + x
    sibling = {"ctx": 2 * p + 1 - c, "dp": d}

    def chip(j):
        return {"ctx": 2 * j + c, "dp": d}

    def deep(j):
        return {"ctx": 2 * (p - z + j) + c, "dp": d}

    def peer(u):
        return {"ctx": ctx, "dp": u}

    def plane(j):
        to_x, to_y = rem(x + rem(j, 4), 4), rem(y + div(j, 4), 4)
        to_h, to_d = div(to_y, 2), 4 * rem(to_y, 2) + to_x
        return {"ctx": 2 * (DEPTH * to_h + z) + c, "dp": to_d}, to_h, to_d

    def rows16(j):
        return pl.ds(pl.multiple_of(16 * j, 16), 16)

    def send(src, dst, ss, rs, dev):
        cp = pltpu.make_async_remote_copy(
            src_ref=src, dst_ref=dst, send_sem=ss, recv_sem=rs, device_id=dev, device_id_type=MESH
        )
        cp.start()
        return cp

    bar = pltpu.get_barrier_semaphore()
    pl.semaphore_signal(bar, inc=1, device_id=sibling, device_id_type=MESH)

    @pl.loop(1, CHIPS)
    def _(j):
        pl.semaphore_signal(bar, inc=1, device_id=chip(rem(p + j, CHIPS)), device_id_type=MESH)

    @pl.loop(1, PLANE)
    def _(j):
        @pl.when(j != PLANE // 2)
        def _():
            pl.semaphore_signal(bar, inc=1, device_id=plane(j)[0], device_id_type=MESH)

    @pl.loop(1, REPL)
    def _(j):
        dev = {"ctx": 2 * p + 1 - c, "dp": rem(d + j, REPL)}
        pl.semaphore_signal(bar, inc=1, device_id=dev, device_id_type=MESH)

    mine = pl.ds(pl.multiple_of(HALF * c, HALF), HALF)
    theirs = pl.ds(pl.multiple_of(HALF * (1 - c), HALF), HALF)
    my_rows = pl.ds(pl.multiple_of(ROWS * c, ROWS), ROWS)
    sib_rows = pl.ds(pl.multiple_of(ROWS * (1 - c), ROWS), ROWS)

    ld_w = pltpu.make_async_copy(w_hbm, wsh, lsem.at[0])
    ld_w.start()
    ld_x = pltpu.make_async_copy(x_hbm.at[0, :, mine], xb.at[my_rows], lsem.at[1])
    ld_x.start()
    ld_c = pltpu.make_async_copy(cot_hbm.at[0, :, mine], cotb.at[my_rows], lsem.at[2])
    ld_c.start()
    lds = []
    for n, (src, dst) in enumerate(
        ((gb_hbm, gb_ref), (lam_hbm, lam_ref), (cw_hbm, cw_ref), (cb_hbm, cb_ref))
    ):
        lds.append(pltpu.make_async_copy(src.at[:, mine], dst, lsem.at[5 + n]))
        lds[-1].start()
    pending = []

    def later(ref, sem):
        pending.append(lambda: wait_for(ref, sem))


    ld_w.wait()
    for i in range(8):
        for g in range(2):
            v = wsh[i, g].astype(F32)
            for lh in range(2):
                wf[lh, i * 16 + g * 8 : i * 16 + g * 8 + 8, :] = v[:, lane_tile(lh)]
    for h in range(2):
        for u in range(REPL):
            for st in range(STAGES):
                first = ((u // 2) % 2) * 8 + 4 * h + 2 * st + u // 4
                wu[h, st, u] = wf[u % 2, pl.ds(first, 8, stride=16), :]

    pl.semaphore_wait(bar, 1 + (CHIPS - 1) + (PLANE - 2) + (REPL - 1))

    part = pl.ds(pl.multiple_of(8 * c, 8), 8)
    s_w = send(wu.at[1 - c, 0, d], wpair.at[0, part], sib_s.at[0], sib_r.at[0], sibling)
    s_v = send(wu.at[1 - c, 1], wpair.at[pl.ds(1, REPL), part], sib_s.at[5], sib_r.at[5], sibling)
    wpair[0, part, :] = wu[c, 0, d]
    s_w.wait_recv()
    mine_w = W0.at[d, y_hi, rows16(z)]
    mine_w[...] = wpair[0].astype(BF16)

    @pl.loop(1, DEPTH)
    def _(j):
        send(mine_w, mine_w, c1_s, c1_r, deep(rem(z + j, DEPTH)))

    s_x = send(x_hbm.at[0, :, theirs], xb.at[my_rows], sib_s.at[1], sib_r.at[1], sibling)
    s_c = send(cot_hbm.at[0, :, theirs], cotb.at[my_rows], sib_s.at[2], sib_r.at[2], sibling)
    seven = W1.at[0, pl.ds(0, DEPTH - 1)]
    later(seven, c1_s)
    wpair[1:, part, :] = wu[c, 1]
    s_v.wait_recv()
    for u in range(REPL):
        W1[p, u] = wpair[1 + u].astype(BF16)
    across = rem(p + DEPTH, CHIPS)
    rows_a, rows_b = W1.at[p], W1.at[across]
    send(rows_a, rows_a, za_s.at[0], za_r.at[0], chip(across))
    later(rows_a, za_s.at[0])

    def at_depth(side, by):
        return (p - z if side == 0 else across - z) + rem(z + by + DEPTH, DEPTH)

    def near(side):
        rows = W1.at[at_depth(side, 0)]
        for by in (1, -1):
            send(rows, rows, za_s.at[1], za_r.at[1], deep(rem(z + by + DEPTH, DEPTH)))
        for by in (2, -2):
            arrive = za_r.at[2 + 2 * side + (0 if by > 0 else 1)]
            send(rows, rows, za_s.at[1], arrive, deep(rem(z + by + DEPTH, DEPTH)))

    def onward(side):
        for way, by in ((0, 1), (1, -1)):
            rows = W1.at[at_depth(side, -2 * by)]
            wait_for(rows, za_r.at[2 + 2 * side + way])
            send(rows, rows, za_s.at[1], za_r.at[1], deep(rem(z + by + DEPTH, DEPTH)))
            half = W1.at[at_depth(side, -2 * by), pl.ds(4 * way, 4)]
            send(half, half, za_s.at[1], za_r.at[1], deep(rem(z + 2 * by + DEPTH, DEPTH)))

    near(0)

    ld_x.wait()
    s_x.wait_recv()
    send(xb.at[pl.ds(SPAN - 16, 16)], xhalo, hal_s, hal_r, chip(rem(p + 1, CHIPS)))
    later(xhalo, hal_s)
    for k in range(TILES):
        nat[k] = xb[:, lane_tile(k)].astype(F32)

    @pl.loop(0, R)
    def _(r):
        for k in range(TILES):
            xs[3 + r, :, lane_tile(k)] = nat[k, pl.ds(r, 8, stride=R), :]

    wait_for(rows_b, za_r.at[0])

    near(1)
    later(W1.at[pl.ds(0, 14)], za_s.at[1])
    ten = W1.at[pl.ds(0, 10)]
    wait_for(seven, c1_r)
    fifteen = frecv.at[0, pl.ds(0, PLANE - 1)]
    mine_s = W0.at[d, y_hi]

    @pl.loop(1, PLANE)
    def _(j):
        send(mine_s, mine_s, c2_s, c2_r, plane(j)[0])

    later(fifteen, c2_s)
    onward(0)
    onward(1)
    ld_c.wait()
    s_c.wait_recv()
    for k in range(TILES):
        natc[k] = cotb[:, lane_tile(k)].astype(F32)

    @pl.loop(0, R)
    def _(r):
        for k in range(TILES):
            cs[r, :, lane_tile(k)] = natc[k, pl.ds(r, 8, stride=R), :]

    wait_for(xhalo, hal_r)
    hal = xhalo[...].astype(F32)
    hal = jnp.where(p == 0, jnp.zeros_like(hal), hal)
    sub = sublane((8, HALF))
    for k in range(3):
        rolled = pltpu.roll(xs[3 + R - 3 + k], 1, 0)
        xs[k] = jnp.where(sub == 0, jnp.broadcast_to(hal[13 + k : 14 + k], (8, HALF)), rolled)

    for ld in lds:
        ld.wait()
    conv_w = cw_ref[...]
    conv_b = cb_ref[...]
    for b in range(NB):
        taps = [jnp.broadcast_to(conv_w[k : k + 1, block(b)], (8, BW)) for k in range(4)]
        shift = jnp.broadcast_to(conv_b[:, block(b)], (8, BW))

        @pl.loop(0, R // 2)
        def _(i):
            v = [xs[2 * i + k, :, block(b)] for k in range(5)]
            out = []
            for o in range(2):
                m = shift + taps[0] * v[o]
                for k in range(1, 4):
                    m = m + taps[k] * v[o + k]
                out.append(m)
            mb[pl.ds(pl.multiple_of(16 * i, 16), 16), block(b)] = jnp.concatenate(out, 0).astype(BF16)

        mt[b] = mb[:, block(b)].astype(F32).T.astype(BF16)

    lam = lam_ref[...]
    neg8rate = -8.0 * softplus(-lam)
    gate_b = gb_ref[...]
    ends = []

    def weights(b, g):
        u = 4 * (b % 2) + 2 * g
        two = (W0[u + lh] if b < 2 else W1[:, u + lh] for lh in range(2))
        return jnp.concatenate([v.reshape(BW, 128) for v in two], 1)

    def gates(b):
        st = b // 2
        for g in range(2):
            pre[2 * b + g] = jnp.dot(mb[:, block(b)], weights(b, g), preferred_element_type=F32)
        nr = jnp.broadcast_to(neg8rate[:, block(b)], (8, BW))
        ba = jnp.broadcast_to(gate_b[0:1, block(b)], (8, BW))
        bx = jnp.broadcast_to(gate_b[1:2, block(b)], (8, BW))

        def step(i, carry):
            prod, hid, kk, logs = carry
            two = mb[pl.ds(pl.multiple_of(16 * i, 16), 16), block(b)].astype(F32)
            for o in range(2):
                r = 2 * i + o
                at = pl.ds(pl.multiple_of(8 * r, 8), 8)
                ga = sigmoid(pre[2 * b, at, :] + ba)
                gx = sigmoid(pre[2 * b + 1, at, :] + bx)
                m = two[8 * o : 8 * o + 8]
                ld = ga * nr
                a = jnp.exp(ld)
                sq = 1.0 - a * a
                mult = jnp.sqrt(sq)
                gm_ = gx * m
                drive = mult * gm_
                dec[r, :, block(b)] = a
                drv[r, :, block(b)] = drive
                qq[r, :, block(b)] = gm_ * a * lax.rsqrt(jnp.maximum(sq, 0.05))
                m1[r, :, block(b)] = a * ga
                oma[r, :, block(b)] = (1.0 - ga) * nr
                m2[r, :, block(b)] = drive * (1.0 - gx)
                m3[r, :, block(b)] = mult * gx
                hid = a * hid + drive
                prod = prod * a
                kk = kk + prod * cs[r, :, block(b)]
                logs = logs + ld
            return prod, hid, kk, logs

        zero = jnp.zeros((8, BW), F32)
        prod, hid, kk, logs = lax.fori_loop(
            0, R // 2, step, (jnp.ones((8, BW), F32), zero, zero, zero), unroll=2
        )
        sb = sublane((8, BW))
        fp, fh = prod, hid
        bp, bk = prod, kk
        for s in (1, 2, 4):
            mp, mh = pltpu.roll(fp, s, 0), pltpu.roll(fh, s, 0)
            fh = jnp.where(sb >= s, fp * mh + fh, fh)
            fp = jnp.where(sb >= s, fp * mp, fp)
            mp, mk = pltpu.roll(bp, 8 - s, 0), pltpu.roll(bk, 8 - s, 0)
            bk = jnp.where(sb < 8 - s, bp * mk + bk, bk)
            bp = jnp.where(sb < 8 - s, bp * mp, bp)
            logs = logs + pltpu.roll(logs, s, 0)
        one = jnp.ones((8, BW), F32)
        ends.append((
            jnp.where(sb == 0, one, pltpu.roll(fp, 1, 0)),
            jnp.where(sb == 0, zero, pltpu.roll(fh, 1, 0)),
            jnp.where(sb == 7, one, pltpu.roll(bp, 7, 0)),
            jnp.where(sb == 7, zero, pltpu.roll(bk, 7, 0)),
        ))
        for lh in range(2):
            k = 2 * (b % 2) + lh
            dsend[st, 0, k : k + 1, :] = logs[0:1, lane_tile(lh)]
            dsend[st, 1, k : k + 1, :] = logs[0:1, lane_tile(lh)]
            dsend[st, 0, 4 + k : 5 + k, :] = fh[7:8, lane_tile(lh)]
            dsend[st, 1, 4 + k : 5 + k, :] = bk[0:1, lane_tile(lh)]

    for st in range(STAGES):
        wait_for(*((fifteen, c2_r) if st == 0 else (ten, za_r.at[1])))
        for b in (2 * st, 2 * st + 1):
            gates(b)

        @pl.loop(1, CHIPS)
        def _(j):
            to = rem(p + j, CHIPS)
            send(dsend.at[st, jnp.where(to > p, 0, 1)], drecv.at[st, p], d_s.at[st], d_r.at[st], chip(to))

        later(drecv.at[st, pl.ds(0, CHIPS - 1)], d_s.at[st])
        drecv[st, p] = jnp.zeros((8, 128), F32)

    sums = []

    def grads(b):
        st, k = b // 2, 2 * (b % 2)

        def wide(n):
            return jnp.concatenate(
                [jnp.broadcast_to(sin[st, n, k + lh : k + lh + 1, :], (8, 128)) for lh in range(2)], 1
            )

        hin = ends[b][1] + ends[b][0] * wide(0)
        kin = ends[b][3] + ends[b][2] * wide(1)

        def up(r, h):
            hp[r, :, block(b)] = h
            return dec[r, :, block(b)] * h + drv[r, :, block(b)]

        lax.fori_loop(0, R, up, hin, unroll=4)

        def down(n, carry):
            kk, t_sum, a_sum, x_sum = carry
            i = R // 2 - 1 - n
            outs = [[None, None], [None, None]]
            for o in (1, 0):
                r = 2 * i + o
                gr = cs[r, :, block(b)] + kk
                kk = dec[r, :, block(b)] * gr
                t = (hp[r, :, block(b)] - qq[r, :, block(b)]) * m1[r, :, block(b)] * gr
                ga = t * oma[r, :, block(b)]
                gx = gr * m2[r, :, block(b)]
                gm[r, :, block(b)] = gr * m3[r, :, block(b)]
                t_sum, a_sum, x_sum = t_sum + t, a_sum + ga, x_sum + gx
                outs[0][o], outs[1][o] = ga, gx
            at = pl.ds(pl.multiple_of(16 * i, 16), 16)
            gp[2 * b, at, :] = jnp.concatenate(outs[0], 0).astype(BF16)
            gp[2 * b + 1, at, :] = jnp.concatenate(outs[1], 0).astype(BF16)
            return kk, t_sum, a_sum, x_sum

        zero = jnp.zeros((8, BW), F32)
        _, t_sum, a_sum, x_sum = lax.fori_loop(0, R // 2, down, (kin, zero, zero, zero), unroll=4)
        sums.append([t_sum, a_sum, x_sum])
        for g in range(2):
            grad = jnp.dot(mt[b], gp[2 * b + g], preferred_element_type=F32).astype(BF16)
            for lh in range(2):
                for h in range(2):
                    if b == 1:
                        for j in range(DEPTH):
                            wz[j, h, 2 * g + lh] = grad[128 * h + 16 * j : 128 * h + 16 * j + 16, lane_tile(lh)]
                    else:
                        wsend[st, 2 * (k + g) + lh, h] = grad[128 * h : 128 * (h + 1), lane_tile(lh)]

    def through(b):
        nt = (((1,), (1,)), ((), ()))
        back = lax.dot_general(gp[2 * b], weights(b, 0), nt, preferred_element_type=F32)
        back = back + lax.dot_general(gp[2 * b + 1], weights(b, 1), nt, preferred_element_type=F32)
        gm[0:R, :, block(b)] = gm[0:R, :, block(b)] + back.reshape(R, 8, BW)

    sig = 1.0 / (1.0 + jnp.exp(lam))

    def small_sums(b):
        def add(r, carry):
            g = gm[r, :, block(b)]
            return tuple(carry[k] + g * xs[r + k, :, block(b)] for k in range(4)) + (carry[4] + g,)

        zero = jnp.zeros((8, BW), F32)
        acc = lax.fori_loop(0, R, add, (zero,) * 5, unroll=4)
        t_sum, a_sum, x_sum = sums[b]
        t_sum = t_sum * (8.0 * jnp.broadcast_to(sig[:, block(b)], (8, BW)))
        sb = sublane((8, BW))
        rows = zero
        for n, v in enumerate((t_sum, a_sum, x_sum) + tuple(acc)):
            for s in (1, 2, 4):
                v = v + pltpu.roll(v, s, 0)
            rows = jnp.where(sb == n, v, rows)
        for lh in range(2):
            ssend[2 * b + lh] = rows[:, lane_tile(lh)]

    for st in range(STAGES):
        wait_for(drecv.at[st, pl.ds(0, CHIPS - 1)], d_r.at[st])
        state = jnp.zeros((4, 128), F32)
        carry_in = jnp.zeros((4, 128), F32)
        for j in range(CHIPS):
            v = drecv[st, j]
            state = jnp.where(j < p, jnp.exp(v[:4]) * state + v[4:], state)
            v = drecv[st, CHIPS - 1 - j]
            carry_in = jnp.where(CHIPS - 1 - j > p, jnp.exp(v[:4]) * carry_in + v[4:], carry_in)
        sin[st, 0] = state
        sin[st, 1] = carry_in
        def to_plane(low):
            @pl.loop(1, PLANE)
            def _(j):
                dev, to_h, to_d = plane(j)

                @pl.when(to_d < 4 if low else to_d >= 4)
                def _():
                    send(
                        wsend.at[st, to_d, to_h], frecv.at[st, spot], f_s.at[st], f_r.at[st], dev
                    )

        grads(2 * st)
        to_plane(True)
        grads(2 * st + 1)
        if st == 0:
            @pl.when(y_odd == 0)
            def _():
                frecv[0, spot] = wsend[0, d, y_hi]

            @pl.loop(1, DEPTH)
            def _(j):
                to = rem(z + j, DEPTH)
                send(wz.at[to], brecv.at[z], b_s.at[0], b_r.at[0], deep(to))

            later(brecv.at[pl.ds(0, DEPTH - 1)], b_s.at[0])
            brecv[z] = wz[z]
        for b in (2 * st, 2 * st + 1):
            through(b)
            small_sums(b)

    @pl.loop(1, PLANE)
    def _(j):
        dev, _, to_d = plane(j)
        send(ssend.at[to_d], srecv.at[spot], fs_s.at[0], fs_r.at[0], dev)

    later(srecv.at[pl.ds(0, PLANE - 1)], fs_s.at[0])
    for k in range(3):
        ghs[k : k + 1, :] = gm[k, 0:1, :]
    send(ghs, ghr, e_s, e_r, chip(rem(p + CHIPS - 1, CHIPS)))
    later(ghr, e_s)
    to_plane(False)
    later(fifteen, f_s.at[1])
    frecv[1, spot] = wsend[1, d, y_hi]
    srecv[spot] = ssend[d]

    def fold(st):
        wait_for(fifteen, f_r.at[st])

        @pl.loop(0, DEPTH)
        def _(i):
            at = rows16(i)
            v = frecv[st, 0, at, :].astype(F32)
            for u in range(1, PLANE):
                v = v + frecv[st, u, at, :].astype(F32)
            fsum[st, i] = v.astype(BF16)

        @pl.loop(1, DEPTH)
        def _(j):
            to = rem(z + j, DEPTH)
            send(fsum.at[st, to], zrecv.at[st, z], z_s.at[st], z_r.at[st], deep(to))

        zrecv[st, z] = fsum[st, z]

    pl.when(y_odd == 0)(lambda: fold(0))
    wait_for(ghr, e_r)
    halo = ghr[...]
    halo = jnp.where(p == CHIPS - 1, jnp.zeros_like(halo), halo)
    for k in range(3):
        rolled = pltpu.roll(gm[k], 7, 0)
        gm[R + k] = jnp.where(sub == 7, jnp.broadcast_to(halo[k : k + 1], (8, HALF)), rolled)

    for b in range(NB):
        taps = [jnp.broadcast_to(conv_w[k : k + 1, block(b)], (8, BW)) for k in range(4)]

        @pl.loop(0, R)
        def _(r):
            v = taps[0] * gm[r + 3, :, block(b)]
            for k in range(1, 4):
                v = v + taps[k] * gm[r + 3 - k, :, block(b)]
            for lh in range(2):
                nat[2 * b + lh, pl.ds(r, 8, stride=R), :] = v[:, lane_tile(lh)]

    for k in range(TILES):
        gib[:, lane_tile(k)] = nat[k].astype(BF16)
    s_g = send(gib.at[sib_rows], gi_hbm.at[:, mine], sib_s.at[3], sib_r.at[3], sibling)
    st_g = pltpu.make_async_copy(gib.at[my_rows], gi_hbm.at[:, mine], lsem.at[3])
    st_g.start()
    later(gib.at[my_rows], lsem.at[3])
    wait_for(brecv.at[pl.ds(0, DEPTH - 1)], b_r.at[0])
    for h in range(2):
        for t in range(4):
            v = brecv[0, h, t].astype(F32)
            for j in range(1, DEPTH):
                v = v + brecv[j, h, t].astype(F32)
            bsum[h, t] = v.astype(BF16)

    @pl.loop(1, PLANE)
    def _(j):
        dev, to_h, to_d = plane(j)

        @pl.when(to_d >= 4)
        def _():
            send(bsum.at[to_h, rem(to_d, 4)], bz.at[spot], b_s.at[1], b_r.at[1], dev)

    @pl.when(y_odd == 1)
    def _():
        bz[spot] = bsum[y_hi, x]

    wait_for(srecv.at[pl.ds(0, PLANE - 1)], fs_r.at[0])
    ssum[...] = jnp.sum(srecv[...], 0)

    @pl.loop(1, DEPTH)
    def _(j):
        send(ssum, szrecv.at[z], fs_s.at[1], fs_r.at[1], deep(rem(z + j, DEPTH)))

    later(szrecv.at[pl.ds(0, DEPTH - 1)], fs_s.at[1])
    szrecv[z] = ssum[...]

    fold(1)
    later(zrecv.at[1, pl.ds(0, DEPTH - 1)], z_s.at[1])

    @pl.when(y_odd == 0)
    def _():
        wait_for(zrecv.at[0, pl.ds(0, DEPTH - 1)], z_s.at[0])
        wait_for(zrecv.at[0, pl.ds(0, DEPTH - 1)], z_r.at[0])
        wait_for(frecv.at[0, pl.ds(0, 7)], f_s.at[0])
        wait_for(bz.at[pl.ds(0, 8)], b_s.at[1])

    @pl.when(y_odd == 1)
    def _():
        wait_for(bz.at[pl.ds(0, PLANE - 1)], b_r.at[1])
        wait_for(frecv.at[0, pl.ds(0, 8)], f_s.at[0])
        wait_for(bz.at[pl.ds(0, 7)], b_s.at[1])


    srecv15 = srecv.at[pl.ds(0, 2 * REPL - 1)]
    kept = []

    def spread(n, tile, out):
        keep = pltpu.make_async_copy(tile(c), out, lsem.at[9 + n])
        keep.start()
        kept.append(keep)

        @pl.loop(1, 2 * REPL)
        def _(j):
            to_c = rem(c + div(j, REPL), 2)
            dev = {"ctx": 2 * p + to_c, "dp": rem(d + j, REPL)}
            send(tile(to_c), out, g_s.at[n], g_r.at[n], dev)

        later(srecv15, g_s.at[n])

    def total(st, parts, count):
        whole = parts(0).astype(F32)
        for j in range(1, count):
            whole = whole + parts(j).astype(F32)
        own[st] = whole

    def finish(st):
        rows = lambda core: own.at[st, pl.ds(pl.multiple_of(8 * core, 8), 8)]
        spread(st, rows, all_hbm.at[d, c, :, lane_tile(st)])

    pl.when(y_odd == 0)(lambda: total(0, lambda j: zrecv[0, j], DEPTH))
    pl.when(y_odd == 1)(lambda: total(0, lambda j: bz[j], PLANE))
    finish(0)
    wait_for(szrecv.at[pl.ds(0, DEPTH - 1)], fs_r.at[1])
    fin[...] = jnp.sum(szrecv[...], 0)
    spread(STAGES, lambda core: fin, small_hbm.at[c, d])
    wait_for(zrecv.at[1, pl.ds(0, DEPTH - 1)], z_r.at[1])
    total(1, lambda j: zrecv[1, j], DEPTH)
    finish(1)
    for n in range(STAGES + 1):
        wait_for(srecv15, g_r.at[n])

    for cp in [s_w, s_v, s_x, s_c, s_g]:
        cp.wait_send()
    s_g.wait_recv()
    for finish_one in pending:
        finish_one()
    for cp in kept:
        cp.wait()


def last_kernel(
    gi_in, all_in, small_in, gi_out, gw_out, dec_out, bias_out, taps_out, shift_out,
    all_ref, small_ref, gws, gw, dec, bias, taps, shift, via, l_sem, s_sem,
):
    get = pltpu.make_async_copy(all_in, all_ref, l_sem.at[4])
    get.start()
    get_small = pltpu.make_async_copy(small_in, small_ref, l_sem.at[5])
    get_small.start()
    parts = [pl.ds(k * (ROWS // 4), ROWS // 4) for k in range(4)]
    loads = [pltpu.make_async_copy(gi_in.at[at], via.at[at], l_sem.at[k]) for k, at in enumerate(parts)]
    stores = [pltpu.make_async_copy(via.at[at], gi_out.at[0, at], s_sem.at[k]) for k, at in enumerate(parts)]
    for cp in loads:
        cp.start()
    get.wait()
    get_small.wait()
    for h in range(2):
        for u in range(8):
            at = slice(h * HALF + 128 * u, h * HALF + 128 * (u + 1))
            v = small_ref[h, u]
            dec[:, at] = v[0:1]
            bias[:, at] = v[1:3]
            taps[:, at] = v[3:7]
            shift[:, at] = v[7:8]
            for st in range(STAGES):
                first = ((u // 2) % 2) * 8 + 4 * h + 2 * st + u // 4
                gws[u % 2, pl.ds(first, 8, stride=16), :] = all_ref[u, h, :, lane_tile(st)]
    for n, (src, dst) in enumerate(((dec, dec_out), (bias, bias_out), (taps, taps_out), (shift, shift_out))):
        stores.append(pltpu.make_async_copy(src, dst, s_sem.at[4 + n]))
        stores[-1].start()
    for k in range(4):
        loads[k].wait()
        stores[k].start()
    for i in range(8):
        for g in range(2):
            for lh in range(2):
                gw[i, g, :, lane_tile(lh)] = gws[lh, i * 16 + g * 8 : i * 16 + g * 8 + 8, :]
    stores.append(pltpu.make_async_copy(gw, gw_out, s_sem.at[8]))
    stores[-1].start()
    for cp in stores:
        cp.wait()


def per_device(inputs, gate_weight, gate_bias, decay_param, conv_weight, conv_bias, cotangent):
    hbm = pl.BlockSpec(memory_space=pltpu.HBM)
    dma = pltpu.SemaphoreType.DMA
    big = pltpu.VMEM((R, 8, HALF), F32)
    gi, packed, small = pl.pallas_call(
        main_kernel,
        name="main",
        out_shape=(
            jax.ShapeDtypeStruct((ROWS, WIDTH), BF16),
            jax.ShapeDtypeStruct((REPL, 2, 8, BW), F32),
            jax.ShapeDtypeStruct((2, REPL, 8, 128), F32),
        ),
        in_specs=[hbm] * 7,
        out_specs=(hbm,) * 3,
        scratch_shapes=[
            pltpu.VMEM((2, HALF), F32),
            pltpu.VMEM((1, HALF), F32),
            pltpu.VMEM((4, HALF), F32),
            pltpu.VMEM((1, HALF), F32),
            pltpu.VMEM((SPAN, HALF), BF16),
            pltpu.VMEM((SPAN, HALF), BF16),
            pltpu.VMEM((8, 2, 8, BW), BF16),
            pltpu.VMEM((2, 128, 128), F32),
            pltpu.VMEM((2, STAGES, REPL, 8, 128), F32),
            pltpu.VMEM((1 + REPL, 16, 128), F32),
            pltpu.VMEM((REPL, 2, 128, 128), BF16),
            pltpu.VMEM((CHIPS, REPL, 16, 128), BF16),
            pltpu.VMEM((16, HALF), BF16),
            pltpu.VMEM((TILES, SPAN, 128), F32),
            pltpu.VMEM((TILES, SPAN, 128), F32),
            pltpu.VMEM((R + 3, 8, HALF), F32),
            big,
            pltpu.VMEM((SPAN, HALF), BF16),
            pltpu.VMEM((NB, BW, SPAN), BF16),
            pltpu.VMEM((8, SPAN, BW), F32),
            big, big, big, big, big, big, big, big,
            pltpu.VMEM((8, SPAN, BW), BF16),
            pltpu.VMEM((R + 3, 8, HALF), F32),
            pltpu.VMEM((STAGES, 2, 8, 128), F32),
            pltpu.VMEM((STAGES, CHIPS, 8, 128), F32),
            pltpu.VMEM((STAGES, 2, 4, 128), F32),
            pltpu.VMEM((8, HALF), F32),
            pltpu.VMEM((8, HALF), F32),
            pltpu.VMEM((STAGES, REPL, 2, 128, 128), BF16),
            pltpu.VMEM((DEPTH, 2, 4, 16, 128), BF16),
            pltpu.VMEM((STAGES, PLANE, 128, 128), BF16),
            pltpu.VMEM((DEPTH, 2, 4, 16, 128), BF16),
            pltpu.VMEM((2, 4, 16, 128), BF16),
            pltpu.VMEM((PLANE, 16, 128), BF16),
            pltpu.VMEM((STAGES, 16, 128), F32),
            pltpu.VMEM((STAGES, DEPTH, 16, 128), BF16),
            pltpu.VMEM((STAGES, DEPTH, 16, 128), BF16),
            pltpu.VMEM((8, 8, 128), F32),
            pltpu.VMEM((PLANE, 8, 128), F32),
            pltpu.VMEM((8, 128), F32),
            pltpu.VMEM((DEPTH, 8, 128), F32),
            pltpu.VMEM((8, 128), F32),
            pltpu.VMEM((SPAN, HALF), BF16),
            dma((12,)), dma((7,)), dma((7,)),
            dma, dma, dma, dma, dma((2,)), dma((6,)), dma, dma,
            dma((STAGES,)), dma((STAGES,)), dma, dma, dma((STAGES,)), dma((STAGES,)),
            dma((2,)), dma((2,)), dma((2,)), dma((2,)),
            dma((STAGES,)), dma((STAGES,)), dma((STAGES + 1,)), dma((STAGES + 1,)),
        ],
        compiler_params=pltpu.CompilerParams(
            collective_id=0, has_side_effects=True, vmem_limit_bytes=60 * 2**20
        ),
    )(
        inputs, gate_weight, gate_bias, decay_param.reshape(1, WIDTH), conv_weight,
        conv_bias.reshape(1, WIDTH), cotangent,
    )
    gi, gw, dec, bias, taps, shift = pl.pallas_call(
        last_kernel,
        name="last",
        out_shape=(
            jax.ShapeDtypeStruct((1, ROWS, WIDTH), BF16),
            jax.ShapeDtypeStruct((8, 2, 8, BW), F32),
            jax.ShapeDtypeStruct((1, WIDTH), F32),
            jax.ShapeDtypeStruct((2, WIDTH), F32),
            jax.ShapeDtypeStruct((4, WIDTH), F32),
            jax.ShapeDtypeStruct((1, WIDTH), F32),
        ),
        in_specs=[hbm] * 3,
        out_specs=(hbm,) * 6,
        scratch_shapes=[
            pltpu.VMEM((REPL, 2, 8, BW), F32),
            pltpu.VMEM((2, REPL, 8, 128), F32),
            pltpu.VMEM((2, 128, 128), F32),
            pltpu.VMEM((8, 2, 8, BW), F32),
            pltpu.VMEM((1, WIDTH), F32),
            pltpu.VMEM((2, WIDTH), F32),
            pltpu.VMEM((4, WIDTH), F32),
            pltpu.VMEM((1, WIDTH), F32),
            pltpu.VMEM((ROWS, WIDTH), BF16),
            dma((6,)),
            dma((9,)),
        ],
        compiler_params=pltpu.CompilerParams(vmem_limit_bytes=60 * 2**20),
    )(gi, packed, small)
    return gi, gw, dec.reshape(WIDTH), bias, taps, shift.reshape(WIDTH)


def solution(mesh):
    placed = (
        P("dp", "ctx", None),
        P("ctx", None, None, None),
        P(),
        P(),
        P(),
        P(),
        P("dp", "ctx", None),
    )
    return jax.shard_map(
        per_device,
        mesh=mesh,
        in_specs=placed,
        out_specs=(P("dp", "ctx", None), P("ctx", None, None, None), P(), P(), P(), P()),
        check_vma=False,
    )
```

```python
import jax
import jax.numpy as jnp
from jax import lax
from jax.experimental import pallas as pl
from jax.experimental.pallas import tpu as pltpu
from jax.sharding import PartitionSpec as P

MESH = pl.DeviceIdType.MESH
F32 = jnp.float32
BF16 = jnp.bfloat16
CHIPS = 16
PLANE = 16
DEPTH = 8
REPL = 8
ROWS = 128
SPAN = 256
WIDTH = 2048
HALF = 1024
BW = 256
NB = HALF // BW
R = SPAN // 8
TILES = HALF // 128
STAGES = 2


def wait_for(ref, sem):
    pltpu.make_async_copy(ref, ref, sem).wait()


def sublane(shape):
    return lax.broadcasted_iota(jnp.int32, shape, 0)


def sigmoid(x):
    return 0.5 * jnp.tanh(0.5 * x) + 0.5


def softplus(x):
    e = jnp.exp(-jnp.abs(x))
    z = e / (2.0 + e)
    z2 = z * z
    s = jnp.full_like(z, 1.0 / 17.0)
    for n in (15, 13, 11, 9, 7, 5, 3, 1):
        s = s * z2 + 1.0 / n
    return jnp.maximum(x, 0.0) + 2.0 * z * s


def lane_tile(i):
    return slice(i * 128, (i + 1) * 128)


def block(b):
    return slice(b * BW, (b + 1) * BW)


def main_kernel(
    x_hbm, w_hbm, gb_hbm, lam_hbm, cw_hbm, cb_hbm, cot_hbm,
    gi_hbm, done_hbm,
    gb_ref, lam_ref, cw_ref, cb_ref, xb, cotb, wsh, wf, wu, wpair, W0, W1, xhalo, nat, natc, xs, cs, mb, mt, pre,
    dec, pp, qq, m1, m2, m3, oma, hp, gp, gm, dsend, drecv, sin, ghs, ghr,
    wsend, wz, frecv, brecv, bsum, bz, own, fsum, zrecv, ssend, srecv, ssum, szrecv, fin, done, gib,
    lsem, sib_s, sib_r, c1_s, c1_r, hal_s, hal_r, za_s, za_r, c2_s, c2_r, d_s, d_r, e_s, e_r,
    f_s, f_r, b_s, b_r, fs_s, fs_r, z_s, z_r, g_s, g_r,
):
    ctx = lax.axis_index("ctx")
    d = lax.axis_index("dp")
    div, rem = lax.div, lax.rem
    p, c = div(ctx, 2), rem(ctx, 2)
    z = rem(p, DEPTH)
    y = 2 * div(p, DEPTH) + div(d, 4)
    x = rem(d, 4)
    y_hi, y_odd = div(y, 2), rem(y, 2)
    spot = 4 * y + x
    sibling = {"ctx": 2 * p + 1 - c, "dp": d}

    def chip(j):
        return {"ctx": 2 * j + c, "dp": d}

    def deep(j):
        return {"ctx": 2 * (p - z + j) + c, "dp": d}

    def peer(u):
        return {"ctx": ctx, "dp": u}

    def plane(j):
        to_x, to_y = rem(x + rem(j, 4), 4), rem(y + div(j, 4), 4)
        to_h, to_d = div(to_y, 2), 4 * rem(to_y, 2) + to_x
        return {"ctx": 2 * (DEPTH * to_h + z) + c, "dp": to_d}, to_h, to_d

    def rows16(j):
        return pl.ds(pl.multiple_of(16 * j, 16), 16)

    def send(src, dst, ss, rs, dev):
        cp = pltpu.make_async_remote_copy(
            src_ref=src, dst_ref=dst, send_sem=ss, recv_sem=rs, device_id=dev, device_id_type=MESH
        )
        cp.start()
        return cp

    bar = pltpu.get_barrier_semaphore()
    pl.semaphore_signal(bar, inc=1, device_id=sibling, device_id_type=MESH)

    @pl.loop(1, CHIPS, unroll=True)
    def _(j):
        pl.semaphore_signal(bar, inc=1, device_id=chip(rem(p + j, CHIPS)), device_id_type=MESH)

    @pl.loop(1, PLANE, unroll=True)
    def _(j):
        @pl.when(j != PLANE // 2)
        def _():
            pl.semaphore_signal(bar, inc=1, device_id=plane(j)[0], device_id_type=MESH)

    @pl.loop(1, REPL, unroll=True)
    def _(j):
        dev = {"ctx": 2 * p + 1 - c, "dp": rem(d + j, REPL)}
        pl.semaphore_signal(bar, inc=1, device_id=dev, device_id_type=MESH)

    mine = pl.ds(pl.multiple_of(HALF * c, HALF), HALF)
    theirs = pl.ds(pl.multiple_of(HALF * (1 - c), HALF), HALF)
    my_rows = pl.ds(pl.multiple_of(ROWS * c, ROWS), ROWS)
    sib_rows = pl.ds(pl.multiple_of(ROWS * (1 - c), ROWS), ROWS)

    ld_w = pltpu.make_async_copy(w_hbm, wsh, lsem.at[0])
    ld_w.start()
    ld_x = pltpu.make_async_copy(x_hbm.at[0, :, mine], xb.at[my_rows], lsem.at[1])
    ld_x.start()
    ld_c = pltpu.make_async_copy(cot_hbm.at[0, :, mine], cotb.at[my_rows], lsem.at[2])
    ld_c.start()
    lds = []
    for n, (src, dst) in enumerate(
        ((gb_hbm, gb_ref), (lam_hbm, lam_ref), (cw_hbm, cw_ref), (cb_hbm, cb_ref))
    ):
        lds.append(pltpu.make_async_copy(src.at[:, mine], dst, lsem.at[5 + n]))
        lds[-1].start()
    pending = []

    def later(ref, sem):
        pending.append(lambda: wait_for(ref, sem))


    ld_w.wait()
    for i in range(8):
        for g in range(2):
            v = wsh[i, g].astype(F32)
            for lh in range(2):
                wf[lh, i * 16 + g * 8 : i * 16 + g * 8 + 8, :] = v[:, lane_tile(lh)]
    for h in range(2):
        for u in range(REPL):
            for st in range(STAGES):
                first = ((u // 2) % 2) * 8 + 4 * h + 2 * st + u // 4
                wu[h, st, u] = wf[u % 2, pl.ds(first, 8, stride=16), :]

    pl.semaphore_wait(bar, 1 + (CHIPS - 1) + (PLANE - 2) + (REPL - 1))

    part = pl.ds(pl.multiple_of(8 * c, 8), 8)
    s_w = send(wu.at[1 - c, 1, d], wpair.at[0, part], sib_s.at[0], sib_r.at[0], sibling)
    s_v = send(wu.at[1 - c, 0], wpair.at[pl.ds(1, REPL), part], sib_s.at[5], sib_r.at[5], sibling)
    wpair[0, part, :] = wu[c, 1, d]
    s_w.wait_recv()
    mine_w = W0.at[d, y_hi, rows16(z)]
    mine_w[...] = wpair[0].astype(BF16)

    @pl.loop(1, DEPTH, unroll=True)
    def _(j):
        send(mine_w, mine_w, c1_s, c1_r, deep(rem(z + j, DEPTH)))

    s_x = send(x_hbm.at[0, :, theirs], xb.at[my_rows], sib_s.at[1], sib_r.at[1], sibling)
    s_c = send(cot_hbm.at[0, :, theirs], cotb.at[my_rows], sib_s.at[2], sib_r.at[2], sibling)
    seven = W1.at[0, pl.ds(0, DEPTH - 1)]
    later(seven, c1_s)
    wpair[1:, part, :] = wu[c, 0]
    s_v.wait_recv()
    for u in range(REPL):
        W1[p, u] = wpair[1 + u].astype(BF16)
    across = rem(p + DEPTH, CHIPS)
    rows_a, rows_b = W1.at[p], W1.at[across]
    send(rows_a, rows_a, za_s.at[0], za_r.at[0], chip(across))
    later(rows_a, za_s.at[0])

    def at_depth(side, by):
        return (p - z if side == 0 else across - z) + rem(z + by + DEPTH, DEPTH)

    def near(side):
        rows = W1.at[at_depth(side, 0)]
        for by in (1, -1):
            send(rows, rows, za_s.at[1], za_r.at[1], deep(rem(z + by + DEPTH, DEPTH)))
        for by in (2, -2):
            arrive = za_r.at[2 + 2 * side + (0 if by > 0 else 1)]
            send(rows, rows, za_s.at[1], arrive, deep(rem(z + by + DEPTH, DEPTH)))

    def onward(side):
        for way, by in ((0, 1), (1, -1)):
            rows = W1.at[at_depth(side, -2 * by)]
            wait_for(rows, za_r.at[2 + 2 * side + way])
            send(rows, rows, za_s.at[1], za_r.at[1], deep(rem(z + by + DEPTH, DEPTH)))
            half = W1.at[at_depth(side, -2 * by), pl.ds(4 * way, 4)]
            send(half, half, za_s.at[1], za_r.at[1], deep(rem(z + 2 * by + DEPTH, DEPTH)))

    near(0)

    ld_x.wait()
    s_x.wait_recv()
    send(xb.at[pl.ds(SPAN - 16, 16)], xhalo, hal_s, hal_r, chip(rem(p + 1, CHIPS)))
    later(xhalo, hal_s)
    for k in range(TILES):
        nat[k] = xb[:, lane_tile(k)].astype(F32)

    @pl.loop(0, R)
    def _(r):
        for k in range(TILES):
            xs[3 + r, :, lane_tile(k)] = nat[k, pl.ds(r, 8, stride=R), :]

    wait_for(rows_b, za_r.at[0])

    near(1)
    later(W1.at[pl.ds(0, 14)], za_s.at[1])
    ten = W1.at[pl.ds(0, 10)]
    wait_for(seven, c1_r)
    fifteen = frecv.at[0, pl.ds(0, PLANE - 1)]
    mine_s = W0.at[d, y_hi]

    @pl.loop(1, PLANE, unroll=True)
    def _(j):
        send(mine_s, mine_s, c2_s, c2_r, plane(j)[0])

    later(fifteen, c2_s)
    onward(0)
    onward(1)
    ld_c.wait()
    s_c.wait_recv()
    for k in range(TILES):
        natc[k] = cotb[:, lane_tile(k)].astype(F32)

    @pl.loop(0, R)
    def _(r):
        for k in range(TILES):
            cs[r, :, lane_tile(k)] = natc[k, pl.ds(r, 8, stride=R), :]

    wait_for(xhalo, hal_r)
    hal = xhalo[...].astype(F32)
    hal = jnp.where(p == 0, jnp.zeros_like(hal), hal)
    sub = sublane((8, HALF))
    for k in range(3):
        rolled = pltpu.roll(xs[3 + R - 3 + k], 1, 0)
        xs[k] = jnp.where(sub == 0, jnp.broadcast_to(hal[13 + k : 14 + k], (8, HALF)), rolled)

    for ld in lds:
        ld.wait()
    conv_w = cw_ref[...]
    conv_b = cb_ref[...]
    for b in range(NB):
        taps = [jnp.broadcast_to(conv_w[k : k + 1, block(b)], (8, BW)) for k in range(4)]
        shift = jnp.broadcast_to(conv_b[:, block(b)], (8, BW))

        @pl.loop(0, R // 2)
        def _(i):
            v = [xs[2 * i + k, :, block(b)] for k in range(5)]
            out = []
            for o in range(2):
                m = shift + taps[0] * v[o]
                for k in range(1, 4):
                    m = m + taps[k] * v[o + k]
                out.append(m)
            mb[pl.ds(pl.multiple_of(16 * i, 16), 16), block(b)] = jnp.concatenate(out, 0).astype(BF16)

        mt[b] = mb[:, block(b)].astype(F32).T.astype(BF16)

    lam = lam_ref[...]
    neg8rate = -8.0 * softplus(-lam)
    gate_b = gb_ref[...]
    ends = []

    def weights(b, g):
        u = 4 * (b % 2) + 2 * g
        two = (W1[:, u + lh] if b < 2 else W0[u + lh] for lh in range(2))
        return jnp.concatenate([v.reshape(BW, 128) for v in two], 1)

    def gates(b):
        st = b // 2
        for g in range(2):
            pre[2 * b + g] = jnp.dot(mb[:, block(b)], weights(b, g), preferred_element_type=F32)
        nr = jnp.broadcast_to(neg8rate[:, block(b)], (8, BW))
        ba = jnp.broadcast_to(gate_b[0:1, block(b)], (8, BW))
        bx = jnp.broadcast_to(gate_b[1:2, block(b)], (8, BW))

        def step(i, carry):
            prod, hid, kk, logs = carry
            two = mb[pl.ds(pl.multiple_of(16 * i, 16), 16), block(b)].astype(F32)
            for o in range(2):
                r = 2 * i + o
                at = pl.ds(pl.multiple_of(8 * r, 8), 8)
                ga = sigmoid(pre[2 * b, at, :] + ba)
                gx = sigmoid(pre[2 * b + 1, at, :] + bx)
                m = two[8 * o : 8 * o + 8]
                ld = ga * nr
                a = jnp.exp(ld)
                sq = 1.0 - a * a
                mult = jnp.sqrt(sq)
                gm_ = gx * m
                drive = mult * gm_
                dec[r, :, block(b)] = a
                qq[r, :, block(b)] = gm_ * a * lax.rsqrt(jnp.maximum(sq, 0.05))
                m1[r, :, block(b)] = a * ga
                oma[r, :, block(b)] = (1.0 - ga) * nr
                m2[r, :, block(b)] = drive * (1.0 - gx)
                m3[r, :, block(b)] = mult * gx
                hp[r, :, block(b)] = hid
                pp[r, :, block(b)] = prod
                hid = a * hid + drive
                prod = prod * a
                kk = kk + prod * cs[r, :, block(b)]
                logs = logs + ld
            return prod, hid, kk, logs

        zero = jnp.zeros((8, BW), F32)
        prod, hid, kk, logs = lax.fori_loop(
            0, R // 2, step, (jnp.ones((8, BW), F32), zero, zero, zero), unroll=2
        )
        sb = sublane((8, BW))
        fp, fh = prod, hid
        bp, bk = prod, kk
        for s in (1, 2, 4):
            mp, mh = pltpu.roll(fp, s, 0), pltpu.roll(fh, s, 0)
            fh = jnp.where(sb >= s, fp * mh + fh, fh)
            fp = jnp.where(sb >= s, fp * mp, fp)
            mp, mk = pltpu.roll(bp, 8 - s, 0), pltpu.roll(bk, 8 - s, 0)
            bk = jnp.where(sb < 8 - s, bp * mk + bk, bk)
            bp = jnp.where(sb < 8 - s, bp * mp, bp)
            logs = logs + pltpu.roll(logs, s, 0)
        one = jnp.ones((8, BW), F32)
        ends.append((
            jnp.where(sb == 0, one, pltpu.roll(fp, 1, 0)),
            jnp.where(sb == 0, zero, pltpu.roll(fh, 1, 0)),
            jnp.where(sb == 7, one, pltpu.roll(bp, 7, 0)),
            jnp.where(sb == 7, zero, pltpu.roll(bk, 7, 0)),
        ))
        for lh in range(2):
            k = 2 * (b % 2) + lh
            dsend[st, 0, k : k + 1, :] = logs[0:1, lane_tile(lh)]
            dsend[st, 1, k : k + 1, :] = logs[0:1, lane_tile(lh)]
            dsend[st, 0, 4 + k : 5 + k, :] = fh[7:8, lane_tile(lh)]
            dsend[st, 1, 4 + k : 5 + k, :] = bk[0:1, lane_tile(lh)]

    for st in range(STAGES):
        wait_for(*((ten, za_r.at[1]) if st == 0 else (fifteen, c2_r)))
        for b in (2 * st, 2 * st + 1):
            gates(b)

        @pl.loop(1, CHIPS, unroll=True)
        def _(j):
            to = rem(p + j, CHIPS)
            send(dsend.at[st, jnp.where(to > p, 0, 1)], drecv.at[st, p], d_s.at[st], d_r.at[st], chip(to))

        later(drecv.at[st, pl.ds(0, CHIPS - 1)], d_s.at[st])
        drecv[st, p] = jnp.zeros((8, 128), F32)

    sums = []

    def grads(b):
        st, k = b // 2, 2 * (b % 2)

        def wide(n):
            return jnp.concatenate(
                [jnp.broadcast_to(sin[st, n, k + lh : k + lh + 1, :], (8, 128)) for lh in range(2)], 1
            )

        hin = ends[b][1] + ends[b][0] * wide(0)
        kin = ends[b][3] + ends[b][2] * wide(1)

        def down(n, carry):
            kk, t_sum, a_sum, x_sum = carry
            i = R // 2 - 1 - n
            outs = [[None, None], [None, None]]
            for o in (1, 0):
                r = 2 * i + o
                gr = cs[r, :, block(b)] + kk
                kk = dec[r, :, block(b)] * gr
                before = hp[r, :, block(b)] + pp[r, :, block(b)] * hin
                t = (before - qq[r, :, block(b)]) * m1[r, :, block(b)] * gr
                ga = t * oma[r, :, block(b)]
                gx = gr * m2[r, :, block(b)]
                gm[r, :, block(b)] = gr * m3[r, :, block(b)]
                t_sum, a_sum, x_sum = t_sum + t, a_sum + ga, x_sum + gx
                outs[0][o], outs[1][o] = ga, gx
            at = pl.ds(pl.multiple_of(16 * i, 16), 16)
            gp[2 * b, at, :] = jnp.concatenate(outs[0], 0).astype(BF16)
            gp[2 * b + 1, at, :] = jnp.concatenate(outs[1], 0).astype(BF16)
            return kk, t_sum, a_sum, x_sum

        zero = jnp.zeros((8, BW), F32)
        _, t_sum, a_sum, x_sum = lax.fori_loop(0, R // 2, down, (kin, zero, zero, zero), unroll=4)
        sums.append([t_sum, a_sum, x_sum])
        for g in range(2):
            grad = jnp.dot(mt[b], gp[2 * b + g], preferred_element_type=F32).astype(BF16)
            for lh in range(2):
                for h in range(2):
                    if b == 1:
                        for j in range(DEPTH):
                            wz[j, h, 2 * g + lh] = grad[128 * h + 16 * j : 128 * h + 16 * j + 16, lane_tile(lh)]
                    else:
                        wsend[st, 2 * (k + g) + lh, h] = grad[128 * h : 128 * (h + 1), lane_tile(lh)]

    def through(b):
        nt = (((1,), (1,)), ((), ()))
        back = lax.dot_general(gp[2 * b], weights(b, 0), nt, preferred_element_type=F32)
        back = back + lax.dot_general(gp[2 * b + 1], weights(b, 1), nt, preferred_element_type=F32)
        gm[0:R, :, block(b)] = gm[0:R, :, block(b)] + back.reshape(R, 8, BW)

    sig = 1.0 / (1.0 + jnp.exp(lam))

    def small_sums(b):
        def add(r, carry):
            g = gm[r, :, block(b)]
            return tuple(carry[k] + g * xs[r + k, :, block(b)] for k in range(4)) + (carry[4] + g,)

        zero = jnp.zeros((8, BW), F32)
        acc = lax.fori_loop(0, R, add, (zero,) * 5, unroll=4)
        t_sum, a_sum, x_sum = sums[b]
        t_sum = t_sum * (8.0 * jnp.broadcast_to(sig[:, block(b)], (8, BW)))
        sb = sublane((8, BW))
        rows = zero
        for n, v in enumerate((t_sum, a_sum, x_sum) + tuple(acc)):
            for s in (1, 2, 4):
                v = v + pltpu.roll(v, s, 0)
            rows = jnp.where(sb == n, v, rows)
        for lh in range(2):
            ssend[2 * b + lh] = rows[:, lane_tile(lh)]

    for st in range(STAGES):
        wait_for(drecv.at[st, pl.ds(0, CHIPS - 1)], d_r.at[st])
        state = jnp.zeros((4, 128), F32)
        carry_in = jnp.zeros((4, 128), F32)
        for j in range(CHIPS):
            v = drecv[st, j]
            state = jnp.where(j < p, jnp.exp(v[:4]) * state + v[4:], state)
            v = drecv[st, CHIPS - 1 - j]
            carry_in = jnp.where(CHIPS - 1 - j > p, jnp.exp(v[:4]) * carry_in + v[4:], carry_in)
        sin[st, 0] = state
        sin[st, 1] = carry_in
        def to_plane(low):
            @pl.loop(1, PLANE, unroll=True)
            def _(j):
                dev, to_h, to_d = plane(j)

                @pl.when(to_d < 4 if low else to_d >= 4)
                def _():
                    send(
                        wsend.at[st, to_d, to_h], frecv.at[st, spot], f_s.at[st], f_r.at[st], dev
                    )

        grads(2 * st)
        to_plane(True)
        grads(2 * st + 1)
        if st == 0:
            @pl.when(y_odd == 0)
            def _():
                frecv[0, spot] = wsend[0, d, y_hi]

            @pl.loop(1, DEPTH, unroll=True)
            def _(j):
                to = rem(z + j, DEPTH)
                send(wz.at[to], brecv.at[z], b_s.at[0], b_r.at[0], deep(to))

            later(brecv.at[pl.ds(0, DEPTH - 1)], b_s.at[0])
            brecv[z] = wz[z]
        else:
            to_plane(False)
            later(fifteen, f_s.at[1])
            frecv[1, spot] = wsend[1, d, y_hi]
        for b in (2 * st, 2 * st + 1):
            through(b)
            small_sums(b)

    @pl.loop(1, PLANE, unroll=True)
    def _(j):
        dev, _, to_d = plane(j)
        send(ssend.at[to_d], srecv.at[spot], fs_s.at[0], fs_r.at[0], dev)

    later(srecv.at[pl.ds(0, PLANE - 1)], fs_s.at[0])
    for k in range(3):
        ghs[k : k + 1, :] = gm[k, 0:1, :]
    send(ghs, ghr, e_s, e_r, chip(rem(p + CHIPS - 1, CHIPS)))
    later(ghr, e_s)
    srecv[spot] = ssend[d]

    def fold(st):
        wait_for(fifteen, f_r.at[st])

        @pl.loop(0, DEPTH)
        def _(i):
            at = rows16(i)
            v = frecv[st, 0, at, :].astype(F32)
            for u in range(1, PLANE):
                v = v + frecv[st, u, at, :].astype(F32)
            fsum[st, i] = v.astype(BF16)

        @pl.loop(1, DEPTH, unroll=True)
        def _(j):
            to = rem(z + j, DEPTH)
            send(fsum.at[st, to], zrecv.at[st, z], z_s.at[st], z_r.at[st], deep(to))

        zrecv[st, z] = fsum[st, z]

    pl.when(y_odd == 0)(lambda: fold(0))
    wait_for(ghr, e_r)
    halo = ghr[...]
    halo = jnp.where(p == CHIPS - 1, jnp.zeros_like(halo), halo)
    for k in range(3):
        rolled = pltpu.roll(gm[k], 7, 0)
        gm[R + k] = jnp.where(sub == 7, jnp.broadcast_to(halo[k : k + 1], (8, HALF)), rolled)

    for b in range(NB):
        taps = [jnp.broadcast_to(conv_w[k : k + 1, block(b)], (8, BW)) for k in range(4)]

        @pl.loop(0, R)
        def _(r):
            v = taps[0] * gm[r + 3, :, block(b)]
            for k in range(1, 4):
                v = v + taps[k] * gm[r + 3 - k, :, block(b)]
            for lh in range(2):
                nat[2 * b + lh, pl.ds(r, 8, stride=R), :] = v[:, lane_tile(lh)]

    for k in range(TILES):
        gib[:, lane_tile(k)] = nat[k].astype(BF16)
    s_g = send(gib.at[sib_rows], gi_hbm.at[:, mine], sib_s.at[3], sib_r.at[3], sibling)
    st_g = pltpu.make_async_copy(gib.at[my_rows], gi_hbm.at[:, mine], lsem.at[3])
    st_g.start()
    later(gib.at[my_rows], lsem.at[3])
    wait_for(brecv.at[pl.ds(0, DEPTH - 1)], b_r.at[0])
    for h in range(2):
        for t in range(4):
            v = brecv[0, h, t].astype(F32)
            for j in range(1, DEPTH):
                v = v + brecv[j, h, t].astype(F32)
            bsum[h, t] = v.astype(BF16)

    @pl.loop(1, PLANE, unroll=True)
    def _(j):
        dev, to_h, to_d = plane(j)

        @pl.when(to_d >= 4)
        def _():
            send(bsum.at[to_h, rem(to_d, 4)], bz.at[spot], b_s.at[1], b_r.at[1], dev)

    @pl.when(y_odd == 1)
    def _():
        bz[spot] = bsum[y_hi, x]

    fold(1)
    wait_for(srecv.at[pl.ds(0, PLANE - 1)], fs_r.at[0])
    ssum[...] = jnp.sum(srecv[...], 0)

    @pl.loop(1, DEPTH, unroll=True)
    def _(j):
        send(ssum, szrecv.at[z], fs_s.at[1], fs_r.at[1], deep(rem(z + j, DEPTH)))

    later(szrecv.at[pl.ds(0, DEPTH - 1)], fs_s.at[1])
    szrecv[z] = ssum[...]

    later(zrecv.at[1, pl.ds(0, DEPTH - 1)], z_s.at[1])

    @pl.when(y_odd == 0)
    def _():
        wait_for(zrecv.at[0, pl.ds(0, DEPTH - 1)], z_s.at[0])
        wait_for(zrecv.at[0, pl.ds(0, DEPTH - 1)], z_r.at[0])
        wait_for(frecv.at[0, pl.ds(0, 7)], f_s.at[0])
        wait_for(bz.at[pl.ds(0, 8)], b_s.at[1])

    @pl.when(y_odd == 1)
    def _():
        wait_for(bz.at[pl.ds(0, PLANE - 1)], b_r.at[1])
        wait_for(frecv.at[0, pl.ds(0, 8)], f_s.at[0])
        wait_for(bz.at[pl.ds(0, 7)], b_s.at[1])


    def total(st, parts, count):
        whole = parts(0).astype(F32)
        for j in range(1, count):
            whole = whole + parts(j).astype(F32)
        own[st] = whole

    pl.when(y_odd == 0)(lambda: total(0, lambda j: zrecv[0, j], DEPTH))
    pl.when(y_odd == 1)(lambda: total(0, lambda j: bz[j], PLANE))
    wait_for(szrecv.at[pl.ds(0, DEPTH - 1)], fs_r.at[1])
    fin[...] = jnp.sum(szrecv[...], 0)
    wait_for(zrecv.at[1, pl.ds(0, DEPTH - 1)], z_r.at[1])
    total(1, lambda j: zrecv[1, j], DEPTH)
    for core in range(2):
        for st in range(STAGES):
            done[core, st] = own[st, 8 * core : 8 * core + 8, :]
        done[core, STAGES] = fin[...]
    keep = pltpu.make_async_copy(done.at[c], done_hbm.at[c, d], lsem.at[9])
    keep.start()

    @pl.loop(1, 2 * REPL, unroll=True)
    def _(j):
        to_c = rem(c + div(j, REPL), 2)
        dev = {"ctx": 2 * p + to_c, "dp": rem(d + j, REPL)}
        send(done.at[to_c], done_hbm.at[c, d], g_s, g_r, dev)

    triples = frecv.at[0, pl.ds(0, 2 * REPL - 1), pl.ds(0, 48)]
    later(triples, g_s)
    later(triples, g_r)
    for cp in [s_w, s_v, s_x, s_c, s_g]:
        cp.wait_send()
    s_g.wait_recv()
    for finish_one in pending:
        finish_one()
    keep.wait()


def last_kernel(
    gi_in, done_in, gi_out, gw_out, dec_out, bias_out, taps_out, shift_out,
    done, gws, gw, dec, bias, taps, shift, via, l_sem, s_sem,
):
    get = pltpu.make_async_copy(done_in, done, l_sem.at[4])
    get.start()
    parts = [pl.ds(k * (ROWS // 4), ROWS // 4) for k in range(4)]
    loads = [pltpu.make_async_copy(gi_in.at[at], via.at[at], l_sem.at[k]) for k, at in enumerate(parts)]
    stores = [pltpu.make_async_copy(via.at[at], gi_out.at[0, at], s_sem.at[k]) for k, at in enumerate(parts)]
    for cp in loads:
        cp.start()
    get.wait()
    for h in range(2):
        for u in range(8):
            at = slice(h * HALF + 128 * u, h * HALF + 128 * (u + 1))
            v = done[h, u, STAGES]
            dec[:, at] = v[0:1]
            bias[:, at] = v[1:3]
            taps[:, at] = v[3:7]
            shift[:, at] = v[7:8]
            for st in range(STAGES):
                first = ((u // 2) % 2) * 8 + 4 * h + 2 * st + u // 4
                gws[u % 2, pl.ds(first, 8, stride=16), :] = done[h, u, st]
    for n, (src, dst) in enumerate(((dec, dec_out), (bias, bias_out), (taps, taps_out), (shift, shift_out))):
        stores.append(pltpu.make_async_copy(src, dst, s_sem.at[4 + n]))
        stores[-1].start()
    for k in range(4):
        loads[k].wait()
        stores[k].start()
    for i in range(8):
        for g in range(2):
            for lh in range(2):
                gw[i, g, :, lane_tile(lh)] = gws[lh, i * 16 + g * 8 : i * 16 + g * 8 + 8, :]
    stores.append(pltpu.make_async_copy(gw, gw_out, s_sem.at[8]))
    stores[-1].start()
    for cp in stores:
        cp.wait()


def per_device(inputs, gate_weight, gate_bias, decay_param, conv_weight, conv_bias, cotangent):
    hbm = pl.BlockSpec(memory_space=pltpu.HBM)
    dma = pltpu.SemaphoreType.DMA
    big = pltpu.VMEM((R, 8, HALF), F32)
    gi, done = pl.pallas_call(
        main_kernel,
        name="main",
        out_shape=(
            jax.ShapeDtypeStruct((ROWS, WIDTH), BF16),
            jax.ShapeDtypeStruct((2, REPL, STAGES + 1, 8, 128), F32),
        ),
        in_specs=[hbm] * 7,
        out_specs=(hbm,) * 2,
        scratch_shapes=[
            pltpu.VMEM((2, HALF), F32),
            pltpu.VMEM((1, HALF), F32),
            pltpu.VMEM((4, HALF), F32),
            pltpu.VMEM((1, HALF), F32),
            pltpu.VMEM((SPAN, HALF), BF16),
            pltpu.VMEM((SPAN, HALF), BF16),
            pltpu.VMEM((8, 2, 8, BW), BF16),
            pltpu.VMEM((2, 128, 128), F32),
            pltpu.VMEM((2, STAGES, REPL, 8, 128), F32),
            pltpu.VMEM((1 + REPL, 16, 128), F32),
            pltpu.VMEM((REPL, 2, 128, 128), BF16),
            pltpu.VMEM((CHIPS, REPL, 16, 128), BF16),
            pltpu.VMEM((16, HALF), BF16),
            pltpu.VMEM((TILES, SPAN, 128), F32),
            pltpu.VMEM((TILES, SPAN, 128), F32),
            pltpu.VMEM((R + 3, 8, HALF), F32),
            big,
            pltpu.VMEM((SPAN, HALF), BF16),
            pltpu.VMEM((NB, BW, SPAN), BF16),
            pltpu.VMEM((8, SPAN, BW), F32),
            big, big, big, big, big, big, big, big,
            pltpu.VMEM((8, SPAN, BW), BF16),
            pltpu.VMEM((R + 3, 8, HALF), F32),
            pltpu.VMEM((STAGES, 2, 8, 128), F32),
            pltpu.VMEM((STAGES, CHIPS, 8, 128), F32),
            pltpu.VMEM((STAGES, 2, 4, 128), F32),
            pltpu.VMEM((8, HALF), F32),
            pltpu.VMEM((8, HALF), F32),
            pltpu.VMEM((STAGES, REPL, 2, 128, 128), BF16),
            pltpu.VMEM((DEPTH, 2, 4, 16, 128), BF16),
            pltpu.VMEM((STAGES, PLANE, 128, 128), BF16),
            pltpu.VMEM((DEPTH, 2, 4, 16, 128), BF16),
            pltpu.VMEM((2, 4, 16, 128), BF16),
            pltpu.VMEM((PLANE, 16, 128), BF16),
            pltpu.VMEM((STAGES, 16, 128), F32),
            pltpu.VMEM((STAGES, DEPTH, 16, 128), BF16),
            pltpu.VMEM((STAGES, DEPTH, 16, 128), BF16),
            pltpu.VMEM((8, 8, 128), F32),
            pltpu.VMEM((PLANE, 8, 128), F32),
            pltpu.VMEM((8, 128), F32),
            pltpu.VMEM((DEPTH, 8, 128), F32),
            pltpu.VMEM((8, 128), F32),
            pltpu.VMEM((2, STAGES + 1, 8, 128), F32),
            pltpu.VMEM((SPAN, HALF), BF16),
            dma((10,)), dma((7,)), dma((7,)),
            dma, dma, dma, dma, dma((2,)), dma((6,)), dma, dma,
            dma((STAGES,)), dma((STAGES,)), dma, dma, dma((STAGES,)), dma((STAGES,)),
            dma((2,)), dma((2,)), dma((2,)), dma((2,)),
            dma((STAGES,)), dma((STAGES,)), dma, dma,
        ],
        compiler_params=pltpu.CompilerParams(
            collective_id=0, has_side_effects=True, vmem_limit_bytes=60 * 2**20
        ),
    )(
        inputs, gate_weight, gate_bias, decay_param.reshape(1, WIDTH), conv_weight,
        conv_bias.reshape(1, WIDTH), cotangent,
    )
    gi, gw, dec, bias, taps, shift = pl.pallas_call(
        last_kernel,
        name="last",
        out_shape=(
            jax.ShapeDtypeStruct((1, ROWS, WIDTH), BF16),
            jax.ShapeDtypeStruct((8, 2, 8, BW), F32),
            jax.ShapeDtypeStruct((1, WIDTH), F32),
            jax.ShapeDtypeStruct((2, WIDTH), F32),
            jax.ShapeDtypeStruct((4, WIDTH), F32),
            jax.ShapeDtypeStruct((1, WIDTH), F32),
        ),
        in_specs=[hbm] * 2,
        out_specs=(hbm,) * 6,
        scratch_shapes=[
            pltpu.VMEM((2, REPL, STAGES + 1, 8, 128), F32),
            pltpu.VMEM((2, 128, 128), F32),
            pltpu.VMEM((8, 2, 8, BW), F32),
            pltpu.VMEM((1, WIDTH), F32),
            pltpu.VMEM((2, WIDTH), F32),
            pltpu.VMEM((4, WIDTH), F32),
            pltpu.VMEM((1, WIDTH), F32),
            pltpu.VMEM((ROWS, WIDTH), BF16),
            dma((5,)),
            dma((9,)),
        ],
        compiler_params=pltpu.CompilerParams(vmem_limit_bytes=60 * 2**20),
    )(gi, done)
    return gi, gw, dec.reshape(WIDTH), bias, taps, shift.reshape(WIDTH)


def solution(mesh):
    placed = (
        P("dp", "ctx", None),
        P("ctx", None, None, None),
        P(),
        P(),
        P(),
        P(),
        P("dp", "ctx", None),
    )
    return jax.shard_map(
        per_device,
        mesh=mesh,
        in_specs=placed,
        out_specs=(P("dp", "ctx", None), P("ctx", None, None, None), P(), P(), P(), P()),
        check_vma=False,
    )
```

```python
import jax
import jax.numpy as jnp
from jax import lax
from jax.experimental import pallas as pl
from jax.experimental.pallas import tpu as pltpu
from jax.sharding import PartitionSpec as P

MESH = pl.DeviceIdType.MESH
F32 = jnp.float32
BF16 = jnp.bfloat16
CHIPS = 16
PLANE = 16
DEPTH = 8
REPL = 8
ROWS = 128
SPAN = 256
WIDTH = 2048
HALF = 1024
BW = 256
NB = HALF // BW
R = SPAN // 8
TILES = HALF // 128
STAGES = 2


def wait_for(ref, sem):
    pltpu.make_async_copy(ref, ref, sem).wait()


def sublane(shape):
    return lax.broadcasted_iota(jnp.int32, shape, 0)


def sigmoid(x):
    return 0.5 * jnp.tanh(0.5 * x) + 0.5


def softplus(x):
    e = jnp.exp(-jnp.abs(x))
    z = e / (2.0 + e)
    z2 = z * z
    s = jnp.full_like(z, 1.0 / 17.0)
    for n in (15, 13, 11, 9, 7, 5, 3, 1):
        s = s * z2 + 1.0 / n
    return jnp.maximum(x, 0.0) + 2.0 * z * s


def lane_tile(i):
    return slice(i * 128, (i + 1) * 128)


def block(b):
    return slice(b * BW, (b + 1) * BW)


def main_kernel(
    x_hbm, w_hbm, gb_hbm, lam_hbm, cw_hbm, cb_hbm, cot_hbm,
    gi_hbm, done_hbm,
    gb_ref, lam_ref, cw_ref, cb_ref, xb, cotb, wsh, wf, wu, column, wpair, W0, W1, xhalo, nat, natc, xs, cs, mb, mt, pre,
    dec, pp, qq, m1, m2, m3, oma, hp, gp, gm, dsend, drecv, sin, ghs, ghr,
    wsend, wz, frecv, brecv, bsum, bz, own, fsum, zrecv, ssend, srecv, ssum, szrecv, fin, done, gib,
    lsem, sib_s, sib_r, c1_s, c1_r, hal_s, hal_r, za_s, za_r, c2_s, c2_r, d_s, d_r, e_s, e_r,
    f_s, f_r, b_s, b_r, fs_s, fs_r, z_s, z_r, g_s, g_r,
):
    ctx = lax.axis_index("ctx")
    d = lax.axis_index("dp")
    div, rem = lax.div, lax.rem
    p, c = div(ctx, 2), rem(ctx, 2)
    z = rem(p, DEPTH)
    y = 2 * div(p, DEPTH) + div(d, 4)
    x = rem(d, 4)
    y_hi, y_odd = div(y, 2), rem(y, 2)
    spot = 4 * y + x
    sibling = {"ctx": 2 * p + 1 - c, "dp": d}

    def chip(j):
        return {"ctx": 2 * j + c, "dp": d}

    def deep(j):
        return {"ctx": 2 * (p - z + j) + c, "dp": d}

    def peer(u):
        return {"ctx": ctx, "dp": u}

    def plane(j):
        to_x, to_y = rem(x + rem(j, 4), 4), rem(y + div(j, 4), 4)
        to_h, to_d = div(to_y, 2), 4 * rem(to_y, 2) + to_x
        return {"ctx": 2 * (DEPTH * to_h + z) + c, "dp": to_d}, to_h, to_d

    def rows16(j):
        return pl.ds(pl.multiple_of(16 * j, 16), 16)

    def send(src, dst, ss, rs, dev):
        cp = pltpu.make_async_remote_copy(
            src_ref=src, dst_ref=dst, send_sem=ss, recv_sem=rs, device_id=dev, device_id_type=MESH
        )
        cp.start()
        return cp

    bar = pltpu.get_barrier_semaphore()
    pl.semaphore_signal(bar, inc=1, device_id=sibling, device_id_type=MESH)

    @pl.loop(1, CHIPS, unroll=True)
    def _(j):
        pl.semaphore_signal(bar, inc=1, device_id=chip(rem(p + j, CHIPS)), device_id_type=MESH)

    @pl.loop(1, PLANE, unroll=True)
    def _(j):
        @pl.when(j != PLANE // 2)
        def _():
            pl.semaphore_signal(bar, inc=1, device_id=plane(j)[0], device_id_type=MESH)

    @pl.loop(1, REPL, unroll=True)
    def _(j):
        dev = {"ctx": 2 * p + 1 - c, "dp": rem(d + j, REPL)}
        pl.semaphore_signal(bar, inc=1, device_id=dev, device_id_type=MESH)

    @pl.loop(1, DEPTH, unroll=True)
    def _(j):
        dev = {"ctx": 2 * (p - z + rem(z + j, DEPTH)) + 1 - c, "dp": d}
        pl.semaphore_signal(bar, inc=1, device_id=dev, device_id_type=MESH)

    mine = pl.ds(pl.multiple_of(HALF * c, HALF), HALF)
    theirs = pl.ds(pl.multiple_of(HALF * (1 - c), HALF), HALF)
    my_rows = pl.ds(pl.multiple_of(ROWS * c, ROWS), ROWS)
    sib_rows = pl.ds(pl.multiple_of(ROWS * (1 - c), ROWS), ROWS)

    ld_w = pltpu.make_async_copy(w_hbm, wsh, lsem.at[0])
    ld_w.start()
    ld_x = pltpu.make_async_copy(x_hbm.at[0, :, mine], xb.at[my_rows], lsem.at[1])
    ld_x.start()
    ld_c = pltpu.make_async_copy(cot_hbm.at[0, :, mine], cotb.at[my_rows], lsem.at[2])
    ld_c.start()
    lds = []
    for n, (src, dst) in enumerate(
        ((gb_hbm, gb_ref), (lam_hbm, lam_ref), (cw_hbm, cw_ref), (cb_hbm, cb_ref))
    ):
        lds.append(pltpu.make_async_copy(src.at[:, mine], dst, lsem.at[5 + n]))
        lds[-1].start()
    pending = []

    def later(ref, sem):
        pending.append(lambda: wait_for(ref, sem))


    ld_w.wait()
    for i in range(8):
        for g in range(2):
            v = wsh[i, g].astype(F32)
            for lh in range(2):
                wf[lh, i * 16 + g * 8 : i * 16 + g * 8 + 8, :] = v[:, lane_tile(lh)]
    for h in range(2):
        for u in range(REPL):
            for st in range(STAGES):
                first = ((u // 2) % 2) * 8 + 4 * h + 2 * st + u // 4
                wu[h, st, u] = wf[u % 2, pl.ds(first, 8, stride=16), :]

    pl.semaphore_wait(bar, 1 + (CHIPS - 1) + (PLANE - 2) + (REPL - 1) + (DEPTH - 1))

    part = pl.ds(pl.multiple_of(8 * c, 8), 8)
    @pl.loop(1, 2 * DEPTH, unroll=True)
    def _(j):
        to_c, to_z = rem(c + div(j, DEPTH), 2), rem(z + j, DEPTH)
        dev = {"ctx": 2 * (p - z + to_z) + to_c, "dp": d}
        send(wu.at[to_c, 1, d], column.at[z, c], c1_s, c1_r, dev)

    column[z, c] = wu[c, 1, d]
    s_v = send(wu.at[1 - c, 0], wpair.at[:, part], sib_s.at[5], sib_r.at[5], sibling)
    s_x = send(x_hbm.at[0, :, theirs], xb.at[my_rows], sib_s.at[1], sib_r.at[1], sibling)
    s_c = send(cot_hbm.at[0, :, theirs], cotb.at[my_rows], sib_s.at[2], sib_r.at[2], sibling)
    others = srecv.at[pl.ds(0, 2 * DEPTH - 1)]
    later(others, c1_s)
    wpair[:, part, :] = wu[c, 0]
    s_v.wait_recv()
    for u in range(REPL):
        W1[p, u] = wpair[u].astype(BF16)
    across = rem(p + DEPTH, CHIPS)
    rows_a, rows_b = W1.at[p], W1.at[across]
    send(rows_a, rows_a, za_s.at[0], za_r.at[0], chip(across))
    later(rows_a, za_s.at[0])

    def at_depth(side, by):
        return (p - z if side == 0 else across - z) + rem(z + by + DEPTH, DEPTH)

    def near(side):
        rows = W1.at[at_depth(side, 0)]
        for by in (1, -1):
            send(rows, rows, za_s.at[1], za_r.at[1], deep(rem(z + by + DEPTH, DEPTH)))
        for by in (2, -2):
            arrive = za_r.at[2 + 2 * side + (0 if by > 0 else 1)]
            send(rows, rows, za_s.at[1], arrive, deep(rem(z + by + DEPTH, DEPTH)))

    def onward(side):
        for way, by in ((0, 1), (1, -1)):
            rows = W1.at[at_depth(side, -2 * by)]
            wait_for(rows, za_r.at[2 + 2 * side + way])
            send(rows, rows, za_s.at[1], za_r.at[1], deep(rem(z + by + DEPTH, DEPTH)))
            half = W1.at[at_depth(side, -2 * by), pl.ds(4 * way, 4)]
            send(half, half, za_s.at[1], za_r.at[1], deep(rem(z + 2 * by + DEPTH, DEPTH)))

    near(0)

    ld_x.wait()
    s_x.wait_recv()
    send(xb.at[pl.ds(SPAN - 16, 16)], xhalo, hal_s, hal_r, chip(rem(p + 1, CHIPS)))
    later(xhalo, hal_s)
    for k in range(TILES):
        nat[k] = xb[:, lane_tile(k)].astype(F32)

    @pl.loop(0, R, unroll=2)
    def _(r):
        for k in range(TILES):
            xs[3 + r, :, lane_tile(k)] = nat[k, pl.ds(r, 8, stride=R), :]

    wait_for(rows_b, za_r.at[0])

    near(1)
    later(W1.at[pl.ds(0, 14)], za_s.at[1])
    ten = W1.at[pl.ds(0, 10)]
    wait_for(others, c1_r)
    W0[d, y_hi] = column[...].reshape(128, 128).astype(BF16)
    fifteen = frecv.at[0, pl.ds(0, PLANE - 1)]
    mine_s = W0.at[d, y_hi]

    @pl.loop(1, PLANE, unroll=True)
    def _(j):
        send(mine_s, mine_s, c2_s, c2_r, plane(j)[0])

    later(fifteen, c2_s)
    onward(0)
    onward(1)
    ld_c.wait()
    s_c.wait_recv()
    for k in range(TILES):
        natc[k] = cotb[:, lane_tile(k)].astype(F32)

    @pl.loop(0, R, unroll=2)
    def _(r):
        for k in range(TILES):
            cs[r, :, lane_tile(k)] = natc[k, pl.ds(r, 8, stride=R), :]

    wait_for(xhalo, hal_r)
    hal = xhalo[...].astype(F32)
    hal = jnp.where(p == 0, jnp.zeros_like(hal), hal)
    sub = sublane((8, HALF))
    for k in range(3):
        rolled = pltpu.roll(xs[3 + R - 3 + k], 1, 0)
        xs[k] = jnp.where(sub == 0, jnp.broadcast_to(hal[13 + k : 14 + k], (8, HALF)), rolled)

    for ld in lds:
        ld.wait()
    conv_w = cw_ref[...]
    conv_b = cb_ref[...]
    for b in range(NB):
        taps = [jnp.broadcast_to(conv_w[k : k + 1, block(b)], (8, BW)) for k in range(4)]
        shift = jnp.broadcast_to(conv_b[:, block(b)], (8, BW))

        @pl.loop(0, R // 2, unroll=2)
        def _(i):
            v = [xs[2 * i + k, :, block(b)] for k in range(5)]
            out = []
            for o in range(2):
                m = shift + taps[0] * v[o]
                for k in range(1, 4):
                    m = m + taps[k] * v[o + k]
                out.append(m)
            mb[pl.ds(pl.multiple_of(16 * i, 16), 16), block(b)] = jnp.concatenate(out, 0).astype(BF16)

        mt[b] = mb[:, block(b)].astype(F32).T.astype(BF16)

    lam = lam_ref[...]
    neg8rate = -8.0 * softplus(-lam)
    gate_b = gb_ref[...]
    ends = []

    def weights(b, g):
        u = 4 * (b % 2) + 2 * g
        two = (W1[:, u + lh] if b < 2 else W0[u + lh] for lh in range(2))
        return jnp.concatenate([v.reshape(BW, 128) for v in two], 1)

    def gates(b):
        st = b // 2
        for g in range(2):
            pre[2 * b + g] = jnp.dot(mb[:, block(b)], weights(b, g), preferred_element_type=F32)
        nr = jnp.broadcast_to(neg8rate[:, block(b)], (8, BW))
        ba = jnp.broadcast_to(gate_b[0:1, block(b)], (8, BW))
        bx = jnp.broadcast_to(gate_b[1:2, block(b)], (8, BW))

        def step(i, carry):
            prod, hid, kk, logs = carry
            two = mb[pl.ds(pl.multiple_of(16 * i, 16), 16), block(b)].astype(F32)
            for o in range(2):
                r = 2 * i + o
                at = pl.ds(pl.multiple_of(8 * r, 8), 8)
                ga = sigmoid(pre[2 * b, at, :] + ba)
                gx = sigmoid(pre[2 * b + 1, at, :] + bx)
                m = two[8 * o : 8 * o + 8]
                ld = ga * nr
                a = jnp.exp(ld)
                sq = 1.0 - a * a
                mult = jnp.sqrt(sq)
                gm_ = gx * m
                drive = mult * gm_
                dec[r, :, block(b)] = a
                qq[r, :, block(b)] = gm_ * a * lax.rsqrt(jnp.maximum(sq, 0.05))
                m1[r, :, block(b)] = a * ga
                oma[r, :, block(b)] = (1.0 - ga) * nr
                m2[r, :, block(b)] = drive * (1.0 - gx)
                m3[r, :, block(b)] = mult * gx
                hp[r, :, block(b)] = hid
                pp[r, :, block(b)] = prod
                hid = a * hid + drive
                prod = prod * a
                kk = kk + prod * cs[r, :, block(b)]
                logs = logs + ld
            return prod, hid, kk, logs

        zero = jnp.zeros((8, BW), F32)
        prod, hid, kk, logs = lax.fori_loop(
            0, R // 2, step, (jnp.ones((8, BW), F32), zero, zero, zero), unroll=2
        )
        sb = sublane((8, BW))
        fp, fh = prod, hid
        bp, bk = prod, kk
        for s in (1, 2, 4):
            mp, mh = pltpu.roll(fp, s, 0), pltpu.roll(fh, s, 0)
            fh = jnp.where(sb >= s, fp * mh + fh, fh)
            fp = jnp.where(sb >= s, fp * mp, fp)
            mp, mk = pltpu.roll(bp, 8 - s, 0), pltpu.roll(bk, 8 - s, 0)
            bk = jnp.where(sb < 8 - s, bp * mk + bk, bk)
            bp = jnp.where(sb < 8 - s, bp * mp, bp)
            logs = logs + pltpu.roll(logs, s, 0)
        one = jnp.ones((8, BW), F32)
        ends.append((
            jnp.where(sb == 0, one, pltpu.roll(fp, 1, 0)),
            jnp.where(sb == 0, zero, pltpu.roll(fh, 1, 0)),
            jnp.where(sb == 7, one, pltpu.roll(bp, 7, 0)),
            jnp.where(sb == 7, zero, pltpu.roll(bk, 7, 0)),
        ))
        for lh in range(2):
            k = 2 * (b % 2) + lh
            dsend[st, 0, k : k + 1, :] = logs[0:1, lane_tile(lh)]
            dsend[st, 1, k : k + 1, :] = logs[0:1, lane_tile(lh)]
            dsend[st, 0, 4 + k : 5 + k, :] = fh[7:8, lane_tile(lh)]
            dsend[st, 1, 4 + k : 5 + k, :] = bk[0:1, lane_tile(lh)]

    for st in range(STAGES):
        wait_for(*((ten, za_r.at[1]) if st == 0 else (fifteen, c2_r)))
        for b in (2 * st, 2 * st + 1):
            gates(b)

        @pl.loop(1, CHIPS, unroll=True)
        def _(j):
            to = rem(p + j, CHIPS)
            send(dsend.at[st, jnp.where(to > p, 0, 1)], drecv.at[st, p], d_s.at[st], d_r.at[st], chip(to))

        later(drecv.at[st, pl.ds(0, CHIPS - 1)], d_s.at[st])
        drecv[st, p] = jnp.zeros((8, 128), F32)

    sums = []

    def grads(b):
        st, k = b // 2, 2 * (b % 2)

        def wide(n):
            return jnp.concatenate(
                [jnp.broadcast_to(sin[st, n, k + lh : k + lh + 1, :], (8, 128)) for lh in range(2)], 1
            )

        hin = ends[b][1] + ends[b][0] * wide(0)
        kin = ends[b][3] + ends[b][2] * wide(1)

        def down(n, carry):
            kk, t_sum, a_sum, x_sum = carry
            i = R // 2 - 1 - n
            outs = [[None, None], [None, None]]
            for o in (1, 0):
                r = 2 * i + o
                gr = cs[r, :, block(b)] + kk
                kk = dec[r, :, block(b)] * gr
                before = hp[r, :, block(b)] + pp[r, :, block(b)] * hin
                t = (before - qq[r, :, block(b)]) * m1[r, :, block(b)] * gr
                ga = t * oma[r, :, block(b)]
                gx = gr * m2[r, :, block(b)]
                gm[r, :, block(b)] = gr * m3[r, :, block(b)]
                t_sum, a_sum, x_sum = t_sum + t, a_sum + ga, x_sum + gx
                outs[0][o], outs[1][o] = ga, gx
            at = pl.ds(pl.multiple_of(16 * i, 16), 16)
            gp[2 * b, at, :] = jnp.concatenate(outs[0], 0).astype(BF16)
            gp[2 * b + 1, at, :] = jnp.concatenate(outs[1], 0).astype(BF16)
            return kk, t_sum, a_sum, x_sum

        zero = jnp.zeros((8, BW), F32)
        _, t_sum, a_sum, x_sum = lax.fori_loop(0, R // 2, down, (kin, zero, zero, zero), unroll=4)
        sums.append([t_sum, a_sum, x_sum])
        for g in range(2):
            grad = jnp.dot(mt[b], gp[2 * b + g], preferred_element_type=F32).astype(BF16)
            for lh in range(2):
                for h in range(2):
                    if b == 1:
                        for j in range(DEPTH):
                            wz[j, h, 2 * g + lh] = grad[128 * h + 16 * j : 128 * h + 16 * j + 16, lane_tile(lh)]
                    else:
                        wsend[st, 2 * (k + g) + lh, h] = grad[128 * h : 128 * (h + 1), lane_tile(lh)]

    def through(b):
        nt = (((1,), (1,)), ((), ()))
        back = lax.dot_general(gp[2 * b], weights(b, 0), nt, preferred_element_type=F32)
        back = back + lax.dot_general(gp[2 * b + 1], weights(b, 1), nt, preferred_element_type=F32)
        gm[0:R, :, block(b)] = gm[0:R, :, block(b)] + back.reshape(R, 8, BW)

    sig = 1.0 / (1.0 + jnp.exp(lam))

    def small_sums(b):
        def add(r, carry):
            g = gm[r, :, block(b)]
            return tuple(carry[k] + g * xs[r + k, :, block(b)] for k in range(4)) + (carry[4] + g,)

        zero = jnp.zeros((8, BW), F32)
        acc = lax.fori_loop(0, R, add, (zero,) * 5, unroll=4)
        t_sum, a_sum, x_sum = sums[b]
        t_sum = t_sum * (8.0 * jnp.broadcast_to(sig[:, block(b)], (8, BW)))
        sb = sublane((8, BW))
        rows = zero
        for n, v in enumerate((t_sum, a_sum, x_sum) + tuple(acc)):
            for s in (1, 2, 4):
                v = v + pltpu.roll(v, s, 0)
            rows = jnp.where(sb == n, v, rows)
        for lh in range(2):
            ssend[2 * b + lh] = rows[:, lane_tile(lh)]

    for st in range(STAGES):
        wait_for(drecv.at[st, pl.ds(0, CHIPS - 1)], d_r.at[st])
        state = jnp.zeros((4, 128), F32)
        carry_in = jnp.zeros((4, 128), F32)
        for j in range(CHIPS):
            v = drecv[st, j]
            state = jnp.where(j < p, jnp.exp(v[:4]) * state + v[4:], state)
            v = drecv[st, CHIPS - 1 - j]
            carry_in = jnp.where(CHIPS - 1 - j > p, jnp.exp(v[:4]) * carry_in + v[4:], carry_in)
        sin[st, 0] = state
        sin[st, 1] = carry_in
        def to_plane(low):
            @pl.loop(1, PLANE, unroll=True)
            def _(j):
                dev, to_h, to_d = plane(j)

                @pl.when(to_d < 4 if low else to_d >= 4)
                def _():
                    send(
                        wsend.at[st, to_d, to_h], frecv.at[st, spot], f_s.at[st], f_r.at[st], dev
                    )

        grads(2 * st)
        to_plane(True)
        grads(2 * st + 1)
        if st == 0:
            @pl.when(y_odd == 0)
            def _():
                frecv[0, spot] = wsend[0, d, y_hi]

            @pl.loop(1, DEPTH, unroll=True)
            def _(j):
                to = rem(z + j, DEPTH)
                send(wz.at[to], brecv.at[z], b_s.at[0], b_r.at[0], deep(to))

            later(brecv.at[pl.ds(0, DEPTH - 1)], b_s.at[0])
            brecv[z] = wz[z]
        else:
            to_plane(False)
            later(fifteen, f_s.at[1])
            frecv[1, spot] = wsend[1, d, y_hi]
        for b in (2 * st, 2 * st + 1):
            through(b)
            small_sums(b)

    @pl.loop(1, PLANE, unroll=True)
    def _(j):
        dev, _, to_d = plane(j)
        send(ssend.at[to_d], srecv.at[spot], fs_s.at[0], fs_r.at[0], dev)

    later(srecv.at[pl.ds(0, PLANE - 1)], fs_s.at[0])
    for k in range(3):
        ghs[k : k + 1, :] = gm[k, 0:1, :]
    send(ghs, ghr, e_s, e_r, chip(rem(p + CHIPS - 1, CHIPS)))
    later(ghr, e_s)
    srecv[spot] = ssend[d]

    def fold(st):
        wait_for(fifteen, f_r.at[st])

        @pl.loop(0, DEPTH)
        def _(i):
            at = rows16(i)
            v = frecv[st, 0, at, :].astype(F32)
            for u in range(1, PLANE):
                v = v + frecv[st, u, at, :].astype(F32)
            fsum[st, i] = v.astype(BF16)

        @pl.loop(1, DEPTH, unroll=True)
        def _(j):
            to = rem(z + j, DEPTH)
            send(fsum.at[st, to], zrecv.at[st, z], z_s.at[st], z_r.at[st], deep(to))

        zrecv[st, z] = fsum[st, z]

    pl.when(y_odd == 0)(lambda: fold(0))
    wait_for(ghr, e_r)
    halo = ghr[...]
    halo = jnp.where(p == CHIPS - 1, jnp.zeros_like(halo), halo)
    for k in range(3):
        rolled = pltpu.roll(gm[k], 7, 0)
        gm[R + k] = jnp.where(sub == 7, jnp.broadcast_to(halo[k : k + 1], (8, HALF)), rolled)

    for b in range(NB):
        taps = [jnp.broadcast_to(conv_w[k : k + 1, block(b)], (8, BW)) for k in range(4)]

        @pl.loop(0, R, unroll=4)
        def _(r):
            v = taps[0] * gm[r + 3, :, block(b)]
            for k in range(1, 4):
                v = v + taps[k] * gm[r + 3 - k, :, block(b)]
            for lh in range(2):
                nat[2 * b + lh, pl.ds(r, 8, stride=R), :] = v[:, lane_tile(lh)]

    for k in range(TILES):
        gib[:, lane_tile(k)] = nat[k].astype(BF16)
    s_g = send(gib.at[sib_rows], gi_hbm.at[:, mine], sib_s.at[3], sib_r.at[3], sibling)
    st_g = pltpu.make_async_copy(gib.at[my_rows], gi_hbm.at[:, mine], lsem.at[3])
    st_g.start()
    later(gib.at[my_rows], lsem.at[3])
    wait_for(brecv.at[pl.ds(0, DEPTH - 1)], b_r.at[0])
    for h in range(2):
        for t in range(4):
            v = brecv[0, h, t].astype(F32)
            for j in range(1, DEPTH):
                v = v + brecv[j, h, t].astype(F32)
            bsum[h, t] = v.astype(BF16)

    @pl.loop(1, PLANE, unroll=True)
    def _(j):
        dev, to_h, to_d = plane(j)

        @pl.when(to_d >= 4)
        def _():
            send(bsum.at[to_h, rem(to_d, 4)], bz.at[spot], b_s.at[1], b_r.at[1], dev)

    @pl.when(y_odd == 1)
    def _():
        bz[spot] = bsum[y_hi, x]

    fold(1)
    wait_for(srecv.at[pl.ds(0, PLANE - 1)], fs_r.at[0])
    ssum[...] = jnp.sum(srecv[...], 0)

    @pl.loop(1, DEPTH, unroll=True)
    def _(j):
        send(ssum, szrecv.at[z], fs_s.at[1], fs_r.at[1], deep(rem(z + j, DEPTH)))

    later(szrecv.at[pl.ds(0, DEPTH - 1)], fs_s.at[1])
    szrecv[z] = ssum[...]

    later(zrecv.at[1, pl.ds(0, DEPTH - 1)], z_s.at[1])

    @pl.when(y_odd == 0)
    def _():
        wait_for(zrecv.at[0, pl.ds(0, DEPTH - 1)], z_s.at[0])
        wait_for(zrecv.at[0, pl.ds(0, DEPTH - 1)], z_r.at[0])
        wait_for(frecv.at[0, pl.ds(0, 7)], f_s.at[0])
        wait_for(bz.at[pl.ds(0, 8)], b_s.at[1])

    @pl.when(y_odd == 1)
    def _():
        wait_for(bz.at[pl.ds(0, PLANE - 1)], b_r.at[1])
        wait_for(frecv.at[0, pl.ds(0, 8)], f_s.at[0])
        wait_for(bz.at[pl.ds(0, 7)], b_s.at[1])


    def total(st, parts, count):
        whole = parts(0).astype(F32)
        for j in range(1, count):
            whole = whole + parts(j).astype(F32)
        own[st] = whole

    pl.when(y_odd == 0)(lambda: total(0, lambda j: zrecv[0, j], DEPTH))
    pl.when(y_odd == 1)(lambda: total(0, lambda j: bz[j], PLANE))
    wait_for(szrecv.at[pl.ds(0, DEPTH - 1)], fs_r.at[1])
    fin[...] = jnp.sum(szrecv[...], 0)
    wait_for(zrecv.at[1, pl.ds(0, DEPTH - 1)], z_r.at[1])
    total(1, lambda j: zrecv[1, j], DEPTH)
    for core in range(2):
        for st in range(STAGES):
            done[core, st] = own[st, 8 * core : 8 * core + 8, :]
        done[core, STAGES] = fin[...]
    keep = pltpu.make_async_copy(done.at[c], done_hbm.at[c, d], lsem.at[9])
    keep.start()

    @pl.loop(1, 2 * REPL, unroll=True)
    def _(j):
        to_c = rem(c + div(j, REPL), 2)
        dev = {"ctx": 2 * p + to_c, "dp": rem(d + j, REPL)}
        send(done.at[to_c], done_hbm.at[c, d], g_s, g_r, dev)

    triples = frecv.at[0, pl.ds(0, 2 * REPL - 1), pl.ds(0, 48)]
    later(triples, g_s)
    later(triples, g_r)
    for cp in [s_v, s_x, s_c, s_g]:
        cp.wait_send()
    s_g.wait_recv()
    for finish_one in pending:
        finish_one()
    keep.wait()


def last_kernel(
    gi_in, done_in, gi_out, gw_out, dec_out, bias_out, taps_out, shift_out,
    done, gws, gw, dec, bias, taps, shift, via, l_sem, s_sem,
):
    get = pltpu.make_async_copy(done_in, done, l_sem.at[4])
    get.start()
    parts = [pl.ds(k * (ROWS // 4), ROWS // 4) for k in range(4)]
    loads = [pltpu.make_async_copy(gi_in.at[at], via.at[at], l_sem.at[k]) for k, at in enumerate(parts)]
    stores = [pltpu.make_async_copy(via.at[at], gi_out.at[0, at], s_sem.at[k]) for k, at in enumerate(parts)]
    for cp in loads:
        cp.start()
    get.wait()
    for h in range(2):
        for u in range(8):
            at = slice(h * HALF + 128 * u, h * HALF + 128 * (u + 1))
            v = done[h, u, STAGES]
            dec[:, at] = v[0:1]
            bias[:, at] = v[1:3]
            taps[:, at] = v[3:7]
            shift[:, at] = v[7:8]
            for st in range(STAGES):
                first = ((u // 2) % 2) * 8 + 4 * h + 2 * st + u // 4
                gws[u % 2, pl.ds(first, 8, stride=16), :] = done[h, u, st]
    for n, (src, dst) in enumerate(((dec, dec_out), (bias, bias_out), (taps, taps_out), (shift, shift_out))):
        stores.append(pltpu.make_async_copy(src, dst, s_sem.at[4 + n]))
        stores[-1].start()
    for k in range(4):
        loads[k].wait()
        stores[k].start()
    for i in range(8):
        for g in range(2):
            for lh in range(2):
                gw[i, g, :, lane_tile(lh)] = gws[lh, i * 16 + g * 8 : i * 16 + g * 8 + 8, :]
    stores.append(pltpu.make_async_copy(gw, gw_out, s_sem.at[8]))
    stores[-1].start()
    for cp in stores:
        cp.wait()


def per_device(inputs, gate_weight, gate_bias, decay_param, conv_weight, conv_bias, cotangent):
    hbm = pl.BlockSpec(memory_space=pltpu.HBM)
    dma = pltpu.SemaphoreType.DMA
    big = pltpu.VMEM((R, 8, HALF), F32)
    gi, done = pl.pallas_call(
        main_kernel,
        name="main",
        out_shape=(
            jax.ShapeDtypeStruct((ROWS, WIDTH), BF16),
            jax.ShapeDtypeStruct((2, REPL, STAGES + 1, 8, 128), F32),
        ),
        in_specs=[hbm] * 7,
        out_specs=(hbm,) * 2,
        scratch_shapes=[
            pltpu.VMEM((2, HALF), F32),
            pltpu.VMEM((1, HALF), F32),
            pltpu.VMEM((4, HALF), F32),
            pltpu.VMEM((1, HALF), F32),
            pltpu.VMEM((SPAN, HALF), BF16),
            pltpu.VMEM((SPAN, HALF), BF16),
            pltpu.VMEM((8, 2, 8, BW), BF16),
            pltpu.VMEM((2, 128, 128), F32),
            pltpu.VMEM((2, STAGES, REPL, 8, 128), F32),
            pltpu.VMEM((DEPTH, 2, 8, 128), F32),
            pltpu.VMEM((REPL, 16, 128), F32),
            pltpu.VMEM((REPL, 2, 128, 128), BF16),
            pltpu.VMEM((CHIPS, REPL, 16, 128), BF16),
            pltpu.VMEM((16, HALF), BF16),
            pltpu.VMEM((TILES, SPAN, 128), F32),
            pltpu.VMEM((TILES, SPAN, 128), F32),
            pltpu.VMEM((R + 3, 8, HALF), F32),
            big,
            pltpu.VMEM((SPAN, HALF), BF16),
            pltpu.VMEM((NB, BW, SPAN), BF16),
            pltpu.VMEM((8, SPAN, BW), F32),
            big, big, big, big, big, big, big, big,
            pltpu.VMEM((8, SPAN, BW), BF16),
            pltpu.VMEM((R + 3, 8, HALF), F32),
            pltpu.VMEM((STAGES, 2, 8, 128), F32),
            pltpu.VMEM((STAGES, CHIPS, 8, 128), F32),
            pltpu.VMEM((STAGES, 2, 4, 128), F32),
            pltpu.VMEM((8, HALF), F32),
            pltpu.VMEM((8, HALF), F32),
            pltpu.VMEM((STAGES, REPL, 2, 128, 128), BF16),
            pltpu.VMEM((DEPTH, 2, 4, 16, 128), BF16),
            pltpu.VMEM((STAGES, PLANE, 128, 128), BF16),
            pltpu.VMEM((DEPTH, 2, 4, 16, 128), BF16),
            pltpu.VMEM((2, 4, 16, 128), BF16),
            pltpu.VMEM((PLANE, 16, 128), BF16),
            pltpu.VMEM((STAGES, 16, 128), F32),
            pltpu.VMEM((STAGES, DEPTH, 16, 128), BF16),
            pltpu.VMEM((STAGES, DEPTH, 16, 128), BF16),
            pltpu.VMEM((8, 8, 128), F32),
            pltpu.VMEM((PLANE, 8, 128), F32),
            pltpu.VMEM((8, 128), F32),
            pltpu.VMEM((DEPTH, 8, 128), F32),
            pltpu.VMEM((8, 128), F32),
            pltpu.VMEM((2, STAGES + 1, 8, 128), F32),
            pltpu.VMEM((SPAN, HALF), BF16),
            dma((10,)), dma((7,)), dma((7,)),
            dma, dma, dma, dma, dma((2,)), dma((6,)), dma, dma,
            dma((STAGES,)), dma((STAGES,)), dma, dma, dma((STAGES,)), dma((STAGES,)),
            dma((2,)), dma((2,)), dma((2,)), dma((2,)),
            dma((STAGES,)), dma((STAGES,)), dma, dma,
        ],
        compiler_params=pltpu.CompilerParams(
            collective_id=0, has_side_effects=True, vmem_limit_bytes=60 * 2**20
        ),
    )(
        inputs, gate_weight, gate_bias, decay_param.reshape(1, WIDTH), conv_weight,
        conv_bias.reshape(1, WIDTH), cotangent,
    )
    gi, gw, dec, bias, taps, shift = pl.pallas_call(
        last_kernel,
        name="last",
        out_shape=(
            jax.ShapeDtypeStruct((1, ROWS, WIDTH), BF16),
            jax.ShapeDtypeStruct((8, 2, 8, BW), F32),
            jax.ShapeDtypeStruct((1, WIDTH), F32),
            jax.ShapeDtypeStruct((2, WIDTH), F32),
            jax.ShapeDtypeStruct((4, WIDTH), F32),
            jax.ShapeDtypeStruct((1, WIDTH), F32),
        ),
        in_specs=[hbm] * 2,
        out_specs=(hbm,) * 6,
        scratch_shapes=[
            pltpu.VMEM((2, REPL, STAGES + 1, 8, 128), F32),
            pltpu.VMEM((2, 128, 128), F32),
            pltpu.VMEM((8, 2, 8, BW), F32),
            pltpu.VMEM((1, WIDTH), F32),
            pltpu.VMEM((2, WIDTH), F32),
            pltpu.VMEM((4, WIDTH), F32),
            pltpu.VMEM((1, WIDTH), F32),
            pltpu.VMEM((ROWS, WIDTH), BF16),
            dma((5,)),
            dma((9,)),
        ],
        compiler_params=pltpu.CompilerParams(vmem_limit_bytes=60 * 2**20),
    )(gi, done)
    return gi, gw, dec.reshape(WIDTH), bias, taps, shift.reshape(WIDTH)


def solution(mesh):
    placed = (
        P("dp", "ctx", None),
        P("ctx", None, None, None),
        P(),
        P(),
        P(),
        P(),
        P("dp", "ctx", None),
    )
    return jax.shard_map(
        per_device,
        mesh=mesh,
        in_specs=placed,
        out_specs=(P("dp", "ctx", None), P("ctx", None, None, None), P(), P(), P(), P()),
        check_vma=False,
    )
```

```python
import jax
import jax.numpy as jnp
from jax import lax
from jax.experimental import pallas as pl
from jax.experimental.pallas import tpu as pltpu
from jax.sharding import PartitionSpec as P

MESH = pl.DeviceIdType.MESH
F32 = jnp.float32
BF16 = jnp.bfloat16
CHIPS = 16
PLANE = 16
DEPTH = 8
REPL = 8
ROWS = 128
SPAN = 256
WIDTH = 2048
HALF = 1024
BW = 256
NB = HALF // BW
R = SPAN // 8
TILES = HALF // 128
STAGES = 2


def wait_for(ref, sem):
    pltpu.make_async_copy(ref, ref, sem).wait()


def sublane(shape):
    return lax.broadcasted_iota(jnp.int32, shape, 0)


def sigmoid(x):
    return 0.5 * jnp.tanh(0.5 * x) + 0.5


def softplus(x):
    e = jnp.exp(-jnp.abs(x))
    z = e / (2.0 + e)
    z2 = z * z
    s = jnp.full_like(z, 1.0 / 17.0)
    for n in (15, 13, 11, 9, 7, 5, 3, 1):
        s = s * z2 + 1.0 / n
    return jnp.maximum(x, 0.0) + 2.0 * z * s


def lane_tile(i):
    return slice(i * 128, (i + 1) * 128)


def block(b):
    return slice(b * BW, (b + 1) * BW)


def main_kernel(
    x_hbm, w_hbm, gb_hbm, lam_hbm, cw_hbm, cb_hbm, cot_hbm,
    gi_hbm, done_hbm,
    gb_ref, lam_ref, cw_ref, cb_ref, xb, cotb, wsh, wf, wu, column, wpair, W0, W1, xhalo, nat, natc, xs, cs, mb, mt, pre,
    dec, pp, qq, m1, m2, m3, oma, hp, gp, gm, dsend, drecv, sin, ghs, ghr,
    wsend, wz, frecv, brecv, bsum, bz, own, fsum, zrecv, ssend, srecv, ssum, szrecv, fin, done, gib,
    lsem, sib_s, sib_r, c1_s, c1_r, hal_s, hal_r, za_s, za_r, c2_s, c2_r, d_s, d_r, e_s, e_r,
    f_s, f_r, b_s, b_r, fs_s, fs_r, z_s, z_r, g_s, g_r,
):
    ctx = lax.axis_index("ctx")
    d = lax.axis_index("dp")
    div, rem = lax.div, lax.rem
    p, c = div(ctx, 2), rem(ctx, 2)
    z = rem(p, DEPTH)
    y = 2 * div(p, DEPTH) + div(d, 4)
    x = rem(d, 4)
    y_hi, y_odd = div(y, 2), rem(y, 2)
    spot = 4 * y + x
    sibling = {"ctx": 2 * p + 1 - c, "dp": d}

    def chip(j):
        return {"ctx": 2 * j + c, "dp": d}

    def deep(j):
        return {"ctx": 2 * (p - z + j) + c, "dp": d}

    def peer(u):
        return {"ctx": ctx, "dp": u}

    def plane(j):
        to_x, to_y = rem(x + rem(j, 4), 4), rem(y + div(j, 4), 4)
        to_h, to_d = div(to_y, 2), 4 * rem(to_y, 2) + to_x
        return {"ctx": 2 * (DEPTH * to_h + z) + c, "dp": to_d}, to_h, to_d

    def rows16(j):
        return pl.ds(pl.multiple_of(16 * j, 16), 16)

    def send(src, dst, ss, rs, dev):
        cp = pltpu.make_async_remote_copy(
            src_ref=src, dst_ref=dst, send_sem=ss, recv_sem=rs, device_id=dev, device_id_type=MESH
        )
        cp.start()
        return cp

    bar = pltpu.get_barrier_semaphore()
    pl.semaphore_signal(bar, inc=1, device_id=sibling, device_id_type=MESH)

    @pl.loop(1, CHIPS, unroll=True)
    def _(j):
        pl.semaphore_signal(bar, inc=1, device_id=chip(rem(p + j, CHIPS)), device_id_type=MESH)

    @pl.loop(1, PLANE, unroll=True)
    def _(j):
        @pl.when(j != PLANE // 2)
        def _():
            pl.semaphore_signal(bar, inc=1, device_id=plane(j)[0], device_id_type=MESH)

    @pl.loop(1, REPL, unroll=True)
    def _(j):
        dev = {"ctx": 2 * p + 1 - c, "dp": rem(d + j, REPL)}
        pl.semaphore_signal(bar, inc=1, device_id=dev, device_id_type=MESH)

    @pl.loop(1, DEPTH, unroll=True)
    def _(j):
        dev = {"ctx": 2 * (p - z + rem(z + j, DEPTH)) + 1 - c, "dp": d}
        pl.semaphore_signal(bar, inc=1, device_id=dev, device_id_type=MESH)

    mine = pl.ds(pl.multiple_of(HALF * c, HALF), HALF)
    theirs = pl.ds(pl.multiple_of(HALF * (1 - c), HALF), HALF)
    my_rows = pl.ds(pl.multiple_of(ROWS * c, ROWS), ROWS)
    sib_rows = pl.ds(pl.multiple_of(ROWS * (1 - c), ROWS), ROWS)

    ld_w = pltpu.make_async_copy(w_hbm, wsh, lsem.at[0])
    ld_w.start()
    ld_x = pltpu.make_async_copy(x_hbm.at[0, :, mine], xb.at[my_rows], lsem.at[1])
    ld_x.start()
    ld_c = pltpu.make_async_copy(cot_hbm.at[0, :, mine], cotb.at[my_rows], lsem.at[2])
    ld_c.start()
    lds = []
    for n, (src, dst) in enumerate(
        ((gb_hbm, gb_ref), (lam_hbm, lam_ref), (cw_hbm, cw_ref), (cb_hbm, cb_ref))
    ):
        lds.append(pltpu.make_async_copy(src.at[:, mine], dst, lsem.at[5 + n]))
        lds[-1].start()
    pending = []

    def later(ref, sem):
        pending.append(lambda: wait_for(ref, sem))


    ld_w.wait()
    for i in range(8):
        for g in range(2):
            v = wsh[i, g].astype(F32)
            for lh in range(2):
                wf[lh, i * 16 + g * 8 : i * 16 + g * 8 + 8, :] = v[:, lane_tile(lh)]
    for h in range(2):
        for u in range(REPL):
            for st in range(STAGES):
                first = ((u // 2) % 2) * 8 + 4 * h + 2 * st + u // 4
                wu[h, st, u] = wf[u % 2, pl.ds(first, 8, stride=16), :]

    pl.semaphore_wait(bar, 1 + (CHIPS - 1) + (PLANE - 2) + (REPL - 1) + (DEPTH - 1))

    part = pl.ds(pl.multiple_of(8 * c, 8), 8)
    @pl.loop(1, 2 * DEPTH, unroll=True)
    def _(j):
        to_c, to_z = rem(c + div(j, DEPTH), 2), rem(z + j, DEPTH)
        dev = {"ctx": 2 * (p - z + to_z) + to_c, "dp": d}
        send(wu.at[to_c, 1, d], column.at[z, c], c1_s, c1_r, dev)

    column[z, c] = wu[c, 1, d]
    s_v = send(wu.at[1 - c, 0], wpair.at[:, part], sib_s.at[5], sib_r.at[5], sibling)
    s_x = send(x_hbm.at[0, :, theirs], xb.at[my_rows], sib_s.at[1], sib_r.at[1], sibling)
    s_c = send(cot_hbm.at[0, :, theirs], cotb.at[my_rows], sib_s.at[2], sib_r.at[2], sibling)
    others = srecv.at[pl.ds(0, 2 * DEPTH - 1)]
    later(others, c1_s)
    wpair[:, part, :] = wu[c, 0]
    s_v.wait_recv()
    for u in range(REPL):
        W1[p, u] = wpair[u].astype(BF16)
    across = rem(p + DEPTH, CHIPS)
    rows_a, rows_b = W1.at[p], W1.at[across]
    send(rows_a, rows_a, za_s.at[0], za_r.at[0], chip(across))
    later(rows_a, za_s.at[0])

    def at_depth(side, by):
        return (p - z if side == 0 else across - z) + rem(z + by + DEPTH, DEPTH)

    def near(side):
        rows = W1.at[at_depth(side, 0)]
        for by in (1, -1):
            send(rows, rows, za_s.at[1], za_r.at[1], deep(rem(z + by + DEPTH, DEPTH)))
        for by in (2, -2):
            arrive = za_r.at[2 + 2 * side + (0 if by > 0 else 1)]
            send(rows, rows, za_s.at[1], arrive, deep(rem(z + by + DEPTH, DEPTH)))

    def onward(side):
        for way, by in ((0, 1), (1, -1)):
            rows = W1.at[at_depth(side, -2 * by)]
            wait_for(rows, za_r.at[2 + 2 * side + way])
            send(rows, rows, za_s.at[1], za_r.at[1], deep(rem(z + by + DEPTH, DEPTH)))
            half = W1.at[at_depth(side, -2 * by), pl.ds(4 * way, 4)]
            send(half, half, za_s.at[1], za_r.at[1], deep(rem(z + 2 * by + DEPTH, DEPTH)))

    near(0)

    ld_x.wait()
    s_x.wait_recv()
    send(xb.at[pl.ds(SPAN - 16, 16)], xhalo, hal_s, hal_r, chip(rem(p + 1, CHIPS)))
    later(xhalo, hal_s)
    for k in range(TILES):
        nat[k] = xb[:, lane_tile(k)].astype(F32)

    @pl.loop(0, R, unroll=2)
    def _(r):
        for k in range(TILES):
            xs[3 + r, :, lane_tile(k)] = nat[k, pl.ds(r, 8, stride=R), :]

    wait_for(rows_b, za_r.at[0])

    near(1)
    later(W1.at[pl.ds(0, 14)], za_s.at[1])
    ten = W1.at[pl.ds(0, 10)]
    wait_for(others, c1_r)
    W0[d, y_hi] = column[...].reshape(128, 128).astype(BF16)
    fifteen = frecv.at[0, pl.ds(0, PLANE - 1)]
    mine_s = W0.at[d, y_hi]

    @pl.loop(1, PLANE, unroll=True)
    def _(j):
        send(mine_s, mine_s, c2_s, c2_r, plane(j)[0])

    later(fifteen, c2_s)
    onward(0)
    onward(1)
    ld_c.wait()
    s_c.wait_recv()
    for k in range(TILES):
        natc[k] = cotb[:, lane_tile(k)].astype(F32)

    @pl.loop(0, R, unroll=2)
    def _(r):
        for k in range(TILES):
            cs[r, :, lane_tile(k)] = natc[k, pl.ds(r, 8, stride=R), :]

    wait_for(xhalo, hal_r)
    hal = xhalo[...].astype(F32)
    hal = jnp.where(p == 0, jnp.zeros_like(hal), hal)
    sub = sublane((8, HALF))
    for k in range(3):
        rolled = pltpu.roll(xs[3 + R - 3 + k], 1, 0)
        xs[k] = jnp.where(sub == 0, jnp.broadcast_to(hal[13 + k : 14 + k], (8, HALF)), rolled)

    for ld in lds:
        ld.wait()
    conv_w = cw_ref[...]
    conv_b = cb_ref[...]
    for b in range(NB):
        taps = [jnp.broadcast_to(conv_w[k : k + 1, block(b)], (8, BW)) for k in range(4)]
        shift = jnp.broadcast_to(conv_b[:, block(b)], (8, BW))

        @pl.loop(0, R // 2, unroll=2)
        def _(i):
            v = [xs[2 * i + k, :, block(b)] for k in range(5)]
            out = []
            for o in range(2):
                m = shift + taps[0] * v[o]
                for k in range(1, 4):
                    m = m + taps[k] * v[o + k]
                out.append(m)
            mb[pl.ds(pl.multiple_of(16 * i, 16), 16), block(b)] = jnp.concatenate(out, 0).astype(BF16)

        mt[b] = mb[:, block(b)].astype(F32).T.astype(BF16)

    lam = lam_ref[...]
    neg8rate = -8.0 * softplus(-lam)
    gate_b = gb_ref[...]
    ends = []

    def weights(b, g):
        u = 4 * (b % 2) + 2 * g
        two = (W1[:, u + lh] if b < 2 else W0[u + lh] for lh in range(2))
        return jnp.concatenate([v.reshape(BW, 128) for v in two], 1)

    def gates(b):
        st = b // 2
        for g in range(2):
            pre[2 * b + g] = jnp.dot(mb[:, block(b)], weights(b, g), preferred_element_type=F32)
        nr = jnp.broadcast_to(neg8rate[:, block(b)], (8, BW))
        ba = jnp.broadcast_to(gate_b[0:1, block(b)], (8, BW))
        bx = jnp.broadcast_to(gate_b[1:2, block(b)], (8, BW))

        def step(i, carry):
            prod, hid, kk, logs = carry
            two = mb[pl.ds(pl.multiple_of(16 * i, 16), 16), block(b)].astype(F32)
            for o in range(2):
                r = 2 * i + o
                at = pl.ds(pl.multiple_of(8 * r, 8), 8)
                ga = sigmoid(pre[2 * b, at, :] + ba)
                gx = sigmoid(pre[2 * b + 1, at, :] + bx)
                m = two[8 * o : 8 * o + 8]
                ld = ga * nr
                a = jnp.exp(ld)
                sq = 1.0 - a * a
                mult = jnp.sqrt(sq)
                gm_ = gx * m
                drive = mult * gm_
                dec[r, :, block(b)] = a
                qq[r, :, block(b)] = gm_ * a * lax.rsqrt(jnp.maximum(sq, 0.05))
                m1[r, :, block(b)] = a * ga
                oma[r, :, block(b)] = (1.0 - ga) * nr
                m2[r, :, block(b)] = drive * (1.0 - gx)
                m3[r, :, block(b)] = mult * gx
                hp[r, :, block(b)] = hid
                pp[r, :, block(b)] = prod
                hid = a * hid + drive
                prod = prod * a
                kk = kk + prod * cs[r, :, block(b)]
                logs = logs + ld
            return prod, hid, kk, logs

        zero = jnp.zeros((8, BW), F32)
        prod, hid, kk, logs = lax.fori_loop(
            0, R // 2, step, (jnp.ones((8, BW), F32), zero, zero, zero), unroll=2
        )
        sb = sublane((8, BW))
        fp, fh = prod, hid
        bp, bk = prod, kk
        for s in (1, 2, 4):
            mp, mh = pltpu.roll(fp, s, 0), pltpu.roll(fh, s, 0)
            fh = jnp.where(sb >= s, fp * mh + fh, fh)
            fp = jnp.where(sb >= s, fp * mp, fp)
            mp, mk = pltpu.roll(bp, 8 - s, 0), pltpu.roll(bk, 8 - s, 0)
            bk = jnp.where(sb < 8 - s, bp * mk + bk, bk)
            bp = jnp.where(sb < 8 - s, bp * mp, bp)
            logs = logs + pltpu.roll(logs, s, 0)
        one = jnp.ones((8, BW), F32)
        ends.append((
            jnp.where(sb == 0, one, pltpu.roll(fp, 1, 0)),
            jnp.where(sb == 0, zero, pltpu.roll(fh, 1, 0)),
            jnp.where(sb == 7, one, pltpu.roll(bp, 7, 0)),
            jnp.where(sb == 7, zero, pltpu.roll(bk, 7, 0)),
        ))
        for lh in range(2):
            k = 2 * (b % 2) + lh
            dsend[st, 0, k : k + 1, :] = logs[0:1, lane_tile(lh)]
            dsend[st, 1, k : k + 1, :] = logs[0:1, lane_tile(lh)]
            dsend[st, 0, 4 + k : 5 + k, :] = fh[7:8, lane_tile(lh)]
            dsend[st, 1, 4 + k : 5 + k, :] = bk[0:1, lane_tile(lh)]

    for st in range(STAGES):
        wait_for(*((ten, za_r.at[1]) if st == 0 else (fifteen, c2_r)))
        for b in (2 * st, 2 * st + 1):
            gates(b)

        @pl.loop(1, CHIPS, unroll=True)
        def _(j):
            to = rem(p + j, CHIPS)
            send(dsend.at[st, jnp.where(to > p, 0, 1)], drecv.at[st, p], d_s.at[st], d_r.at[st], chip(to))

        later(drecv.at[st, pl.ds(0, CHIPS - 1)], d_s.at[st])
        drecv[st, p] = jnp.zeros((8, 128), F32)

    sums = []

    def grads(b):
        st, k = b // 2, 2 * (b % 2)

        def wide(n):
            return jnp.concatenate(
                [jnp.broadcast_to(sin[st, n, k + lh : k + lh + 1, :], (8, 128)) for lh in range(2)], 1
            )

        hin = ends[b][1] + ends[b][0] * wide(0)
        kin = ends[b][3] + ends[b][2] * wide(1)

        def down(n, carry):
            kk, t_sum, a_sum, x_sum = carry
            i = R // 2 - 1 - n
            outs = [[None, None], [None, None]]
            for o in (1, 0):
                r = 2 * i + o
                gr = cs[r, :, block(b)] + kk
                kk = dec[r, :, block(b)] * gr
                before = hp[r, :, block(b)] + pp[r, :, block(b)] * hin
                t = (before - qq[r, :, block(b)]) * m1[r, :, block(b)] * gr
                ga = t * oma[r, :, block(b)]
                gx = gr * m2[r, :, block(b)]
                gm[r, :, block(b)] = gr * m3[r, :, block(b)]
                t_sum, a_sum, x_sum = t_sum + t, a_sum + ga, x_sum + gx
                outs[0][o], outs[1][o] = ga, gx
            at = pl.ds(pl.multiple_of(16 * i, 16), 16)
            gp[2 * b, at, :] = jnp.concatenate(outs[0], 0).astype(BF16)
            gp[2 * b + 1, at, :] = jnp.concatenate(outs[1], 0).astype(BF16)
            return kk, t_sum, a_sum, x_sum

        zero = jnp.zeros((8, BW), F32)
        _, t_sum, a_sum, x_sum = lax.fori_loop(0, R // 2, down, (kin, zero, zero, zero), unroll=4)
        sums.append([t_sum, a_sum, x_sum])
        for g in range(2):
            grad = jnp.dot(mt[b], gp[2 * b + g], preferred_element_type=F32).astype(BF16)
            for lh in range(2):
                for h in range(2):
                    if b == 1:
                        for j in range(DEPTH):
                            wz[j, h, 2 * g + lh] = grad[128 * h + 16 * j : 128 * h + 16 * j + 16, lane_tile(lh)]
                    else:
                        wsend[st, 2 * (k + g) + lh, h] = grad[128 * h : 128 * (h + 1), lane_tile(lh)]

    def through(b):
        nt = (((1,), (1,)), ((), ()))
        back = lax.dot_general(gp[2 * b], weights(b, 0), nt, preferred_element_type=F32)
        back = back + lax.dot_general(gp[2 * b + 1], weights(b, 1), nt, preferred_element_type=F32)
        gm[0:R, :, block(b)] = gm[0:R, :, block(b)] + back.reshape(R, 8, BW)

    sig = 1.0 / (1.0 + jnp.exp(lam))

    def small_sums(b):
        def add(r, carry):
            g = gm[r, :, block(b)]
            return tuple(carry[k] + g * xs[r + k, :, block(b)] for k in range(4)) + (carry[4] + g,)

        zero = jnp.zeros((8, BW), F32)
        acc = lax.fori_loop(0, R, add, (zero,) * 5, unroll=4)
        t_sum, a_sum, x_sum = sums[b]
        t_sum = t_sum * (8.0 * jnp.broadcast_to(sig[:, block(b)], (8, BW)))
        sb = sublane((8, BW))
        rows = zero
        for n, v in enumerate((t_sum, a_sum, x_sum) + tuple(acc)):
            for s in (1, 2, 4):
                v = v + pltpu.roll(v, s, 0)
            rows = jnp.where(sb == n, v, rows)
        for lh in range(2):
            ssend[2 * b + lh] = rows[:, lane_tile(lh)]

    for st in range(STAGES):
        wait_for(drecv.at[st, pl.ds(0, CHIPS - 1)], d_r.at[st])
        state = jnp.zeros((4, 128), F32)
        carry_in = jnp.zeros((4, 128), F32)
        for j in range(CHIPS):
            v = drecv[st, j]
            state = jnp.where(j < p, jnp.exp(v[:4]) * state + v[4:], state)
            v = drecv[st, CHIPS - 1 - j]
            carry_in = jnp.where(CHIPS - 1 - j > p, jnp.exp(v[:4]) * carry_in + v[4:], carry_in)
        sin[st, 0] = state
        sin[st, 1] = carry_in
        def to_plane(low):
            @pl.loop(1, PLANE, unroll=True)
            def _(j):
                dev, to_h, to_d = plane(j)

                @pl.when(to_d < 4 if low else to_d >= 4)
                def _():
                    send(
                        wsend.at[st, to_d, to_h], frecv.at[st, spot], f_s.at[st], f_r.at[st], dev
                    )

        grads(2 * st)
        to_plane(True)
        grads(2 * st + 1)
        if st == 0:
            @pl.when(y_odd == 0)
            def _():
                frecv[0, spot] = wsend[0, d, y_hi]

            @pl.loop(1, DEPTH, unroll=True)
            def _(j):
                to = rem(z + j, DEPTH)
                send(wz.at[to], brecv.at[z], b_s.at[0], b_r.at[0], deep(to))

            later(brecv.at[pl.ds(0, DEPTH - 1)], b_s.at[0])
            brecv[z] = wz[z]
        else:
            to_plane(False)
            later(fifteen, f_s.at[1])
            frecv[1, spot] = wsend[1, d, y_hi]
        for b in (2 * st, 2 * st + 1):
            through(b)
            small_sums(b)

    @pl.loop(1, PLANE, unroll=True)
    def _(j):
        dev, _, to_d = plane(j)
        send(ssend.at[to_d], srecv.at[spot], fs_s.at[0], fs_r.at[0], dev)

    later(srecv.at[pl.ds(0, PLANE - 1)], fs_s.at[0])
    for k in range(3):
        ghs[k : k + 1, :] = gm[k, 0:1, :]
    send(ghs, ghr, e_s, e_r, chip(rem(p + CHIPS - 1, CHIPS)))
    later(ghr, e_s)
    srecv[spot] = ssend[d]

    def fold(st):
        wait_for(fifteen, f_r.at[st])

        @pl.loop(0, DEPTH)
        def _(i):
            at = rows16(i)
            v = frecv[st, 0, at, :].astype(F32)
            for u in range(1, PLANE):
                v = v + frecv[st, u, at, :].astype(F32)
            fsum[st, i] = v.astype(BF16)

        @pl.loop(1, DEPTH, unroll=True)
        def _(j):
            to = rem(z + j, DEPTH)
            send(fsum.at[st, to], zrecv.at[st, z], z_s.at[st], z_r.at[st], deep(to))

        zrecv[st, z] = fsum[st, z]

    pl.when(y_odd == 0)(lambda: fold(0))
    wait_for(brecv.at[pl.ds(0, DEPTH - 1)], b_r.at[0])
    for h in range(2):
        for t in range(4):
            v = brecv[0, h, t].astype(F32)
            for j in range(1, DEPTH):
                v = v + brecv[j, h, t].astype(F32)
            bsum[h, t] = v.astype(BF16)

    @pl.loop(1, PLANE, unroll=True)
    def _(j):
        dev, to_h, to_d = plane(j)

        @pl.when(to_d >= 4)
        def _():
            send(bsum.at[to_h, rem(to_d, 4)], bz.at[spot], b_s.at[1], b_r.at[1], dev)

    @pl.when(y_odd == 1)
    def _():
        bz[spot] = bsum[y_hi, x]

    fold(1)
    wait_for(srecv.at[pl.ds(0, PLANE - 1)], fs_r.at[0])
    ssum[...] = jnp.sum(srecv[...], 0)

    @pl.loop(1, DEPTH, unroll=True)
    def _(j):
        send(ssum, szrecv.at[z], fs_s.at[1], fs_r.at[1], deep(rem(z + j, DEPTH)))

    later(szrecv.at[pl.ds(0, DEPTH - 1)], fs_s.at[1])
    szrecv[z] = ssum[...]

    wait_for(ghr, e_r)
    halo = ghr[...]
    halo = jnp.where(p == CHIPS - 1, jnp.zeros_like(halo), halo)
    for k in range(3):
        rolled = pltpu.roll(gm[k], 7, 0)
        gm[R + k] = jnp.where(sub == 7, jnp.broadcast_to(halo[k : k + 1], (8, HALF)), rolled)

    for b in range(NB):
        taps = [jnp.broadcast_to(conv_w[k : k + 1, block(b)], (8, BW)) for k in range(4)]

        @pl.loop(0, R, unroll=4)
        def _(r):
            v = taps[0] * gm[r + 3, :, block(b)]
            for k in range(1, 4):
                v = v + taps[k] * gm[r + 3 - k, :, block(b)]
            for lh in range(2):
                nat[2 * b + lh, pl.ds(r, 8, stride=R), :] = v[:, lane_tile(lh)]

    for k in range(TILES):
        gib[:, lane_tile(k)] = nat[k].astype(BF16)
    s_g = send(gib.at[sib_rows], gi_hbm.at[:, mine], sib_s.at[3], sib_r.at[3], sibling)
    st_g = pltpu.make_async_copy(gib.at[my_rows], gi_hbm.at[:, mine], lsem.at[3])
    st_g.start()
    later(gib.at[my_rows], lsem.at[3])
    later(zrecv.at[1, pl.ds(0, DEPTH - 1)], z_s.at[1])

    @pl.when(y_odd == 0)
    def _():
        wait_for(zrecv.at[0, pl.ds(0, DEPTH - 1)], z_s.at[0])
        wait_for(zrecv.at[0, pl.ds(0, DEPTH - 1)], z_r.at[0])
        wait_for(frecv.at[0, pl.ds(0, 7)], f_s.at[0])
        wait_for(bz.at[pl.ds(0, 8)], b_s.at[1])

    @pl.when(y_odd == 1)
    def _():
        wait_for(bz.at[pl.ds(0, PLANE - 1)], b_r.at[1])
        wait_for(frecv.at[0, pl.ds(0, 8)], f_s.at[0])
        wait_for(bz.at[pl.ds(0, 7)], b_s.at[1])


    def total(st, parts, count):
        whole = parts(0).astype(F32)
        for j in range(1, count):
            whole = whole + parts(j).astype(F32)
        own[st] = whole

    pl.when(y_odd == 0)(lambda: total(0, lambda j: zrecv[0, j], DEPTH))
    pl.when(y_odd == 1)(lambda: total(0, lambda j: bz[j], PLANE))
    wait_for(szrecv.at[pl.ds(0, DEPTH - 1)], fs_r.at[1])
    fin[...] = jnp.sum(szrecv[...], 0)
    wait_for(zrecv.at[1, pl.ds(0, DEPTH - 1)], z_r.at[1])
    total(1, lambda j: zrecv[1, j], DEPTH)
    for core in range(2):
        for st in range(STAGES):
            done[core, st] = own[st, 8 * core : 8 * core + 8, :]
        done[core, STAGES] = fin[...]
    keep = pltpu.make_async_copy(done.at[c], done_hbm.at[c, d], lsem.at[9])
    keep.start()

    @pl.loop(1, 2 * REPL, unroll=True)
    def _(j):
        to_c = rem(c + div(j, REPL), 2)
        dev = {"ctx": 2 * p + to_c, "dp": rem(d + j, REPL)}
        send(done.at[to_c], done_hbm.at[c, d], g_s, g_r, dev)

    triples = frecv.at[0, pl.ds(0, 2 * REPL - 1), pl.ds(0, 48)]
    later(triples, g_s)
    later(triples, g_r)
    for cp in [s_v, s_x, s_c, s_g]:
        cp.wait_send()
    s_g.wait_recv()
    for finish_one in pending:
        finish_one()
    keep.wait()


def last_kernel(
    gi_in, done_in, gi_out, gw_out, dec_out, bias_out, taps_out, shift_out,
    done, gws, gw, dec, bias, taps, shift, via, l_sem, s_sem,
):
    get = pltpu.make_async_copy(done_in, done, l_sem.at[4])
    get.start()
    parts = [pl.ds(k * (ROWS // 4), ROWS // 4) for k in range(4)]
    loads = [pltpu.make_async_copy(gi_in.at[at], via.at[at], l_sem.at[k]) for k, at in enumerate(parts)]
    stores = [pltpu.make_async_copy(via.at[at], gi_out.at[0, at], s_sem.at[k]) for k, at in enumerate(parts)]
    for cp in loads:
        cp.start()
    get.wait()
    for h in range(2):
        for u in range(8):
            at = slice(h * HALF + 128 * u, h * HALF + 128 * (u + 1))
            v = done[h, u, STAGES]
            dec[:, at] = v[0:1]
            bias[:, at] = v[1:3]
            taps[:, at] = v[3:7]
            shift[:, at] = v[7:8]
            for st in range(STAGES):
                first = ((u // 2) % 2) * 8 + 4 * h + 2 * st + u // 4
                gws[u % 2, pl.ds(first, 8, stride=16), :] = done[h, u, st]
    for n, (src, dst) in enumerate(((dec, dec_out), (bias, bias_out), (taps, taps_out), (shift, shift_out))):
        stores.append(pltpu.make_async_copy(src, dst, s_sem.at[4 + n]))
        stores[-1].start()
    for k in range(4):
        loads[k].wait()
        stores[k].start()
    for i in range(8):
        for g in range(2):
            for lh in range(2):
                gw[i, g, :, lane_tile(lh)] = gws[lh, i * 16 + g * 8 : i * 16 + g * 8 + 8, :]
    stores.append(pltpu.make_async_copy(gw, gw_out, s_sem.at[8]))
    stores[-1].start()
    for cp in stores:
        cp.wait()


def per_device(inputs, gate_weight, gate_bias, decay_param, conv_weight, conv_bias, cotangent):
    hbm = pl.BlockSpec(memory_space=pltpu.HBM)
    dma = pltpu.SemaphoreType.DMA
    big = pltpu.VMEM((R, 8, HALF), F32)
    gi, done = pl.pallas_call(
        main_kernel,
        name="main",
        out_shape=(
            jax.ShapeDtypeStruct((ROWS, WIDTH), BF16),
            jax.ShapeDtypeStruct((2, REPL, STAGES + 1, 8, 128), F32),
        ),
        in_specs=[hbm] * 7,
        out_specs=(hbm,) * 2,
        scratch_shapes=[
            pltpu.VMEM((2, HALF), F32),
            pltpu.VMEM((1, HALF), F32),
            pltpu.VMEM((4, HALF), F32),
            pltpu.VMEM((1, HALF), F32),
            pltpu.VMEM((SPAN, HALF), BF16),
            pltpu.VMEM((SPAN, HALF), BF16),
            pltpu.VMEM((8, 2, 8, BW), BF16),
            pltpu.VMEM((2, 128, 128), F32),
            pltpu.VMEM((2, STAGES, REPL, 8, 128), F32),
            pltpu.VMEM((DEPTH, 2, 8, 128), F32),
            pltpu.VMEM((REPL, 16, 128), F32),
            pltpu.VMEM((REPL, 2, 128, 128), BF16),
            pltpu.VMEM((CHIPS, REPL, 16, 128), BF16),
            pltpu.VMEM((16, HALF), BF16),
            pltpu.VMEM((TILES, SPAN, 128), F32),
            pltpu.VMEM((TILES, SPAN, 128), F32),
            pltpu.VMEM((R + 3, 8, HALF), F32),
            big,
            pltpu.VMEM((SPAN, HALF), BF16),
            pltpu.VMEM((NB, BW, SPAN), BF16),
            pltpu.VMEM((8, SPAN, BW), F32),
            big, big, big, big, big, big, big, big,
            pltpu.VMEM((8, SPAN, BW), BF16),
            pltpu.VMEM((R + 3, 8, HALF), F32),
            pltpu.VMEM((STAGES, 2, 8, 128), F32),
            pltpu.VMEM((STAGES, CHIPS, 8, 128), F32),
            pltpu.VMEM((STAGES, 2, 4, 128), F32),
            pltpu.VMEM((8, HALF), F32),
            pltpu.VMEM((8, HALF), F32),
            pltpu.VMEM((STAGES, REPL, 2, 128, 128), BF16),
            pltpu.VMEM((DEPTH, 2, 4, 16, 128), BF16),
            pltpu.VMEM((STAGES, PLANE, 128, 128), BF16),
            pltpu.VMEM((DEPTH, 2, 4, 16, 128), BF16),
            pltpu.VMEM((2, 4, 16, 128), BF16),
            pltpu.VMEM((PLANE, 16, 128), BF16),
            pltpu.VMEM((STAGES, 16, 128), F32),
            pltpu.VMEM((STAGES, DEPTH, 16, 128), BF16),
            pltpu.VMEM((STAGES, DEPTH, 16, 128), BF16),
            pltpu.VMEM((8, 8, 128), F32),
            pltpu.VMEM((PLANE, 8, 128), F32),
            pltpu.VMEM((8, 128), F32),
            pltpu.VMEM((DEPTH, 8, 128), F32),
            pltpu.VMEM((8, 128), F32),
            pltpu.VMEM((2, STAGES + 1, 8, 128), F32),
            pltpu.VMEM((SPAN, HALF), BF16),
            dma((10,)), dma((7,)), dma((7,)),
            dma, dma, dma, dma, dma((2,)), dma((6,)), dma, dma,
            dma((STAGES,)), dma((STAGES,)), dma, dma, dma((STAGES,)), dma((STAGES,)),
            dma((2,)), dma((2,)), dma((2,)), dma((2,)),
            dma((STAGES,)), dma((STAGES,)), dma, dma,
        ],
        compiler_params=pltpu.CompilerParams(
            collective_id=0, has_side_effects=True, vmem_limit_bytes=60 * 2**20
        ),
    )(
        inputs, gate_weight, gate_bias, decay_param.reshape(1, WIDTH), conv_weight,
        conv_bias.reshape(1, WIDTH), cotangent,
    )
    gi, gw, dec, bias, taps, shift = pl.pallas_call(
        last_kernel,
        name="last",
        out_shape=(
            jax.ShapeDtypeStruct((1, ROWS, WIDTH), BF16),
            jax.ShapeDtypeStruct((8, 2, 8, BW), F32),
            jax.ShapeDtypeStruct((1, WIDTH), F32),
            jax.ShapeDtypeStruct((2, WIDTH), F32),
            jax.ShapeDtypeStruct((4, WIDTH), F32),
            jax.ShapeDtypeStruct((1, WIDTH), F32),
        ),
        in_specs=[hbm] * 2,
        out_specs=(hbm,) * 6,
        scratch_shapes=[
            pltpu.VMEM((2, REPL, STAGES + 1, 8, 128), F32),
            pltpu.VMEM((2, 128, 128), F32),
            pltpu.VMEM((8, 2, 8, BW), F32),
            pltpu.VMEM((1, WIDTH), F32),
            pltpu.VMEM((2, WIDTH), F32),
            pltpu.VMEM((4, WIDTH), F32),
            pltpu.VMEM((1, WIDTH), F32),
            pltpu.VMEM((ROWS, WIDTH), BF16),
            dma((5,)),
            dma((9,)),
        ],
        compiler_params=pltpu.CompilerParams(vmem_limit_bytes=60 * 2**20),
    )(gi, done)
    return gi, gw, dec.reshape(WIDTH), bias, taps, shift.reshape(WIDTH)


def solution(mesh):
    placed = (
        P("dp", "ctx", None),
        P("ctx", None, None, None),
        P(),
        P(),
        P(),
        P(),
        P("dp", "ctx", None),
    )
    return jax.shard_map(
        per_device,
        mesh=mesh,
        in_specs=placed,
        out_specs=(P("dp", "ctx", None), P("ctx", None, None, None), P(), P(), P(), P()),
        check_vma=False,
    )
```

```python
import jax
import jax.numpy as jnp
from jax import lax
from jax.experimental import pallas as pl
from jax.experimental.pallas import tpu as pltpu
from jax.sharding import PartitionSpec as P

MESH = pl.DeviceIdType.MESH
F32 = jnp.float32
BF16 = jnp.bfloat16
CHIPS = 16
PLANE = 16
DEPTH = 8
REPL = 8
ROWS = 128
SPAN = 256
WIDTH = 2048
HALF = 1024
BW = 256
NB = HALF // BW
R = SPAN // 8
TILES = HALF // 128
STAGES = 2


def wait_for(ref, sem):
    pltpu.make_async_copy(ref, ref, sem).wait()


def sublane(shape):
    return lax.broadcasted_iota(jnp.int32, shape, 0)


def sigmoid(x):
    return 0.5 * jnp.tanh(0.5 * x) + 0.5


def softplus(x):
    e = jnp.exp(-jnp.abs(x))
    z = e / (2.0 + e)
    z2 = z * z
    s = jnp.full_like(z, 1.0 / 17.0)
    for n in (15, 13, 11, 9, 7, 5, 3, 1):
        s = s * z2 + 1.0 / n
    return jnp.maximum(x, 0.0) + 2.0 * z * s


def lane_tile(i):
    return slice(i * 128, (i + 1) * 128)


def block(b):
    return slice(b * BW, (b + 1) * BW)


def main_kernel(
    x_hbm, w_hbm, gb_hbm, lam_hbm, cw_hbm, cb_hbm, cot_hbm,
    gi_hbm, done_hbm,
    gb_ref, lam_ref, cw_ref, cb_ref, xb, cotb, wsh, wf, wu, column, wpair, W0, W1, xhalo, nat, natc, xs, cs, mb, mt, pre,
    dec, pp, qq, m1, m2, m3, oma, hp, gp, gm, dsend, drecv, sin, ghs, ghr,
    wsend, wz, frecv, brecv, bsum, bz, own, fsum, zrecv, ssend, srecv, ssum, szrecv, fin, done, gib,
    lsem, sib_s, sib_r, c1_s, c1_r, hal_s, hal_r, za_s, za_r, c2_s, c2_r, d_s, d_r, e_s, e_r,
    f_s, f_r, b_s, b_r, fs_s, fs_r, z_s, z_r, g_s, g_r,
):
    ctx = lax.axis_index("ctx")
    d = lax.axis_index("dp")
    div, rem = lax.div, lax.rem
    p, c = div(ctx, 2), rem(ctx, 2)
    z = rem(p, DEPTH)
    y = 2 * div(p, DEPTH) + div(d, 4)
    x = rem(d, 4)
    y_hi, y_odd = div(y, 2), rem(y, 2)
    spot = 4 * y + x
    sibling = {"ctx": 2 * p + 1 - c, "dp": d}

    def chip(j):
        return {"ctx": 2 * j + c, "dp": d}

    def deep(j):
        return {"ctx": 2 * (p - z + j) + c, "dp": d}

    def peer(u):
        return {"ctx": ctx, "dp": u}

    def plane(j):
        to_x, to_y = rem(x + rem(j, 4), 4), rem(y + div(j, 4), 4)
        to_h, to_d = div(to_y, 2), 4 * rem(to_y, 2) + to_x
        return {"ctx": 2 * (DEPTH * to_h + z) + c, "dp": to_d}, to_h, to_d

    def rows16(j):
        return pl.ds(pl.multiple_of(16 * j, 16), 16)

    def send(src, dst, ss, rs, dev):
        cp = pltpu.make_async_remote_copy(
            src_ref=src, dst_ref=dst, send_sem=ss, recv_sem=rs, device_id=dev, device_id_type=MESH
        )
        cp.start()
        return cp

    bar = pltpu.get_barrier_semaphore()
    pl.semaphore_signal(bar, inc=1, device_id=sibling, device_id_type=MESH)

    @pl.loop(1, CHIPS, unroll=True)
    def _(j):
        pl.semaphore_signal(bar, inc=1, device_id=chip(rem(p + j, CHIPS)), device_id_type=MESH)

    @pl.loop(1, PLANE, unroll=True)
    def _(j):
        @pl.when(j != PLANE // 2)
        def _():
            pl.semaphore_signal(bar, inc=1, device_id=plane(j)[0], device_id_type=MESH)

    @pl.loop(1, REPL, unroll=True)
    def _(j):
        dev = {"ctx": 2 * p + 1 - c, "dp": rem(d + j, REPL)}
        pl.semaphore_signal(bar, inc=1, device_id=dev, device_id_type=MESH)

    @pl.loop(1, DEPTH, unroll=True)
    def _(j):
        dev = {"ctx": 2 * (p - z + rem(z + j, DEPTH)) + 1 - c, "dp": d}
        pl.semaphore_signal(bar, inc=1, device_id=dev, device_id_type=MESH)

    mine = pl.ds(pl.multiple_of(HALF * c, HALF), HALF)
    theirs = pl.ds(pl.multiple_of(HALF * (1 - c), HALF), HALF)
    my_rows = pl.ds(pl.multiple_of(ROWS * c, ROWS), ROWS)
    sib_rows = pl.ds(pl.multiple_of(ROWS * (1 - c), ROWS), ROWS)

    ld_w = pltpu.make_async_copy(w_hbm, wsh, lsem.at[0])
    ld_w.start()
    ld_x = pltpu.make_async_copy(x_hbm.at[0, :, mine], xb.at[my_rows], lsem.at[1])
    ld_x.start()
    ld_c = pltpu.make_async_copy(cot_hbm.at[0, :, mine], cotb.at[my_rows], lsem.at[2])
    ld_c.start()
    lds = []
    for n, (src, dst) in enumerate(
        ((gb_hbm, gb_ref), (lam_hbm, lam_ref), (cw_hbm, cw_ref), (cb_hbm, cb_ref))
    ):
        lds.append(pltpu.make_async_copy(src.at[:, mine], dst, lsem.at[5 + n]))
        lds[-1].start()
    pending = []

    def later(ref, sem):
        pending.append(lambda: wait_for(ref, sem))


    ld_w.wait()
    for i in range(8):
        for g in range(2):
            v = wsh[i, g].astype(F32)
            for lh in range(2):
                wf[lh, i * 16 + g * 8 : i * 16 + g * 8 + 8, :] = v[:, lane_tile(lh)]
    for h in range(2):
        for u in range(REPL):
            for st in range(STAGES):
                first = ((u // 2) % 2) * 8 + 4 * h + 2 * st + u // 4
                wu[h, st, u] = wf[u % 2, pl.ds(first, 8, stride=16), :]

    pl.semaphore_wait(bar, 1 + (CHIPS - 1) + (PLANE - 2) + (REPL - 1) + (DEPTH - 1))

    part = pl.ds(pl.multiple_of(8 * c, 8), 8)
    @pl.loop(1, 2 * DEPTH, unroll=True)
    def _(j):
        to_c, to_z = rem(c + div(j, DEPTH), 2), rem(z + j, DEPTH)
        dev = {"ctx": 2 * (p - z + to_z) + to_c, "dp": d}
        send(wu.at[to_c, 1, d], column.at[z, c], c1_s, c1_r, dev)

    column[z, c] = wu[c, 1, d]
    s_v = send(wu.at[1 - c, 0], wpair.at[:, part], sib_s.at[5], sib_r.at[5], sibling)
    s_x = send(x_hbm.at[0, :, theirs], xb.at[my_rows], sib_s.at[1], sib_r.at[1], sibling)
    s_c = send(cot_hbm.at[0, :, theirs], cotb.at[my_rows], sib_s.at[2], sib_r.at[2], sibling)
    others = srecv.at[pl.ds(0, 2 * DEPTH - 1)]
    later(others, c1_s)
    wpair[:, part, :] = wu[c, 0]
    s_v.wait_recv()
    for u in range(REPL):
        W1[p, u] = wpair[u].astype(BF16)
    across = rem(p + DEPTH, CHIPS)
    rows_a, rows_b = W1.at[p], W1.at[across]
    send(rows_a, rows_a, za_s.at[0], za_r.at[0], chip(across))
    later(rows_a, za_s.at[0])

    def at_depth(side, by):
        return (p - z if side == 0 else across - z) + rem(z + by + DEPTH, DEPTH)

    def near(side):
        rows = W1.at[at_depth(side, 0)]
        for by in (1, -1):
            send(rows, rows, za_s.at[1], za_r.at[1], deep(rem(z + by + DEPTH, DEPTH)))
        for by in (2, -2):
            arrive = za_r.at[2 + 2 * side + (0 if by > 0 else 1)]
            send(rows, rows, za_s.at[1], arrive, deep(rem(z + by + DEPTH, DEPTH)))

    def onward(side):
        for way, by in ((0, 1), (1, -1)):
            rows = W1.at[at_depth(side, -2 * by)]
            wait_for(rows, za_r.at[2 + 2 * side + way])
            send(rows, rows, za_s.at[1], za_r.at[1], deep(rem(z + by + DEPTH, DEPTH)))
            half = W1.at[at_depth(side, -2 * by), pl.ds(4 * way, 4)]
            send(half, half, za_s.at[1], za_r.at[1], deep(rem(z + 2 * by + DEPTH, DEPTH)))

    near(0)

    ld_x.wait()
    s_x.wait_recv()
    send(xb.at[pl.ds(SPAN - 16, 16)], xhalo, hal_s, hal_r, chip(rem(p + 1, CHIPS)))
    later(xhalo, hal_s)
    for k in range(TILES):
        nat[k] = xb[:, lane_tile(k)].astype(F32)

    @pl.loop(0, R, unroll=2)
    def _(r):
        for k in range(TILES):
            xs[3 + r, :, lane_tile(k)] = nat[k, pl.ds(r, 8, stride=R), :]

    wait_for(rows_b, za_r.at[0])

    near(1)
    later(W1.at[pl.ds(0, 14)], za_s.at[1])
    ten = W1.at[pl.ds(0, 10)]
    wait_for(others, c1_r)
    W0[d, y_hi] = column[...].reshape(128, 128).astype(BF16)
    fifteen = frecv.at[0, pl.ds(0, PLANE - 1)]
    mine_s = W0.at[d, y_hi]

    @pl.loop(1, PLANE, unroll=True)
    def _(j):
        send(mine_s, mine_s, c2_s, c2_r, plane(j)[0])

    later(fifteen, c2_s)
    onward(0)
    onward(1)
    ld_c.wait()
    s_c.wait_recv()
    for k in range(TILES):
        natc[k] = cotb[:, lane_tile(k)].astype(F32)

    @pl.loop(0, R, unroll=2)
    def _(r):
        for k in range(TILES):
            cs[r, :, lane_tile(k)] = natc[k, pl.ds(r, 8, stride=R), :]

    wait_for(xhalo, hal_r)
    hal = xhalo[...].astype(F32)
    hal = jnp.where(p == 0, jnp.zeros_like(hal), hal)
    sub = sublane((8, HALF))
    for k in range(3):
        rolled = pltpu.roll(xs[3 + R - 3 + k], 1, 0)
        xs[k] = jnp.where(sub == 0, jnp.broadcast_to(hal[13 + k : 14 + k], (8, HALF)), rolled)

    for ld in lds:
        ld.wait()
    conv_w = cw_ref[...]
    conv_b = cb_ref[...]
    for b in range(NB):
        taps = [jnp.broadcast_to(conv_w[k : k + 1, block(b)], (8, BW)) for k in range(4)]
        shift = jnp.broadcast_to(conv_b[:, block(b)], (8, BW))

        @pl.loop(0, R // 2, unroll=2)
        def _(i):
            v = [xs[2 * i + k, :, block(b)] for k in range(5)]
            out = []
            for o in range(2):
                m = shift + taps[0] * v[o]
                for k in range(1, 4):
                    m = m + taps[k] * v[o + k]
                out.append(m)
            mb[pl.ds(pl.multiple_of(16 * i, 16), 16), block(b)] = jnp.concatenate(out, 0).astype(BF16)

        mt[b] = mb[:, block(b)].astype(F32).T.astype(BF16)

    lam = lam_ref[...]
    neg8rate = -8.0 * softplus(-lam)
    gate_b = gb_ref[...]
    ends = []

    def weights(b, g):
        u = 4 * (b % 2) + 2 * g
        two = (W1[:, u + lh] if b < 2 else W0[u + lh] for lh in range(2))
        return jnp.concatenate([v.reshape(BW, 128) for v in two], 1)

    def gates(b):
        st = b // 2
        for g in range(2):
            pre[2 * b + g] = jnp.dot(mb[:, block(b)], weights(b, g), preferred_element_type=F32)
        nr = jnp.broadcast_to(neg8rate[:, block(b)], (8, BW))
        ba = jnp.broadcast_to(gate_b[0:1, block(b)], (8, BW))
        bx = jnp.broadcast_to(gate_b[1:2, block(b)], (8, BW))

        def step(i, carry):
            prod, hid, kk, logs = carry
            two = mb[pl.ds(pl.multiple_of(16 * i, 16), 16), block(b)].astype(F32)
            for o in range(2):
                r = 2 * i + o
                at = pl.ds(pl.multiple_of(8 * r, 8), 8)
                ga = sigmoid(pre[2 * b, at, :] + ba)
                gx = sigmoid(pre[2 * b + 1, at, :] + bx)
                m = two[8 * o : 8 * o + 8]
                ld = ga * nr
                a = jnp.exp(ld)
                sq = 1.0 - a * a
                mult = jnp.sqrt(sq)
                gm_ = gx * m
                drive = mult * gm_
                dec[r, :, block(b)] = a
                qq[r, :, block(b)] = gm_ * a * lax.rsqrt(jnp.maximum(sq, 0.05))
                m1[r, :, block(b)] = a * ga
                oma[r, :, block(b)] = (1.0 - ga) * nr
                m2[r, :, block(b)] = drive * (1.0 - gx)
                m3[r, :, block(b)] = mult * gx
                hp[r, :, block(b)] = hid
                pp[r, :, block(b)] = prod
                hid = a * hid + drive
                prod = prod * a
                kk = kk + prod * cs[r, :, block(b)]
                logs = logs + ld
            return prod, hid, kk, logs

        zero = jnp.zeros((8, BW), F32)
        prod, hid, kk, logs = lax.fori_loop(
            0, R // 2, step, (jnp.ones((8, BW), F32), zero, zero, zero), unroll=2
        )
        sb = sublane((8, BW))
        fp, fh = prod, hid
        bp, bk = prod, kk
        for s in (1, 2, 4):
            mp, mh = pltpu.roll(fp, s, 0), pltpu.roll(fh, s, 0)
            fh = jnp.where(sb >= s, fp * mh + fh, fh)
            fp = jnp.where(sb >= s, fp * mp, fp)
            mp, mk = pltpu.roll(bp, 8 - s, 0), pltpu.roll(bk, 8 - s, 0)
            bk = jnp.where(sb < 8 - s, bp * mk + bk, bk)
            bp = jnp.where(sb < 8 - s, bp * mp, bp)
            logs = logs + pltpu.roll(logs, s, 0)
        one = jnp.ones((8, BW), F32)
        ends.append((
            jnp.where(sb == 0, one, pltpu.roll(fp, 1, 0)),
            jnp.where(sb == 0, zero, pltpu.roll(fh, 1, 0)),
            jnp.where(sb == 7, one, pltpu.roll(bp, 7, 0)),
            jnp.where(sb == 7, zero, pltpu.roll(bk, 7, 0)),
        ))
        for lh in range(2):
            k = 2 * (b % 2) + lh
            dsend[st, 0, k : k + 1, :] = logs[0:1, lane_tile(lh)]
            dsend[st, 1, k : k + 1, :] = logs[0:1, lane_tile(lh)]
            dsend[st, 0, 4 + k : 5 + k, :] = fh[7:8, lane_tile(lh)]
            dsend[st, 1, 4 + k : 5 + k, :] = bk[0:1, lane_tile(lh)]

    for st in range(STAGES):
        wait_for(*((ten, za_r.at[1]) if st == 0 else (fifteen, c2_r)))
        for b in (2 * st, 2 * st + 1):
            gates(b)

        @pl.loop(1, CHIPS, unroll=True)
        def _(j):
            to = rem(p + j, CHIPS)
            send(dsend.at[st, jnp.where(to > p, 0, 1)], drecv.at[st, p], d_s.at[st], d_r.at[st], chip(to))

        later(drecv.at[st, pl.ds(0, CHIPS - 1)], d_s.at[st])
        drecv[st, p] = jnp.zeros((8, 128), F32)

    sums = []

    def grads(b):
        st, k = b // 2, 2 * (b % 2)

        def wide(n):
            return jnp.concatenate(
                [jnp.broadcast_to(sin[st, n, k + lh : k + lh + 1, :], (8, 128)) for lh in range(2)], 1
            )

        hin = ends[b][1] + ends[b][0] * wide(0)
        kin = ends[b][3] + ends[b][2] * wide(1)

        def down(n, carry):
            kk, t_sum, a_sum, x_sum = carry
            i = R // 2 - 1 - n
            outs = [[None, None], [None, None]]
            for o in (1, 0):
                r = 2 * i + o
                gr = cs[r, :, block(b)] + kk
                kk = dec[r, :, block(b)] * gr
                before = hp[r, :, block(b)] + pp[r, :, block(b)] * hin
                t = (before - qq[r, :, block(b)]) * m1[r, :, block(b)] * gr
                ga = t * oma[r, :, block(b)]
                gx = gr * m2[r, :, block(b)]
                gm[r, :, block(b)] = gr * m3[r, :, block(b)]
                t_sum, a_sum, x_sum = t_sum + t, a_sum + ga, x_sum + gx
                outs[0][o], outs[1][o] = ga, gx
            at = pl.ds(pl.multiple_of(16 * i, 16), 16)
            gp[2 * b, at, :] = jnp.concatenate(outs[0], 0).astype(BF16)
            gp[2 * b + 1, at, :] = jnp.concatenate(outs[1], 0).astype(BF16)
            return kk, t_sum, a_sum, x_sum

        zero = jnp.zeros((8, BW), F32)
        _, t_sum, a_sum, x_sum = lax.fori_loop(0, R // 2, down, (kin, zero, zero, zero), unroll=4)
        sums.append([t_sum, a_sum, x_sum])
        for g in range(2):
            grad = jnp.dot(mt[b], gp[2 * b + g], preferred_element_type=F32).astype(BF16)
            for lh in range(2):
                for h in range(2):
                    if b == 1:
                        for j in range(DEPTH):
                            wz[j, h, 2 * g + lh] = grad[128 * h + 16 * j : 128 * h + 16 * j + 16, lane_tile(lh)]
                    else:
                        wsend[st, 2 * (k + g) + lh, h] = grad[128 * h : 128 * (h + 1), lane_tile(lh)]

    def through(b):
        nt = (((1,), (1,)), ((), ()))
        back = lax.dot_general(gp[2 * b], weights(b, 0), nt, preferred_element_type=F32)
        back = back + lax.dot_general(gp[2 * b + 1], weights(b, 1), nt, preferred_element_type=F32)
        gm[0:R, :, block(b)] = gm[0:R, :, block(b)] + back.reshape(R, 8, BW)

    sig = 1.0 / (1.0 + jnp.exp(lam))

    def small_sums(b):
        def add(r, carry):
            g = gm[r, :, block(b)]
            return tuple(carry[k] + g * xs[r + k, :, block(b)] for k in range(4)) + (carry[4] + g,)

        zero = jnp.zeros((8, BW), F32)
        acc = lax.fori_loop(0, R, add, (zero,) * 5, unroll=4)
        t_sum, a_sum, x_sum = sums[b]
        t_sum = t_sum * (8.0 * jnp.broadcast_to(sig[:, block(b)], (8, BW)))
        sb = sublane((8, BW))
        rows = zero
        for n, v in enumerate((t_sum, a_sum, x_sum) + tuple(acc)):
            for s in (1, 2, 4):
                v = v + pltpu.roll(v, s, 0)
            rows = jnp.where(sb == n, v, rows)
        for lh in range(2):
            ssend[2 * b + lh] = rows[:, lane_tile(lh)]

    for st in range(STAGES):
        wait_for(drecv.at[st, pl.ds(0, CHIPS - 1)], d_r.at[st])
        state = jnp.zeros((4, 128), F32)
        carry_in = jnp.zeros((4, 128), F32)
        for j in range(CHIPS):
            v = drecv[st, j]
            state = jnp.where(j < p, jnp.exp(v[:4]) * state + v[4:], state)
            v = drecv[st, CHIPS - 1 - j]
            carry_in = jnp.where(CHIPS - 1 - j > p, jnp.exp(v[:4]) * carry_in + v[4:], carry_in)
        sin[st, 0] = state
        sin[st, 1] = carry_in
        def to_plane(low):
            @pl.loop(1, PLANE, unroll=True)
            def _(j):
                dev, to_h, to_d = plane(j)

                @pl.when(to_d < 4 if low else to_d >= 4)
                def _():
                    send(
                        wsend.at[st, to_d, to_h], frecv.at[st, spot], f_s.at[st], f_r.at[st], dev
                    )

        grads(2 * st)
        to_plane(True)
        grads(2 * st + 1)
        if st == 0:
            @pl.when(y_odd == 0)
            def _():
                frecv[0, spot] = wsend[0, d, y_hi]

            @pl.loop(1, DEPTH, unroll=True)
            def _(j):
                to = rem(z + j, DEPTH)
                send(wz.at[to], brecv.at[z], b_s.at[0], b_r.at[0], deep(to))

            later(brecv.at[pl.ds(0, DEPTH - 1)], b_s.at[0])
            brecv[z] = wz[z]
        else:
            to_plane(False)
            later(fifteen, f_s.at[1])
            frecv[1, spot] = wsend[1, d, y_hi]

    for b in range(NB):
        through(b)
        small_sums(b)

    @pl.loop(1, PLANE, unroll=True)
    def _(j):
        dev, _, to_d = plane(j)
        send(ssend.at[to_d], srecv.at[spot], fs_s.at[0], fs_r.at[0], dev)

    later(srecv.at[pl.ds(0, PLANE - 1)], fs_s.at[0])
    for k in range(3):
        ghs[k : k + 1, :] = gm[k, 0:1, :]
    send(ghs, ghr, e_s, e_r, chip(rem(p + CHIPS - 1, CHIPS)))
    later(ghr, e_s)
    srecv[spot] = ssend[d]

    def fold(st):
        wait_for(fifteen, f_r.at[st])

        @pl.loop(0, DEPTH, unroll=4)
        def _(i):
            at = rows16(i)
            v = frecv[st, 0, at, :].astype(F32)
            for u in range(1, PLANE):
                v = v + frecv[st, u, at, :].astype(F32)
            fsum[st, i] = v.astype(BF16)

        @pl.loop(1, DEPTH, unroll=True)
        def _(j):
            to = rem(z + j, DEPTH)
            send(fsum.at[st, to], zrecv.at[st, z], z_s.at[st], z_r.at[st], deep(to))

        zrecv[st, z] = fsum[st, z]

    pl.when(y_odd == 0)(lambda: fold(0))
    wait_for(brecv.at[pl.ds(0, DEPTH - 1)], b_r.at[0])
    for h in range(2):
        for t in range(4):
            v = brecv[0, h, t].astype(F32)
            for j in range(1, DEPTH):
                v = v + brecv[j, h, t].astype(F32)
            bsum[h, t] = v.astype(BF16)

    @pl.loop(1, PLANE, unroll=True)
    def _(j):
        dev, to_h, to_d = plane(j)

        @pl.when(to_d >= 4)
        def _():
            send(bsum.at[to_h, rem(to_d, 4)], bz.at[spot], b_s.at[1], b_r.at[1], dev)

    @pl.when(y_odd == 1)
    def _():
        bz[spot] = bsum[y_hi, x]

    fold(1)
    wait_for(srecv.at[pl.ds(0, PLANE - 1)], fs_r.at[0])
    ssum[...] = jnp.sum(srecv[...], 0)

    @pl.loop(1, DEPTH, unroll=True)
    def _(j):
        send(ssum, szrecv.at[z], fs_s.at[1], fs_r.at[1], deep(rem(z + j, DEPTH)))

    later(szrecv.at[pl.ds(0, DEPTH - 1)], fs_s.at[1])
    szrecv[z] = ssum[...]

    wait_for(ghr, e_r)
    halo = ghr[...]
    halo = jnp.where(p == CHIPS - 1, jnp.zeros_like(halo), halo)
    for k in range(3):
        rolled = pltpu.roll(gm[k], 7, 0)
        gm[R + k] = jnp.where(sub == 7, jnp.broadcast_to(halo[k : k + 1], (8, HALF)), rolled)

    for b in range(NB):
        taps = [jnp.broadcast_to(conv_w[k : k + 1, block(b)], (8, BW)) for k in range(4)]

        @pl.loop(0, R, unroll=4)
        def _(r):
            v = taps[0] * gm[r + 3, :, block(b)]
            for k in range(1, 4):
                v = v + taps[k] * gm[r + 3 - k, :, block(b)]
            for lh in range(2):
                nat[2 * b + lh, pl.ds(r, 8, stride=R), :] = v[:, lane_tile(lh)]

    for k in range(TILES):
        gib[:, lane_tile(k)] = nat[k].astype(BF16)
    s_g = send(gib.at[sib_rows], gi_hbm.at[:, mine], sib_s.at[3], sib_r.at[3], sibling)
    st_g = pltpu.make_async_copy(gib.at[my_rows], gi_hbm.at[:, mine], lsem.at[3])
    st_g.start()
    later(gib.at[my_rows], lsem.at[3])
    later(zrecv.at[1, pl.ds(0, DEPTH - 1)], z_s.at[1])

    @pl.when(y_odd == 0)
    def _():
        wait_for(zrecv.at[0, pl.ds(0, DEPTH - 1)], z_s.at[0])
        wait_for(zrecv.at[0, pl.ds(0, DEPTH - 1)], z_r.at[0])
        wait_for(frecv.at[0, pl.ds(0, 7)], f_s.at[0])
        wait_for(bz.at[pl.ds(0, 8)], b_s.at[1])

    @pl.when(y_odd == 1)
    def _():
        wait_for(bz.at[pl.ds(0, PLANE - 1)], b_r.at[1])
        wait_for(frecv.at[0, pl.ds(0, 8)], f_s.at[0])
        wait_for(bz.at[pl.ds(0, 7)], b_s.at[1])


    def total(st, parts, count):
        whole = parts(0).astype(F32)
        for j in range(1, count):
            whole = whole + parts(j).astype(F32)
        own[st] = whole

    pl.when(y_odd == 0)(lambda: total(0, lambda j: zrecv[0, j], DEPTH))
    pl.when(y_odd == 1)(lambda: total(0, lambda j: bz[j], PLANE))
    wait_for(szrecv.at[pl.ds(0, DEPTH - 1)], fs_r.at[1])
    fin[...] = jnp.sum(szrecv[...], 0)
    wait_for(zrecv.at[1, pl.ds(0, DEPTH - 1)], z_r.at[1])
    total(1, lambda j: zrecv[1, j], DEPTH)
    for core in range(2):
        for st in range(STAGES):
            done[core, st] = own[st, 8 * core : 8 * core + 8, :]
        done[core, STAGES] = fin[...]
    keep = pltpu.make_async_copy(done.at[c], done_hbm.at[c, d], lsem.at[9])
    keep.start()

    @pl.loop(1, 2 * REPL, unroll=True)
    def _(j):
        to_c = rem(c + div(j, REPL), 2)
        dev = {"ctx": 2 * p + to_c, "dp": rem(d + j, REPL)}
        send(done.at[to_c], done_hbm.at[c, d], g_s, g_r, dev)

    triples = frecv.at[0, pl.ds(0, 2 * REPL - 1), pl.ds(0, 48)]
    later(triples, g_s)
    later(triples, g_r)
    for cp in [s_v, s_x, s_c, s_g]:
        cp.wait_send()
    s_g.wait_recv()
    for finish_one in pending:
        finish_one()
    keep.wait()


def last_kernel(
    gi_in, done_in, gi_out, gw_out, dec_out, bias_out, taps_out, shift_out,
    done, gws, gw, dec, bias, taps, shift, via, l_sem, s_sem,
):
    get = pltpu.make_async_copy(done_in, done, l_sem.at[4])
    get.start()
    parts = [pl.ds(k * (ROWS // 4), ROWS // 4) for k in range(4)]
    loads = [pltpu.make_async_copy(gi_in.at[at], via.at[at], l_sem.at[k]) for k, at in enumerate(parts)]
    stores = [pltpu.make_async_copy(via.at[at], gi_out.at[0, at], s_sem.at[k]) for k, at in enumerate(parts)]
    for cp in loads:
        cp.start()
    get.wait()
    for h in range(2):
        for u in range(8):
            at = slice(h * HALF + 128 * u, h * HALF + 128 * (u + 1))
            v = done[h, u, STAGES]
            dec[:, at] = v[0:1]
            bias[:, at] = v[1:3]
            taps[:, at] = v[3:7]
            shift[:, at] = v[7:8]
            for st in range(STAGES):
                first = ((u // 2) % 2) * 8 + 4 * h + 2 * st + u // 4
                gws[u % 2, pl.ds(first, 8, stride=16), :] = done[h, u, st]
    for n, (src, dst) in enumerate(((dec, dec_out), (bias, bias_out), (taps, taps_out), (shift, shift_out))):
        stores.append(pltpu.make_async_copy(src, dst, s_sem.at[4 + n]))
        stores[-1].start()
    for k in range(4):
        loads[k].wait()
        stores[k].start()
    for i in range(8):
        for g in range(2):
            for lh in range(2):
                gw[i, g, :, lane_tile(lh)] = gws[lh, i * 16 + g * 8 : i * 16 + g * 8 + 8, :]
    stores.append(pltpu.make_async_copy(gw, gw_out, s_sem.at[8]))
    stores[-1].start()
    for cp in stores:
        cp.wait()


def per_device(inputs, gate_weight, gate_bias, decay_param, conv_weight, conv_bias, cotangent):
    hbm = pl.BlockSpec(memory_space=pltpu.HBM)
    dma = pltpu.SemaphoreType.DMA
    big = pltpu.VMEM((R, 8, HALF), F32)
    gi, done = pl.pallas_call(
        main_kernel,
        name="main",
        out_shape=(
            jax.ShapeDtypeStruct((ROWS, WIDTH), BF16),
            jax.ShapeDtypeStruct((2, REPL, STAGES + 1, 8, 128), F32),
        ),
        in_specs=[hbm] * 7,
        out_specs=(hbm,) * 2,
        scratch_shapes=[
            pltpu.VMEM((2, HALF), F32),
            pltpu.VMEM((1, HALF), F32),
            pltpu.VMEM((4, HALF), F32),
            pltpu.VMEM((1, HALF), F32),
            pltpu.VMEM((SPAN, HALF), BF16),
            pltpu.VMEM((SPAN, HALF), BF16),
            pltpu.VMEM((8, 2, 8, BW), BF16),
            pltpu.VMEM((2, 128, 128), F32),
            pltpu.VMEM((2, STAGES, REPL, 8, 128), F32),
            pltpu.VMEM((DEPTH, 2, 8, 128), F32),
            pltpu.VMEM((REPL, 16, 128), F32),
            pltpu.VMEM((REPL, 2, 128, 128), BF16),
            pltpu.VMEM((CHIPS, REPL, 16, 128), BF16),
            pltpu.VMEM((16, HALF), BF16),
            pltpu.VMEM((TILES, SPAN, 128), F32),
            pltpu.VMEM((TILES, SPAN, 128), F32),
            pltpu.VMEM((R + 3, 8, HALF), F32),
            big,
            pltpu.VMEM((SPAN, HALF), BF16),
            pltpu.VMEM((NB, BW, SPAN), BF16),
            pltpu.VMEM((8, SPAN, BW), F32),
            big, big, big, big, big, big, big, big,
            pltpu.VMEM((8, SPAN, BW), BF16),
            pltpu.VMEM((R + 3, 8, HALF), F32),
            pltpu.VMEM((STAGES, 2, 8, 128), F32),
            pltpu.VMEM((STAGES, CHIPS, 8, 128), F32),
            pltpu.VMEM((STAGES, 2, 4, 128), F32),
            pltpu.VMEM((8, HALF), F32),
            pltpu.VMEM((8, HALF), F32),
            pltpu.VMEM((STAGES, REPL, 2, 128, 128), BF16),
            pltpu.VMEM((DEPTH, 2, 4, 16, 128), BF16),
            pltpu.VMEM((STAGES, PLANE, 128, 128), BF16),
            pltpu.VMEM((DEPTH, 2, 4, 16, 128), BF16),
            pltpu.VMEM((2, 4, 16, 128), BF16),
            pltpu.VMEM((PLANE, 16, 128), BF16),
            pltpu.VMEM((STAGES, 16, 128), F32),
            pltpu.VMEM((STAGES, DEPTH, 16, 128), BF16),
            pltpu.VMEM((STAGES, DEPTH, 16, 128), BF16),
            pltpu.VMEM((8, 8, 128), F32),
            pltpu.VMEM((PLANE, 8, 128), F32),
            pltpu.VMEM((8, 128), F32),
            pltpu.VMEM((DEPTH, 8, 128), F32),
            pltpu.VMEM((8, 128), F32),
            pltpu.VMEM((2, STAGES + 1, 8, 128), F32),
            pltpu.VMEM((SPAN, HALF), BF16),
            dma((10,)), dma((7,)), dma((7,)),
            dma, dma, dma, dma, dma((2,)), dma((6,)), dma, dma,
            dma((STAGES,)), dma((STAGES,)), dma, dma, dma((STAGES,)), dma((STAGES,)),
            dma((2,)), dma((2,)), dma((2,)), dma((2,)),
            dma((STAGES,)), dma((STAGES,)), dma, dma,
        ],
        compiler_params=pltpu.CompilerParams(
            collective_id=0, has_side_effects=True, vmem_limit_bytes=60 * 2**20
        ),
    )(
        inputs, gate_weight, gate_bias, decay_param.reshape(1, WIDTH), conv_weight,
        conv_bias.reshape(1, WIDTH), cotangent,
    )
    gi, gw, dec, bias, taps, shift = pl.pallas_call(
        last_kernel,
        name="last",
        out_shape=(
            jax.ShapeDtypeStruct((1, ROWS, WIDTH), BF16),
            jax.ShapeDtypeStruct((8, 2, 8, BW), F32),
            jax.ShapeDtypeStruct((1, WIDTH), F32),
            jax.ShapeDtypeStruct((2, WIDTH), F32),
            jax.ShapeDtypeStruct((4, WIDTH), F32),
            jax.ShapeDtypeStruct((1, WIDTH), F32),
        ),
        in_specs=[hbm] * 2,
        out_specs=(hbm,) * 6,
        scratch_shapes=[
            pltpu.VMEM((2, REPL, STAGES + 1, 8, 128), F32),
            pltpu.VMEM((2, 128, 128), F32),
            pltpu.VMEM((8, 2, 8, BW), F32),
            pltpu.VMEM((1, WIDTH), F32),
            pltpu.VMEM((2, WIDTH), F32),
            pltpu.VMEM((4, WIDTH), F32),
            pltpu.VMEM((1, WIDTH), F32),
            pltpu.VMEM((ROWS, WIDTH), BF16),
            dma((5,)),
            dma((9,)),
        ],
        compiler_params=pltpu.CompilerParams(vmem_limit_bytes=60 * 2**20),
    )(gi, done)
    return gi, gw, dec.reshape(WIDTH), bias, taps, shift.reshape(WIDTH)


def solution(mesh):
    placed = (
        P("dp", "ctx", None),
        P("ctx", None, None, None),
        P(),
        P(),
        P(),
        P(),
        P("dp", "ctx", None),
    )
    return jax.shard_map(
        per_device,
        mesh=mesh,
        in_specs=placed,
        out_specs=(P("dp", "ctx", None), P("ctx", None, None, None), P(), P(), P(), P()),
        check_vma=False,
    )
```
